32 devices in a mesh: doc: 4 (over y, x), tm: 8 (over z, core).
Axes of the slice: x: 2, y: 2, z: 4, core: 2. Of those that a mesh axis runs over, the one named last changes fastest.
Arguments:
- tokens: bfloat16 [2, 4, 1024, 1024], P(None, 'doc', 'tm'), may hold values from -6 to 6
- cotangent: bfloat16 [2, 4, 1024, 1024], P(None, 'doc', 'tm'), may hold values from -6 to 6
- given_cache: bfloat16 [2, 4, 8192, 896], P(None, 'doc', 'tm'), may hold values from -6 to 6
- value_routes: int32 [2, 4, 1024, 4, 2], P(None, 'doc', 'tm'), may hold values from 0 to 4, all different within a row
- output_routes: int32 [2, 4, 1024, 4, 2], P(None, 'doc', 'tm'), may hold values from 0 to 4, all different within a row
- valid_counts: int32 [2, 4, 8], P(None, 'doc', 'tm'), may hold values from 1 to 128, as said below
- doc_starts: int32 [2, 4, 8], P(None, 'doc', 'tm'), may hold values from 0 to 1, as said below
- norm1_gain: bfloat16 [1024], P(('doc', 'tm')), may hold values from 0.5 to 1.5
- norm1_shift: bfloat16 [1024], P(('doc', 'tm')), may hold values from -1 to 1
- qk_weight: bfloat16 [1024, 896], P(('doc', 'tm')), may hold values from -0.1875 to 0.1875
- router_weight: bfloat16 [1024, 40], P(('doc', 'tm')), may hold values from -0.125 to 0.125
- value_weight: bfloat16 [1024, 2240], P(('doc', 'tm')), may hold values from -0.1875 to 0.1875
- output_weight: bfloat16 [2240, 1024], P(None, ('doc', 'tm')), may hold values from -2 to 2
- rel_bias: bfloat16 [4, 256], P(None, ('doc', 'tm')), may hold values from -4 to 4
- norm2_gain: bfloat16 [1024], P(('doc', 'tm')), may hold values from 0.5 to 1.5
- norm2_shift: bfloat16 [1024], P(('doc', 'tm')), may hold values from -1 to 1
- ffn_in: bfloat16 [1024, 4096], P(('doc', 'tm')), may hold values from -0.1875 to 0.1875
- ffn_out: bfloat16 [4096, 1024], P(('doc', 'tm')), may hold values from -0.09375 to 0.09375
Outputs:
- layer_out: bfloat16 [2, 4, 1024, 1024], P(None, 'doc', 'tm')
- input_grad: float32 [2, 4, 1024, 1024], P(None, 'doc', 'tm')
- norm1_gain_grad: float32 [1024], P(('doc', 'tm'))
- norm1_shift_grad: float32 [1024], P(('doc', 'tm'))
- qk_weight_grad: float32 [1024, 896], P(('doc', 'tm'))
- router_weight_grad: float32 [1024, 40], P(('doc', 'tm'))
- value_weight_grad: float32 [1024, 2240], P(('doc', 'tm'))
- output_weight_grad: float32 [2240, 1024], P(None, ('doc', 'tm'))
- rel_bias_grad: float32 [4, 256], P(None, ('doc', 'tm'))
- norm2_gain_grad: float32 [1024], P(('doc', 'tm'))
- norm2_shift_grad: float32 [1024], P(('doc', 'tm'))
- ffn_in_grad: float32 [1024, 4096], P(('doc', 'tm'))
- ffn_out_grad: float32 [4096, 1024], P(('doc', 'tm'))
The draws below stay inside these ranges and needn't reach their ends.
Inputs may be any that keep to these rules, and one draw needn't show every extreme that they name: `doc_starts`: 1 marks a block where a document begins; the first block of every row is 1, and so is every block after one with fewer than 128 valid tokens. `valid_counts`: the valid tokens lead their block; fewer than 128 only in the last block of a document. `value_routes`: the 2 experts of a token and head differ. `output_routes`: the 2 experts of a token and head differ.
All inputs are finite; a program needn't handle non-finite values.
Results may differ from the reference program's by a relative error of at most 0.017.
Values may be sent and summed in bfloat16 or wider, within the bound.
A program may use at most 320 MiB of HBM per device.

```python
import jax
import jax.numpy as jnp
from jax import lax

D = 1024
HEADS = 4
HEAD_DIM = 112
EXPERTS = 5
TOPK = 2
FF = 4096
MEM = 1024
BLOCK = 128
MICRO = 2
BUCKETS = 256
NEAR = 128
STEP = 16
DOC_ROWS = 4
LENGTH = 1024


def document_layout(key):
    blocks = LENGTH // BLOCK
    full_pick = jax.random.randint(jax.random.fold_in(key, 11), (DOC_ROWS,), 0, MICRO)
    coins = jax.random.randint(jax.random.fold_in(key, 12), (MICRO, DOC_ROWS, blocks), 0, 4)
    block_ids = jnp.arange(blocks, dtype=jnp.int32)[None, None, :]
    whole_doc = (jnp.arange(MICRO, dtype=jnp.int32)[:, None] == full_pick[None, :])[:, :, None]
    random_starts = (coins == 0).astype(jnp.int32)
    starts = jnp.where(block_ids == 0, 1, jnp.where(whole_doc, 0, random_starts)).astype(jnp.int32)
    following = jnp.concatenate([starts[:, :, 1:], jnp.ones_like(starts[:, :, :1])], axis=2)
    raw_draw = jax.random.randint(jax.random.fold_in(key, 13), (MICRO, DOC_ROWS, blocks), 0, BLOCK)
    tail_len = 1 + raw_draw * raw_draw // BLOCK
    counts = jnp.where(following > 0, tail_len, BLOCK).astype(jnp.int32)
    return (starts, counts)


def draw_doc_starts(key, part):
    starts, counts = document_layout(key)
    return starts


def draw_valid_counts(key, part):
    starts, counts = document_layout(key)
    return counts


def steps_of(own_key, dims, shards, least, top_value):
    level, own = 1.0, jax.random.fold_in(own_key, 6)
    for axis_at, blocks in shards:
        draws = jnp.exp(jax.random.uniform(jax.random.fold_in(own, axis_at), (blocks,), jnp.float32, least / len(shards), top_value / len(shards)))
        level = level * jnp.repeat(draws, dims[axis_at] // blocks).reshape([-1 if axis == axis_at else 1 for axis in range(len(dims))])
    return level


def different_ones(key, rows, count, top, lift):
    sequence = jax.random.permutation(jax.random.fold_in(key, 1), count)
    boost = sequence
    for power in range(3):
        boost = boost * boost // count
    boost = boost * lift // count
    tickets = jax.random.randint(jax.random.fold_in(key, 2), (rows, count), 0, 4096) + boost
    fixed_rows = jax.random.permutation(jax.random.fold_in(key, 3), rows)[jnp.arange(count) % rows]
    tickets = jnp.where(jnp.arange(rows)[:, None] == fixed_rows[None, :], 1 << 14, tickets)
    priority = tickets * count + jnp.arange(count)
    return lax.top_k(priority.astype(jnp.int32), top)[1].astype(jnp.int32)


def normal_values(key, dims, scale, bound, pieces=(), held_as=jnp.bfloat16):
    drawn = scale * jax.random.normal(key, dims, jnp.float32)
    if pieces:
        drawn = drawn * steps_of(key, dims, pieces, -0.22, 0.18)
    return jnp.clip(drawn, -bound, bound).astype(held_as)


def setup_inputs(seed: int = 0) -> dict:
    seeds = jax.random.split(jax.random.key(seed), 19)
    tokens = normal_values(seeds[0], (MICRO, DOC_ROWS, LENGTH, D), 1.0, 6.0, ((1, 4), (2, 8)))
    cotangent = normal_values(seeds[1], (MICRO, DOC_ROWS, LENGTH, D), 1.0, 6.0, ((1, 4), (2, 8)))
    given_cache = normal_values(seeds[2], (MICRO, DOC_ROWS, LENGTH // BLOCK * MEM, 2 * HEADS * HEAD_DIM), 1.0, 6.0, ((1, 4), (2, 8)))
    value_routes = different_ones(seeds[3], MICRO * DOC_ROWS * LENGTH * HEADS, EXPERTS, TOPK, 3276).reshape((MICRO, DOC_ROWS, LENGTH, HEADS, TOPK))
    output_routes = different_ones(seeds[4], MICRO * DOC_ROWS * LENGTH * HEADS, EXPERTS, TOPK, 3276).reshape((MICRO, DOC_ROWS, LENGTH, HEADS, TOPK))
    valid_counts = draw_valid_counts(jax.random.fold_in(seeds[18], 71), 0)
    doc_starts = draw_doc_starts(jax.random.fold_in(seeds[18], 71), 0)
    norm1_gain = jnp.clip(1.0 + 0.1 * jax.random.normal(seeds[7], (D,), jnp.float32), 0.5, 1.5).astype(jnp.bfloat16)
    norm1_shift = normal_values(seeds[8], (D,), 0.2, 1.0, ((0, 32),))
    qk_weight = normal_values(seeds[9], (D, 2 * HEADS * HEAD_DIM), D ** -0.5, 0.1875, ((0, 32),))
    router_weight = normal_values(seeds[10], (D, 2 * HEADS * EXPERTS), (2 * D) ** -0.5, 0.125, ((0, 32),))
    value_weight = normal_values(seeds[11], (D, EXPERTS * HEADS * HEAD_DIM), D ** -0.5, 0.1875, ((0, 32),))
    output_weight = normal_values(seeds[12], (EXPERTS * HEADS * HEAD_DIM, D), (HEAD_DIM // 16) ** -0.5, 2.0, ((1, 32),))
    rel_bias = normal_values(seeds[13], (HEADS, BUCKETS), 1.0, 4.0, ((1, 32),))
    norm2_gain = jnp.clip(1.0 + 0.1 * jax.random.normal(seeds[14], (D,), jnp.float32), 0.5, 1.5).astype(jnp.bfloat16)
    norm2_shift = normal_values(seeds[15], (D,), 0.2, 1.0, ((0, 32),))
    ffn_in = normal_values(seeds[16], (D, FF), D ** -0.5, 0.1875, ((0, 32),))
    ffn_out = normal_values(seeds[17], (FF, D), FF ** -0.5, 0.09375, ((0, 32),))
    return dict(tokens=tokens, cotangent=cotangent, given_cache=given_cache, value_routes=value_routes, output_routes=output_routes, valid_counts=valid_counts, doc_starts=doc_starts, norm1_gain=norm1_gain, norm1_shift=norm1_shift, qk_weight=qk_weight, router_weight=router_weight, value_weight=value_weight, output_weight=output_weight, rel_bias=rel_bias, norm2_gain=norm2_gain, norm2_shift=norm2_shift, ffn_in=ffn_in, ffn_out=ffn_out)


@jax.custom_vjp
def low(v):
    return lax.optimization_barrier(v.astype(jnp.bfloat16)).astype(jnp.float32)

@jax.custom_vjp
def low_back(v):
    return v

def low_keep(v):
    return (low(v), None)

def low_pass(kept, grad):
    return (grad,)

def back_keep(v):
    return (v, None)

def back_low(kept, grad):
    return (low(grad),)
low.defvjp(low_keep, low_pass)
low_back.defvjp(back_keep, back_low)
EPS = 1e-05
NEG = -1e+30
HIGH = lax.Precision.HIGHEST

def matmul(left, right):
    return jnp.dot(left, right, precision=HIGH, preferred_element_type=jnp.float32)

def layer_norm(values, gain, shift):
    center_mean = lax.optimization_barrier(jnp.mean(values, axis=-1, keepdims=True))
    centered = values - center_mean
    variance = lax.optimization_barrier(jnp.mean(centered * centered, axis=-1, keepdims=True))
    return centered * lax.rsqrt(variance + EPS) * gain + shift

def selection(routes):
    expert_ids = jnp.arange(EXPERTS, dtype=jnp.int32)
    return lax.optimization_barrier(jnp.sum((routes[..., None] == expert_ids).astype(jnp.float32), axis=-2))

def bucket_index(distance):
    far_bucket = NEAR + (distance - NEAR) // STEP
    return jnp.clip(jnp.where(distance < NEAR, distance, far_bucket), 0, BUCKETS - 1).astype(jnp.int32)

def front(inputs, params, value_pick, output_pick):
    gain_one, shift_one, qk_weight, router_weight, value_weight = params[:5]
    total = inputs.shape[0]
    inner = HEADS * HEAD_DIM
    normed = low(layer_norm(inputs, gain_one, shift_one))
    projected = low(low_back(matmul(normed, qk_weight)))
    gates = jax.nn.sigmoid(matmul(normed, router_weight))
    gate_value = gates[:, :HEADS * EXPERTS].reshape(total, HEADS, EXPERTS) * value_pick
    gate_output = gates[:, HEADS * EXPERTS:].reshape(total, HEADS, EXPERTS) * output_pick
    parts = low_back(matmul(normed, value_weight)).reshape(total, EXPERTS, HEADS, HEAD_DIM)
    values = lax.optimization_barrier(jnp.sum(jnp.transpose(gate_value, (0, 2, 1))[..., None] * parts, axis=1))
    values = low(low_back(values.reshape(total, inner)))
    return (projected, values, gate_output)

def block_attention(queries, keys, vals, memory, count, rel_bias):
    inner = HEADS * HEAD_DIM
    local_len = queries.shape[0]
    keys = jnp.concatenate([memory[:, :inner].reshape(MEM, HEADS, HEAD_DIM), keys], axis=0)
    vals = jnp.concatenate([memory[:, inner:].reshape(MEM, HEADS, HEAD_DIM), vals], axis=0)
    raw = low_back(jnp.einsum('qhd,khd->hqk', queries, keys, precision=HIGH) * HEAD_DIM ** (-0.5))
    row_ids = jnp.arange(local_len, dtype=jnp.int32)[:, None]
    col_ids = jnp.arange(MEM + local_len, dtype=jnp.int32)[None, :]
    bias = jnp.take(rel_bias, bucket_index(MEM + row_ids - col_ids), axis=1)
    own_ids = col_ids - MEM
    valid = jnp.logical_or(col_ids < MEM, jnp.logical_and(own_ids <= row_ids, own_ids < count))
    scores = jnp.where(valid, raw + bias, NEG)
    top = lax.optimization_barrier(jnp.max(scores, axis=-1, keepdims=True))
    expo = jnp.exp(scores - top)
    probs = low(expo / lax.optimization_barrier(jnp.sum(expo, axis=-1, keepdims=True)))
    attended = jnp.einsum('hqk,khd->qhd', probs, vals, precision=HIGH)
    return low(low_back(attended.reshape(local_len, inner)))

def layer_forward(inputs, params, source, memory_rows, counts, value_pick, output_pick, valid):
    output_weight, rel_bias, gain_two, shift_two, ffn_in, ffn_out = params[5:]
    total = inputs.shape[0]
    blocks = counts.shape[0]
    local_len = total // blocks
    inner = HEADS * HEAD_DIM
    projected, values, gate_output = front(inputs, params, value_pick, output_pick)
    queries = projected[:, :inner].reshape(blocks, local_len, HEADS, HEAD_DIM)
    keys = projected[:, inner:].reshape(blocks, local_len, HEADS, HEAD_DIM)
    vals = values.reshape(blocks, local_len, HEADS, HEAD_DIM)

    def attend_one(item):
        query_part, key_part, value_part, rows, count = item
        memory = jnp.take(source, rows, axis=0)
        return block_attention(query_part, key_part, value_part, memory, count, rel_bias)
    attended = lax.map(jax.checkpoint(attend_one), (queries, keys, vals, memory_rows, counts))
    attended = attended.reshape(total, inner)
    mixed = jnp.transpose(gate_output, (0, 2, 1))[..., None] * attended.reshape(total, 1, HEADS, HEAD_DIM)
    mixed = low(low_back(mixed.reshape(total, EXPERTS * inner)))
    hidden = inputs + low_back(matmul(mixed, output_weight))
    normed = low(layer_norm(hidden, gain_two, shift_two))
    pre_act = low_back(matmul(normed, ffn_in))
    activated = low(jax.nn.gelu(pre_act, approximate=False))
    return valid * (hidden + low_back(matmul(activated, ffn_out)))

def reference(tokens, cotangent, given_cache, value_routes, output_routes, valid_counts, doc_starts, norm1_gain, norm1_shift, qk_weight, router_weight, value_weight, output_weight, rel_bias, norm2_gain, norm2_shift, ffn_in, ffn_out):
    params = tuple((weight.astype(jnp.float32) for weight in (norm1_gain, norm1_shift, qk_weight, router_weight, value_weight, output_weight, rel_bias, norm2_gain, norm2_shift, ffn_in, ffn_out)))
    micro_count, row_count, length, width = tokens.shape
    blocks = valid_counts.shape[2]
    local_len = length // blocks
    lanes = micro_count * row_count
    cache_width = given_cache.shape[3]
    inner = HEADS * HEAD_DIM
    items = (tokens.reshape(lanes, length, width), cotangent.reshape(lanes, length, width), given_cache.reshape(lanes, blocks * MEM, cache_width), value_routes.reshape(lanes, length, HEADS, TOPK), output_routes.reshape(lanes, length, HEADS, TOPK), valid_counts.reshape(lanes, blocks), doc_starts.reshape(lanes, blocks))

    def one_row(totals, item):
        row_tokens, row_cot, row_given, row_vroutes, row_oroutes, row_counts, row_starts = item
        inputs = row_tokens.astype(jnp.float32)
        value_pick = selection(row_vroutes)
        output_pick = selection(row_oroutes)
        projected, values, gate_unused = front(inputs, params, value_pick, output_pick)
        cache = jnp.concatenate([projected[:, inner:], values], axis=1)
        source = jnp.concatenate([cache, row_given.astype(jnp.float32)], axis=0)
        block_ids = jnp.arange(blocks, dtype=jnp.int32)
        last_start = lax.cummax(jnp.where(row_starts > 0, block_ids, 0).astype(jnp.int32), axis=0)
        slot_ids = jnp.arange(MEM, dtype=jnp.int32)
        source_block = block_ids[:, None] - MEM // local_len + (slot_ids // local_len)[None, :]
        own_row = source_block * local_len + (slot_ids % local_len)[None, :]
        given_row = length + last_start[:, None] * MEM + (block_ids - last_start)[:, None] * local_len + slot_ids[None, :]
        memory_rows = jnp.where(source_block >= last_start[:, None], own_row, given_row).astype(jnp.int32)
        position = jnp.arange(length, dtype=jnp.int32) % local_len
        valid = (position < jnp.repeat(row_counts, local_len)).astype(jnp.float32)[:, None]

        def forward(layer_in, weights):
            return layer_forward(layer_in, weights, source, memory_rows, row_counts, value_pick, output_pick, valid)
        layer_out, pull = jax.vjp(forward, inputs, params)
        d_inputs, d_params = pull(row_cot.astype(jnp.float32))
        totals = jax.tree.map(jnp.add, totals, d_params)
        return (totals, (layer_out.astype(jnp.bfloat16), d_inputs))
    zeros = tuple((jnp.zeros(weight.shape, jnp.float32) for weight in params))
    grads, (outputs, input_grads) = lax.scan(one_row, zeros, items)
    return (outputs.reshape(micro_count, row_count, length, width), input_grads.reshape(micro_count, row_count, length, width), grads[0], grads[1], grads[2], grads[3], grads[4], grads[5], grads[6], grads[7], grads[8], grads[9], grads[10])
```

```python
import functools

import jax
import jax.numpy as jnp
from jax import lax
from jax.experimental import pallas as pl
from jax.experimental.pallas import tpu as pltpu
from jax.sharding import PartitionSpec as P

HEADS = 4
HEAD_DIM = 112
EXPERTS = 5
TOPK = 2
MEM = 1024
BUCKETS = 256
NEAR = 128
STEP = 16


EPS = 1e-05
NEG = -1e30
HIGH = lax.Precision.HIGHEST


def shortened(array):
    return jax.tree.map(lambda a: a.astype(jnp.bfloat16) if a.dtype == jnp.float32 else a, array)


def from_behind(value, axis, steps):
    count = lax.axis_size(axis)
    first, last = (max(0, -steps), min(count, count - steps))
    return lax.ppermute(value, axis, [(source, source + steps) for source in range(first, last)])


def norm_forward(values, gain, shift):
    center_mean = jnp.mean(values, axis=-1, keepdims=True)
    centered = values - center_mean
    inverse = lax.rsqrt(jnp.mean(centered * centered, axis=-1, keepdims=True) + EPS)
    normed = centered * inverse
    return (normed * gain + shift, normed, inverse)


def norm_backward(upstream, normed, inverse, gain):
    scaled = upstream * gain
    inside = (
        scaled
        - jnp.mean(scaled, axis=-1, keepdims=True)
        - normed * jnp.mean(scaled * normed, axis=-1, keepdims=True)
    )
    return (inside * inverse, jnp.sum(upstream * normed, axis=0), jnp.sum(upstream, axis=0))


def selection(routes):
    expert_ids = jnp.arange(EXPERTS, dtype=jnp.int32)
    return jnp.sum((routes[..., None] == expert_ids).astype(jnp.float32), axis=-2)


def bucket_index(distance):
    far_bucket = NEAR + (distance - NEAR) // STEP
    return jnp.clip(jnp.where(distance < NEAR, distance, far_bucket), 0, BUCKETS - 1)


def gelu_slope(pre_act):
    return (
        0.5 * (1.0 + lax.erf(pre_act * 0.7071067811865476))
        + pre_act * jnp.exp(-0.5 * pre_act * pre_act) * 0.3989422804014327
    )


def flatten(matrix):
    return matrix.reshape(-1)


def bucket_matrix(local_len):
    spread = MEM + 2 * local_len - 1
    distance = jnp.arange(spread, dtype=jnp.int32) - (local_len - 1)
    bucket_ids = jnp.arange(BUCKETS, dtype=jnp.int32)
    return (bucket_index(distance)[:, None] == bucket_ids[None, :]).astype(jnp.float32)


def bias_matrix(table, local_len):
    spread = MEM + 2 * local_len - 1
    window = MEM + local_len
    by_distance = jnp.einsum("hc,kc->hk", table, bucket_matrix(local_len), precision=HIGH)
    turned = jnp.concatenate([by_distance[:, ::-1], jnp.zeros((HEADS, 1), jnp.float32)], axis=1)
    tiled = jnp.tile(turned, (1, local_len))[:, : local_len * spread].reshape(
        HEADS, local_len, spread
    )
    return tiled[:, :, local_len - 1 : local_len - 1 + window]


def bias_backward(score_sum, local_len):
    spread = MEM + 2 * local_len - 1
    padded = jnp.pad(score_sum, ((0, 0), (0, 0), (local_len - 1, 0))).reshape(
        HEADS, local_len * spread
    )
    padded = jnp.pad(padded, ((0, 0), (0, local_len))).reshape(HEADS, local_len, spread + 1)
    by_distance = jnp.sum(padded, axis=1)[:, :spread][:, ::-1]
    return jnp.einsum("hk,kc->hc", by_distance, bucket_matrix(local_len), precision=HIGH)


def attention_scores(queries, keys, table, counts):
    local_len = queries.shape[1]
    window = keys.shape[1]
    raw = jnp.einsum(
        "bqhd,bkhd->bhqk", queries, keys, preferred_element_type=jnp.float32
    ) * HEAD_DIM ** (-0.5)
    row_ids = jnp.arange(local_len, dtype=jnp.int32)[:, None]
    col_ids = jnp.arange(window, dtype=jnp.int32)[None, :]
    bias = bias_matrix(table, local_len)
    own_ids = col_ids - MEM
    causal = (own_ids <= row_ids)[None, None]
    live = own_ids[None, None] < counts[:, None, None, None]
    valid = jnp.logical_or((col_ids < MEM)[None, None], jnp.logical_and(causal, live))
    return (jnp.where(valid, raw + bias[None], NEG), valid)


def memory_by_hops(cache_own, given, starts, local_len):
    hops_total = MEM // local_len
    open_flag = jnp.logical_not(starts)[:, None, None]
    memory_slots = [jnp.zeros_like(cache_own) for _ in range(hops_total)]
    start_marks = starts.astype(jnp.bfloat16)
    for distance in range(1, hops_total + 1):
        if distance < hops_total:
            outgoing = (cache_own, start_marks, given[:, distance * local_len :])
        else:
            outgoing = (cache_own, start_marks)
        incoming = jax.tree.map(
            lambda part, own: part.astype(own.dtype),
            from_behind(shortened(outgoing), "tm", distance),
            outgoing,
        )
        memory_slots[hops_total - distance] = jnp.where(
            open_flag, incoming[0], memory_slots[hops_total - distance]
        )
        arrived = jnp.logical_and(open_flag, (incoming[1] > 0)[:, None, None])
        if distance < hops_total:
            for position in range(hops_total - distance):
                portion = incoming[2][:, position * local_len : (position + 1) * local_len]
                memory_slots[position] = jnp.where(arrived, portion, memory_slots[position])
        open_flag = jnp.logical_and(open_flag, jnp.logical_not(arrived))
    assembled = jnp.concatenate(memory_slots, axis=1)
    return jnp.where(starts[:, None, None], given, assembled)


def on_device(
    tokens,
    cotangent,
    given_cache,
    value_routes,
    output_routes,
    valid_counts,
    doc_starts,
    norm1_gain,
    norm1_shift,
    qk_weight,
    router_weight,
    value_weight,
    output_weight,
    rel_bias,
    norm2_gain,
    norm2_shift,
    ffn_in,
    ffn_out,
):
    batches, unused_row, local_len, model_width = tokens.shape
    row_count = batches * local_len
    inner_width = HEADS * HEAD_DIM
    head_experts = HEADS * EXPERTS
    full_weights = (
        lax.all_gather(norm1_gain, ("doc", "tm"), axis=0, tiled=True),
        lax.all_gather(norm1_shift, ("doc", "tm"), axis=0, tiled=True),
        lax.all_gather(qk_weight, ("doc", "tm"), axis=0, tiled=True),
        lax.all_gather(router_weight, ("doc", "tm"), axis=0, tiled=True),
        lax.all_gather(value_weight, ("doc", "tm"), axis=0, tiled=True),
        lax.all_gather(output_weight, ("doc", "tm"), axis=1, tiled=True),
        lax.all_gather(rel_bias, ("doc", "tm"), axis=1, tiled=True),
        lax.all_gather(norm2_gain, ("doc", "tm"), axis=0, tiled=True),
        lax.all_gather(norm2_shift, ("doc", "tm"), axis=0, tiled=True),
        lax.all_gather(ffn_in, ("doc", "tm"), axis=0, tiled=True),
        lax.all_gather(ffn_out, ("doc", "tm"), axis=0, tiled=True),
    )
    (
        gain_one,
        shift_one,
        w_qk,
        w_router,
        w_value,
        w_output,
        table_bf,
        gain_two,
        shift_two,
        w_in,
        w_out,
    ) = full_weights
    gain_one = gain_one.astype(jnp.float32)
    shift_one = shift_one.astype(jnp.float32)
    gain_two = gain_two.astype(jnp.float32)
    shift_two = shift_two.astype(jnp.float32)
    table = table_bf.astype(jnp.float32)
    router_f = w_router.astype(jnp.float32)
    inputs = tokens.reshape(row_count, model_width).astype(jnp.float32)
    counts = valid_counts.reshape(batches)
    starts = doc_starts.reshape(batches) > 0
    token_mask = (
        (jnp.arange(local_len, dtype=jnp.int32)[None, :] < counts[:, None])
        .astype(jnp.float32)
        .reshape(row_count, 1)
    )
    value_pick = selection(value_routes.reshape(row_count, HEADS, TOPK))
    output_pick = selection(output_routes.reshape(row_count, HEADS, TOPK))
    normed_one, norm1_unit, norm1_inv = norm_forward(inputs, gain_one, shift_one)
    act_one = normed_one.astype(jnp.bfloat16)
    qk_vals = jnp.dot(act_one, w_qk, preferred_element_type=jnp.float32).astype(jnp.bfloat16)
    gates = jax.nn.sigmoid(jnp.dot(act_one, w_router, preferred_element_type=jnp.float32))
    gate_value = gates[:, :head_experts].reshape(row_count, HEADS, EXPERTS) * value_pick
    gate_output = gates[:, head_experts:].reshape(row_count, HEADS, EXPERTS) * output_pick
    value_gate_t = jnp.transpose(gate_value, (0, 2, 1))[..., None]
    output_gate_t = jnp.transpose(gate_output, (0, 2, 1))[..., None]
    parts = jnp.dot(act_one, w_value, preferred_element_type=jnp.float32).reshape(
        row_count, EXPERTS, HEADS, HEAD_DIM
    )
    values = (
        jnp.sum(value_gate_t * parts, axis=1).reshape(row_count, inner_width).astype(jnp.bfloat16)
    )
    cache_own = jnp.concatenate([qk_vals[:, inner_width:], values], axis=1).reshape(
        batches, local_len, 2 * inner_width
    )
    given = given_cache.reshape(batches, MEM, 2 * inner_width)
    memory = memory_by_hops(cache_own, given, starts, local_len)
    queries = qk_vals[:, :inner_width].reshape(batches, local_len, HEADS, HEAD_DIM)
    keys = jnp.concatenate([memory[:, :, :inner_width], cache_own[:, :, :inner_width]], axis=1)
    keys = keys.reshape(batches, MEM + local_len, HEADS, HEAD_DIM)
    vals = jnp.concatenate([memory[:, :, inner_width:], cache_own[:, :, inner_width:]], axis=1)
    vals = vals.reshape(batches, MEM + local_len, HEADS, HEAD_DIM)
    scores, valid = attention_scores(queries, keys, table, counts)
    top = jnp.max(scores, axis=-1, keepdims=True)
    expo = jnp.exp(scores - top)
    denom = jnp.sum(expo, axis=-1, keepdims=True)
    log_total = top + jnp.log(denom)
    probs_b = (expo / denom).astype(jnp.bfloat16)
    attended = jnp.einsum("bhqk,bkhd->bqhd", probs_b, vals, preferred_element_type=jnp.float32)
    attended = attended.reshape(row_count, inner_width).astype(jnp.bfloat16)
    attended_f = attended.astype(jnp.float32).reshape(row_count, 1, HEADS, HEAD_DIM)
    mixed = (
        (output_gate_t * attended_f).reshape(row_count, EXPERTS * inner_width).astype(jnp.bfloat16)
    )
    hidden = inputs + jnp.dot(mixed, w_output, preferred_element_type=jnp.float32)
    normed_two, norm2_unit, norm2_inv = norm_forward(hidden, gain_two, shift_two)
    act_two = normed_two.astype(jnp.bfloat16)
    pre_act = jnp.dot(act_two, w_in, preferred_element_type=jnp.float32)
    activated = jax.nn.gelu(pre_act, approximate=False).astype(jnp.bfloat16)
    ffn_result = jnp.dot(activated, w_out, preferred_element_type=jnp.float32)
    layer_out = (token_mask * (hidden + ffn_result)).astype(jnp.bfloat16).reshape(tokens.shape)
    upstream = cotangent.reshape(row_count, model_width).astype(jnp.float32) * token_mask
    upstream_b = upstream.astype(jnp.bfloat16)
    d_out_w = jnp.einsum("nf,nd->fd", activated, upstream_b, preferred_element_type=jnp.float32)
    d_act = jnp.einsum("nd,fd->nf", upstream_b, w_out, preferred_element_type=jnp.float32)
    d_pre = (d_act * gelu_slope(pre_act)).astype(jnp.bfloat16)
    d_in_w = jnp.einsum("nd,nf->df", act_two, d_pre, preferred_element_type=jnp.float32)
    d_norm_two = jnp.einsum("nf,df->nd", d_pre, w_in, preferred_element_type=jnp.float32)
    d_from_two, d_gain_two, d_shift_two = norm_backward(d_norm_two, norm2_unit, norm2_inv, gain_two)
    d_hidden = upstream + d_from_two
    ffn_width = d_in_w.shape[1]
    d_branch = d_hidden.astype(jnp.bfloat16)
    d_output_t = jnp.einsum("nd,nk->dk", d_branch, mixed, preferred_element_type=jnp.float32)
    d_mixed = jnp.einsum(
        "nd,kd->nk", d_branch, w_output, preferred_element_type=jnp.float32
    ).astype(jnp.bfloat16)
    d_mixed = d_mixed.astype(jnp.float32).reshape(row_count, EXPERTS, HEADS, HEAD_DIM)
    d_gate_out = jnp.sum(d_mixed * attended_f, axis=-1)
    d_attended = (
        jnp.sum(d_mixed * output_gate_t, axis=1)
        .astype(jnp.bfloat16)
        .reshape(batches, local_len, HEADS, HEAD_DIM)
    )
    probs = jnp.where(valid, jnp.exp(scores - log_total), 0.0)
    d_probs = jnp.einsum("bqhd,bkhd->bhqk", d_attended, vals, preferred_element_type=jnp.float32)
    delta = jnp.sum(d_probs * probs, axis=-1, keepdims=True)
    d_scores = probs * (d_probs - delta)
    score_sum = jnp.sum(d_scores, axis=0)
    d_table = bias_backward(score_sum, local_len)
    d_scores_b = d_scores.astype(jnp.bfloat16)
    scale = HEAD_DIM ** (-0.5)
    d_queries = (
        jnp.einsum("bhqk,bkhd->bqhd", d_scores_b, keys, preferred_element_type=jnp.float32) * scale
    )
    d_keys = (
        jnp.einsum(
            "bhqk,bqhd->bkhd", d_scores_b[..., MEM:], queries, preferred_element_type=jnp.float32
        )
        * scale
    )
    d_vals = jnp.einsum(
        "bhqk,bqhd->bkhd", probs_b[..., MEM:], d_attended, preferred_element_type=jnp.float32
    )
    d_qk = jnp.concatenate(
        [d_queries.reshape(row_count, inner_width), d_keys.reshape(row_count, inner_width)], axis=1
    ).astype(jnp.bfloat16)
    d_values = (
        d_vals.reshape(row_count, 1, HEADS, HEAD_DIM).astype(jnp.bfloat16).astype(jnp.float32)
    )
    d_gate_val = jnp.sum(parts * d_values, axis=-1)
    d_parts = (
        (value_gate_t * d_values).reshape(row_count, EXPERTS * inner_width).astype(jnp.bfloat16)
    )
    d_gates = jnp.concatenate(
        [
            jnp.transpose(d_gate_val, (0, 2, 1)).reshape(row_count, head_experts)
            * value_pick.reshape(row_count, head_experts),
            jnp.transpose(d_gate_out, (0, 2, 1)).reshape(row_count, head_experts)
            * output_pick.reshape(row_count, head_experts),
        ],
        axis=1,
    )
    d_logits = d_gates * gates * (1.0 - gates)
    d_qk_w = jnp.einsum("nd,nk->dk", act_one, d_qk, preferred_element_type=jnp.float32)
    d_value_w = jnp.einsum("nd,nk->dk", act_one, d_parts, preferred_element_type=jnp.float32)
    d_router_w = jnp.einsum("nd,nk->dk", act_one.astype(jnp.float32), d_logits, precision=HIGH)
    d_norm_one = jnp.einsum("nk,dk->nd", d_qk, w_qk, preferred_element_type=jnp.float32)
    d_norm_one = d_norm_one + jnp.einsum(
        "nk,dk->nd", d_parts, w_value, preferred_element_type=jnp.float32
    )
    d_norm_one = d_norm_one + jnp.einsum("nk,dk->nd", d_logits, router_f, precision=HIGH)
    d_from_one, d_gain_one, d_shift_one = norm_backward(d_norm_one, norm1_unit, norm1_inv, gain_one)
    input_grad = (d_hidden + d_from_one).reshape(tokens.shape)
    shares = (
        lax.psum_scatter(d_gain_one, ("doc", "tm"), scatter_dimension=0, tiled=True),
        lax.psum_scatter(d_shift_one, ("doc", "tm"), scatter_dimension=0, tiled=True),
        lax.psum_scatter(flatten(d_qk_w), ("doc", "tm"), scatter_dimension=0, tiled=True),
        lax.psum_scatter(flatten(d_router_w), ("doc", "tm"), scatter_dimension=0, tiled=True),
        lax.psum_scatter(flatten(d_value_w), ("doc", "tm"), scatter_dimension=0, tiled=True),
        lax.psum_scatter(flatten(d_output_t), ("doc", "tm"), scatter_dimension=0, tiled=True),
        lax.psum_scatter(d_table, ("doc", "tm"), scatter_dimension=1, tiled=True),
        lax.psum_scatter(d_gain_two, ("doc", "tm"), scatter_dimension=0, tiled=True),
        lax.psum_scatter(d_shift_two, ("doc", "tm"), scatter_dimension=0, tiled=True),
        lax.psum_scatter(flatten(d_in_w), ("doc", "tm"), scatter_dimension=0, tiled=True),
        lax.psum_scatter(flatten(d_out_w), ("doc", "tm"), scatter_dimension=0, tiled=True),
    )
    qk_share = shares[2].reshape(-1, 2 * inner_width)
    router_share = shares[3].reshape(-1, 2 * head_experts)
    value_share = shares[4].reshape(-1, EXPERTS * inner_width)
    output_share = shares[5].reshape(-1, EXPERTS * inner_width).T
    in_share = shares[9].reshape(-1, ffn_width)
    out_share = shares[10].reshape(-1, model_width)
    return (
        layer_out,
        input_grad,
        shares[0],
        shares[1],
        qk_share,
        router_share,
        value_share,
        output_share,
        shares[6],
        shares[7],
        shares[8],
        in_share,
        out_share,
    )


MESH = pl.DeviceIdType.MESH
PAD = 128
SIDE = 2
HALF_HEADS = HEADS // SIDE
W_QK = 2 * HALF_HEADS * PAD
W_VAL = EXPERTS * HALF_HEADS * PAD
W_MISC = 128
W_A = W_QK + W_VAL + W_MISC
W_O = EXPERTS * HALF_HEADS * PAD
MISC = W_QK + W_VAL
N_ROUTE = 2 * HALF_HEADS * EXPERTS
COL_NORM = N_ROUTE
COL_BIAS = N_ROUTE + 4
VMEM_BYTES = 60 * 1024 * 1024
SCALE = HEAD_DIM ** (-0.5)


def pad_last(a, width):
    return jnp.pad(a, [(0, 0)] * (a.ndim - 1) + [(0, width - a.shape[-1])])


def swap(a):
    count = lax.axis_size("tm")
    return lax.ppermute(a, "tm", [(i, i ^ 1) for i in range(count)])


def neighbours(count):
    d, t = lax.axis_index("doc"), lax.axis_index("tm")
    z, c = t // 2, t % 2
    return dict(
        c=(d, z * 2 + 1 - c),
        x=(d + 1 - 2 * (d % 2), t),
        y=((d + 2) % 4, t),
        up=(d, jnp.minimum(t + 2, count - 1)),
        down=(d, jnp.maximum(t - 2, 0)),
    )


def enter(nb, z, levels):
    barrier = pltpu.get_barrier_semaphore()
    for name in ("c", "x", "y"):
        pl.semaphore_signal(barrier, inc=1, device_id=nb[name], device_id_type=MESH)

    @pl.when(z < levels - 1)
    def _():
        pl.semaphore_signal(barrier, inc=1, device_id=nb["up"], device_id_type=MESH)

    @pl.when(z > 0)
    def _():
        pl.semaphore_signal(barrier, inc=1, device_id=nb["down"], device_id_type=MESH)

    ends = jnp.where(z < levels - 1, 1, 0) + jnp.where(z > 0, 1, 0)
    pl.semaphore_wait(barrier, 3 + ends)


class Gather:
    def __init__(self, ref, sems, nb, d, z, levels):
        self.ref, self.nb, self.d, self.z, self.levels = ref, nb, d, z, levels
        self.send, self.recv = sems
        self.half = ref.shape[2] // 2

    def copy(self, part, slot, to):
        return pltpu.make_async_remote_copy(
            src_ref=part, dst_ref=part, send_sem=self.send.at[slot], recv_sem=self.recv.at[slot],
            device_id=self.nb[to], device_id_type=MESH)

    def along(self, level, distance, to):
        base = 0 if to == "up" else self.levels
        return self.copy(self.ref.at[self.d, level], base + distance, to)

    def across(self, level, to, column=None):
        base = (2 if to == "x" else 3) * self.levels
        column = self.d if column is None else column
        return self.copy(self.ref.at[column, level], base + level, to)

    def corner(self, level, to, column):
        base = (4 if to == "x" else 5) * self.levels
        rows = pl.ds(self.half, self.half) if to == "x" else pl.ds(0, self.half)
        return self.copy(self.ref.at[column, level, rows], base + level, to)

    def begin(self):
        z, levels = self.z, self.levels

        @pl.when(z < levels - 1)
        def _():
            self.along(z, 1, "up").start()

        @pl.when(z > 0)
        def _():
            self.along(z, 1, "down").start()

        self.across(z, "x").start()
        self.across(z, "y").start()

    def line(self, k):
        z, levels = self.z, self.levels

        @pl.when(z >= k)
        def _():
            self.along(z - k, k, "up").wait_recv()

            @pl.when(z < levels - 1)
            def _():
                self.along(z - k, k + 1, "up").start()

            self.across(z - k, "x").start()
            self.across(z - k, "y").start()

        @pl.when(z + k < levels)
        def _():
            self.along(z + k, k, "down").wait_recv()

            @pl.when(z > 0)
            def _():
                self.along(z + k, k + 1, "down").start()

            self.across(z + k, "x").start()
            self.across(z + k, "y").start()

    def turn(self, k):
        z, levels, d = self.z, self.levels, self.d
        by_x, by_y = d + 1 - 2 * (d % 2), (d + 2) % 4

        def one(level):
            self.across(level, "x").wait_recv()
            self.corner(level, "y", by_x).start()
            self.across(level, "y").wait_recv()
            self.corner(level, "x", by_y).start()

        if k == 0:
            one(z)
        else:
            pl.when(z >= k)(lambda: one(z - k))
            pl.when(z + k < levels)(lambda: one(z + k))

    def finish(self, k):
        z, levels, d = self.z, self.levels, self.d
        by_x, by_y = d + 1 - 2 * (d % 2), (d + 2) % 4

        def one(level):
            self.corner(level, "x", by_y).wait_recv()
            self.corner(level, "y", by_x).wait_recv()

        if k == 0:
            one(z)
        else:
            pl.when(z >= k)(lambda: one(z - k))
            pl.when(z + k < levels)(lambda: one(z + k))

    def drain(self):
        z, levels, d = self.z, self.levels, self.d
        by_x, by_y = d + 1 - 2 * (d % 2), (d + 2) % 4
        for level in range(levels):
            self.across(level, "x").wait_send()
            self.across(level, "y").wait_send()
            self.corner(level, "x", by_y).wait_send()
            self.corner(level, "y", by_x).wait_send()
        for k in range(1, levels):

            @pl.when(jnp.logical_and(z >= k - 1, z < levels - 1))
            def _():
                self.along(z - k + 1, k, "up").wait_send()

            @pl.when(jnp.logical_and(z + k - 1 < levels, z > 0))
            def _():
                self.along(z + k - 1, k, "down").wait_send()


def gather_kernel(
    levels, a_in, o_in, i_in, f_in, x_in, g_in,
    a_all, o_all, i_all, f_all, x_all, g_all,
    send, recv, csend, crecv, lsem,
):
    d, t = lax.axis_index("doc"), lax.axis_index("tm")
    z, c = t // 2, t % 2
    nb = neighbours(2 * levels)
    rows = a_in.shape[1]
    own = pl.ds(pl.multiple_of(c * rows, 16), rows)
    locals_, remotes = [], []

    def place(index, src_mine, src_other, dst):
        locals_.append(pltpu.make_async_copy(src_mine, dst, lsem.at[index]))
        if src_other is not None:
            remotes.append(pltpu.make_async_remote_copy(
                src_ref=src_other, dst_ref=dst, send_sem=csend.at[index], recv_sem=crecv.at[index],
                device_id=nb["c"], device_id_type=MESH))

    place(0, a_in.at[c], a_in.at[1 - c], a_all.at[d, z, own])
    place(1, o_in.at[c], o_in.at[1 - c], o_all.at[d, z, own])
    place(2, i_in.at[c], i_in.at[1 - c], i_all.at[d, z, own])
    place(3, x_in, x_in, x_all.at[c])
    place(4, g_in.at[c], g_in.at[1 - c], g_all.at[c])
    place(5, f_in, None, f_all.at[d, z])
    for cp in locals_:
        cp.start()
    enter(nb, z, levels)
    for cp in remotes:
        cp.start()
    groups = [
        Gather(ref, (send.at[i], recv.at[i]), nb, d, z, levels)
        for i, ref in enumerate((a_all, o_all, i_all, f_all))
    ]
    for i, group in enumerate(groups):
        if i < 3:
            locals_[i].wait()
            remotes[i].wait()
        else:
            locals_[5].wait()
        group.begin()
        for k in range(1, levels):
            group.line(k)
        if i:
            for k in range(levels):
                groups[i - 1].turn(k)
    for k in range(levels):
        groups[-1].turn(k)
    for group in groups:
        for k in range(levels):
            group.finish(k)
        group.drain()
    locals_[3].wait()
    locals_[4].wait()
    remotes[3].wait()
    remotes[4].wait()


def gather(levels, packs):
    a, o, i, f, x, g = packs
    two = lambda v: (4, levels, 2 * v.shape[1], v.shape[2])
    shapes = [two(a), two(o), two(i), (4, levels) + f.shape, (2,) + x.shape, (2,) + g.shape[1:]]
    hbm = pl.BlockSpec(memory_space=pl.ANY)
    return pl.pallas_call(
        functools.partial(gather_kernel, levels),
        out_shape=[jax.ShapeDtypeStruct(s, jnp.bfloat16) for s in shapes],
        in_specs=[hbm] * 6,
        out_specs=[hbm] * 6,
        scratch_shapes=[
            pltpu.SemaphoreType.DMA((4, 6 * levels)),
            pltpu.SemaphoreType.DMA((4, 6 * levels)),
            pltpu.SemaphoreType.DMA((6,)),
            pltpu.SemaphoreType.DMA((6,)),
            pltpu.SemaphoreType.DMA((6,)),
        ],
        compiler_params=pltpu.CompilerParams(
            collective_id=1, has_side_effects=True, vmem_limit_bytes=VMEM_BYTES),
    )(a, o, i, f, x, g)


def add_rows(dst, terms):
    rows, width = dst.shape
    step = 16

    def body(i, carry):
        at = pl.ds(pl.multiple_of(i * step, step), step)
        total = terms[0][at].astype(jnp.float32)
        for term in terms[1:]:
            total = total + term[at].astype(jnp.float32)
        dst[at] = total.astype(dst.dtype)
        return carry

    lax.fori_loop(0, rows // step, body, 0)


class Scatter:
    def __init__(self, src, bufs, sems, nb, d, z, levels):
        self.src, self.nb, self.d, self.z, self.levels = src, nb, d, z, levels
        self.cx, self.cy, self.rx, self.ry, self.up, self.down = bufs
        self.send, self.recv = sems
        self.half = src.shape[2] // 2
        self.by_x, self.by_y = d + 1 - 2 * (d % 2), (d + 2) % 4
        self.low, self.high = pl.ds(0, self.half), pl.ds(self.half, self.half)

    def copy(self, src, dst, slot, to):
        return pltpu.make_async_remote_copy(
            src_ref=src, dst_ref=dst, send_sem=self.send.at[slot], recv_sem=self.recv.at[slot],
            device_id=self.nb[to], device_id_type=MESH)

    def corner(self, j, to):
        part = self.low if to == "x" else self.high
        buf = self.cx if to == "x" else self.cy
        return self.copy(self.src.at[3 - self.d, j, part], buf.at[j], (0 if to == "x" else self.levels) + j, to)

    def direct(self, j, to):
        part = self.low if to == "x" else self.high
        column = self.by_x if to == "x" else self.by_y
        buf = self.rx if to == "x" else self.ry
        return self.copy(self.src.at[column, j, part], buf.at[j, part], (2 if to == "x" else 3) * self.levels + j, to)

    def relay(self, j, to):
        part = self.high if to == "x" else self.low
        held = self.cy if to == "x" else self.cx
        buf = self.rx if to == "x" else self.ry
        return self.copy(held.at[j], buf.at[j, part], (4 if to == "x" else 5) * self.levels + j, to)

    def along(self, j, to):
        buf = self.up if to == "up" else self.down
        return self.copy(buf.at[j], buf.at[j], (6 if to == "up" else 7) * self.levels + j, to)

    def begin(self):
        for j in range(self.levels):
            self.corner(j, "x").start()
            self.corner(j, "y").start()
        for j in range(self.levels):
            self.direct(j, "x").start()
            self.direct(j, "y").start()

    def turn(self, j):
        self.corner(j, "x").wait_recv()
        add_rows(self.cx.at[j], [self.cx.at[j], self.src.at[self.by_y, j, self.low]])
        self.relay(j, "y").start()
        self.corner(j, "y").wait_recv()
        add_rows(self.cy.at[j], [self.cy.at[j], self.src.at[self.by_x, j, self.high]])
        self.relay(j, "x").start()

    def column(self, j):
        self.direct(j, "x").wait_recv()
        self.direct(j, "y").wait_recv()
        self.relay(j, "x").wait_recv()
        self.relay(j, "y").wait_recv()
        add_rows(self.rx.at[j], [self.rx.at[j], self.ry.at[j], self.src.at[self.d, j]])

    def line(self, j):
        z, levels = self.z, self.levels

        @pl.when(z < j)
        def _():
            @pl.when(z > 0)
            def _():
                self.along(j, "up").wait_recv()
                add_rows(self.up.at[j], [self.up.at[j], self.rx.at[j]])

            @pl.when(z == 0)
            def _():
                add_rows(self.up.at[j], [self.rx.at[j]])

            self.along(j, "up").start()

        @pl.when(z > j)
        def _():
            @pl.when(z < levels - 1)
            def _():
                self.along(j, "down").wait_recv()
                add_rows(self.down.at[j], [self.down.at[j], self.rx.at[j]])

            @pl.when(z == levels - 1)
            def _():
                add_rows(self.down.at[j], [self.rx.at[j]])

            self.along(j, "down").start()

    def total(self, dst):
        z, levels = self.z, self.levels

        @pl.when(z == 0)
        def _():
            self.along(z, "down").wait_recv()
            add_rows(dst, [self.rx.at[z], self.down.at[z]])

        @pl.when(z == levels - 1)
        def _():
            self.along(z, "up").wait_recv()
            add_rows(dst, [self.rx.at[z], self.up.at[z]])

        @pl.when(jnp.logical_and(z > 0, z < levels - 1))
        def _():
            self.along(z, "up").wait_recv()
            self.along(z, "down").wait_recv()
            add_rows(dst, [self.rx.at[z], self.up.at[z], self.down.at[z]])

    def drain(self):
        for j in range(self.levels):
            for to in ("x", "y"):
                self.corner(j, to).wait_send()
                self.direct(j, to).wait_send()
                self.relay(j, to).wait_send()
            pl.when(self.z < j)(lambda: self.along(j, "up").wait_send())
            pl.when(self.z > j)(lambda: self.along(j, "down").wait_send())


def scatter_kernel(levels, *refs):
    d, t = lax.axis_index("doc"), lax.axis_index("tm")
    z = t // 2
    nb = neighbours(2 * levels)
    count = 4
    srcs, dsts = refs[:count], refs[count : 2 * count]
    bufs = refs[2 * count : -2]
    send, recv = refs[-2:]
    enter(nb, z, levels)
    groups = [
        Scatter(srcs[i], bufs[6 * i : 6 * i + 6], (send.at[i], recv.at[i]), nb, d, z, levels)
        for i in range(count)
    ]
    for group in groups:
        group.begin()
    for group in groups:
        for j in range(levels):
            group.turn(j)
    for group in groups:
        for j in range(levels):
            group.column(j)
        for j in range(levels):
            group.line(j)
    for group, dst in zip(groups, dsts):
        group.total(dst)
    for group in groups:
        group.drain()


def scatter(levels, parts):
    scratch = []
    for p in parts:
        rows, width = p.shape[2:]
        for r in (rows // 2, rows // 2, rows, rows, rows, rows):
            scratch.append(pltpu.VMEM((levels, r, width), jnp.bfloat16))
    vmem = pl.BlockSpec(memory_space=pltpu.VMEM)
    return pl.pallas_call(
        functools.partial(scatter_kernel, levels),
        out_shape=[jax.ShapeDtypeStruct(p.shape[2:], jnp.float32) for p in parts],
        in_specs=[vmem] * 4,
        out_specs=[vmem] * 4,
        scratch_shapes=scratch + [pltpu.SemaphoreType.DMA((4, 8 * levels))] * 2,
        compiler_params=pltpu.CompilerParams(
            collective_id=2, has_side_effects=True, vmem_limit_bytes=VMEM_BYTES),
    )(*parts)


def split_heads(a, lead):
    rows = a.shape[0]
    a = pad_last(a.reshape(rows, lead, SIDE, HALF_HEADS, HEAD_DIM), PAD)
    return jnp.transpose(a, (2, 0, 1, 3, 4)).reshape(SIDE, rows, lead * HALF_HEADS * PAD)


def join_heads(a, lead):
    rows = a.shape[1]
    a = a.reshape(SIDE, rows, lead, HALF_HEADS, PAD)[..., :HEAD_DIM]
    return jnp.transpose(a, (1, 2, 0, 3, 4)).reshape(rows, lead * HEADS * HEAD_DIM)


def shared_memory(cache, given, starts, levels):
    count = 2 * levels
    up = [(i, i + 2) for i in range(count - 2)]
    local_len = cache.shape[2]

    def follow(before, block):
        moved = jnp.concatenate([before[0][:, local_len:], before[1]], axis=1)
        return jnp.where(starts[block][:, None, None], given[block], moved)

    odd = given[1]
    for _ in range(levels):
        arrived = lax.ppermute((odd, cache[1]), "tm", up)
        even = follow(arrived, 0)
        odd = follow((even, cache[0]), 1)
    return jnp.stack([even, odd])


def bias_of(table, local_len):
    spread = MEM + 2 * local_len - 1
    window = MEM + local_len
    by_distance = jnp.einsum("hc,kc->hk", table, bucket_matrix(local_len), precision=HIGH)
    heads = table.shape[0]
    turned = jnp.concatenate([by_distance[:, ::-1], jnp.zeros((heads, 1), jnp.float32)], axis=1)
    tiled = jnp.tile(turned, (1, local_len))[:, : local_len * spread].reshape(heads, local_len, spread)
    return tiled[:, :, local_len - 1 : local_len - 1 + window]


def bias_grad(score_sum, local_len):
    heads = score_sum.shape[0]
    spread = MEM + 2 * local_len - 1
    padded = jnp.pad(score_sum, ((0, 0), (0, 0), (local_len - 1, 0))).reshape(heads, local_len * spread)
    padded = jnp.pad(padded, ((0, 0), (0, local_len))).reshape(heads, local_len, spread + 1)
    by_distance = jnp.sum(padded, axis=1)[:, :spread][:, ::-1]
    return jnp.einsum("hk,kc->hc", by_distance, bucket_matrix(local_len), precision=HIGH)


def on_chip(
    tokens, cotangent, given_cache, value_routes, output_routes, valid_counts, doc_starts,
    norm1_gain, norm1_shift, qk_weight, router_weight, value_weight, output_weight, rel_bias,
    norm2_gain, norm2_shift, ffn_in, ffn_out,
):
    batches, unused_row, local_len, width = tokens.shape
    count = lax.axis_size("tm")
    levels = count // 2
    side = lax.axis_index("tm") % 2
    rows = batches * local_len
    shard = qk_weight.shape[0]
    blocks = 4 * levels
    bf16, f32 = jnp.bfloat16, jnp.float32

    a_qk = split_heads(qk_weight, 2)
    a_v = split_heads(value_weight, EXPERTS)
    a_o = split_heads(output_weight.T, EXPERTS)
    route = jnp.transpose(
        router_weight.reshape(shard, 2, SIDE, HALF_HEADS * EXPERTS), (2, 0, 1, 3)
    ).reshape(SIDE, shard, N_ROUTE)
    norms = jnp.broadcast_to(
        jnp.stack([norm1_gain, norm1_shift, norm2_gain, norm2_shift], axis=1)[None], (SIDE, shard, 4))
    buckets = rel_bias.shape[1]
    bias_cols = jnp.pad(
        jnp.transpose(rel_bias.reshape(SIDE, HALF_HEADS, buckets), (0, 2, 1)),
        ((0, 0), (0, shard - buckets), (0, 0)))
    misc = pad_last(jnp.concatenate([route, norms, bias_cols], axis=2), W_MISC)
    a_pack = jnp.concatenate([a_qk, a_v, misc], axis=2)
    hidden_block = ffn_out.shape[0]
    i_pack = jnp.transpose(
        ffn_in.reshape(shard, blocks, SIDE, hidden_block), (2, 0, 1, 3)
    ).reshape(SIDE, shard, blocks * hidden_block)

    mask = (jnp.arange(local_len)[None, :] < valid_counts.reshape(batches, 1)).astype(f32).reshape(rows, 1)
    x_own = tokens.reshape(rows, width)
    grad_own = (cotangent.reshape(rows, width).astype(f32) * mask).astype(bf16)
    picks = [
        jnp.transpose(
            selection(r.reshape(rows, SIDE, HALF_HEADS, TOPK)).reshape(rows, SIDE, HALF_HEADS * EXPERTS), (1, 0, 2))
        for r in (value_routes, output_routes)
    ]
    starts_col = jnp.repeat(doc_starts.reshape(batches), local_len).reshape(rows, 1).astype(bf16)
    counts_col = jnp.repeat(valid_counts.reshape(batches), local_len).reshape(rows, 1).astype(bf16)
    meta = pad_last(
        jnp.concatenate(
            [picks[0][0], picks[1][0], picks[0][1], picks[1][1], starts_col, counts_col], axis=1).astype(bf16),
        128)
    x_pack = jnp.concatenate([x_own, grad_own, meta], axis=1)
    given = given_cache.reshape(batches * MEM, 2 * HEADS * HEAD_DIM)
    g_pack = split_heads(given, 2)

    a_all, o_all, i_all, f_all, x_all, g_all = gather(levels, (a_pack, a_o, i_pack, ffn_out, x_pack, g_pack))
    w_a = a_all.reshape(width, W_A)
    w_o = o_all.reshape(width, W_O)
    w_i = i_all.reshape(width, -1)
    w_f = f_all.reshape(-1, width)

    vectors = w_a[:, MISC + COL_NORM : MISC + COL_NORM + 4].T.astype(f32)
    gain_one, shift_one, gain_two, shift_two = [v.reshape(1, width) for v in vectors]
    table = w_a[:, MISC + COL_BIAS : MISC + COL_BIAS + HALF_HEADS].reshape(4 * count, shard, HALF_HEADS)
    table = jnp.transpose(table[:, :buckets].reshape(BUCKETS, HALF_HEADS)).astype(f32)

    both = 2 * rows
    inputs = x_all[:, :, :width].reshape(both, width).astype(f32)
    grad_all = x_all[:, :, width : 2 * width].reshape(both, width)
    meta_all = x_all[:, :, 2 * width :].reshape(both, 128)
    pick_mine = jnp.where(side == 0, meta_all[:, :N_ROUTE], meta_all[:, N_ROUTE : 2 * N_ROUTE]).astype(f32)
    tail = meta_all[:, 2 * N_ROUTE : 2 * N_ROUTE + 2].reshape(2, batches, local_len, 2)[:, :, 0]
    starts = tail[..., 0] > 0
    counts = tail[..., 1].astype(jnp.int32)

    normed_one, unit_one, inv_one = norm_forward(inputs, gain_one, shift_one)
    act_one = normed_one.astype(bf16)
    front = jnp.dot(act_one, w_a, preferred_element_type=f32)
    qk = front[:, :W_QK].astype(bf16)
    parts = front[:, W_QK:MISC].reshape(both, EXPERTS, HALF_HEADS, PAD)
    gates = jax.nn.sigmoid(front[:, MISC : MISC + N_ROUTE])
    gated = (gates * pick_mine).reshape(both, 2, HALF_HEADS, EXPERTS)
    value_gate = jnp.transpose(gated[:, 0], (0, 2, 1))[..., None]
    output_gate = jnp.transpose(gated[:, 1], (0, 2, 1))[..., None]
    values = jnp.sum(value_gate * parts, axis=1).reshape(both, HALF_HEADS * PAD).astype(bf16)
    wide = HALF_HEADS * PAD
    queries, keys_own = qk[:, :wide], qk[:, wide:]
    cache = jnp.concatenate([keys_own, values], axis=1).reshape(2, batches, local_len, 2 * wide)
    memory = shared_memory(cache, g_all.reshape(2, batches, MEM, 2 * wide), starts, levels)
    window = jnp.concatenate([memory, cache], axis=2).reshape(2 * batches, MEM + local_len, 2, HALF_HEADS, PAD)
    keys, vals = window[:, :, 0], window[:, :, 1]
    queries = queries.reshape(2 * batches, local_len, HALF_HEADS, PAD)
    raw = jnp.einsum("bqhd,bkhd->bhqk", queries, keys, preferred_element_type=f32) * SCALE
    row_ids = jnp.arange(local_len, dtype=jnp.int32)[:, None]
    own_ids = jnp.arange(MEM + local_len, dtype=jnp.int32)[None, :] - MEM
    valid = jnp.logical_or(
        own_ids[None, None] < 0,
        jnp.logical_and((own_ids <= row_ids)[None, None], own_ids[None, None] < counts.reshape(-1)[:, None, None, None]))
    scores = jnp.where(valid, raw + bias_of(table, local_len)[None], NEG)
    top = jnp.max(scores, axis=-1, keepdims=True)
    expo = jnp.exp(scores - top)
    denom = jnp.sum(expo, axis=-1, keepdims=True)
    probs = expo / denom
    probs_b = probs.astype(bf16)
    attended = jnp.einsum("bhqk,bkhd->bqhd", probs_b, vals, preferred_element_type=f32)
    attended = attended.reshape(both, wide).astype(bf16)
    attended_f = attended.astype(f32).reshape(both, 1, HALF_HEADS, PAD)
    mixed = (output_gate * attended_f).reshape(both, W_O).astype(bf16)
    branch = jnp.dot(mixed, w_o.T, preferred_element_type=f32).reshape(2, rows, width)

    def mine(a):
        return lax.dynamic_index_in_dim(a, side, 0, keepdims=False)

    def other(a):
        return lax.dynamic_index_in_dim(a, 1 - side, 0, keepdims=False)

    def paired(own):
        arrived = swap(own)
        return jnp.where(side == 0, jnp.stack([own, arrived]), jnp.stack([arrived, own])).reshape(both, -1)

    hidden = x_own.astype(f32) + mine(branch) + swap(other(branch))

    normed_two, unit_two, inv_two = norm_forward(hidden, gain_two, shift_two)
    act_two = paired(normed_two.astype(bf16))
    pre_act = jnp.dot(act_two, w_i, preferred_element_type=f32)
    activated = jax.nn.gelu(pre_act, approximate=False).astype(bf16)
    ffn = jnp.dot(activated, w_f, preferred_element_type=f32).reshape(2, rows, width)
    layer_out = (mask * (hidden + mine(ffn) + swap(other(ffn)))).astype(bf16).reshape(tokens.shape)
    d_f = jnp.einsum("nf,nd->fd", activated, grad_all, preferred_element_type=f32).astype(bf16)
    d_act = jnp.einsum("nd,fd->nf", grad_all, w_f, preferred_element_type=f32)
    d_pre = (d_act * gelu_slope(pre_act)).astype(bf16)
    d_i = jnp.einsum("nd,nf->df", act_two, d_pre, preferred_element_type=f32).astype(bf16)
    d_two = jnp.einsum("nf,df->nd", d_pre, w_i, preferred_element_type=f32).reshape(2, rows, width)
    d_two = mine(d_two) + swap(other(d_two))
    d_from_two, d_gain_two, d_shift_two = norm_backward(d_two, unit_two, inv_two, gain_two)
    upstream = cotangent.reshape(rows, width).astype(f32) * mask
    d_hidden = upstream + d_from_two

    d_branch = paired(d_hidden.astype(bf16))
    d_o = jnp.einsum("nd,nk->dk", d_branch, mixed, preferred_element_type=f32).astype(bf16)
    d_mixed = jnp.dot(d_branch, w_o, preferred_element_type=f32).astype(bf16)
    d_mixed = d_mixed.astype(f32).reshape(both, EXPERTS, HALF_HEADS, PAD)
    d_gate_out = jnp.sum(d_mixed * attended_f, axis=-1)
    d_attended = jnp.sum(d_mixed * output_gate, axis=1).astype(bf16).reshape(2 * batches, local_len, HALF_HEADS, PAD)
    d_probs = jnp.einsum("bqhd,bkhd->bhqk", d_attended, vals, preferred_element_type=f32)
    delta = jnp.sum(d_probs * probs, axis=-1, keepdims=True)
    d_scores = probs * (d_probs - delta)
    d_table = bias_grad(jnp.sum(d_scores, axis=0), local_len)
    d_scores_b = d_scores.astype(bf16)
    d_queries = jnp.einsum("bhqk,bkhd->bqhd", d_scores_b, keys, preferred_element_type=f32) * SCALE
    d_keys = jnp.einsum("bhqk,bqhd->bkhd", d_scores_b[..., MEM:], queries, preferred_element_type=f32) * SCALE
    d_vals = jnp.einsum("bhqk,bqhd->bkhd", probs_b[..., MEM:], d_attended, preferred_element_type=f32)
    d_values = d_vals.reshape(both, 1, HALF_HEADS, PAD).astype(bf16).astype(f32)
    d_gate_val = jnp.sum(parts * d_values, axis=-1)
    d_parts = (value_gate * d_values).reshape(both, W_VAL).astype(bf16)
    d_gates = jnp.concatenate(
        [jnp.transpose(g, (0, 2, 1)).reshape(both, HALF_HEADS * EXPERTS) for g in (d_gate_val, d_gate_out)], axis=1)
    d_logits = d_gates * pick_mine * gates * (1.0 - gates)
    d_front = jnp.concatenate(
        [
            d_queries.reshape(both, wide).astype(bf16),
            d_keys.reshape(both, wide).astype(bf16),
            d_parts,
            pad_last(d_logits.astype(bf16), W_MISC),
        ],
        axis=1,
    )
    d_a = jnp.einsum("nd,nk->dk", act_one, d_front, preferred_element_type=f32).astype(bf16)
    d_one = jnp.einsum("nk,dk->nd", d_front, w_a, preferred_element_type=f32).reshape(2, rows, width)
    d_one = mine(d_one) + swap(other(d_one))
    d_from_one, d_gain_one, d_shift_one = norm_backward(
        d_one, mine(unit_one.reshape(2, rows, width)), mine(inv_one.reshape(2, rows, 1)), gain_one)
    input_grad = (d_hidden + d_from_one).reshape(tokens.shape)
    d_norms = jnp.stack([d_gain_one, d_shift_one, d_gain_two, d_shift_two], axis=1)
    d_bias = jnp.pad(
        d_table.T.reshape(4 * count, buckets, HALF_HEADS), ((0, 0), (0, shard - buckets), (0, 0))
    ).reshape(width, HALF_HEADS)
    d_misc = jnp.concatenate([d_norms, d_bias], axis=1).astype(bf16)
    d_a = jnp.concatenate([d_a[:, : MISC + N_ROUTE], d_misc, d_a[:, MISC + N_ROUTE + 4 + HALF_HEADS :]], axis=1)

    s_a, s_o, s_i, s_f = scatter(
        levels,
        (
            d_a.reshape(4, levels, 2 * shard, W_A),
            d_o.reshape(4, levels, 2 * shard, W_O),
            d_i.reshape(4, levels, 2 * shard, -1),
            d_f.reshape(4, levels, hidden_block, width),
        ),
    )
    chip = jnp.concatenate([s_a, s_o, s_i], axis=1).reshape(2, shard, -1)
    kept, arrived = mine(chip), swap(other(chip))
    sides = jnp.where(side == 0, jnp.stack([kept, arrived]), jnp.stack([arrived, kept]))
    qk_share = join_heads(sides[:, :, :W_QK], 2)
    value_share = join_heads(sides[:, :, W_QK:MISC], EXPERTS)
    output_share = join_heads(sides[:, :, W_A : W_A + W_O], EXPERTS).T
    misc = sides[:, :, MISC:W_A]
    router_share = jnp.transpose(
        misc[:, :, :N_ROUTE].reshape(SIDE, shard, 2, HALF_HEADS * EXPERTS), (1, 2, 0, 3)
    ).reshape(shard, 2 * HEADS * EXPERTS)
    norm_share = misc[0, :, COL_NORM : COL_NORM + 4] + misc[1, :, COL_NORM : COL_NORM + 4]
    bias_share = jnp.transpose(misc[:, :buckets, COL_BIAS : COL_BIAS + HALF_HEADS], (0, 2, 1)).reshape(HEADS, buckets)
    in_share = jnp.transpose(
        sides[:, :, W_A + W_O :].reshape(SIDE, shard, blocks, hidden_block), (1, 2, 0, 3)
    ).reshape(shard, -1)
    return (
        layer_out, input_grad, norm_share[:, 0], norm_share[:, 1], qk_share, router_share, value_share,
        output_share, bias_share, norm_share[:, 2], norm_share[:, 3], in_share, s_f,
    )


def by_size(*args):
    thin = args[9].shape[0] % 16 != 0
    paired = lax.axis_size("doc") == 4 and lax.axis_size("tm") % 2 == 0
    return on_device(*args) if thin or not paired else on_chip(*args)


def solution(mesh):
    return jax.shard_map(
        by_size,
        mesh=mesh,
        in_specs=(
            P(None, "doc", "tm", None),
            P(None, "doc", "tm", None),
            P(None, "doc", "tm", None),
            P(None, "doc", "tm", None, None),
            P(None, "doc", "tm", None, None),
            P(None, "doc", "tm"),
            P(None, "doc", "tm"),
            P(("doc", "tm")),
            P(("doc", "tm")),
            P(("doc", "tm"), None),
            P(("doc", "tm"), None),
            P(("doc", "tm"), None),
            P(None, ("doc", "tm")),
            P(None, ("doc", "tm")),
            P(("doc", "tm")),
            P(("doc", "tm")),
            P(("doc", "tm"), None),
            P(("doc", "tm"), None),
        ),
        out_specs=(
            P(None, "doc", "tm", None),
            P(None, "doc", "tm", None),
            P(("doc", "tm")),
            P(("doc", "tm")),
            P(("doc", "tm"), None),
            P(("doc", "tm"), None),
            P(("doc", "tm"), None),
            P(None, ("doc", "tm")),
            P(None, ("doc", "tm")),
            P(("doc", "tm")),
            P(("doc", "tm")),
            P(("doc", "tm"), None),
            P(("doc", "tm"), None),
        ),
        check_vma=False,
    )
```

```python
import functools

import jax
import jax.numpy as jnp
from jax import lax
from jax.experimental import pallas as pl
from jax.experimental.pallas import tpu as pltpu
from jax.sharding import PartitionSpec as P

HEADS = 4
HEAD_DIM = 112
EXPERTS = 5
TOPK = 2
MEM = 1024
BUCKETS = 256
NEAR = 128
STEP = 16


EPS = 1e-05
NEG = -1e30
HIGH = lax.Precision.HIGHEST


def shortened(array):
    return jax.tree.map(lambda a: a.astype(jnp.bfloat16) if a.dtype == jnp.float32 else a, array)


def from_behind(value, axis, steps):
    count = lax.axis_size(axis)
    first, last = (max(0, -steps), min(count, count - steps))
    return lax.ppermute(value, axis, [(source, source + steps) for source in range(first, last)])


def norm_forward(values, gain, shift):
    center_mean = jnp.mean(values, axis=-1, keepdims=True)
    centered = values - center_mean
    inverse = lax.rsqrt(jnp.mean(centered * centered, axis=-1, keepdims=True) + EPS)
    normed = centered * inverse
    return (normed * gain + shift, normed, inverse)


def norm_backward(upstream, normed, inverse, gain):
    scaled = upstream * gain
    inside = (
        scaled
        - jnp.mean(scaled, axis=-1, keepdims=True)
        - normed * jnp.mean(scaled * normed, axis=-1, keepdims=True)
    )
    return (inside * inverse, jnp.sum(upstream * normed, axis=0), jnp.sum(upstream, axis=0))


def selection(routes):
    expert_ids = jnp.arange(EXPERTS, dtype=jnp.int32)
    return jnp.sum((routes[..., None] == expert_ids).astype(jnp.float32), axis=-2)


def bucket_index(distance):
    far_bucket = NEAR + (distance - NEAR) // STEP
    return jnp.clip(jnp.where(distance < NEAR, distance, far_bucket), 0, BUCKETS - 1)


def gelu_slope(pre_act):
    return (
        0.5 * (1.0 + lax.erf(pre_act * 0.7071067811865476))
        + pre_act * jnp.exp(-0.5 * pre_act * pre_act) * 0.3989422804014327
    )


def flatten(matrix):
    return matrix.reshape(-1)


def bucket_matrix(local_len):
    spread = MEM + 2 * local_len - 1
    distance = jnp.arange(spread, dtype=jnp.int32) - (local_len - 1)
    bucket_ids = jnp.arange(BUCKETS, dtype=jnp.int32)
    return (bucket_index(distance)[:, None] == bucket_ids[None, :]).astype(jnp.float32)


def bias_matrix(table, local_len):
    spread = MEM + 2 * local_len - 1
    window = MEM + local_len
    by_distance = jnp.einsum("hc,kc->hk", table, bucket_matrix(local_len), precision=HIGH)
    turned = jnp.concatenate([by_distance[:, ::-1], jnp.zeros((HEADS, 1), jnp.float32)], axis=1)
    tiled = jnp.tile(turned, (1, local_len))[:, : local_len * spread].reshape(
        HEADS, local_len, spread
    )
    return tiled[:, :, local_len - 1 : local_len - 1 + window]


def bias_backward(score_sum, local_len):
    spread = MEM + 2 * local_len - 1
    padded = jnp.pad(score_sum, ((0, 0), (0, 0), (local_len - 1, 0))).reshape(
        HEADS, local_len * spread
    )
    padded = jnp.pad(padded, ((0, 0), (0, local_len))).reshape(HEADS, local_len, spread + 1)
    by_distance = jnp.sum(padded, axis=1)[:, :spread][:, ::-1]
    return jnp.einsum("hk,kc->hc", by_distance, bucket_matrix(local_len), precision=HIGH)


def attention_scores(queries, keys, table, counts):
    local_len = queries.shape[1]
    window = keys.shape[1]
    raw = jnp.einsum(
        "bqhd,bkhd->bhqk", queries, keys, preferred_element_type=jnp.float32
    ) * HEAD_DIM ** (-0.5)
    row_ids = jnp.arange(local_len, dtype=jnp.int32)[:, None]
    col_ids = jnp.arange(window, dtype=jnp.int32)[None, :]
    bias = bias_matrix(table, local_len)
    own_ids = col_ids - MEM
    causal = (own_ids <= row_ids)[None, None]
    live = own_ids[None, None] < counts[:, None, None, None]
    valid = jnp.logical_or((col_ids < MEM)[None, None], jnp.logical_and(causal, live))
    return (jnp.where(valid, raw + bias[None], NEG), valid)


def memory_by_hops(cache_own, given, starts, local_len):
    hops_total = MEM // local_len
    open_flag = jnp.logical_not(starts)[:, None, None]
    memory_slots = [jnp.zeros_like(cache_own) for _ in range(hops_total)]
    start_marks = starts.astype(jnp.bfloat16)
    for distance in range(1, hops_total + 1):
        if distance < hops_total:
            outgoing = (cache_own, start_marks, given[:, distance * local_len :])
        else:
            outgoing = (cache_own, start_marks)
        incoming = jax.tree.map(
            lambda part, own: part.astype(own.dtype),
            from_behind(shortened(outgoing), "tm", distance),
            outgoing,
        )
        memory_slots[hops_total - distance] = jnp.where(
            open_flag, incoming[0], memory_slots[hops_total - distance]
        )
        arrived = jnp.logical_and(open_flag, (incoming[1] > 0)[:, None, None])
        if distance < hops_total:
            for position in range(hops_total - distance):
                portion = incoming[2][:, position * local_len : (position + 1) * local_len]
                memory_slots[position] = jnp.where(arrived, portion, memory_slots[position])
        open_flag = jnp.logical_and(open_flag, jnp.logical_not(arrived))
    assembled = jnp.concatenate(memory_slots, axis=1)
    return jnp.where(starts[:, None, None], given, assembled)


def on_device(
    tokens,
    cotangent,
    given_cache,
    value_routes,
    output_routes,
    valid_counts,
    doc_starts,
    norm1_gain,
    norm1_shift,
    qk_weight,
    router_weight,
    value_weight,
    output_weight,
    rel_bias,
    norm2_gain,
    norm2_shift,
    ffn_in,
    ffn_out,
):
    batches, unused_row, local_len, model_width = tokens.shape
    row_count = batches * local_len
    inner_width = HEADS * HEAD_DIM
    head_experts = HEADS * EXPERTS
    full_weights = (
        lax.all_gather(norm1_gain, ("doc", "tm"), axis=0, tiled=True),
        lax.all_gather(norm1_shift, ("doc", "tm"), axis=0, tiled=True),
        lax.all_gather(qk_weight, ("doc", "tm"), axis=0, tiled=True),
        lax.all_gather(router_weight, ("doc", "tm"), axis=0, tiled=True),
        lax.all_gather(value_weight, ("doc", "tm"), axis=0, tiled=True),
        lax.all_gather(output_weight, ("doc", "tm"), axis=1, tiled=True),
        lax.all_gather(rel_bias, ("doc", "tm"), axis=1, tiled=True),
        lax.all_gather(norm2_gain, ("doc", "tm"), axis=0, tiled=True),
        lax.all_gather(norm2_shift, ("doc", "tm"), axis=0, tiled=True),
        lax.all_gather(ffn_in, ("doc", "tm"), axis=0, tiled=True),
        lax.all_gather(ffn_out, ("doc", "tm"), axis=0, tiled=True),
    )
    (
        gain_one,
        shift_one,
        w_qk,
        w_router,
        w_value,
        w_output,
        table_bf,
        gain_two,
        shift_two,
        w_in,
        w_out,
    ) = full_weights
    gain_one = gain_one.astype(jnp.float32)
    shift_one = shift_one.astype(jnp.float32)
    gain_two = gain_two.astype(jnp.float32)
    shift_two = shift_two.astype(jnp.float32)
    table = table_bf.astype(jnp.float32)
    router_f = w_router.astype(jnp.float32)
    inputs = tokens.reshape(row_count, model_width).astype(jnp.float32)
    counts = valid_counts.reshape(batches)
    starts = doc_starts.reshape(batches) > 0
    token_mask = (
        (jnp.arange(local_len, dtype=jnp.int32)[None, :] < counts[:, None])
        .astype(jnp.float32)
        .reshape(row_count, 1)
    )
    value_pick = selection(value_routes.reshape(row_count, HEADS, TOPK))
    output_pick = selection(output_routes.reshape(row_count, HEADS, TOPK))
    normed_one, norm1_unit, norm1_inv = norm_forward(inputs, gain_one, shift_one)
    act_one = normed_one.astype(jnp.bfloat16)
    qk_vals = jnp.dot(act_one, w_qk, preferred_element_type=jnp.float32).astype(jnp.bfloat16)
    gates = jax.nn.sigmoid(jnp.dot(act_one, w_router, preferred_element_type=jnp.float32))
    gate_value = gates[:, :head_experts].reshape(row_count, HEADS, EXPERTS) * value_pick
    gate_output = gates[:, head_experts:].reshape(row_count, HEADS, EXPERTS) * output_pick
    value_gate_t = jnp.transpose(gate_value, (0, 2, 1))[..., None]
    output_gate_t = jnp.transpose(gate_output, (0, 2, 1))[..., None]
    parts = jnp.dot(act_one, w_value, preferred_element_type=jnp.float32).reshape(
        row_count, EXPERTS, HEADS, HEAD_DIM
    )
    values = (
        jnp.sum(value_gate_t * parts, axis=1).reshape(row_count, inner_width).astype(jnp.bfloat16)
    )
    cache_own = jnp.concatenate([qk_vals[:, inner_width:], values], axis=1).reshape(
        batches, local_len, 2 * inner_width
    )
    given = given_cache.reshape(batches, MEM, 2 * inner_width)
    memory = memory_by_hops(cache_own, given, starts, local_len)
    queries = qk_vals[:, :inner_width].reshape(batches, local_len, HEADS, HEAD_DIM)
    keys = jnp.concatenate([memory[:, :, :inner_width], cache_own[:, :, :inner_width]], axis=1)
    keys = keys.reshape(batches, MEM + local_len, HEADS, HEAD_DIM)
    vals = jnp.concatenate([memory[:, :, inner_width:], cache_own[:, :, inner_width:]], axis=1)
    vals = vals.reshape(batches, MEM + local_len, HEADS, HEAD_DIM)
    scores, valid = attention_scores(queries, keys, table, counts)
    top = jnp.max(scores, axis=-1, keepdims=True)
    expo = jnp.exp(scores - top)
    denom = jnp.sum(expo, axis=-1, keepdims=True)
    log_total = top + jnp.log(denom)
    probs_b = (expo / denom).astype(jnp.bfloat16)
    attended = jnp.einsum("bhqk,bkhd->bqhd", probs_b, vals, preferred_element_type=jnp.float32)
    attended = attended.reshape(row_count, inner_width).astype(jnp.bfloat16)
    attended_f = attended.astype(jnp.float32).reshape(row_count, 1, HEADS, HEAD_DIM)
    mixed = (
        (output_gate_t * attended_f).reshape(row_count, EXPERTS * inner_width).astype(jnp.bfloat16)
    )
    hidden = inputs + jnp.dot(mixed, w_output, preferred_element_type=jnp.float32)
    normed_two, norm2_unit, norm2_inv = norm_forward(hidden, gain_two, shift_two)
    act_two = normed_two.astype(jnp.bfloat16)
    pre_act = jnp.dot(act_two, w_in, preferred_element_type=jnp.float32)
    activated = jax.nn.gelu(pre_act, approximate=False).astype(jnp.bfloat16)
    ffn_result = jnp.dot(activated, w_out, preferred_element_type=jnp.float32)
    layer_out = (token_mask * (hidden + ffn_result)).astype(jnp.bfloat16).reshape(tokens.shape)
    upstream = cotangent.reshape(row_count, model_width).astype(jnp.float32) * token_mask
    upstream_b = upstream.astype(jnp.bfloat16)
    d_out_w = jnp.einsum("nf,nd->fd", activated, upstream_b, preferred_element_type=jnp.float32)
    d_act = jnp.einsum("nd,fd->nf", upstream_b, w_out, preferred_element_type=jnp.float32)
    d_pre = (d_act * gelu_slope(pre_act)).astype(jnp.bfloat16)
    d_in_w = jnp.einsum("nd,nf->df", act_two, d_pre, preferred_element_type=jnp.float32)
    d_norm_two = jnp.einsum("nf,df->nd", d_pre, w_in, preferred_element_type=jnp.float32)
    d_from_two, d_gain_two, d_shift_two = norm_backward(d_norm_two, norm2_unit, norm2_inv, gain_two)
    d_hidden = upstream + d_from_two
    ffn_width = d_in_w.shape[1]
    d_branch = d_hidden.astype(jnp.bfloat16)
    d_output_t = jnp.einsum("nd,nk->dk", d_branch, mixed, preferred_element_type=jnp.float32)
    d_mixed = jnp.einsum(
        "nd,kd->nk", d_branch, w_output, preferred_element_type=jnp.float32
    ).astype(jnp.bfloat16)
    d_mixed = d_mixed.astype(jnp.float32).reshape(row_count, EXPERTS, HEADS, HEAD_DIM)
    d_gate_out = jnp.sum(d_mixed * attended_f, axis=-1)
    d_attended = (
        jnp.sum(d_mixed * output_gate_t, axis=1)
        .astype(jnp.bfloat16)
        .reshape(batches, local_len, HEADS, HEAD_DIM)
    )
    probs = jnp.where(valid, jnp.exp(scores - log_total), 0.0)
    d_probs = jnp.einsum("bqhd,bkhd->bhqk", d_attended, vals, preferred_element_type=jnp.float32)
    delta = jnp.sum(d_probs * probs, axis=-1, keepdims=True)
    d_scores = probs * (d_probs - delta)
    score_sum = jnp.sum(d_scores, axis=0)
    d_table = bias_backward(score_sum, local_len)
    d_scores_b = d_scores.astype(jnp.bfloat16)
    scale = HEAD_DIM ** (-0.5)
    d_queries = (
        jnp.einsum("bhqk,bkhd->bqhd", d_scores_b, keys, preferred_element_type=jnp.float32) * scale
    )
    d_keys = (
        jnp.einsum(
            "bhqk,bqhd->bkhd", d_scores_b[..., MEM:], queries, preferred_element_type=jnp.float32
        )
        * scale
    )
    d_vals = jnp.einsum(
        "bhqk,bqhd->bkhd", probs_b[..., MEM:], d_attended, preferred_element_type=jnp.float32
    )
    d_qk = jnp.concatenate(
        [d_queries.reshape(row_count, inner_width), d_keys.reshape(row_count, inner_width)], axis=1
    ).astype(jnp.bfloat16)
    d_values = (
        d_vals.reshape(row_count, 1, HEADS, HEAD_DIM).astype(jnp.bfloat16).astype(jnp.float32)
    )
    d_gate_val = jnp.sum(parts * d_values, axis=-1)
    d_parts = (
        (value_gate_t * d_values).reshape(row_count, EXPERTS * inner_width).astype(jnp.bfloat16)
    )
    d_gates = jnp.concatenate(
        [
            jnp.transpose(d_gate_val, (0, 2, 1)).reshape(row_count, head_experts)
            * value_pick.reshape(row_count, head_experts),
            jnp.transpose(d_gate_out, (0, 2, 1)).reshape(row_count, head_experts)
            * output_pick.reshape(row_count, head_experts),
        ],
        axis=1,
    )
    d_logits = d_gates * gates * (1.0 - gates)
    d_qk_w = jnp.einsum("nd,nk->dk", act_one, d_qk, preferred_element_type=jnp.float32)
    d_value_w = jnp.einsum("nd,nk->dk", act_one, d_parts, preferred_element_type=jnp.float32)
    d_router_w = jnp.einsum("nd,nk->dk", act_one.astype(jnp.float32), d_logits, precision=HIGH)
    d_norm_one = jnp.einsum("nk,dk->nd", d_qk, w_qk, preferred_element_type=jnp.float32)
    d_norm_one = d_norm_one + jnp.einsum(
        "nk,dk->nd", d_parts, w_value, preferred_element_type=jnp.float32
    )
    d_norm_one = d_norm_one + jnp.einsum("nk,dk->nd", d_logits, router_f, precision=HIGH)
    d_from_one, d_gain_one, d_shift_one = norm_backward(d_norm_one, norm1_unit, norm1_inv, gain_one)
    input_grad = (d_hidden + d_from_one).reshape(tokens.shape)
    shares = (
        lax.psum_scatter(d_gain_one, ("doc", "tm"), scatter_dimension=0, tiled=True),
        lax.psum_scatter(d_shift_one, ("doc", "tm"), scatter_dimension=0, tiled=True),
        lax.psum_scatter(flatten(d_qk_w), ("doc", "tm"), scatter_dimension=0, tiled=True),
        lax.psum_scatter(flatten(d_router_w), ("doc", "tm"), scatter_dimension=0, tiled=True),
        lax.psum_scatter(flatten(d_value_w), ("doc", "tm"), scatter_dimension=0, tiled=True),
        lax.psum_scatter(flatten(d_output_t), ("doc", "tm"), scatter_dimension=0, tiled=True),
        lax.psum_scatter(d_table, ("doc", "tm"), scatter_dimension=1, tiled=True),
        lax.psum_scatter(d_gain_two, ("doc", "tm"), scatter_dimension=0, tiled=True),
        lax.psum_scatter(d_shift_two, ("doc", "tm"), scatter_dimension=0, tiled=True),
        lax.psum_scatter(flatten(d_in_w), ("doc", "tm"), scatter_dimension=0, tiled=True),
        lax.psum_scatter(flatten(d_out_w), ("doc", "tm"), scatter_dimension=0, tiled=True),
    )
    qk_share = shares[2].reshape(-1, 2 * inner_width)
    router_share = shares[3].reshape(-1, 2 * head_experts)
    value_share = shares[4].reshape(-1, EXPERTS * inner_width)
    output_share = shares[5].reshape(-1, EXPERTS * inner_width).T
    in_share = shares[9].reshape(-1, ffn_width)
    out_share = shares[10].reshape(-1, model_width)
    return (
        layer_out,
        input_grad,
        shares[0],
        shares[1],
        qk_share,
        router_share,
        value_share,
        output_share,
        shares[6],
        shares[7],
        shares[8],
        in_share,
        out_share,
    )


MESH = pl.DeviceIdType.MESH
PAD = 128
SIDE = 2
HALF_HEADS = HEADS // SIDE
W_QK = 2 * HALF_HEADS * PAD
W_VAL = EXPERTS * HALF_HEADS * PAD
W_MISC = 128
W_A = W_QK + W_VAL + W_MISC
W_O = EXPERTS * HALF_HEADS * PAD
MISC = W_QK + W_VAL
N_ROUTE = 2 * HALF_HEADS * EXPERTS
COL_NORM = N_ROUTE
COL_BIAS = N_ROUTE + 4
VMEM_BYTES = 60 * 1024 * 1024
SCALE = HEAD_DIM ** (-0.5)


def pad_last(a, width):
    return jnp.pad(a, [(0, 0)] * (a.ndim - 1) + [(0, width - a.shape[-1])])


def swap(a):
    count = lax.axis_size("tm")
    return lax.ppermute(a, "tm", [(i, i ^ 1) for i in range(count)])


def neighbours(count):
    d, t = lax.axis_index("doc"), lax.axis_index("tm")
    z, c = t // 2, t % 2
    return dict(
        c=(d, z * 2 + 1 - c),
        x=(d + 1 - 2 * (d % 2), t),
        y=((d + 2) % 4, t),
        up=(d, jnp.minimum(t + 2, count - 1)),
        down=(d, jnp.maximum(t - 2, 0)),
    )


def enter(nb, z, levels):
    barrier = pltpu.get_barrier_semaphore()
    for name in ("c", "x", "y"):
        pl.semaphore_signal(barrier, inc=1, device_id=nb[name], device_id_type=MESH)

    @pl.when(z < levels - 1)
    def _():
        pl.semaphore_signal(barrier, inc=1, device_id=nb["up"], device_id_type=MESH)

    @pl.when(z > 0)
    def _():
        pl.semaphore_signal(barrier, inc=1, device_id=nb["down"], device_id_type=MESH)

    ends = jnp.where(z < levels - 1, 1, 0) + jnp.where(z > 0, 1, 0)
    pl.semaphore_wait(barrier, 3 + ends)


class Gather:
    def __init__(self, ref, sems, nb, d, z, levels):
        self.ref, self.nb, self.d, self.z, self.levels = ref, nb, d, z, levels
        self.send, self.recv = sems
        self.half = ref.shape[2] // 2

    def copy(self, part, slot, to):
        return pltpu.make_async_remote_copy(
            src_ref=part, dst_ref=part, send_sem=self.send.at[slot], recv_sem=self.recv.at[slot],
            device_id=self.nb[to], device_id_type=MESH)

    def along(self, level, distance, to):
        base = 0 if to == "up" else self.levels
        return self.copy(self.ref.at[self.d, level], base + distance, to)

    def across(self, level, to, column=None):
        base = (2 if to == "x" else 3) * self.levels
        column = self.d if column is None else column
        return self.copy(self.ref.at[column, level], base + level, to)

    def corner(self, level, to, column):
        base = (4 if to == "x" else 5) * self.levels
        rows = pl.ds(self.half, self.half) if to == "x" else pl.ds(0, self.half)
        return self.copy(self.ref.at[column, level, rows], base + level, to)

    def begin(self):
        z, levels = self.z, self.levels

        @pl.when(z < levels - 1)
        def _():
            self.along(z, 1, "up").start()

        @pl.when(z > 0)
        def _():
            self.along(z, 1, "down").start()

        self.across(z, "x").start()
        self.across(z, "y").start()

    def line(self, k):
        z, levels = self.z, self.levels

        @pl.when(z >= k)
        def _():
            self.along(z - k, k, "up").wait_recv()

            @pl.when(z < levels - 1)
            def _():
                self.along(z - k, k + 1, "up").start()

            self.across(z - k, "x").start()
            self.across(z - k, "y").start()

        @pl.when(z + k < levels)
        def _():
            self.along(z + k, k, "down").wait_recv()

            @pl.when(z > 0)
            def _():
                self.along(z + k, k + 1, "down").start()

            self.across(z + k, "x").start()
            self.across(z + k, "y").start()

    def turn(self, k):
        z, levels, d = self.z, self.levels, self.d
        by_x, by_y = d + 1 - 2 * (d % 2), (d + 2) % 4

        def one(level):
            self.across(level, "x").wait_recv()
            self.corner(level, "y", by_x).start()
            self.across(level, "y").wait_recv()
            self.corner(level, "x", by_y).start()

        if k == 0:
            one(z)
        else:
            pl.when(z >= k)(lambda: one(z - k))
            pl.when(z + k < levels)(lambda: one(z + k))

    def finish(self, k):
        z, levels, d = self.z, self.levels, self.d
        by_x, by_y = d + 1 - 2 * (d % 2), (d + 2) % 4

        def one(level):
            self.corner(level, "x", by_y).wait_recv()
            self.corner(level, "y", by_x).wait_recv()

        if k == 0:
            one(z)
        else:
            pl.when(z >= k)(lambda: one(z - k))
            pl.when(z + k < levels)(lambda: one(z + k))

    def drain(self):
        z, levels, d = self.z, self.levels, self.d
        by_x, by_y = d + 1 - 2 * (d % 2), (d + 2) % 4
        for level in range(levels):
            self.across(level, "x").wait_send()
            self.across(level, "y").wait_send()
            self.corner(level, "x", by_y).wait_send()
            self.corner(level, "y", by_x).wait_send()
        for k in range(1, levels):

            @pl.when(jnp.logical_and(z >= k - 1, z < levels - 1))
            def _():
                self.along(z - k + 1, k, "up").wait_send()

            @pl.when(jnp.logical_and(z + k - 1 < levels, z > 0))
            def _():
                self.along(z + k - 1, k, "down").wait_send()


def selector(side):
    inner = HEADS * HEAD_DIM
    wide = HALF_HEADS * PAD
    src = lax.broadcasted_iota(jnp.int32, (2 * inner, 2 * wide), 0)
    dst = lax.broadcasted_iota(jnp.int32, (2 * inner, 2 * wide), 1)
    kind, head, feature = dst // wide, (dst // PAD) % HALF_HEADS, dst % PAD
    wanted = kind * inner + (side * HALF_HEADS + head) * HEAD_DIM + feature
    hit = jnp.logical_and(src == wanted, feature < HEAD_DIM)
    return jnp.where(hit, 1.0, 0.0).astype(jnp.bfloat16)


def table_by_offset(w_a, per_device, shard, local_len, spread):
    distance = MEM + local_len - 1 - lax.broadcasted_iota(jnp.int32, (1, spread), 1)
    bucket = bucket_index(distance)
    wanted = (bucket // per_device) * shard + bucket % per_device
    step = 128

    def body(i, total):
        at = pl.ds(pl.multiple_of(i * step, step), step)
        ids = lax.broadcasted_iota(jnp.int32, (step, spread), 0) + i * step
        one_hot = jnp.where(ids == wanted, 1.0, 0.0).astype(jnp.bfloat16)
        return total + dot_f32(w_a[at, MISC:W_A], one_hot, TN)

    return lax.fori_loop(0, w_a.shape[0] // step, body, jnp.zeros((W_MISC, spread), jnp.float32))


NT = (((1,), (1,)), ((), ()))
TN = (((0,), (0,)), ((), ()))


def dot_f32(a, b, dims=(((1,), (0,)), ((), ()))):
    return lax.dot_general(a, b, dims, preferred_element_type=jnp.float32)


def forward_kernel(
    levels, batches, local_len, per_device,
    a_in, o_in, i_in, f_in, x_in, g_in,
    a_out, o_out, i_all, f_all, xs_out, act_out, front_out, gates_out, win_out, probs_out, att_out,
    mixed_out, hidden_out, n2_out,
    a_all, o_all, xs, graw, win, cr, sel, unit, act, front, gates, vec, bias, probs, att, mixed,
    branch, arrived, hidden, n2,
    send, recv, csend, crecv, lsem, gsend, grecv, msend, mrecv, esend, erecv, osem,
):
    bf16, f32 = jnp.bfloat16, jnp.float32
    d, t = lax.axis_index("doc"), lax.axis_index("tm")
    z, c = t // 2, t % 2
    nb = neighbours(2 * levels)
    shard = a_in.shape[1]
    width = f_in.shape[1]
    rows = batches * local_len
    both = 2 * rows
    wide = HALF_HEADS * PAD
    own = pl.ds(pl.multiple_of(c * shard, 16), shard)
    reach = cr.shape[0]

    def local(src, dst, index):
        cp = pltpu.make_async_copy(src, dst, lsem.at[index])
        cp.start()
        return cp

    def sibling(src, dst, index):
        return pltpu.make_async_remote_copy(
            src_ref=src, dst_ref=dst, send_sem=csend.at[index], recv_sem=crecv.at[index],
            device_id=nb["c"], device_id_type=MESH)

    loc_a = local(a_in.at[c], a_all.at[d, z, own], 0)
    loc_x = local(x_in, xs.at[c], 1)
    loc_g = local(g_in, graw.at[c], 2)
    loc_o = local(o_in.at[c], o_all.at[d, z, own], 3)
    loc_i = local(i_in.at[c], i_all.at[d, z, own], 4)
    loc_f = local(f_in, f_all.at[d, z], 5)
    enter(nb, z, levels)
    rem_a = sibling(a_in.at[1 - c], a_all.at[d, z, own], 0)
    rem_x = sibling(x_in, xs.at[c], 1)
    rem_g = sibling(g_in, graw.at[c], 2)
    rem_o = sibling(o_in.at[1 - c], o_all.at[d, z, own], 3)
    rem_i = sibling(i_in.at[1 - c], i_all.at[d, z, own], 4)
    for cp in (rem_a, rem_x, rem_g, rem_o, rem_i):
        cp.start()
    ga, go, gi, gf = [
        Gather(ref, (send.at[i], recv.at[i]), nb, d, z, levels)
        for i, ref in enumerate((a_all, o_all, i_all, f_all))
    ]
    loc_a.wait()
    rem_a.wait()
    ga.begin()
    sel[...] = selector(c)

    loc_x.wait()
    rem_x.wait()
    step = 64

    def stats(i, carry):
        at = pl.ds(pl.multiple_of((i % (rows // step)) * step, step), step)
        block = i // (rows // step)
        values = xs[block, at, :width].astype(f32)
        centered = values - jnp.mean(values, axis=-1, keepdims=True)
        inverse = lax.rsqrt(jnp.mean(centered * centered, axis=-1, keepdims=True) + EPS)
        unit[pl.ds(pl.multiple_of(i * step, step), step)] = centered * inverse
        return carry

    lax.fori_loop(0, both // step, stats, 0)
    ga.line(1)

    def slot(s):
        return pl.ds(s * local_len, local_len)

    def starts_of(block, batch):
        column = xs[block, pl.ds(batch * local_len, local_len), 2 * width : 2 * width + 128]
        return column[:, 40:41].astype(f32)

    def place(block, s, follow):
        for batch in range(batches):
            at = block * batches + batch
            mine = dot_f32(graw[block, batch, slot(s)], sel[...]).astype(bf16)
            if follow:
                moved = win[at, slot(s)] if block == 0 else win[batch, slot(s + 1)]
                first = jnp.broadcast_to(starts_of(block, batch), mine.shape) > 0.5
                mine = jnp.where(first, mine.astype(f32), moved.astype(f32)).astype(bf16)
            win[at, slot(s)] = mine

    slots = MEM // local_len

    def chain(k):
        count = min(2, slots - 1 - 2 * k)
        top = slots - 2 * k
        src = win.at[pl.ds(batches, batches), pl.ds((top - count) * local_len, count * local_len)]
        dst = win.at[pl.ds(0, batches), pl.ds((top - count - 1) * local_len, count * local_len)]
        return pltpu.make_async_remote_copy(
            src_ref=src, dst_ref=dst, send_sem=gsend.at[k], recv_sem=grecv.at[k],
            device_id=nb["up"], device_id_type=MESH)

    rounds = slots // 2
    has_up, has_down = z < levels - 1, z > 0

    def chain_start(k):
        pl.when(has_up)(lambda: chain(k).start())

    def chain_round(k):
        pl.when(has_down)(lambda: chain(k).wait_recv())
        for s in (slots - 2 - 2 * k, slots - 3 - 2 * k):
            if s >= 0:
                place(0, s, True)
        for s in (slots - 3 - 2 * k, slots - 4 - 2 * k):
            if s >= 0:
                place(1, s, True)
        if k + 1 < rounds:
            chain_start(k + 1)

    loc_g.wait()
    rem_g.wait()
    place(0, slots - 1, False)
    place(1, slots - 1, False)
    place(1, slots - 2, True)
    chain_start(0)
    ga.turn(0)
    ga.line(2)
    ga.turn(1)
    chain_round(0)
    ga.line(3) if levels > 3 else None
    for k in range(4, levels):
        ga.line(k)
    loc_o.wait()
    rem_o.wait()
    go.begin()
    for k in range(2, levels):
        ga.turn(k)
    chain_round(1)
    for k in range(levels):
        ga.finish(k)
    out_a = pltpu.make_async_copy(a_all, a_out, osem.at[0])
    out_a.start()
    go.line(1)

    w_a = a_all.reshape(4 * levels * 2 * shard, W_A)
    vec[...] = w_a[:, MISC:W_A].astype(f32).T

    def norm(i, carry):
        at = pl.ds(pl.multiple_of(i * step, step), step)
        act[at] = (unit[at] * vec[COL_NORM : COL_NORM + 1] + vec[COL_NORM + 1 : COL_NORM + 2]).astype(bf16)
        return carry

    lax.fori_loop(0, both // step, norm, 0)

    def project(i, carry):
        at = pl.ds(pl.multiple_of(i * 256, 256), 256)
        front[:, at] = dot_f32(act[...], w_a[:, at])
        return carry

    lax.fori_loop(0, MISC // 256, project, 0)
    front[:, MISC:W_A] = dot_f32(act[...], w_a[:, MISC:W_A])
    go.line(2)
    go.turn(0)
    meta_at = pl.ds(pl.multiple_of(2 * width + c * 128, 128), 128)

    def gate(i, carry):
        at = pl.ds(pl.multiple_of(i * local_len, local_len), local_len)
        gated = jax.nn.sigmoid(front[at, MISC:W_A])
        gates[at] = gated
        picks = xs[i // batches, pl.ds(pl.multiple_of((i % batches) * local_len, local_len), local_len), meta_at]
        gated = gated * picks.astype(f32)
        for h in range(HALF_HEADS):
            total = jnp.zeros((local_len, PAD), f32)
            for e in range(EXPERTS):
                lane = h * EXPERTS + e
                col = W_QK + (e * HALF_HEADS + h) * PAD
                total = total + gated[:, lane : lane + 1] * front[at, col : col + PAD]
            win[i, pl.ds(MEM, local_len), wide + h * PAD : wide + (h + 1) * PAD] = total.astype(bf16)
        win[i, pl.ds(MEM, local_len), :wide] = front[at, wide : 2 * wide].astype(bf16)
        return carry

    lax.fori_loop(0, 2 * batches, gate, 0)

    def hop(k):
        src = win.at[:, pl.ds(MEM, local_len)] if k == 1 else cr.at[k - 2]
        return pltpu.make_async_remote_copy(
            src_ref=src, dst_ref=cr.at[k - 1], send_sem=msend.at[k - 1], recv_sem=mrecv.at[k - 1],
            device_id=nb["up"], device_id_type=MESH)

    def hop_start(k):
        pl.when(jnp.logical_and(has_up, z >= k - 1))(lambda: hop(k).start())

    def hop_arrived(k):
        pl.when(z >= k)(lambda: hop(k).wait_recv())

    hop_start(1)
    go.line(3) if levels > 3 else None
    for k in range(4, levels):
        go.line(k)
    go.turn(1)
    chain_round(2)
    chain_round(3)
    for k in range(4, rounds):
        chain_round(k)

    spread = MEM + 2 * local_len
    table = table_by_offset(w_a, per_device, shard, local_len, spread)
    for h in range(HALF_HEADS):
        line = jnp.broadcast_to(table[COL_BIAS + h : COL_BIAS + h + 1], (local_len, spread))
        turned = pltpu.roll(line, spread - local_len + 1, 1, stride=1, stride_axis=0)
        bias[h] = turned[:, : MEM + local_len]
    loc_i.wait()
    rem_i.wait()
    gi.begin()
    for k in range(2, levels):
        go.turn(k)
    for k in range(1, reach + 1):
        hop_arrived(k)
        if k < reach:
            hop_start(k + 1)
    gi.line(1)

    for k in range(rounds):
        pl.when(has_up)(lambda: chain(k).wait_send())
    for batch in range(batches):
        seen = []
        for back in range(slots + 1):
            block = jnp.maximum(t - c + 1 - back, 0) + d * 2 * levels
            tile = w_a[pl.ds(pl.multiple_of(block * shard, 16), 16), MISC:W_A].astype(f32)
            col = COL_BIAS + HALF_HEADS + batch
            seen.append(tile[0:1, col : col + 1])
        for block in range(2):
            stopped = jnp.zeros((1, 1), f32)
            for n in range(1, slots + 1):
                stopped = jnp.maximum(stopped, seen[n - 1 if block else n])
                if block:
                    k, which = n // 2, 1 - n % 2
                else:
                    k, which = (n + 1) // 2, n % 2
                if k > reach:
                    continue
                at = which * batches + batch
                source = win[at, pl.ds(MEM, local_len)] if k == 0 else cr[k - 1, at]
                into = block * batches + batch
                held = win[into, slot(slots - n)]
                stop = jnp.broadcast_to(stopped, held.shape) > 0.5
                win[into, slot(slots - n)] = jnp.where(stop, held.astype(f32), source.astype(f32)).astype(bf16)
    out_w = pltpu.make_async_copy(win, win_out, osem.at[1])
    out_w.start()

    key_ids = lax.broadcasted_iota(jnp.int32, (local_len, local_len), 1)
    row_ids = lax.broadcasted_iota(jnp.int32, (local_len, local_len), 0)

    def attend(i, carry):
        at = pl.ds(pl.multiple_of(i * local_len, local_len), local_len)
        block, batch = i // batches, i % batches
        rows_at = pl.ds(pl.multiple_of(batch * local_len, local_len), local_len)
        count = xs[block, rows_at, 2 * width : 2 * width + 128][:, 41:42].astype(f32)
        seen = jnp.logical_and(key_ids <= row_ids, key_ids.astype(f32) < count)
        picks = xs[block, rows_at, meta_at].astype(f32) * gates[at]
        for h in range(HALF_HEADS):
            cols = slice(h * PAD, (h + 1) * PAD)
            q = front[at, cols].astype(bf16)
            s = dot_f32(q, win[i, :, cols], NT) * SCALE + bias[h]
            s = jnp.concatenate([s[:, :MEM], jnp.where(seen, s[:, MEM:], NEG)], axis=1)
            top = jnp.max(s, axis=-1, keepdims=True)
            expo = jnp.exp(s - top)
            p = (expo * (1.0 / jnp.sum(expo, axis=-1, keepdims=True))).astype(bf16)
            probs[i, h] = p
            got = dot_f32(p, win[i, :, wide + h * PAD : wide + (h + 1) * PAD]).astype(bf16)
            att[at, cols] = got
            got = got.astype(f32)
            for e in range(EXPERTS):
                lane = HALF_HEADS * EXPERTS + h * EXPERTS + e
                col = (e * HALF_HEADS + h) * PAD
                mixed[at, col : col + PAD] = (picks[:, lane : lane + 1] * got).astype(bf16)
        return carry

    lax.fori_loop(0, 2 * batches, attend, 0)
    gi.line(2)
    gi.turn(0)
    for k in range(levels):
        go.finish(k)

    w_o = o_all.reshape(4 * levels * 2 * shard, W_O)
    far = pl.ds(pl.multiple_of((1 - c) * rows, rows), rows)
    near = pl.ds(pl.multiple_of(c * rows, rows), rows)

    def out_project(at):
        def body(i, carry):
            cols = pl.ds(pl.multiple_of(i * 256, 256), 256)
            branch[at, cols] = dot_f32(mixed[at], w_o[cols], NT)
            return carry

        lax.fori_loop(0, width // 256, body, 0)

    def exchange(src, dst, index):
        return pltpu.make_async_remote_copy(
            src_ref=src, dst_ref=dst, send_sem=esend.at[index], recv_sem=erecv.at[index],
            device_id=nb["c"], device_id_type=MESH)

    out_project(far)
    give = exchange(branch.at[far], arrived, 0)
    give.start()
    out_project(near)
    out_o = pltpu.make_async_copy(o_all, o_out, osem.at[2])
    out_o.start()
    give.wait_recv()

    def second(i, carry):
        at = pl.ds(pl.multiple_of(i * step, step), step)
        total_at = pl.ds(pl.multiple_of(c * rows + i * step, step), step)
        values = xs[c, at, :width].astype(f32) + branch[total_at] + arrived[at]
        hidden[at] = values
        centered = values - jnp.mean(values, axis=-1, keepdims=True)
        inverse = lax.rsqrt(jnp.mean(centered * centered, axis=-1, keepdims=True) + EPS)
        normed = centered * inverse * vec[COL_NORM + 2 : COL_NORM + 3] + vec[COL_NORM + 3 : COL_NORM + 4]
        n2[total_at] = normed.astype(bf16)
        return carry

    lax.fori_loop(0, rows // step, second, 0)
    pair = exchange(n2.at[near], n2.at[near], 1)
    pair.start()
    gi.line(3) if levels > 3 else None
    for k in range(4, levels):
        gi.line(k)
    loc_f.wait()
    gf.begin()
    for k in range(1, levels):
        gi.turn(k)
        gf.line(k)
    for k in range(levels):
        gf.turn(k)
    pair.wait_recv()
    outs = [
        pltpu.make_async_copy(src, dst, osem.at[3 + i])
        for i, (src, dst) in enumerate((
            (xs, xs_out), (act, act_out), (front, front_out), (gates, gates_out), (probs, probs_out),
            (att, att_out), (mixed, mixed_out), (hidden, hidden_out), (n2, n2_out)))
    ]
    for cp in outs:
        cp.start()
    for group in (gi, gf):
        for k in range(levels):
            group.finish(k)
    for group in (ga, go, gi, gf):
        group.drain()
    for cp in (give, pair):
        cp.wait_send()
    for k in range(1, reach + 1):
        pl.when(jnp.logical_and(has_up, z >= k - 1))(lambda: hop(k).wait_send())
    out_a.wait()
    out_w.wait()
    out_o.wait()
    for cp in outs:
        cp.wait()


def forward(levels, batches, local_len, per_device, packs):
    a, o, i, f, x, g = packs
    bf16, f32 = jnp.bfloat16, jnp.float32
    width = f.shape[1]
    rows = batches * local_len
    both = 2 * rows
    wide = HALF_HEADS * PAD
    two = lambda v: (4, levels, 2 * v.shape[1], v.shape[2])
    window = (2 * batches, MEM + local_len, 2 * wide)
    probs = (2 * batches, HALF_HEADS, local_len, MEM + local_len)
    outs = [
        (two(a), bf16), (two(o), bf16), (two(i), bf16), ((4, levels) + f.shape, bf16),
        ((2,) + x.shape, bf16), ((both, width), bf16), ((both, W_A), f32), ((both, W_MISC), f32),
        (window, bf16), (probs, bf16), ((both, wide), bf16), ((both, W_O), bf16),
        ((rows, width), f32), ((both, width), bf16),
    ]
    reach = min(MEM // local_len // 2, levels - 1)
    scratch = [
        (two(a), bf16), (two(o), bf16), ((2,) + x.shape, bf16), ((2,) + g.shape, bf16), (window, bf16),
        ((reach, 2 * batches, local_len, 2 * wide), bf16), ((g.shape[2], 2 * wide), bf16),
        ((both, width), f32), ((both, width), bf16), ((both, W_A), f32), ((both, W_MISC), f32),
        ((W_MISC, width), f32), ((HALF_HEADS, local_len, MEM + local_len), f32), (probs, bf16),
        ((both, wide), bf16), ((both, W_O), bf16), ((both, width), f32), ((rows, width), f32),
        ((rows, width), f32), ((both, width), bf16),
    ]
    rounds = MEM // local_len // 2
    sems = [(4, 6 * levels), (4, 6 * levels), (6,), (6,), (6,), (rounds,), (rounds,), (reach,), (reach,), (2,), (2,), (12,)]
    hbm = pl.BlockSpec(memory_space=pl.ANY)
    return pl.pallas_call(
        functools.partial(forward_kernel, levels, batches, local_len, per_device),
        out_shape=[jax.ShapeDtypeStruct(s, k) for s, k in outs],
        in_specs=[hbm] * 6,
        out_specs=[hbm] * len(outs),
        scratch_shapes=[pltpu.VMEM(s, k) for s, k in scratch] + [pltpu.SemaphoreType.DMA(s) for s in sems],
        compiler_params=pltpu.CompilerParams(
            collective_id=1, has_side_effects=True, vmem_limit_bytes=VMEM_BYTES),
    )(a, o, i, f, x, g)


def add_rows(dst, terms):
    rows, width = dst.shape
    step = 16

    def body(i, carry):
        at = pl.ds(pl.multiple_of(i * step, step), step)
        total = terms[0][at].astype(jnp.float32)
        for term in terms[1:]:
            total = total + term[at].astype(jnp.float32)
        dst[at] = total.astype(dst.dtype)
        return carry

    lax.fori_loop(0, rows // step, body, 0)


class Scatter:
    def __init__(self, src, bufs, sems, nb, d, z, levels):
        self.src, self.nb, self.d, self.z, self.levels = src, nb, d, z, levels
        self.cx, self.cy, self.rx, self.ry, self.up, self.down = bufs
        self.send, self.recv = sems
        self.half = src.shape[2] // 2
        self.by_x, self.by_y = d + 1 - 2 * (d % 2), (d + 2) % 4
        self.low, self.high = pl.ds(0, self.half), pl.ds(self.half, self.half)

    def copy(self, src, dst, slot, to):
        return pltpu.make_async_remote_copy(
            src_ref=src, dst_ref=dst, send_sem=self.send.at[slot], recv_sem=self.recv.at[slot],
            device_id=self.nb[to], device_id_type=MESH)

    def corner(self, j, to):
        part = self.low if to == "x" else self.high
        buf = self.cx if to == "x" else self.cy
        return self.copy(self.src.at[3 - self.d, j, part], buf.at[j], (0 if to == "x" else self.levels) + j, to)

    def direct(self, j, to):
        part = self.low if to == "x" else self.high
        column = self.by_x if to == "x" else self.by_y
        buf = self.rx if to == "x" else self.ry
        return self.copy(self.src.at[column, j, part], buf.at[j, part], (2 if to == "x" else 3) * self.levels + j, to)

    def relay(self, j, to):
        part = self.high if to == "x" else self.low
        held = self.cy if to == "x" else self.cx
        buf = self.rx if to == "x" else self.ry
        return self.copy(held.at[j], buf.at[j, part], (4 if to == "x" else 5) * self.levels + j, to)

    def along(self, j, to):
        buf = self.up if to == "up" else self.down
        return self.copy(buf.at[j], buf.at[j], (6 if to == "up" else 7) * self.levels + j, to)

    def begin(self):
        for j in range(self.levels):
            self.corner(j, "x").start()
            self.corner(j, "y").start()
        for j in range(self.levels):
            self.direct(j, "x").start()
            self.direct(j, "y").start()

    def turn(self, j):
        self.corner(j, "x").wait_recv()
        add_rows(self.cx.at[j], [self.cx.at[j], self.src.at[self.by_y, j, self.low]])
        self.relay(j, "y").start()
        self.corner(j, "y").wait_recv()
        add_rows(self.cy.at[j], [self.cy.at[j], self.src.at[self.by_x, j, self.high]])
        self.relay(j, "x").start()

    def column(self, j):
        self.direct(j, "x").wait_recv()
        self.direct(j, "y").wait_recv()
        self.relay(j, "x").wait_recv()
        self.relay(j, "y").wait_recv()
        add_rows(self.rx.at[j], [self.rx.at[j], self.ry.at[j], self.src.at[self.d, j]])

    def line(self, j):
        z, levels = self.z, self.levels

        @pl.when(z < j)
        def _():
            @pl.when(z > 0)
            def _():
                self.along(j, "up").wait_recv()
                add_rows(self.up.at[j], [self.up.at[j], self.rx.at[j]])

            @pl.when(z == 0)
            def _():
                add_rows(self.up.at[j], [self.rx.at[j]])

            self.along(j, "up").start()

        @pl.when(z > j)
        def _():
            @pl.when(z < levels - 1)
            def _():
                self.along(j, "down").wait_recv()
                add_rows(self.down.at[j], [self.down.at[j], self.rx.at[j]])

            @pl.when(z == levels - 1)
            def _():
                add_rows(self.down.at[j], [self.rx.at[j]])

            self.along(j, "down").start()

    def total(self, dst):
        z, levels = self.z, self.levels

        @pl.when(z == 0)
        def _():
            self.along(z, "down").wait_recv()
            add_rows(dst, [self.rx.at[z], self.down.at[z]])

        @pl.when(z == levels - 1)
        def _():
            self.along(z, "up").wait_recv()
            add_rows(dst, [self.rx.at[z], self.up.at[z]])

        @pl.when(jnp.logical_and(z > 0, z < levels - 1))
        def _():
            self.along(z, "up").wait_recv()
            self.along(z, "down").wait_recv()
            add_rows(dst, [self.rx.at[z], self.up.at[z], self.down.at[z]])

    def drain(self):
        for j in range(self.levels):
            for to in ("x", "y"):
                self.corner(j, to).wait_send()
                self.direct(j, to).wait_send()
                self.relay(j, to).wait_send()
            pl.when(self.z < j)(lambda: self.along(j, "up").wait_send())
            pl.when(self.z > j)(lambda: self.along(j, "down").wait_send())


def scatter_kernel(levels, *refs):
    d, t = lax.axis_index("doc"), lax.axis_index("tm")
    z = t // 2
    nb = neighbours(2 * levels)
    count = 4
    srcs, dsts = refs[:count], refs[count : 2 * count]
    bufs = refs[2 * count : -2]
    send, recv = refs[-2:]
    enter(nb, z, levels)
    groups = [
        Scatter(srcs[i], bufs[6 * i : 6 * i + 6], (send.at[i], recv.at[i]), nb, d, z, levels)
        for i in range(count)
    ]
    for group in groups:
        group.begin()
    for group in groups:
        for j in range(levels):
            group.turn(j)
    for group in groups:
        for j in range(levels):
            group.column(j)
        for j in range(levels):
            group.line(j)
    for group, dst in zip(groups, dsts):
        group.total(dst)
    for group in groups:
        group.drain()


def scatter(levels, parts):
    scratch = []
    for p in parts:
        rows, width = p.shape[2:]
        for r in (rows // 2, rows // 2, rows, rows, rows, rows):
            scratch.append(pltpu.VMEM((levels, r, width), jnp.bfloat16))
    vmem = pl.BlockSpec(memory_space=pltpu.VMEM)
    return pl.pallas_call(
        functools.partial(scatter_kernel, levels),
        out_shape=[jax.ShapeDtypeStruct(p.shape[2:], jnp.float32) for p in parts],
        in_specs=[vmem] * 4,
        out_specs=[vmem] * 4,
        scratch_shapes=scratch + [pltpu.SemaphoreType.DMA((4, 8 * levels))] * 2,
        compiler_params=pltpu.CompilerParams(
            collective_id=2, has_side_effects=True, vmem_limit_bytes=VMEM_BYTES),
    )(*parts)


def split_heads(a, lead):
    rows = a.shape[0]
    a = pad_last(a.reshape(rows, lead, SIDE, HALF_HEADS, HEAD_DIM), PAD)
    return jnp.transpose(a, (2, 0, 1, 3, 4)).reshape(SIDE, rows, lead * HALF_HEADS * PAD)


def join_heads(a, lead):
    rows = a.shape[1]
    a = a.reshape(SIDE, rows, lead, HALF_HEADS, PAD)[..., :HEAD_DIM]
    return jnp.transpose(a, (1, 2, 0, 3, 4)).reshape(rows, lead * HEADS * HEAD_DIM)


def bias_grad(score_sum, local_len):
    heads = score_sum.shape[0]
    spread = MEM + 2 * local_len - 1
    padded = jnp.pad(score_sum, ((0, 0), (0, 0), (local_len - 1, 0))).reshape(heads, local_len * spread)
    padded = jnp.pad(padded, ((0, 0), (0, local_len))).reshape(heads, local_len, spread + 1)
    by_distance = jnp.sum(padded, axis=1)[:, :spread][:, ::-1]
    return jnp.einsum("hk,kc->hc", by_distance, bucket_matrix(local_len), precision=HIGH)


def on_chip(
    tokens, cotangent, given_cache, value_routes, output_routes, valid_counts, doc_starts,
    norm1_gain, norm1_shift, qk_weight, router_weight, value_weight, output_weight, rel_bias,
    norm2_gain, norm2_shift, ffn_in, ffn_out,
):
    batches, unused_row, local_len, width = tokens.shape
    count = lax.axis_size("tm")
    levels = count // 2
    side = lax.axis_index("tm") % 2
    rows = batches * local_len
    shard = qk_weight.shape[0]
    blocks = 4 * levels
    bf16, f32 = jnp.bfloat16, jnp.float32

    a_qk = split_heads(qk_weight, 2)
    a_v = split_heads(value_weight, EXPERTS)
    a_o = split_heads(output_weight.T, EXPERTS)
    route = jnp.transpose(
        router_weight.reshape(shard, 2, SIDE, HALF_HEADS * EXPERTS), (2, 0, 1, 3)
    ).reshape(SIDE, shard, N_ROUTE)
    norms = jnp.broadcast_to(
        jnp.stack([norm1_gain, norm1_shift, norm2_gain, norm2_shift], axis=1)[None], (SIDE, shard, 4))
    buckets = rel_bias.shape[1]
    bias_cols = jnp.pad(
        jnp.transpose(rel_bias.reshape(SIDE, HALF_HEADS, buckets), (0, 2, 1)),
        ((0, 0), (0, shard - buckets), (0, 0)))
    starts_cols = jnp.broadcast_to(
        doc_starts.reshape(1, 1, batches).astype(bf16), (SIDE, shard, batches))
    misc = pad_last(jnp.concatenate([route, norms, bias_cols, starts_cols], axis=2), W_MISC)
    a_pack = jnp.concatenate([a_qk, a_v, misc], axis=2)
    hidden_block = ffn_out.shape[0]
    i_pack = jnp.transpose(
        ffn_in.reshape(shard, blocks, SIDE, hidden_block), (2, 0, 1, 3)
    ).reshape(SIDE, shard, blocks * hidden_block)

    mask = (jnp.arange(local_len)[None, :] < valid_counts.reshape(batches, 1)).astype(f32).reshape(rows, 1)
    x_own = tokens.reshape(rows, width)
    grad_own = (cotangent.reshape(rows, width).astype(f32) * mask).astype(bf16)
    picks = [
        jnp.transpose(
            selection(r.reshape(rows, SIDE, HALF_HEADS, TOPK)).reshape(rows, SIDE, HALF_HEADS * EXPERTS), (1, 0, 2))
        for r in (value_routes, output_routes)
    ]
    starts_col = jnp.repeat(doc_starts.reshape(batches), local_len).reshape(rows, 1).astype(bf16)
    counts_col = jnp.repeat(valid_counts.reshape(batches), local_len).reshape(rows, 1).astype(bf16)
    metas = [
        pad_last(jnp.concatenate([picks[0][s], picks[1][s]], axis=1).astype(bf16), 40) for s in range(SIDE)]
    metas = [pad_last(jnp.concatenate([m, starts_col, counts_col], axis=1), 128) for m in metas]
    x_pack = jnp.concatenate([x_own, grad_own] + metas, axis=1)
    g_pack = given_cache.reshape(batches, MEM, 2 * HEADS * HEAD_DIM)

    (a_all, o_all, i_all, f_all, x_all, act_one, front, gates, window, probs_b, attended, mixed, hidden, act_two
     ) = forward(levels, batches, local_len, buckets, (a_pack, a_o, i_pack, ffn_out, x_pack, g_pack))
    w_a = a_all.reshape(width, W_A)
    w_o = o_all.reshape(width, W_O)
    w_i = i_all.reshape(width, -1)
    w_f = f_all.reshape(-1, width)

    vectors = w_a[:, MISC + COL_NORM : MISC + COL_NORM + 4].T.astype(f32)
    gain_one, shift_one, gain_two, shift_two = [v.reshape(1, width) for v in vectors]
    both = 2 * rows
    wide = HALF_HEADS * PAD
    grad_all = x_all[:, :, width : 2 * width].reshape(both, width)
    meta_all = x_all[:, :, 2 * width :].reshape(both, 2, 128)
    pick_mine = jnp.where(side == 0, meta_all[:, 0, :N_ROUTE], meta_all[:, 1, :N_ROUTE]).astype(f32)
    gates = gates[:, :N_ROUTE]
    gated = (gates * pick_mine).reshape(both, 2, HALF_HEADS, EXPERTS)
    value_gate = jnp.transpose(gated[:, 0], (0, 2, 1))[..., None]
    output_gate = jnp.transpose(gated[:, 1], (0, 2, 1))[..., None]
    parts = front[:, W_QK:MISC].reshape(both, EXPERTS, HALF_HEADS, PAD)
    window = window.reshape(2 * batches, MEM + local_len, 2, HALF_HEADS, PAD)
    keys, vals = window[:, :, 0], window[:, :, 1]
    queries = front[:, :wide].astype(bf16).reshape(2 * batches, local_len, HALF_HEADS, PAD)
    probs = probs_b.astype(f32)
    attended_f = attended.astype(f32).reshape(both, 1, HALF_HEADS, PAD)

    def mine(a):
        return lax.dynamic_index_in_dim(a, side, 0, keepdims=False)

    def other(a):
        return lax.dynamic_index_in_dim(a, 1 - side, 0, keepdims=False)

    def paired(own):
        arrived = swap(own)
        return jnp.where(side == 0, jnp.stack([own, arrived]), jnp.stack([arrived, own])).reshape(both, -1)

    unused, unit_one, inv_one = norm_forward(x_own.astype(f32), gain_one, shift_one)

    unused, unit_two, inv_two = norm_forward(hidden, gain_two, shift_two)
    pre_act = jnp.dot(act_two, w_i, preferred_element_type=f32)
    activated = jax.nn.gelu(pre_act, approximate=False).astype(bf16)
    ffn = jnp.dot(activated, w_f, preferred_element_type=f32).reshape(2, rows, width)
    layer_out = (mask * (hidden + mine(ffn) + swap(other(ffn)))).astype(bf16).reshape(tokens.shape)
    d_f = jnp.einsum("nf,nd->fd", activated, grad_all, preferred_element_type=f32).astype(bf16)
    d_act = jnp.einsum("nd,fd->nf", grad_all, w_f, preferred_element_type=f32)
    d_pre = (d_act * gelu_slope(pre_act)).astype(bf16)
    d_i = jnp.einsum("nd,nf->df", act_two, d_pre, preferred_element_type=f32).astype(bf16)
    d_two = jnp.einsum("nf,df->nd", d_pre, w_i, preferred_element_type=f32).reshape(2, rows, width)
    d_two = mine(d_two) + swap(other(d_two))
    d_from_two, d_gain_two, d_shift_two = norm_backward(d_two, unit_two, inv_two, gain_two)
    upstream = cotangent.reshape(rows, width).astype(f32) * mask
    d_hidden = upstream + d_from_two

    d_branch = paired(d_hidden.astype(bf16))
    d_o = jnp.einsum("nd,nk->dk", d_branch, mixed, preferred_element_type=f32).astype(bf16)
    d_mixed = jnp.dot(d_branch, w_o, preferred_element_type=f32).astype(bf16)
    d_mixed = d_mixed.astype(f32).reshape(both, EXPERTS, HALF_HEADS, PAD)
    d_gate_out = jnp.sum(d_mixed * attended_f, axis=-1)
    d_attended = jnp.sum(d_mixed * output_gate, axis=1).astype(bf16).reshape(2 * batches, local_len, HALF_HEADS, PAD)
    d_probs = jnp.einsum("bqhd,bkhd->bhqk", d_attended, vals, preferred_element_type=f32)
    delta = jnp.sum(d_probs * probs, axis=-1, keepdims=True)
    d_scores = probs * (d_probs - delta)
    d_table = bias_grad(jnp.sum(d_scores, axis=0), local_len)
    d_scores_b = d_scores.astype(bf16)
    d_queries = jnp.einsum("bhqk,bkhd->bqhd", d_scores_b, keys, preferred_element_type=f32) * SCALE
    d_keys = jnp.einsum("bhqk,bqhd->bkhd", d_scores_b[..., MEM:], queries, preferred_element_type=f32) * SCALE
    d_vals = jnp.einsum("bhqk,bqhd->bkhd", probs_b[..., MEM:], d_attended, preferred_element_type=f32)
    d_values = d_vals.reshape(both, 1, HALF_HEADS, PAD).astype(bf16).astype(f32)
    d_gate_val = jnp.sum(parts * d_values, axis=-1)
    d_parts = (value_gate * d_values).reshape(both, W_VAL).astype(bf16)
    d_gates = jnp.concatenate(
        [jnp.transpose(g, (0, 2, 1)).reshape(both, HALF_HEADS * EXPERTS) for g in (d_gate_val, d_gate_out)], axis=1)
    d_logits = d_gates * pick_mine * gates * (1.0 - gates)
    d_front = jnp.concatenate(
        [
            d_queries.reshape(both, wide).astype(bf16),
            d_keys.reshape(both, wide).astype(bf16),
            d_parts,
            pad_last(d_logits.astype(bf16), W_MISC),
        ],
        axis=1,
    )
    d_a = jnp.einsum("nd,nk->dk", act_one, d_front, preferred_element_type=f32).astype(bf16)
    d_one = jnp.einsum("nk,dk->nd", d_front, w_a, preferred_element_type=f32).reshape(2, rows, width)
    d_one = mine(d_one) + swap(other(d_one))
    d_from_one, d_gain_one, d_shift_one = norm_backward(
        d_one, unit_one, inv_one, gain_one)
    input_grad = (d_hidden + d_from_one).reshape(tokens.shape)
    d_norms = jnp.stack([d_gain_one, d_shift_one, d_gain_two, d_shift_two], axis=1)
    d_bias = jnp.pad(
        d_table.T.reshape(4 * count, buckets, HALF_HEADS), ((0, 0), (0, shard - buckets), (0, 0))
    ).reshape(width, HALF_HEADS)
    d_misc = jnp.concatenate([d_norms, d_bias], axis=1).astype(bf16)
    d_a = jnp.concatenate([d_a[:, : MISC + N_ROUTE], d_misc, d_a[:, MISC + N_ROUTE + 4 + HALF_HEADS :]], axis=1)

    s_a, s_o, s_i, s_f = scatter(
        levels,
        (
            d_a.reshape(4, levels, 2 * shard, W_A),
            d_o.reshape(4, levels, 2 * shard, W_O),
            d_i.reshape(4, levels, 2 * shard, -1),
            d_f.reshape(4, levels, hidden_block, width),
        ),
    )
    chip = jnp.concatenate([s_a, s_o, s_i], axis=1).reshape(2, shard, -1)
    kept, arrived = mine(chip), swap(other(chip))
    sides = jnp.where(side == 0, jnp.stack([kept, arrived]), jnp.stack([arrived, kept]))
    qk_share = join_heads(sides[:, :, :W_QK], 2)
    value_share = join_heads(sides[:, :, W_QK:MISC], EXPERTS)
    output_share = join_heads(sides[:, :, W_A : W_A + W_O], EXPERTS).T
    misc = sides[:, :, MISC:W_A]
    router_share = jnp.transpose(
        misc[:, :, :N_ROUTE].reshape(SIDE, shard, 2, HALF_HEADS * EXPERTS), (1, 2, 0, 3)
    ).reshape(shard, 2 * HEADS * EXPERTS)
    norm_share = misc[0, :, COL_NORM : COL_NORM + 4] + misc[1, :, COL_NORM : COL_NORM + 4]
    bias_share = jnp.transpose(misc[:, :buckets, COL_BIAS : COL_BIAS + HALF_HEADS], (0, 2, 1)).reshape(HEADS, buckets)
    in_share = jnp.transpose(
        sides[:, :, W_A + W_O :].reshape(SIDE, shard, blocks, hidden_block), (1, 2, 0, 3)
    ).reshape(shard, -1)
    return (
        layer_out, input_grad, norm_share[:, 0], norm_share[:, 1], qk_share, router_share, value_share,
        output_share, bias_share, norm_share[:, 2], norm_share[:, 3], in_share, s_f,
    )


def by_size(*args):
    thin = args[9].shape[0] % 16 != 0
    paired = lax.axis_size("doc") == 4 and lax.axis_size("tm") % 2 == 0
    return on_device(*args) if thin or not paired else on_chip(*args)


def solution(mesh):
    return jax.shard_map(
        by_size,
        mesh=mesh,
        in_specs=(
            P(None, "doc", "tm", None),
            P(None, "doc", "tm", None),
            P(None, "doc", "tm", None),
            P(None, "doc", "tm", None, None),
            P(None, "doc", "tm", None, None),
            P(None, "doc", "tm"),
            P(None, "doc", "tm"),
            P(("doc", "tm")),
            P(("doc", "tm")),
            P(("doc", "tm"), None),
            P(("doc", "tm"), None),
            P(("doc", "tm"), None),
            P(None, ("doc", "tm")),
            P(None, ("doc", "tm")),
            P(("doc", "tm")),
            P(("doc", "tm")),
            P(("doc", "tm"), None),
            P(("doc", "tm"), None),
        ),
        out_specs=(
            P(None, "doc", "tm", None),
            P(None, "doc", "tm", None),
            P(("doc", "tm")),
            P(("doc", "tm")),
            P(("doc", "tm"), None),
            P(("doc", "tm"), None),
            P(("doc", "tm"), None),
            P(None, ("doc", "tm")),
            P(None, ("doc", "tm")),
            P(("doc", "tm")),
            P(("doc", "tm")),
            P(("doc", "tm"), None),
            P(("doc", "tm"), None),
        ),
        check_vma=False,
    )
```

```python
import functools

import jax
import jax.numpy as jnp
from jax import lax
from jax.experimental import pallas as pl
from jax.experimental.pallas import tpu as pltpu
from jax.sharding import PartitionSpec as P

HEADS = 4
HEAD_DIM = 112
EXPERTS = 5
TOPK = 2
MEM = 1024
BUCKETS = 256
NEAR = 128
STEP = 16


EPS = 1e-05
NEG = -1e30
HIGH = lax.Precision.HIGHEST


def shortened(array):
    return jax.tree.map(lambda a: a.astype(jnp.bfloat16) if a.dtype == jnp.float32 else a, array)


def from_behind(value, axis, steps):
    count = lax.axis_size(axis)
    first, last = (max(0, -steps), min(count, count - steps))
    return lax.ppermute(value, axis, [(source, source + steps) for source in range(first, last)])


def norm_forward(values, gain, shift):
    center_mean = jnp.mean(values, axis=-1, keepdims=True)
    centered = values - center_mean
    inverse = lax.rsqrt(jnp.mean(centered * centered, axis=-1, keepdims=True) + EPS)
    normed = centered * inverse
    return (normed * gain + shift, normed, inverse)


def norm_backward(upstream, normed, inverse, gain):
    scaled = upstream * gain
    inside = (
        scaled
        - jnp.mean(scaled, axis=-1, keepdims=True)
        - normed * jnp.mean(scaled * normed, axis=-1, keepdims=True)
    )
    return (inside * inverse, jnp.sum(upstream * normed, axis=0), jnp.sum(upstream, axis=0))


def selection(routes):
    expert_ids = jnp.arange(EXPERTS, dtype=jnp.int32)
    return jnp.sum((routes[..., None] == expert_ids).astype(jnp.float32), axis=-2)


def bucket_index(distance):
    far_bucket = NEAR + (distance - NEAR) // STEP
    return jnp.clip(jnp.where(distance < NEAR, distance, far_bucket), 0, BUCKETS - 1)


def gelu_slope(pre_act):
    return (
        0.5 * (1.0 + lax.erf(pre_act * 0.7071067811865476))
        + pre_act * jnp.exp(-0.5 * pre_act * pre_act) * 0.3989422804014327
    )


def flatten(matrix):
    return matrix.reshape(-1)


def bucket_matrix(local_len):
    spread = MEM + 2 * local_len - 1
    distance = jnp.arange(spread, dtype=jnp.int32) - (local_len - 1)
    bucket_ids = jnp.arange(BUCKETS, dtype=jnp.int32)
    return (bucket_index(distance)[:, None] == bucket_ids[None, :]).astype(jnp.float32)


def bias_matrix(table, local_len):
    spread = MEM + 2 * local_len - 1
    window = MEM + local_len
    by_distance = jnp.einsum("hc,kc->hk", table, bucket_matrix(local_len), precision=HIGH)
    turned = jnp.concatenate([by_distance[:, ::-1], jnp.zeros((HEADS, 1), jnp.float32)], axis=1)
    tiled = jnp.tile(turned, (1, local_len))[:, : local_len * spread].reshape(
        HEADS, local_len, spread
    )
    return tiled[:, :, local_len - 1 : local_len - 1 + window]


def bias_backward(score_sum, local_len):
    spread = MEM + 2 * local_len - 1
    padded = jnp.pad(score_sum, ((0, 0), (0, 0), (local_len - 1, 0))).reshape(
        HEADS, local_len * spread
    )
    padded = jnp.pad(padded, ((0, 0), (0, local_len))).reshape(HEADS, local_len, spread + 1)
    by_distance = jnp.sum(padded, axis=1)[:, :spread][:, ::-1]
    return jnp.einsum("hk,kc->hc", by_distance, bucket_matrix(local_len), precision=HIGH)


def attention_scores(queries, keys, table, counts):
    local_len = queries.shape[1]
    window = keys.shape[1]
    raw = jnp.einsum(
        "bqhd,bkhd->bhqk", queries, keys, preferred_element_type=jnp.float32
    ) * HEAD_DIM ** (-0.5)
    row_ids = jnp.arange(local_len, dtype=jnp.int32)[:, None]
    col_ids = jnp.arange(window, dtype=jnp.int32)[None, :]
    bias = bias_matrix(table, local_len)
    own_ids = col_ids - MEM
    causal = (own_ids <= row_ids)[None, None]
    live = own_ids[None, None] < counts[:, None, None, None]
    valid = jnp.logical_or((col_ids < MEM)[None, None], jnp.logical_and(causal, live))
    return (jnp.where(valid, raw + bias[None], NEG), valid)


def memory_by_hops(cache_own, given, starts, local_len):
    hops_total = MEM // local_len
    open_flag = jnp.logical_not(starts)[:, None, None]
    memory_slots = [jnp.zeros_like(cache_own) for _ in range(hops_total)]
    start_marks = starts.astype(jnp.bfloat16)
    for distance in range(1, hops_total + 1):
        if distance < hops_total:
            outgoing = (cache_own, start_marks, given[:, distance * local_len :])
        else:
            outgoing = (cache_own, start_marks)
        incoming = jax.tree.map(
            lambda part, own: part.astype(own.dtype),
            from_behind(shortened(outgoing), "tm", distance),
            outgoing,
        )
        memory_slots[hops_total - distance] = jnp.where(
            open_flag, incoming[0], memory_slots[hops_total - distance]
        )
        arrived = jnp.logical_and(open_flag, (incoming[1] > 0)[:, None, None])
        if distance < hops_total:
            for position in range(hops_total - distance):
                portion = incoming[2][:, position * local_len : (position + 1) * local_len]
                memory_slots[position] = jnp.where(arrived, portion, memory_slots[position])
        open_flag = jnp.logical_and(open_flag, jnp.logical_not(arrived))
    assembled = jnp.concatenate(memory_slots, axis=1)
    return jnp.where(starts[:, None, None], given, assembled)


def on_device(
    tokens,
    cotangent,
    given_cache,
    value_routes,
    output_routes,
    valid_counts,
    doc_starts,
    norm1_gain,
    norm1_shift,
    qk_weight,
    router_weight,
    value_weight,
    output_weight,
    rel_bias,
    norm2_gain,
    norm2_shift,
    ffn_in,
    ffn_out,
):
    batches, unused_row, local_len, model_width = tokens.shape
    row_count = batches * local_len
    inner_width = HEADS * HEAD_DIM
    head_experts = HEADS * EXPERTS
    full_weights = (
        lax.all_gather(norm1_gain, ("doc", "tm"), axis=0, tiled=True),
        lax.all_gather(norm1_shift, ("doc", "tm"), axis=0, tiled=True),
        lax.all_gather(qk_weight, ("doc", "tm"), axis=0, tiled=True),
        lax.all_gather(router_weight, ("doc", "tm"), axis=0, tiled=True),
        lax.all_gather(value_weight, ("doc", "tm"), axis=0, tiled=True),
        lax.all_gather(output_weight, ("doc", "tm"), axis=1, tiled=True),
        lax.all_gather(rel_bias, ("doc", "tm"), axis=1, tiled=True),
        lax.all_gather(norm2_gain, ("doc", "tm"), axis=0, tiled=True),
        lax.all_gather(norm2_shift, ("doc", "tm"), axis=0, tiled=True),
        lax.all_gather(ffn_in, ("doc", "tm"), axis=0, tiled=True),
        lax.all_gather(ffn_out, ("doc", "tm"), axis=0, tiled=True),
    )
    (
        gain_one,
        shift_one,
        w_qk,
        w_router,
        w_value,
        w_output,
        table_bf,
        gain_two,
        shift_two,
        w_in,
        w_out,
    ) = full_weights
    gain_one = gain_one.astype(jnp.float32)
    shift_one = shift_one.astype(jnp.float32)
    gain_two = gain_two.astype(jnp.float32)
    shift_two = shift_two.astype(jnp.float32)
    table = table_bf.astype(jnp.float32)
    router_f = w_router.astype(jnp.float32)
    inputs = tokens.reshape(row_count, model_width).astype(jnp.float32)
    counts = valid_counts.reshape(batches)
    starts = doc_starts.reshape(batches) > 0
    token_mask = (
        (jnp.arange(local_len, dtype=jnp.int32)[None, :] < counts[:, None])
        .astype(jnp.float32)
        .reshape(row_count, 1)
    )
    value_pick = selection(value_routes.reshape(row_count, HEADS, TOPK))
    output_pick = selection(output_routes.reshape(row_count, HEADS, TOPK))
    normed_one, norm1_unit, norm1_inv = norm_forward(inputs, gain_one, shift_one)
    act_one = normed_one.astype(jnp.bfloat16)
    qk_vals = jnp.dot(act_one, w_qk, preferred_element_type=jnp.float32).astype(jnp.bfloat16)
    gates = jax.nn.sigmoid(jnp.dot(act_one, w_router, preferred_element_type=jnp.float32))
    gate_value = gates[:, :head_experts].reshape(row_count, HEADS, EXPERTS) * value_pick
    gate_output = gates[:, head_experts:].reshape(row_count, HEADS, EXPERTS) * output_pick
    value_gate_t = jnp.transpose(gate_value, (0, 2, 1))[..., None]
    output_gate_t = jnp.transpose(gate_output, (0, 2, 1))[..., None]
    parts = jnp.dot(act_one, w_value, preferred_element_type=jnp.float32).reshape(
        row_count, EXPERTS, HEADS, HEAD_DIM
    )
    values = (
        jnp.sum(value_gate_t * parts, axis=1).reshape(row_count, inner_width).astype(jnp.bfloat16)
    )
    cache_own = jnp.concatenate([qk_vals[:, inner_width:], values], axis=1).reshape(
        batches, local_len, 2 * inner_width
    )
    given = given_cache.reshape(batches, MEM, 2 * inner_width)
    memory = memory_by_hops(cache_own, given, starts, local_len)
    queries = qk_vals[:, :inner_width].reshape(batches, local_len, HEADS, HEAD_DIM)
    keys = jnp.concatenate([memory[:, :, :inner_width], cache_own[:, :, :inner_width]], axis=1)
    keys = keys.reshape(batches, MEM + local_len, HEADS, HEAD_DIM)
    vals = jnp.concatenate([memory[:, :, inner_width:], cache_own[:, :, inner_width:]], axis=1)
    vals = vals.reshape(batches, MEM + local_len, HEADS, HEAD_DIM)
    scores, valid = attention_scores(queries, keys, table, counts)
    top = jnp.max(scores, axis=-1, keepdims=True)
    expo = jnp.exp(scores - top)
    denom = jnp.sum(expo, axis=-1, keepdims=True)
    log_total = top + jnp.log(denom)
    probs_b = (expo / denom).astype(jnp.bfloat16)
    attended = jnp.einsum("bhqk,bkhd->bqhd", probs_b, vals, preferred_element_type=jnp.float32)
    attended = attended.reshape(row_count, inner_width).astype(jnp.bfloat16)
    attended_f = attended.astype(jnp.float32).reshape(row_count, 1, HEADS, HEAD_DIM)
    mixed = (
        (output_gate_t * attended_f).reshape(row_count, EXPERTS * inner_width).astype(jnp.bfloat16)
    )
    hidden = inputs + jnp.dot(mixed, w_output, preferred_element_type=jnp.float32)
    normed_two, norm2_unit, norm2_inv = norm_forward(hidden, gain_two, shift_two)
    act_two = normed_two.astype(jnp.bfloat16)
    pre_act = jnp.dot(act_two, w_in, preferred_element_type=jnp.float32)
    activated = jax.nn.gelu(pre_act, approximate=False).astype(jnp.bfloat16)
    ffn_result = jnp.dot(activated, w_out, preferred_element_type=jnp.float32)
    layer_out = (token_mask * (hidden + ffn_result)).astype(jnp.bfloat16).reshape(tokens.shape)
    upstream = cotangent.reshape(row_count, model_width).astype(jnp.float32) * token_mask
    upstream_b = upstream.astype(jnp.bfloat16)
    d_out_w = jnp.einsum("nf,nd->fd", activated, upstream_b, preferred_element_type=jnp.float32)
    d_act = jnp.einsum("nd,fd->nf", upstream_b, w_out, preferred_element_type=jnp.float32)
    d_pre = (d_act * gelu_slope(pre_act)).astype(jnp.bfloat16)
    d_in_w = jnp.einsum("nd,nf->df", act_two, d_pre, preferred_element_type=jnp.float32)
    d_norm_two = jnp.einsum("nf,df->nd", d_pre, w_in, preferred_element_type=jnp.float32)
    d_from_two, d_gain_two, d_shift_two = norm_backward(d_norm_two, norm2_unit, norm2_inv, gain_two)
    d_hidden = upstream + d_from_two
    ffn_width = d_in_w.shape[1]
    d_branch = d_hidden.astype(jnp.bfloat16)
    d_output_t = jnp.einsum("nd,nk->dk", d_branch, mixed, preferred_element_type=jnp.float32)
    d_mixed = jnp.einsum(
        "nd,kd->nk", d_branch, w_output, preferred_element_type=jnp.float32
    ).astype(jnp.bfloat16)
    d_mixed = d_mixed.astype(jnp.float32).reshape(row_count, EXPERTS, HEADS, HEAD_DIM)
    d_gate_out = jnp.sum(d_mixed * attended_f, axis=-1)
    d_attended = (
        jnp.sum(d_mixed * output_gate_t, axis=1)
        .astype(jnp.bfloat16)
        .reshape(batches, local_len, HEADS, HEAD_DIM)
    )
    probs = jnp.where(valid, jnp.exp(scores - log_total), 0.0)
    d_probs = jnp.einsum("bqhd,bkhd->bhqk", d_attended, vals, preferred_element_type=jnp.float32)
    delta = jnp.sum(d_probs * probs, axis=-1, keepdims=True)
    d_scores = probs * (d_probs - delta)
    score_sum = jnp.sum(d_scores, axis=0)
    d_table = bias_backward(score_sum, local_len)
    d_scores_b = d_scores.astype(jnp.bfloat16)
    scale = HEAD_DIM ** (-0.5)
    d_queries = (
        jnp.einsum("bhqk,bkhd->bqhd", d_scores_b, keys, preferred_element_type=jnp.float32) * scale
    )
    d_keys = (
        jnp.einsum(
            "bhqk,bqhd->bkhd", d_scores_b[..., MEM:], queries, preferred_element_type=jnp.float32
        )
        * scale
    )
    d_vals = jnp.einsum(
        "bhqk,bqhd->bkhd", probs_b[..., MEM:], d_attended, preferred_element_type=jnp.float32
    )
    d_qk = jnp.concatenate(
        [d_queries.reshape(row_count, inner_width), d_keys.reshape(row_count, inner_width)], axis=1
    ).astype(jnp.bfloat16)
    d_values = (
        d_vals.reshape(row_count, 1, HEADS, HEAD_DIM).astype(jnp.bfloat16).astype(jnp.float32)
    )
    d_gate_val = jnp.sum(parts * d_values, axis=-1)
    d_parts = (
        (value_gate_t * d_values).reshape(row_count, EXPERTS * inner_width).astype(jnp.bfloat16)
    )
    d_gates = jnp.concatenate(
        [
            jnp.transpose(d_gate_val, (0, 2, 1)).reshape(row_count, head_experts)
            * value_pick.reshape(row_count, head_experts),
            jnp.transpose(d_gate_out, (0, 2, 1)).reshape(row_count, head_experts)
            * output_pick.reshape(row_count, head_experts),
        ],
        axis=1,
    )
    d_logits = d_gates * gates * (1.0 - gates)
    d_qk_w = jnp.einsum("nd,nk->dk", act_one, d_qk, preferred_element_type=jnp.float32)
    d_value_w = jnp.einsum("nd,nk->dk", act_one, d_parts, preferred_element_type=jnp.float32)
    d_router_w = jnp.einsum("nd,nk->dk", act_one.astype(jnp.float32), d_logits, precision=HIGH)
    d_norm_one = jnp.einsum("nk,dk->nd", d_qk, w_qk, preferred_element_type=jnp.float32)
    d_norm_one = d_norm_one + jnp.einsum(
        "nk,dk->nd", d_parts, w_value, preferred_element_type=jnp.float32
    )
    d_norm_one = d_norm_one + jnp.einsum("nk,dk->nd", d_logits, router_f, precision=HIGH)
    d_from_one, d_gain_one, d_shift_one = norm_backward(d_norm_one, norm1_unit, norm1_inv, gain_one)
    input_grad = (d_hidden + d_from_one).reshape(tokens.shape)
    shares = (
        lax.psum_scatter(d_gain_one, ("doc", "tm"), scatter_dimension=0, tiled=True),
        lax.psum_scatter(d_shift_one, ("doc", "tm"), scatter_dimension=0, tiled=True),
        lax.psum_scatter(flatten(d_qk_w), ("doc", "tm"), scatter_dimension=0, tiled=True),
        lax.psum_scatter(flatten(d_router_w), ("doc", "tm"), scatter_dimension=0, tiled=True),
        lax.psum_scatter(flatten(d_value_w), ("doc", "tm"), scatter_dimension=0, tiled=True),
        lax.psum_scatter(flatten(d_output_t), ("doc", "tm"), scatter_dimension=0, tiled=True),
        lax.psum_scatter(d_table, ("doc", "tm"), scatter_dimension=1, tiled=True),
        lax.psum_scatter(d_gain_two, ("doc", "tm"), scatter_dimension=0, tiled=True),
        lax.psum_scatter(d_shift_two, ("doc", "tm"), scatter_dimension=0, tiled=True),
        lax.psum_scatter(flatten(d_in_w), ("doc", "tm"), scatter_dimension=0, tiled=True),
        lax.psum_scatter(flatten(d_out_w), ("doc", "tm"), scatter_dimension=0, tiled=True),
    )
    qk_share = shares[2].reshape(-1, 2 * inner_width)
    router_share = shares[3].reshape(-1, 2 * head_experts)
    value_share = shares[4].reshape(-1, EXPERTS * inner_width)
    output_share = shares[5].reshape(-1, EXPERTS * inner_width).T
    in_share = shares[9].reshape(-1, ffn_width)
    out_share = shares[10].reshape(-1, model_width)
    return (
        layer_out,
        input_grad,
        shares[0],
        shares[1],
        qk_share,
        router_share,
        value_share,
        output_share,
        shares[6],
        shares[7],
        shares[8],
        in_share,
        out_share,
    )


MESH = pl.DeviceIdType.MESH
PAD = 128
SIDE = 2
HALF_HEADS = HEADS // SIDE
W_QK = 2 * HALF_HEADS * PAD
W_VAL = EXPERTS * HALF_HEADS * PAD
W_MISC = 128
W_A = W_QK + W_VAL + W_MISC
W_O = EXPERTS * HALF_HEADS * PAD
MISC = W_QK + W_VAL
N_ROUTE = 2 * HALF_HEADS * EXPERTS
COL_NORM = N_ROUTE
COL_BIAS = N_ROUTE + 4
VMEM_BYTES = 60 * 1024 * 1024
SCALE = HEAD_DIM ** (-0.5)


def pad_last(a, width):
    return jnp.pad(a, [(0, 0)] * (a.ndim - 1) + [(0, width - a.shape[-1])])


def neighbours(count):
    d, t = lax.axis_index("doc"), lax.axis_index("tm")
    z, c = t // 2, t % 2
    return dict(
        c=(d, z * 2 + 1 - c),
        x=(d + 1 - 2 * (d % 2), t),
        y=((d + 2) % 4, t),
        up=(d, jnp.minimum(t + 2, count - 1)),
        down=(d, jnp.maximum(t - 2, 0)),
    )


def enter(nb, z, levels):
    barrier = pltpu.get_barrier_semaphore()
    for name in ("c", "x", "y"):
        pl.semaphore_signal(barrier, inc=1, device_id=nb[name], device_id_type=MESH)

    @pl.when(z < levels - 1)
    def _():
        pl.semaphore_signal(barrier, inc=1, device_id=nb["up"], device_id_type=MESH)

    @pl.when(z > 0)
    def _():
        pl.semaphore_signal(barrier, inc=1, device_id=nb["down"], device_id_type=MESH)

    ends = jnp.where(z < levels - 1, 1, 0) + jnp.where(z > 0, 1, 0)
    pl.semaphore_wait(barrier, 3 + ends)


class Gather:
    def __init__(self, ref, sems, nb, d, z, levels):
        self.ref, self.nb, self.d, self.z, self.levels = ref, nb, d, z, levels
        self.send, self.recv = sems
        self.half = ref.shape[2] // 2

    def copy(self, part, slot, to):
        return pltpu.make_async_remote_copy(
            src_ref=part, dst_ref=part, send_sem=self.send.at[slot], recv_sem=self.recv.at[slot],
            device_id=self.nb[to], device_id_type=MESH)

    def along(self, level, distance, to):
        base = 0 if to == "up" else self.levels
        return self.copy(self.ref.at[self.d, level], base + distance, to)

    def across(self, level, to, column=None):
        base = (2 if to == "x" else 3) * self.levels
        column = self.d if column is None else column
        return self.copy(self.ref.at[column, level], base + level, to)

    def corner(self, level, to, column):
        base = (4 if to == "x" else 5) * self.levels
        rows = pl.ds(self.half, self.half) if to == "x" else pl.ds(0, self.half)
        return self.copy(self.ref.at[column, level, rows], base + level, to)

    def begin(self):
        z, levels = self.z, self.levels

        @pl.when(z < levels - 1)
        def _():
            self.along(z, 1, "up").start()

        @pl.when(z > 0)
        def _():
            self.along(z, 1, "down").start()

        self.across(z, "x").start()
        self.across(z, "y").start()

    def line(self, k):
        z, levels = self.z, self.levels

        @pl.when(z >= k)
        def _():
            self.along(z - k, k, "up").wait_recv()

            @pl.when(z < levels - 1)
            def _():
                self.along(z - k, k + 1, "up").start()

            self.across(z - k, "x").start()
            self.across(z - k, "y").start()

        @pl.when(z + k < levels)
        def _():
            self.along(z + k, k, "down").wait_recv()

            @pl.when(z > 0)
            def _():
                self.along(z + k, k + 1, "down").start()

            self.across(z + k, "x").start()
            self.across(z + k, "y").start()

    def turn(self, k):
        z, levels, d = self.z, self.levels, self.d
        by_x, by_y = d + 1 - 2 * (d % 2), (d + 2) % 4

        def one(level):
            self.across(level, "x").wait_recv()
            self.corner(level, "y", by_x).start()
            self.across(level, "y").wait_recv()
            self.corner(level, "x", by_y).start()

        if k == 0:
            one(z)
        else:
            pl.when(z >= k)(lambda: one(z - k))
            pl.when(z + k < levels)(lambda: one(z + k))

    def finish(self, k):
        z, levels, d = self.z, self.levels, self.d
        by_x, by_y = d + 1 - 2 * (d % 2), (d + 2) % 4

        def one(level):
            self.corner(level, "x", by_y).wait_recv()
            self.corner(level, "y", by_x).wait_recv()

        if k == 0:
            one(z)
        else:
            pl.when(z >= k)(lambda: one(z - k))
            pl.when(z + k < levels)(lambda: one(z + k))

    def drain(self):
        z, levels, d = self.z, self.levels, self.d
        by_x, by_y = d + 1 - 2 * (d % 2), (d + 2) % 4
        for level in range(levels):
            self.across(level, "x").wait_send()
            self.across(level, "y").wait_send()
            self.corner(level, "x", by_y).wait_send()
            self.corner(level, "y", by_x).wait_send()
        for k in range(1, levels):

            @pl.when(jnp.logical_and(z >= k - 1, z < levels - 1))
            def _():
                self.along(z - k + 1, k, "up").wait_send()

            @pl.when(jnp.logical_and(z + k - 1 < levels, z > 0))
            def _():
                self.along(z + k - 1, k, "down").wait_send()


def selector(side):
    inner = HEADS * HEAD_DIM
    wide = HALF_HEADS * PAD
    src = lax.broadcasted_iota(jnp.int32, (2 * inner, 2 * wide), 0)
    dst = lax.broadcasted_iota(jnp.int32, (2 * inner, 2 * wide), 1)
    kind, head, feature = dst // wide, (dst // PAD) % HALF_HEADS, dst % PAD
    wanted = kind * inner + (side * HALF_HEADS + head) * HEAD_DIM + feature
    hit = jnp.logical_and(src == wanted, feature < HEAD_DIM)
    return jnp.where(hit, 1.0, 0.0).astype(jnp.bfloat16)


def table_by_offset(w_a, per_device, shard, local_len, spread):
    distance = MEM + local_len - 1 - lax.broadcasted_iota(jnp.int32, (1, spread), 1)
    bucket = bucket_index(distance)
    wanted = (bucket // per_device) * shard + bucket % per_device
    step = 128

    def body(i, total):
        at = pl.ds(pl.multiple_of(i * step, step), step)
        ids = lax.broadcasted_iota(jnp.int32, (step, spread), 0) + i * step
        one_hot = jnp.where(ids == wanted, 1.0, 0.0).astype(jnp.bfloat16)
        return total + dot_f32(w_a[at, MISC:W_A], one_hot, TN)

    return lax.fori_loop(0, w_a.shape[0] // step, body, jnp.zeros((W_MISC, spread), jnp.float32))


NT = (((1,), (1,)), ((), ()))
TN = (((0,), (0,)), ((), ()))


def dot_f32(a, b, dims=(((1,), (0,)), ((), ()))):
    return lax.dot_general(a, b, dims, preferred_element_type=jnp.float32)


def forward_kernel(
    levels, batches, local_len, per_device,
    a_in, o_in, i_in, f_in, x_in, g_in,
    a_out, o_out, i_out, f_all, xs_out, act_out, front_out, gates_out, win_out, probs_out, att_out,
    mixed_out, hidden_out, n2_out, vec_out, ffn_out, slope_out,
    a_all, o_all, i_all, xs, graw, win, cr, sel, unit, act, front, gates, vec, bias, probs, att, mixed,
    arrived, hidden, n2, ffn, slope,
    send, recv, csend, crecv, lsem, gsend, grecv, msend, mrecv, esend, erecv, osem, psem,
):
    bf16, f32 = jnp.bfloat16, jnp.float32
    d, t = lax.axis_index("doc"), lax.axis_index("tm")
    z, c = t // 2, t % 2
    nb = neighbours(2 * levels)
    shard = a_in.shape[1]
    width = f_in.shape[1]
    rows = batches * local_len
    both = 2 * rows
    wide = HALF_HEADS * PAD
    own = pl.ds(pl.multiple_of(c * shard, 16), shard)
    reach = cr.shape[0]

    def local(src, dst, index):
        cp = pltpu.make_async_copy(src, dst, lsem.at[index])
        cp.start()
        return cp

    def sibling(src, dst, index):
        return pltpu.make_async_remote_copy(
            src_ref=src, dst_ref=dst, send_sem=csend.at[index], recv_sem=crecv.at[index],
            device_id=nb["c"], device_id_type=MESH)

    loc_a = local(a_in.at[c], a_all.at[d, z, own], 0)
    loc_x = local(x_in, xs.at[c], 1)
    loc_g = local(g_in, graw.at[c], 2)
    loc_o = local(o_in.at[c], o_all.at[d, z, own], 3)
    loc_i = local(i_in.at[c], i_all.at[d, z, own], 4)
    loc_f = local(f_in, f_all.at[d, z], 5)
    enter(nb, z, levels)
    rem_a = sibling(a_in.at[1 - c], a_all.at[d, z, own], 0)
    rem_x = sibling(x_in, xs.at[c], 1)
    rem_g = sibling(g_in, graw.at[c], 2)
    rem_o = sibling(o_in.at[1 - c], o_all.at[d, z, own], 3)
    rem_i = sibling(i_in.at[1 - c], i_all.at[d, z, own], 4)
    for cp in (rem_a, rem_x, rem_g, rem_o, rem_i):
        cp.start()
    ga, go, gi, gf = [
        Gather(ref, (send.at[i], recv.at[i]), nb, d, z, levels)
        for i, ref in enumerate((a_all, o_all, i_all, f_all))
    ]
    loc_a.wait()
    rem_a.wait()
    ga.begin()
    sel[...] = selector(c)

    loc_x.wait()
    rem_x.wait()
    step = 64

    def stats(i, carry):
        at = pl.ds(pl.multiple_of((i % (rows // step)) * step, step), step)
        block = i // (rows // step)
        values = xs[block, at, :width].astype(f32)
        centered = values - jnp.mean(values, axis=-1, keepdims=True)
        inverse = lax.rsqrt(jnp.mean(centered * centered, axis=-1, keepdims=True) + EPS)
        unit[pl.ds(pl.multiple_of(i * step, step), step)] = centered * inverse
        return carry

    lax.fori_loop(0, both // step, stats, 0)
    ga.line(1)

    def slot(s):
        return pl.ds(s * local_len, local_len)

    def starts_of(block, batch):
        column = xs[block, pl.ds(batch * local_len, local_len), 2 * width : 2 * width + 128]
        return column[:, 40:41].astype(f32)

    def place(block, s, follow):
        for batch in range(batches):
            at = block * batches + batch
            mine = dot_f32(graw[block, batch, slot(s)], sel[...]).astype(bf16)
            if follow:
                moved = win[at, slot(s)] if block == 0 else win[batch, slot(s + 1)]
                first = jnp.broadcast_to(starts_of(block, batch), mine.shape) > 0.5
                mine = jnp.where(first, mine.astype(f32), moved.astype(f32)).astype(bf16)
            win[at, slot(s)] = mine

    slots = MEM // local_len

    def chain(k):
        count = min(2, slots - 1 - 2 * k)
        top = slots - 2 * k
        src = win.at[pl.ds(batches, batches), pl.ds((top - count) * local_len, count * local_len)]
        dst = win.at[pl.ds(0, batches), pl.ds((top - count - 1) * local_len, count * local_len)]
        return pltpu.make_async_remote_copy(
            src_ref=src, dst_ref=dst, send_sem=gsend.at[k], recv_sem=grecv.at[k],
            device_id=nb["up"], device_id_type=MESH)

    rounds = slots // 2
    has_up, has_down = z < levels - 1, z > 0

    def chain_start(k):
        pl.when(has_up)(lambda: chain(k).start())

    def chain_round(k):
        pl.when(has_down)(lambda: chain(k).wait_recv())
        for s in (slots - 2 - 2 * k, slots - 3 - 2 * k):
            if s >= 0:
                place(0, s, True)
        for s in (slots - 3 - 2 * k, slots - 4 - 2 * k):
            if s >= 0:
                place(1, s, True)
        if k + 1 < rounds:
            chain_start(k + 1)

    loc_g.wait()
    rem_g.wait()
    place(0, slots - 1, False)
    place(1, slots - 1, False)
    place(1, slots - 2, True)
    chain_start(0)
    ga.turn(0)
    ga.line(2)
    ga.turn(1)
    chain_round(0)
    ga.line(3) if levels > 3 else None
    for k in range(4, levels):
        ga.line(k)
    loc_o.wait()
    rem_o.wait()
    go.begin()
    for k in range(2, levels):
        ga.turn(k)
    chain_round(1)
    for k in range(levels):
        ga.finish(k)
    out_a = pltpu.make_async_copy(a_all, a_out, osem.at[0])
    out_a.start()
    go.line(1)

    w_a = a_all.reshape(4 * levels * 2 * shard, W_A)
    vec[...] = w_a[:, MISC:W_A].astype(f32).T

    def norm(i, carry):
        at = pl.ds(pl.multiple_of(i * step, step), step)
        act[at] = (unit[at] * vec[COL_NORM : COL_NORM + 1] + vec[COL_NORM + 1 : COL_NORM + 2]).astype(bf16)
        return carry

    lax.fori_loop(0, both // step, norm, 0)

    def project(i, carry):
        at = pl.ds(pl.multiple_of(i * 256, 256), 256)
        front[:, at] = dot_f32(act[...], w_a[:, at])
        return carry

    lax.fori_loop(0, MISC // 256, project, 0)
    front[:, MISC:W_A] = dot_f32(act[...], w_a[:, MISC:W_A])
    go.line(2)
    go.turn(0)
    meta_at = pl.ds(pl.multiple_of(2 * width + c * 128, 128), 128)

    def gate(i, carry):
        at = pl.ds(pl.multiple_of(i * local_len, local_len), local_len)
        gated = jax.nn.sigmoid(front[at, MISC:W_A])
        gates[at] = gated
        picks = xs[i // batches, pl.ds(pl.multiple_of((i % batches) * local_len, local_len), local_len), meta_at]
        gated = gated * picks.astype(f32)
        for h in range(HALF_HEADS):
            total = jnp.zeros((local_len, PAD), f32)
            for e in range(EXPERTS):
                lane = h * EXPERTS + e
                col = W_QK + (e * HALF_HEADS + h) * PAD
                total = total + gated[:, lane : lane + 1] * front[at, col : col + PAD]
            win[i, pl.ds(MEM, local_len), wide + h * PAD : wide + (h + 1) * PAD] = total.astype(bf16)
        win[i, pl.ds(MEM, local_len), :wide] = front[at, wide : 2 * wide].astype(bf16)
        return carry

    lax.fori_loop(0, 2 * batches, gate, 0)

    def hop(k):
        src = win.at[:, pl.ds(MEM, local_len)] if k == 1 else cr.at[k - 2]
        return pltpu.make_async_remote_copy(
            src_ref=src, dst_ref=cr.at[k - 1], send_sem=msend.at[k - 1], recv_sem=mrecv.at[k - 1],
            device_id=nb["up"], device_id_type=MESH)

    def hop_start(k):
        pl.when(jnp.logical_and(has_up, z >= k - 1))(lambda: hop(k).start())

    def hop_arrived(k):
        pl.when(z >= k)(lambda: hop(k).wait_recv())

    hop_start(1)
    go.line(3) if levels > 3 else None
    for k in range(4, levels):
        go.line(k)
    go.turn(1)
    chain_round(2)
    chain_round(3)
    for k in range(4, rounds):
        chain_round(k)

    spread = MEM + 2 * local_len
    table = table_by_offset(w_a, per_device, shard, local_len, spread)
    for h in range(HALF_HEADS):
        line = jnp.broadcast_to(table[COL_BIAS + h : COL_BIAS + h + 1], (local_len, spread))
        turned = pltpu.roll(line, spread - local_len + 1, 1, stride=1, stride_axis=0)
        bias[h] = turned[:, : MEM + local_len]
    loc_i.wait()
    rem_i.wait()
    gi.begin()
    for k in range(2, levels):
        go.turn(k)
    for k in range(1, reach + 1):
        hop_arrived(k)
        if k < reach:
            hop_start(k + 1)
    gi.line(1)

    for k in range(rounds):
        pl.when(has_up)(lambda: chain(k).wait_send())
    for batch in range(batches):
        seen = []
        for back in range(slots + 1):
            block = jnp.maximum(t - c + 1 - back, 0) + d * 2 * levels
            tile = w_a[pl.ds(pl.multiple_of(block * shard, 16), 16), MISC:W_A].astype(f32)
            col = COL_BIAS + HALF_HEADS + batch
            seen.append(tile[0:1, col : col + 1])
        for block in range(2):
            stopped = jnp.zeros((1, 1), f32)
            for n in range(1, slots + 1):
                stopped = jnp.maximum(stopped, seen[n - 1 if block else n])
                if block:
                    k, which = n // 2, 1 - n % 2
                else:
                    k, which = (n + 1) // 2, n % 2
                if k > reach:
                    continue
                at = which * batches + batch
                source = win[at, pl.ds(MEM, local_len)] if k == 0 else cr[k - 1, at]
                into = block * batches + batch
                held = win[into, slot(slots - n)]
                stop = jnp.broadcast_to(stopped, held.shape) > 0.5
                win[into, slot(slots - n)] = jnp.where(stop, held.astype(f32), source.astype(f32)).astype(bf16)
    out_w = pltpu.make_async_copy(win, win_out, osem.at[1])
    out_w.start()

    key_ids = lax.broadcasted_iota(jnp.int32, (local_len, local_len), 1)
    row_ids = lax.broadcasted_iota(jnp.int32, (local_len, local_len), 0)

    def probs_copy(i, slot_of):
        return pltpu.make_async_copy(probs.at[slot_of], probs_out.at[i], psem.at[slot_of])

    def attend(i, carry):
        at = pl.ds(pl.multiple_of(i * local_len, local_len), local_len)
        block, batch = i // batches, i % batches
        rows_at = pl.ds(pl.multiple_of(batch * local_len, local_len), local_len)
        count = xs[block, rows_at, 2 * width : 2 * width + 128][:, 41:42].astype(f32)
        seen = jnp.logical_and(key_ids <= row_ids, key_ids.astype(f32) < count)
        picks = xs[block, rows_at, meta_at].astype(f32) * gates[at]
        slot_of = lax.rem(i, 2)
        pl.when(i >= 2)(lambda: probs_copy(i - 2, slot_of).wait())
        for h in range(HALF_HEADS):
            cols = slice(h * PAD, (h + 1) * PAD)
            q = front[at, cols].astype(bf16)
            s = dot_f32(q, win[i, :, cols], NT) * SCALE + bias[h]
            s = jnp.concatenate([s[:, :MEM], jnp.where(seen, s[:, MEM:], NEG)], axis=1)
            top = jnp.max(s, axis=-1, keepdims=True)
            expo = jnp.exp(s - top)
            p = expo * (1.0 / jnp.sum(expo, axis=-1, keepdims=True))
            probs[slot_of, h] = p
            p = p.astype(bf16)
            got = dot_f32(p, win[i, :, wide + h * PAD : wide + (h + 1) * PAD]).astype(bf16)
            att[at, cols] = got
            got = got.astype(f32)
            for e in range(EXPERTS):
                lane = HALF_HEADS * EXPERTS + h * EXPERTS + e
                col = (e * HALF_HEADS + h) * PAD
                mixed[at, col : col + PAD] = (picks[:, lane : lane + 1] * got).astype(bf16)
        probs_copy(i, slot_of).start()
        return carry

    lax.fori_loop(0, 2 * batches, attend, 0)
    for i in range(2 * batches - 2, 2 * batches):
        probs_copy(i, i % 2).wait()
    gi.line(2)
    gi.turn(0)
    for k in range(levels):
        go.finish(k)

    w_o = o_all.reshape(4 * levels * 2 * shard, W_O)
    branch = unit
    far = pl.ds(pl.multiple_of((1 - c) * rows, rows), rows)
    near = pl.ds(pl.multiple_of(c * rows, rows), rows)

    def out_project(at):
        def body(i, carry):
            cols = pl.ds(pl.multiple_of(i * 256, 256), 256)
            branch[at, cols] = dot_f32(mixed[at], w_o[cols], NT)
            return carry

        lax.fori_loop(0, width // 256, body, 0)

    def exchange(src, dst, index):
        return pltpu.make_async_remote_copy(
            src_ref=src, dst_ref=dst, send_sem=esend.at[index], recv_sem=erecv.at[index],
            device_id=nb["c"], device_id_type=MESH)

    out_project(far)
    give = exchange(branch.at[far], arrived, 0)
    give.start()
    out_project(near)
    out_o = pltpu.make_async_copy(o_all, o_out, osem.at[2])
    out_o.start()
    give.wait_recv()

    def second(i, carry):
        at = pl.ds(pl.multiple_of(i * step, step), step)
        total_at = pl.ds(pl.multiple_of(c * rows + i * step, step), step)
        values = xs[c, at, :width].astype(f32) + branch[total_at] + arrived[at]
        hidden[at] = values
        centered = values - jnp.mean(values, axis=-1, keepdims=True)
        inverse = lax.rsqrt(jnp.mean(centered * centered, axis=-1, keepdims=True) + EPS)
        normed = centered * inverse * vec[COL_NORM + 2 : COL_NORM + 3] + vec[COL_NORM + 3 : COL_NORM + 4]
        n2[total_at] = normed.astype(bf16)
        return carry

    lax.fori_loop(0, rows // step, second, 0)
    pair = exchange(n2.at[near], n2.at[near], 1)
    pair.start()
    gi.line(3) if levels > 3 else None
    for k in range(4, levels):
        gi.line(k)
    loc_f.wait()
    gf.begin()
    for k in range(1, levels):
        gi.turn(k)
        gf.line(k)
    gf.turn(0)
    pair.wait_recv()
    outs = [
        pltpu.make_async_copy(src, dst, osem.at[3 + i])
        for i, (src, dst) in enumerate((
            (xs, xs_out), (act, act_out), (front, front_out), (gates, gates_out),
            (att, att_out), (mixed, mixed_out), (hidden, hidden_out), (n2, n2_out), (vec, vec_out)))
    ]
    for cp in outs:
        cp.start()
    for k in range(levels):
        gi.finish(k)
    out_i = pltpu.make_async_copy(i_all, i_out, osem.at[13])
    out_i.start()

    w_i = i_all.reshape(4 * levels * 2 * shard, i_all.shape[3])

    def activate(i, carry):
        at = pl.ds(pl.multiple_of(i * 256, 256), 256)
        pre = dot_f32(n2[...], w_i[:, at])
        below = 0.5 * (1.0 + lax.erf(pre * 0.7071067811865476))
        ffn[:, at] = (pre * below).astype(bf16)
        slope[:, at] = (below + pre * jnp.exp(-0.5 * pre * pre) * 0.3989422804014327).astype(bf16)
        return carry

    steps = ffn.shape[1] // 256
    lax.fori_loop(0, steps // 2, activate, 0)
    gf.turn(1)
    lax.fori_loop(steps // 2, steps, activate, 0)
    outs += [pltpu.make_async_copy(ffn, ffn_out, osem.at[14]), pltpu.make_async_copy(slope, slope_out, osem.at[15])]
    outs[-2].start()
    outs[-1].start()
    for k in range(2, levels):
        gf.turn(k)
    for k in range(levels):
        gf.finish(k)
    for group in (ga, go, gi, gf):
        group.drain()
    for cp in (give, pair):
        cp.wait_send()
    for k in range(1, reach + 1):
        pl.when(jnp.logical_and(has_up, z >= k - 1))(lambda: hop(k).wait_send())
    out_a.wait()
    out_w.wait()
    out_o.wait()
    out_i.wait()
    for cp in outs:
        cp.wait()


def forward(levels, batches, local_len, per_device, packs):
    a, o, i, f, x, g = packs
    bf16, f32 = jnp.bfloat16, jnp.float32
    width = f.shape[1]
    rows = batches * local_len
    both = 2 * rows
    wide = HALF_HEADS * PAD
    two = lambda v: (4, levels, 2 * v.shape[1], v.shape[2])
    window = (2 * batches, MEM + local_len, 2 * wide)
    probs = (2 * batches, HALF_HEADS, local_len, MEM + local_len)
    outs = [
        (two(a), bf16), (two(o), bf16), (two(i), bf16), ((4, levels) + f.shape, bf16),
        ((2,) + x.shape, bf16), ((both, width), bf16), ((both, W_A), f32), ((both, W_MISC), f32),
        (window, bf16), (probs, f32), ((both, wide), bf16), ((both, W_O), bf16),
        ((rows, width), f32), ((both, width), bf16), ((W_MISC, width), f32), ((both, i.shape[2]), bf16),
        ((both, i.shape[2]), bf16),
    ]
    reach = min(MEM // local_len // 2, levels - 1)
    scratch = [
        (two(a), bf16), (two(o), bf16), (two(i), bf16), ((2,) + x.shape, bf16), ((2,) + g.shape, bf16),
        (window, bf16), ((reach, 2 * batches, local_len, 2 * wide), bf16), ((g.shape[2], 2 * wide), bf16),
        ((both, width), f32), ((both, width), bf16), ((both, W_A), f32), ((both, W_MISC), f32),
        ((W_MISC, width), f32), ((HALF_HEADS, local_len, MEM + local_len), f32), ((2,) + probs[1:], f32),
        ((both, wide), bf16), ((both, W_O), bf16), ((rows, width), f32),
        ((rows, width), f32), ((both, width), bf16), ((both, i.shape[2]), bf16), ((both, i.shape[2]), bf16),
    ]
    rounds = MEM // local_len // 2
    sems = [(4, 6 * levels), (4, 6 * levels), (6,), (6,), (6,), (rounds,), (rounds,), (reach,), (reach,), (2,), (2,), (16,), (2,)]
    hbm = pl.BlockSpec(memory_space=pl.ANY)
    return pl.pallas_call(
        functools.partial(forward_kernel, levels, batches, local_len, per_device),
        out_shape=[jax.ShapeDtypeStruct(s, k) for s, k in outs],
        in_specs=[hbm] * 6,
        out_specs=[hbm] * len(outs),
        scratch_shapes=[pltpu.VMEM(s, k) for s, k in scratch] + [pltpu.SemaphoreType.DMA(s) for s in sems],
        compiler_params=pltpu.CompilerParams(
            collective_id=1, has_side_effects=True, vmem_limit_bytes=VMEM_BYTES),
    )(a, o, i, f, x, g)


def add_rows(dst, terms):
    rows, width = dst.shape
    step = 16

    def body(i, carry):
        at = pl.ds(pl.multiple_of(i * step, step), step)
        total = terms[0][at].astype(jnp.float32)
        for term in terms[1:]:
            total = total + term[at].astype(jnp.float32)
        dst[at] = total.astype(dst.dtype)
        return carry

    lax.fori_loop(0, rows // step, body, 0)


class Scatter:
    def __init__(self, src, bufs, sems, nb, d, z, levels):
        self.src, self.nb, self.d, self.z, self.levels = src, nb, d, z, levels
        self.cx, self.cy, self.rx, self.ry, self.up, self.down = bufs
        self.send, self.recv = sems
        self.half = src.shape[2] // 2
        self.by_x, self.by_y = d + 1 - 2 * (d % 2), (d + 2) % 4
        self.low, self.high = pl.ds(0, self.half), pl.ds(self.half, self.half)
        self.columns = (3 - d, self.by_x, self.by_y, d)
        self.order = []
        for k in range((levels + 1) // 2):
            self.order += [levels - 1 - k, k] if levels - 1 - k != k else [k]

    def copy(self, src, dst, slot, to):
        return pltpu.make_async_remote_copy(
            src_ref=src, dst_ref=dst, send_sem=self.send.at[slot], recv_sem=self.recv.at[slot],
            device_id=self.nb[to], device_id_type=MESH)

    def corner(self, j, to):
        part = self.low if to == "x" else self.high
        buf = self.cx if to == "x" else self.cy
        return self.copy(self.src.at[3 - self.d, j, part], buf.at[j], (0 if to == "x" else self.levels) + j, to)

    def direct(self, j, to):
        part = self.low if to == "x" else self.high
        column = self.by_x if to == "x" else self.by_y
        buf = self.rx if to == "x" else self.ry
        return self.copy(self.src.at[column, j, part], buf.at[j, part], (2 if to == "x" else 3) * self.levels + j, to)

    def relay(self, j, to):
        part = self.high if to == "x" else self.low
        held = self.cy if to == "x" else self.cx
        buf = self.rx if to == "x" else self.ry
        return self.copy(held.at[j], buf.at[j, part], (4 if to == "x" else 5) * self.levels + j, to)

    def along(self, j, to):
        buf = self.up if to == "up" else self.down
        return self.copy(buf.at[j], buf.at[j], (6 if to == "up" else 7) * self.levels + j, to)

    def begin(self, place):
        for j in self.order:
            if place == 0:
                self.corner(j, "x").start()
                self.corner(j, "y").start()
            elif place == 1:
                self.direct(j, "x").start()
            elif place == 2:
                self.direct(j, "y").start()

    def turn(self, j):
        self.corner(j, "x").wait_recv()
        add_rows(self.cx.at[j], [self.cx.at[j], self.src.at[self.by_y, j, self.low]])
        self.relay(j, "y").start()
        self.corner(j, "y").wait_recv()
        add_rows(self.cy.at[j], [self.cy.at[j], self.src.at[self.by_x, j, self.high]])
        self.relay(j, "x").start()

    def column(self, j):
        self.direct(j, "x").wait_recv()
        self.direct(j, "y").wait_recv()
        self.relay(j, "x").wait_recv()
        self.relay(j, "y").wait_recv()
        add_rows(self.rx.at[j], [self.rx.at[j], self.ry.at[j], self.src.at[self.d, j]])

    def line(self, j):
        z, levels = self.z, self.levels

        @pl.when(z < j)
        def _():
            @pl.when(z > 0)
            def _():
                self.along(j, "up").wait_recv()
                add_rows(self.up.at[j], [self.up.at[j], self.rx.at[j]])

            @pl.when(z == 0)
            def _():
                add_rows(self.up.at[j], [self.rx.at[j]])

            self.along(j, "up").start()

        @pl.when(z > j)
        def _():
            @pl.when(z < levels - 1)
            def _():
                self.along(j, "down").wait_recv()
                add_rows(self.down.at[j], [self.down.at[j], self.rx.at[j]])

            @pl.when(z == levels - 1)
            def _():
                add_rows(self.down.at[j], [self.rx.at[j]])

            self.along(j, "down").start()

    def total(self, dst):
        z, levels = self.z, self.levels

        @pl.when(z == 0)
        def _():
            self.along(z, "down").wait_recv()
            add_rows(dst, [self.rx.at[z], self.down.at[z]])

        @pl.when(z == levels - 1)
        def _():
            self.along(z, "up").wait_recv()
            add_rows(dst, [self.rx.at[z], self.up.at[z]])

        @pl.when(jnp.logical_and(z > 0, z < levels - 1))
        def _():
            self.along(z, "up").wait_recv()
            self.along(z, "down").wait_recv()
            add_rows(dst, [self.rx.at[z], self.up.at[z], self.down.at[z]])

    def drain(self):
        for j in range(self.levels):
            for to in ("x", "y"):
                self.corner(j, to).wait_send()
                self.direct(j, to).wait_send()
                self.relay(j, to).wait_send()
            pl.when(self.z < j)(lambda: self.along(j, "up").wait_send())
            pl.when(self.z > j)(lambda: self.along(j, "down").wait_send())


def scatter_scratch(levels, shapes):
    out = []
    for rows, width in shapes:
        out.append(((4, levels, rows, width), jnp.bfloat16))
        for r in (rows // 2, rows // 2, rows, rows, rows, rows):
            out.append(((levels, r, width), jnp.bfloat16))
    return out


def norm_rows(values):
    centered = values - jnp.mean(values, axis=-1, keepdims=True)
    inverse = lax.rsqrt(jnp.mean(centered * centered, axis=-1, keepdims=True) + EPS)
    return centered * inverse, inverse


def norm_rows_backward(upstream, normed, inverse, gain):
    scaled = upstream * gain
    inside = (
        scaled
        - jnp.mean(scaled, axis=-1, keepdims=True)
        - normed * jnp.mean(scaled * normed, axis=-1, keepdims=True)
    )
    return inside * inverse


def middle_kernel(
    levels, batches, local_len, per_device, shard,
    wf_in, wi_in, wo_in, act_in, slope_in, xs_in, n2_in, hidden_in, vec_in, att_in, gates_in, front_in,
    win_in, probs_in,
    f_out, i_out, layer_out, dfront_out, db_out, dhid_out, dnorm_out, mbias_out,
    w_f, w_i, w_o, act, slope, grad, meta, n2, hidden, vec, att, gates, front, win, probs,
    branch, arrived, dhid, db, dmix, dfront, dsum, datt, dnorm, result, mbias, f_total, i_total,
    *rest,
):
    bf16, f32 = jnp.bfloat16, jnp.float32
    f_bufs, i_bufs = rest[:7], rest[7:14]
    send, recv, lsem, tsem, esend, erecv, osem = rest[14:]
    d, t = lax.axis_index("doc"), lax.axis_index("tm")
    z, c = t // 2, t % 2
    nb = neighbours(2 * levels)
    width = w_f.shape[1]
    rows = batches * local_len
    both = 2 * rows
    wide = HALF_HEADS * PAD
    ff = act.shape[1]
    far = pl.ds(pl.multiple_of((1 - c) * rows, rows), rows)
    near = pl.ds(pl.multiple_of(c * rows, rows), rows)

    def load(src, dst, index):
        cp = pltpu.make_async_copy(src, dst, lsem.at[index])
        cp.start()
        return cp

    meta_at = pl.ds(pl.multiple_of(2 * width + c * 128, 128), 128)
    l_act = load(act_in, act, 0)
    l_grad = load(xs_in.at[:, :, pl.ds(width, width)], grad, 1)
    l_wf = load(wf_in, w_f, 2)
    l_slope = load(slope_in, slope, 3)
    l_n2 = load(n2_in, n2, 4)
    l_wi = load(wi_in, w_i, 5)
    l_hid = load(hidden_in, hidden, 6)
    l_vec = load(vec_in, vec, 7)
    l_meta = load(xs_in.at[:, :, meta_at], meta, 8)
    l_att = load(att_in, att, 9)
    l_gates = load(gates_in, gates, 10)
    l_wo = load(wo_in, w_o, 11)

    def tiles(i, slot):
        at = pl.ds(pl.multiple_of(i * local_len, local_len), local_len)
        return [
            pltpu.make_async_copy(win_in.at[i], win.at[slot], tsem.at[0, slot]),
            pltpu.make_async_copy(probs_in.at[i], probs.at[slot], tsem.at[1, slot]),
            pltpu.make_async_copy(front_in.at[at], front.at[slot], tsem.at[2, slot]),
        ]

    for cp in tiles(0, 0):
        cp.start()
    enter(nb, z, levels)
    sf = Scatter(f_bufs[0], f_bufs[1:], (send.at[0], recv.at[0]), nb, d, z, levels)
    si = Scatter(i_bufs[0], i_bufs[1:], (send.at[1], recv.at[1]), nb, d, z, levels)

    l_act.wait()
    l_grad.wait()
    g_all = grad.reshape(both, width)
    f_rows = f_bufs[0].shape[2]
    span = levels * f_rows
    for place, column in enumerate(sf.columns):
        at = pl.ds(pl.multiple_of(column * span, span), span)
        got = dot_f32(act[:, at], g_all[...], TN).astype(bf16)
        f_bufs[0][column] = got.reshape(levels, f_rows, width)
        sf.begin(place)

    l_wf.wait()
    l_slope.wait()

    def back(i, carry):
        at = pl.ds(pl.multiple_of(i * 256, 256), 256)
        slope[:, at] = (dot_f32(g_all[...], w_f[at], NT) * slope[:, at].astype(f32)).astype(bf16)
        return carry

    lax.fori_loop(0, ff // 256, back, 0)
    l_n2.wait()
    i_rows = i_bufs[0].shape[2]
    span = levels * i_rows
    for place, column in enumerate(si.columns):
        at = pl.ds(pl.multiple_of(column * span, span), span)

        def weights(i, carry):
            cols = pl.ds(pl.multiple_of(i * 512, 512), 512)
            got = dot_f32(n2[:, at], slope[:, cols], TN).astype(bf16)
            i_bufs[0][column, :, :, cols] = got.reshape(levels, i_rows, 512)
            return carry

        lax.fori_loop(0, ff // 512, weights, 0)
        si.begin(place)

    def exchange(src, dst, index):
        return pltpu.make_async_remote_copy(
            src_ref=src, dst_ref=dst, send_sem=esend.at[index], recv_sem=erecv.at[index],
            device_id=nb["c"], device_id_type=MESH)

    l_wi.wait()

    def input_side(at):
        def body(i, carry):
            cols = pl.ds(pl.multiple_of(i * 256, 256), 256)
            branch[at, cols] = dot_f32(slope[at], w_i[cols], NT)
            return carry

        lax.fori_loop(0, width // 256, body, 0)

    input_side(far)
    give = exchange(branch.at[far], arrived, 0)
    give.start()
    input_side(near)
    for j in sf.order:
        sf.turn(j)
    l_hid.wait()
    l_vec.wait()
    give.wait()
    dnorm[...] = jnp.zeros_like(dnorm)
    step = 64

    def second(i, carry):
        at = pl.ds(pl.multiple_of(i * step, step), step)
        total_at = pl.ds(pl.multiple_of(c * rows + i * step, step), step)
        normed, inverse = norm_rows(hidden[at])
        up = branch[total_at] + arrived[at]
        dnorm[0:1] += jnp.sum(up * normed, axis=0, keepdims=True)
        dnorm[1:2] += jnp.sum(up, axis=0, keepdims=True)
        got = norm_rows_backward(up, normed, inverse, vec[COL_NORM + 2 : COL_NORM + 3])
        got = got + grad[c, at].astype(f32)
        dhid[at] = got
        db[total_at] = got.astype(bf16)
        return carry

    lax.fori_loop(0, rows // step, second, 0)
    pair = exchange(db.at[near], db.at[near], 1)
    pair.start()

    def output_side(at):
        def body(i, carry):
            cols = pl.ds(pl.multiple_of(i * 256, 256), 256)
            branch[at, cols] = dot_f32(act[at], w_f[:, cols])
            return carry

        lax.fori_loop(0, width // 256, body, 0)

    output_side(far)
    pair.wait()
    last = exchange(branch.at[far], arrived, 2)
    last.start()
    l_wo.wait()

    def mix(i, carry):
        cols = pl.ds(pl.multiple_of(i * wide, wide), wide)
        dmix[:, cols] = dot_f32(db[...], w_o[:, cols]).astype(bf16)
        return carry

    lax.fori_loop(0, EXPERTS, mix, 0)
    l_meta.wait()
    l_att.wait()
    l_gates.wait()
    dsum[...] = jnp.zeros_like(dsum)
    lanes = lax.broadcasted_iota(jnp.int32, (local_len, W_MISC), 1)

    def attend(i, carry):
        slot = lax.rem(i, 2)

        @pl.when(i + 1 < 2 * batches)
        def _():
            for cp in tiles(i + 1, 1 - slot):
                cp.start()

        for cp in tiles(i, slot):
            cp.wait()
        at = pl.ds(pl.multiple_of(i * local_len, local_len), local_len)
        block, batch = i // batches, i % batches
        rows_at = pl.ds(pl.multiple_of(batch * local_len, local_len), local_len)
        gate = gates[at]
        picks = meta[block, rows_at].astype(f32)
        gated = gate * picks
        d_gates = jnp.zeros((local_len, W_MISC), f32)
        for h in range(HALF_HEADS):
            cols = slice(h * PAD, (h + 1) * PAD)
            v_cols = slice(wide + h * PAD, wide + (h + 1) * PAD)
            got = att[at, cols].astype(f32)
            d_att = jnp.zeros((local_len, PAD), f32)
            for e in range(EXPERTS):
                lane = HALF_HEADS * EXPERTS + h * EXPERTS + e
                col = (e * HALF_HEADS + h) * PAD
                part = dmix[at, col : col + PAD].astype(f32)
                d_att = d_att + gated[:, lane : lane + 1] * part
                d_gates = jnp.where(lanes == lane, jnp.sum(part * got, axis=-1, keepdims=True), d_gates)
            d_att = d_att.astype(bf16)
            p = probs[slot, h]
            d_p = dot_f32(d_att, win[slot, :, v_cols], NT)
            delta = jnp.sum(d_p * p, axis=-1, keepdims=True)
            d_s = p * (d_p - delta)
            dsum[h] += d_s
            d_s = d_s.astype(bf16)
            q = front[slot, :, cols].astype(bf16)
            d_q = dot_f32(d_s, win[slot, :, cols]) * SCALE
            d_k = dot_f32(d_s[:, MEM:], q, TN) * SCALE
            d_v = dot_f32(p[:, MEM:].astype(bf16), d_att, TN).astype(bf16).astype(f32)
            dfront[at, cols] = d_q.astype(bf16)
            dfront[at, wide + h * PAD : wide + (h + 1) * PAD] = d_k.astype(bf16)
            for e in range(EXPERTS):
                lane = h * EXPERTS + e
                col = W_QK + (e * HALF_HEADS + h) * PAD
                part = front[slot, :, col : col + PAD]
                d_gates = jnp.where(lanes == lane, jnp.sum(part * d_v, axis=-1, keepdims=True), d_gates)
                dfront[at, col : col + PAD] = (gated[:, lane : lane + 1] * d_v).astype(bf16)
        d_logits = jnp.where(lanes < N_ROUTE, d_gates * picks * gate * (1.0 - gate), 0.0)
        dfront[at, MISC:W_A] = d_logits.astype(bf16)
        return carry

    lax.fori_loop(0, batches, attend, 0)
    for j in sf.order:
        sf.column(j)
    for j in sf.order:
        sf.line(j)
    for j in si.order:
        si.turn(j)
    lax.fori_loop(batches, 2 * batches, attend, 0)
    outs = [
        pltpu.make_async_copy(src, dst, osem.at[i])
        for i, (src, dst) in enumerate(((dfront, dfront_out), (db, db_out), (dhid, dhid_out), (dnorm, dnorm_out)))
    ]
    for cp in outs:
        cp.start()
    output_side(near)
    last.wait()

    def final(i, carry):
        at = pl.ds(pl.multiple_of(i * step, step), step)
        total_at = pl.ds(pl.multiple_of(c * rows + i * step, step), step)
        tail = meta[c, at].astype(f32)
        position = lax.broadcasted_iota(jnp.int32, (step, 1), 0) + (i * step) % local_len
        keep = position.astype(f32) < tail[:, 41:42]
        total = hidden[at] + branch[total_at] + arrived[at]
        result[at] = jnp.where(keep, total, 0.0).astype(bf16)
        return carry

    lax.fori_loop(0, rows // step, final, 0)
    out_r = pltpu.make_async_copy(result, layer_out, osem.at[4])
    out_r.start()
    for j in si.order:
        si.column(j)
    for j in si.order:
        si.line(j)
    sf.total(f_total)
    out_f = pltpu.make_async_copy(f_total, f_out, osem.at[5])
    out_f.start()

    spread = MEM + 2 * local_len
    ids = lax.broadcasted_iota(jnp.int32, (local_len, 1), 0)
    lines = []
    for h in range(HALF_HEADS):
        turned = jnp.concatenate([dsum[h], jnp.zeros((local_len, local_len), f32)], axis=1)
        bit = 1
        while bit < local_len:
            moved = pltpu.roll(turned, bit, 1)
            turned = jnp.where(((local_len - 1 - ids) // bit) % 2 == 1, moved, turned)
            bit *= 2
        lines.append(jnp.sum(turned, axis=0, keepdims=True))
    row_of = lax.broadcasted_iota(jnp.int32, (W_MISC, spread), 0)
    table = jnp.zeros((W_MISC, spread), f32)
    for h in range(HALF_HEADS):
        table = jnp.where(row_of == COL_BIAS + h, lines[h], table)
    high = table.astype(bf16)
    low = (table - high.astype(f32)).astype(bf16)
    distance = MEM + local_len - 1 - lax.broadcasted_iota(jnp.int32, (1, spread), 1)
    bucket = bucket_index(distance)
    wanted = (bucket // per_device) * shard + bucket % per_device

    def by_bucket(i, carry):
        at = pl.ds(pl.multiple_of(i * 128, 128), 128)
        row_ids = lax.broadcasted_iota(jnp.int32, (128, spread), 0) + i * 128
        one_hot = jnp.where(row_ids == wanted, 1.0, 0.0).astype(bf16)
        mbias[at] = dot_f32(one_hot, high, NT) + dot_f32(one_hot, low, NT)
        return carry

    lax.fori_loop(0, mbias.shape[0] // 128, by_bucket, 0)
    out_m = pltpu.make_async_copy(mbias, mbias_out, osem.at[6])
    out_m.start()
    si.total(i_total)
    mine, other = [pl.ds(pl.multiple_of(k * shard, 16), shard) for k in (c, 1 - c)]
    keep = pltpu.make_async_copy(i_total.at[mine], i_out.at[c], osem.at[7])
    keep.start()
    swap_i = exchange(i_total.at[other], i_out.at[c], 3)
    swap_i.start()
    sf.drain()
    si.drain()
    for cp in outs + [out_r, out_f, out_m, keep, swap_i]:
        cp.wait()


def kernel_call(body, ins, outs, scratch, sems, collective):
    hbm = pl.BlockSpec(memory_space=pl.ANY)
    return pl.pallas_call(
        body,
        out_shape=[jax.ShapeDtypeStruct(s, k) for s, k in outs],
        in_specs=[hbm] * len(ins),
        out_specs=[hbm] * len(outs),
        scratch_shapes=[pltpu.VMEM(s, k) for s, k in scratch] + [pltpu.SemaphoreType.DMA(s) for s in sems],
        compiler_params=pltpu.CompilerParams(
            collective_id=collective, has_side_effects=True, vmem_limit_bytes=VMEM_BYTES),
    )(*ins)


def middle(levels, batches, local_len, per_device, shard, ins):
    bf16, f32 = jnp.bfloat16, jnp.float32
    w_f, w_i, w_o, act, slope, xs, n2, hidden, vec, att, gates, front, win, probs = ins
    ff, width = w_f.shape
    rows = batches * local_len
    both = 2 * rows
    f_rows = ff // (4 * levels)
    i_rows = width // (4 * levels)
    outs = [
        ((f_rows, width), f32), ((SIDE, shard, ff), f32), ((rows, width), bf16), ((both, W_A), bf16),
        ((both, width), bf16), ((rows, width), f32), ((8, width), f32), ((width, W_MISC), f32),
    ]
    scratch = [(v.shape, v.dtype) for v in (w_f, w_i, w_o, act, slope)]
    scratch += [((2, rows, width), bf16), ((2, rows, 128), bf16)]
    scratch += [(v.shape, v.dtype) for v in (n2, hidden, vec, att, gates)]
    scratch += [((2, local_len, W_A), f32), ((2,) + win.shape[1:], bf16), ((2,) + probs.shape[1:], f32)]
    scratch += [
        ((both, width), f32), ((rows, width), f32), ((rows, width), f32), ((both, width), bf16),
        ((both, W_O), bf16), ((both, W_A), bf16), ((HALF_HEADS, local_len, MEM + local_len), f32),
        ((8, 128), f32), ((8, width), f32), ((rows, width), bf16), ((width, W_MISC), f32),
        ((f_rows, width), f32), ((i_rows, ff), f32),
    ]
    scratch += scatter_scratch(levels, [(f_rows, width), (i_rows, ff)])
    sems = [(2, 8 * levels), (2, 8 * levels), (12,), (3, 2), (4,), (4,), (8,)]
    body = functools.partial(middle_kernel, levels, batches, local_len, per_device, shard)
    return kernel_call(body, ins, outs, scratch, sems, 2)


def last_kernel(
    levels, batches, local_len, shard,
    db_in, mixed_in, act_in, dfront_in, wa_in, mbias_in, dnorm_in, dhid_in, xs_in, vec_in,
    a_out, o_out, m_out, grad_out,
    db, mixed, act, dfront, w_a, mbias, dnorm, dhid, x_own, vec, branch, arrived, result, norms,
    a_total, o_total, m_total, *rest,
):
    bf16, f32 = jnp.bfloat16, jnp.float32
    a_bufs, o_bufs, m_bufs = rest[:7], rest[7:14], rest[14:21]
    send, recv, lsem, esend, erecv, osem = rest[21:]
    d, t = lax.axis_index("doc"), lax.axis_index("tm")
    z, c = t // 2, t % 2
    nb = neighbours(2 * levels)
    width = db.shape[1]
    rows = batches * local_len
    far = pl.ds(pl.multiple_of((1 - c) * rows, rows), rows)
    near = pl.ds(pl.multiple_of(c * rows, rows), rows)
    pairs = (
        (db_in, db), (mixed_in, mixed), (act_in, act), (dfront_in, dfront), (wa_in, w_a), (mbias_in, mbias),
        (dnorm_in, dnorm), (dhid_in, dhid), (xs_in.at[c, :, pl.ds(0, width)], x_own), (vec_in, vec))
    loads = [pltpu.make_async_copy(src, dst, lsem.at[i]) for i, (src, dst) in enumerate(pairs)]
    for cp in loads:
        cp.start()
    enter(nb, z, levels)
    so, sa, sm = [
        Scatter(bufs[0], bufs[1:], (send.at[i], recv.at[i]), nb, d, z, levels)
        for i, bufs in enumerate((o_bufs, a_bufs, m_bufs))
    ]
    block_rows = o_bufs[0].shape[2]
    span = levels * block_rows

    def weight_grad(scatter, left, right, chunk):
        total = right.shape[1] if scatter is so else MISC
        for place, column in enumerate(scatter.columns):
            at = pl.ds(pl.multiple_of(column * span, span), span)

            def body(i, carry):
                cols = pl.ds(pl.multiple_of(i * chunk, chunk), chunk)
                got = dot_f32(left[:, at], right[:, cols], TN).astype(bf16)
                scatter.src[column, :, :, cols] = got.reshape(levels, block_rows, chunk)
                return carry

            lax.fori_loop(0, total // chunk, body, 0)
            scatter.begin(place)

    loads[0].wait()
    loads[1].wait()
    weight_grad(so, db, mixed, 640)
    loads[2].wait()
    loads[3].wait()
    weight_grad(sa, act, dfront, 896)
    for j in so.order:
        so.turn(j)
    loads[4].wait()

    def exchange(src, dst, index):
        return pltpu.make_async_remote_copy(
            src_ref=src, dst_ref=dst, send_sem=esend.at[index], recv_sem=erecv.at[index],
            device_id=nb["c"], device_id_type=MESH)

    def input_side(at):
        def body(i, carry):
            cols = pl.ds(pl.multiple_of(i * 256, 256), 256)
            branch[at, cols] = dot_f32(dfront[at], w_a[cols], NT)
            return carry

        lax.fori_loop(0, width // 256, body, 0)

    input_side(far)
    give = exchange(branch.at[far], arrived, 0)
    give.start()
    input_side(near)
    for cp in loads[5:]:
        cp.wait()
    give.wait()
    norms[...] = jnp.zeros_like(norms)
    norms[COL_NORM + 2 : COL_NORM + 4] = dnorm[0:2]
    step = 64

    def first(i, carry):
        at = pl.ds(pl.multiple_of(i * step, step), step)
        total_at = pl.ds(pl.multiple_of(c * rows + i * step, step), step)
        normed, inverse = norm_rows(x_own[at].astype(f32))
        up = branch[total_at] + arrived[at]
        norms[COL_NORM : COL_NORM + 1] += jnp.sum(up * normed, axis=0, keepdims=True)
        norms[COL_NORM + 1 : COL_NORM + 2] += jnp.sum(up, axis=0, keepdims=True)
        got = norm_rows_backward(up, normed, inverse, vec[COL_NORM : COL_NORM + 1])
        result[at] = dhid[at] + got
        return carry

    lax.fori_loop(0, rows // step, first, 0)
    out_g = pltpu.make_async_copy(result, grad_out, osem.at[0])
    out_g.start()
    misc = dot_f32(act[...], dfront[:, MISC:W_A], TN) + mbias[...] + norms[...].T
    misc = misc.astype(bf16).reshape(4, levels, block_rows, W_MISC)
    for column in range(4):
        m_bufs[0][column] = misc[column]
    for place in range(3):
        sm.begin(place)
    for j in sa.order:
        sa.turn(j)
    for j in so.order:
        so.column(j)
    for j in so.order:
        so.line(j)
    for j in sm.order:
        sm.turn(j)
    for j in sa.order:
        sa.column(j)
    for j in sa.order:
        sa.line(j)
    for j in sm.order:
        sm.column(j)
    for j in sm.order:
        sm.line(j)
    mine, other = [pl.ds(pl.multiple_of(k * shard, 16), shard) for k in (c, 1 - c)]
    ends = []
    for i, (scatter, total, out) in enumerate(((so, o_total, o_out), (sa, a_total, a_out), (sm, m_total, m_out))):
        scatter.total(total)
        keep = pltpu.make_async_copy(total.at[mine], out.at[c], osem.at[1 + i])
        keep.start()
        move = exchange(total.at[other], out.at[c], 1 + i)
        move.start()
        ends += [keep, move]
    for scatter in (so, sa, sm):
        scatter.drain()
    for cp in ends + [out_g]:
        cp.wait()


def last(levels, batches, local_len, shard, ins):
    bf16, f32 = jnp.bfloat16, jnp.float32
    db, mixed, act, dfront, w_a, mbias, dnorm, dhid, xs, vec = ins
    both, width = db.shape
    rows = both // 2
    block_rows = width // (4 * levels)
    outs = [((SIDE, shard, w), f32) for w in (MISC, W_O, W_MISC)] + [((rows, width), f32)]
    scratch = [(v.shape, v.dtype) for v in (db, mixed, act, dfront, w_a, mbias, dnorm, dhid)]
    scratch += [((rows, width), bf16), (vec.shape, f32), ((both, width), f32), ((rows, width), f32)]
    scratch += [((rows, width), f32), ((W_MISC, width), f32)]
    scratch += [((block_rows, w), f32) for w in (MISC, W_O, W_MISC)]
    scratch += scatter_scratch(levels, [(block_rows, w) for w in (MISC, W_O, W_MISC)])
    sems = [(3, 8 * levels), (3, 8 * levels), (10,), (4,), (4,), (4,)]
    body = functools.partial(last_kernel, levels, batches, local_len, shard)
    return kernel_call(body, ins, outs, scratch, sems, 3)


def split_heads(a, lead):
    rows = a.shape[0]
    a = pad_last(a.reshape(rows, lead, SIDE, HALF_HEADS, HEAD_DIM), PAD)
    return jnp.transpose(a, (2, 0, 1, 3, 4)).reshape(SIDE, rows, lead * HALF_HEADS * PAD)


def join_heads(a, lead):
    rows = a.shape[1]
    a = a.reshape(SIDE, rows, lead, HALF_HEADS, PAD)[..., :HEAD_DIM]
    return jnp.transpose(a, (1, 2, 0, 3, 4)).reshape(rows, lead * HEADS * HEAD_DIM)


def on_chip(
    tokens, cotangent, given_cache, value_routes, output_routes, valid_counts, doc_starts,
    norm1_gain, norm1_shift, qk_weight, router_weight, value_weight, output_weight, rel_bias,
    norm2_gain, norm2_shift, ffn_in, ffn_out,
):
    batches, unused_row, local_len, width = tokens.shape
    count = lax.axis_size("tm")
    levels = count // 2
    side = lax.axis_index("tm") % 2
    rows = batches * local_len
    shard = qk_weight.shape[0]
    blocks = 4 * levels
    bf16, f32 = jnp.bfloat16, jnp.float32

    a_qk = split_heads(qk_weight, 2)
    a_v = split_heads(value_weight, EXPERTS)
    a_o = split_heads(output_weight.T, EXPERTS)
    route = jnp.transpose(
        router_weight.reshape(shard, 2, SIDE, HALF_HEADS * EXPERTS), (2, 0, 1, 3)
    ).reshape(SIDE, shard, N_ROUTE)
    norms = jnp.broadcast_to(
        jnp.stack([norm1_gain, norm1_shift, norm2_gain, norm2_shift], axis=1)[None], (SIDE, shard, 4))
    buckets = rel_bias.shape[1]
    bias_cols = jnp.pad(
        jnp.transpose(rel_bias.reshape(SIDE, HALF_HEADS, buckets), (0, 2, 1)),
        ((0, 0), (0, shard - buckets), (0, 0)))
    starts_cols = jnp.broadcast_to(
        doc_starts.reshape(1, 1, batches).astype(bf16), (SIDE, shard, batches))
    misc = pad_last(jnp.concatenate([route, norms, bias_cols, starts_cols], axis=2), W_MISC)
    a_pack = jnp.concatenate([a_qk, a_v, misc], axis=2)
    hidden_block = ffn_out.shape[0]
    i_pack = jnp.transpose(
        ffn_in.reshape(shard, blocks, SIDE, hidden_block), (2, 0, 1, 3)
    ).reshape(SIDE, shard, blocks * hidden_block)

    mask = (jnp.arange(local_len)[None, :] < valid_counts.reshape(batches, 1)).astype(f32).reshape(rows, 1)
    x_own = tokens.reshape(rows, width)
    grad_own = (cotangent.reshape(rows, width).astype(f32) * mask).astype(bf16)
    picks = [
        jnp.transpose(
            selection(r.reshape(rows, SIDE, HALF_HEADS, TOPK)).reshape(rows, SIDE, HALF_HEADS * EXPERTS), (1, 0, 2))
        for r in (value_routes, output_routes)
    ]
    starts_col = jnp.repeat(doc_starts.reshape(batches), local_len).reshape(rows, 1).astype(bf16)
    counts_col = jnp.repeat(valid_counts.reshape(batches), local_len).reshape(rows, 1).astype(bf16)
    metas = [
        pad_last(jnp.concatenate([picks[0][s], picks[1][s]], axis=1).astype(bf16), 40) for s in range(SIDE)]
    metas = [pad_last(jnp.concatenate([m, starts_col, counts_col], axis=1), 128) for m in metas]
    x_pack = jnp.concatenate([x_own, grad_own] + metas, axis=1)
    g_pack = given_cache.reshape(batches, MEM, 2 * HEADS * HEAD_DIM)

    (a_all, o_all, i_all, f_all, xs, act_one, front, gates, win, probs, attended, mixed, hidden, n2, vec, act,
     slope) = forward(levels, batches, local_len, buckets, (a_pack, a_o, i_pack, ffn_out, x_pack, g_pack))
    w_a = a_all.reshape(width, W_A)
    w_o = o_all.reshape(width, W_O)
    w_i = i_all.reshape(width, -1)
    w_f = f_all.reshape(-1, width)
    out_share, i_sides, layer_out, d_front, d_branch, d_hidden, d_norm, d_bias = middle(
        levels, batches, local_len, buckets, shard,
        (w_f, w_i, w_o, act, slope, xs, n2, hidden, vec, attended, gates, front, win, probs))
    a_sides, o_sides, misc, input_grad = last(
        levels, batches, local_len, shard,
        (d_branch, mixed, act_one, d_front, w_a, d_bias, d_norm, d_hidden, xs, vec))
    layer_out = layer_out.reshape(tokens.shape)
    input_grad = input_grad.reshape(tokens.shape)
    qk_share = join_heads(a_sides[:, :, :W_QK], 2)
    value_share = join_heads(a_sides[:, :, W_QK:], EXPERTS)
    output_share = join_heads(o_sides, EXPERTS).T
    router_share = jnp.transpose(
        misc[:, :, :N_ROUTE].reshape(SIDE, shard, 2, HALF_HEADS * EXPERTS), (1, 2, 0, 3)
    ).reshape(shard, 2 * HEADS * EXPERTS)
    norm_share = misc[0, :, COL_NORM : COL_NORM + 4] + misc[1, :, COL_NORM : COL_NORM + 4]
    bias_share = jnp.transpose(misc[:, :buckets, COL_BIAS : COL_BIAS + HALF_HEADS], (0, 2, 1)).reshape(HEADS, buckets)
    in_share = jnp.transpose(
        i_sides.reshape(SIDE, shard, blocks, hidden_block), (1, 2, 0, 3)
    ).reshape(shard, -1)
    return (
        layer_out, input_grad, norm_share[:, 0], norm_share[:, 1], qk_share, router_share, value_share,
        output_share, bias_share, norm_share[:, 2], norm_share[:, 3], in_share, out_share,
    )


def by_size(*args):
    thin = args[9].shape[0] % 16 != 0
    paired = lax.axis_size("doc") == 4 and lax.axis_size("tm") % 2 == 0
    return on_device(*args) if thin or not paired else on_chip(*args)


def solution(mesh):
    return jax.shard_map(
        by_size,
        mesh=mesh,
        in_specs=(
            P(None, "doc", "tm", None),
            P(None, "doc", "tm", None),
            P(None, "doc", "tm", None),
            P(None, "doc", "tm", None, None),
            P(None, "doc", "tm", None, None),
            P(None, "doc", "tm"),
            P(None, "doc", "tm"),
            P(("doc", "tm")),
            P(("doc", "tm")),
            P(("doc", "tm"), None),
            P(("doc", "tm"), None),
            P(("doc", "tm"), None),
            P(None, ("doc", "tm")),
            P(None, ("doc", "tm")),
            P(("doc", "tm")),
            P(("doc", "tm")),
            P(("doc", "tm"), None),
            P(("doc", "tm"), None),
        ),
        out_specs=(
            P(None, "doc", "tm", None),
            P(None, "doc", "tm", None),
            P(("doc", "tm")),
            P(("doc", "tm")),
            P(("doc", "tm"), None),
            P(("doc", "tm"), None),
            P(("doc", "tm"), None),
            P(None, ("doc", "tm")),
            P(None, ("doc", "tm")),
            P(("doc", "tm")),
            P(("doc", "tm")),
            P(("doc", "tm"), None),
            P(("doc", "tm"), None),
        ),
        check_vma=False,
    )
```

```python
import functools

import jax
import jax.numpy as jnp
from jax import lax
from jax.experimental import pallas as pl
from jax.experimental.pallas import tpu as pltpu
from jax.sharding import PartitionSpec as P

HEADS = 4
HEAD_DIM = 112
EXPERTS = 5
TOPK = 2
MEM = 1024
BUCKETS = 256
NEAR = 128
STEP = 16


EPS = 1e-05
NEG = -1e30
HIGH = lax.Precision.HIGHEST


def shortened(array):
    return jax.tree.map(lambda a: a.astype(jnp.bfloat16) if a.dtype == jnp.float32 else a, array)


def from_behind(value, axis, steps):
    count = lax.axis_size(axis)
    first, last = (max(0, -steps), min(count, count - steps))
    return lax.ppermute(value, axis, [(source, source + steps) for source in range(first, last)])


def norm_forward(values, gain, shift):
    center_mean = jnp.mean(values, axis=-1, keepdims=True)
    centered = values - center_mean
    inverse = lax.rsqrt(jnp.mean(centered * centered, axis=-1, keepdims=True) + EPS)
    normed = centered * inverse
    return (normed * gain + shift, normed, inverse)


def norm_backward(upstream, normed, inverse, gain):
    scaled = upstream * gain
    inside = (
        scaled
        - jnp.mean(scaled, axis=-1, keepdims=True)
        - normed * jnp.mean(scaled * normed, axis=-1, keepdims=True)
    )
    return (inside * inverse, jnp.sum(upstream * normed, axis=0), jnp.sum(upstream, axis=0))


def selection(routes):
    expert_ids = jnp.arange(EXPERTS, dtype=jnp.int32)
    return jnp.sum((routes[..., None] == expert_ids).astype(jnp.float32), axis=-2)


def bucket_index(distance):
    far_bucket = NEAR + (distance - NEAR) // STEP
    return jnp.clip(jnp.where(distance < NEAR, distance, far_bucket), 0, BUCKETS - 1)


def gelu_slope(pre_act):
    return (
        0.5 * (1.0 + lax.erf(pre_act * 0.7071067811865476))
        + pre_act * jnp.exp(-0.5 * pre_act * pre_act) * 0.3989422804014327
    )


def flatten(matrix):
    return matrix.reshape(-1)


def bucket_matrix(local_len):
    spread = MEM + 2 * local_len - 1
    distance = jnp.arange(spread, dtype=jnp.int32) - (local_len - 1)
    bucket_ids = jnp.arange(BUCKETS, dtype=jnp.int32)
    return (bucket_index(distance)[:, None] == bucket_ids[None, :]).astype(jnp.float32)


def bias_matrix(table, local_len):
    spread = MEM + 2 * local_len - 1
    window = MEM + local_len
    by_distance = jnp.einsum("hc,kc->hk", table, bucket_matrix(local_len), precision=HIGH)
    turned = jnp.concatenate([by_distance[:, ::-1], jnp.zeros((HEADS, 1), jnp.float32)], axis=1)
    tiled = jnp.tile(turned, (1, local_len))[:, : local_len * spread].reshape(
        HEADS, local_len, spread
    )
    return tiled[:, :, local_len - 1 : local_len - 1 + window]


def bias_backward(score_sum, local_len):
    spread = MEM + 2 * local_len - 1
    padded = jnp.pad(score_sum, ((0, 0), (0, 0), (local_len - 1, 0))).reshape(
        HEADS, local_len * spread
    )
    padded = jnp.pad(padded, ((0, 0), (0, local_len))).reshape(HEADS, local_len, spread + 1)
    by_distance = jnp.sum(padded, axis=1)[:, :spread][:, ::-1]
    return jnp.einsum("hk,kc->hc", by_distance, bucket_matrix(local_len), precision=HIGH)


def attention_scores(queries, keys, table, counts):
    local_len = queries.shape[1]
    window = keys.shape[1]
    raw = jnp.einsum(
        "bqhd,bkhd->bhqk", queries, keys, preferred_element_type=jnp.float32
    ) * HEAD_DIM ** (-0.5)
    row_ids = jnp.arange(local_len, dtype=jnp.int32)[:, None]
    col_ids = jnp.arange(window, dtype=jnp.int32)[None, :]
    bias = bias_matrix(table, local_len)
    own_ids = col_ids - MEM
    causal = (own_ids <= row_ids)[None, None]
    live = own_ids[None, None] < counts[:, None, None, None]
    valid = jnp.logical_or((col_ids < MEM)[None, None], jnp.logical_and(causal, live))
    return (jnp.where(valid, raw + bias[None], NEG), valid)


def memory_by_hops(cache_own, given, starts, local_len):
    hops_total = MEM // local_len
    open_flag = jnp.logical_not(starts)[:, None, None]
    memory_slots = [jnp.zeros_like(cache_own) for _ in range(hops_total)]
    start_marks = starts.astype(jnp.bfloat16)
    for distance in range(1, hops_total + 1):
        if distance < hops_total:
            outgoing = (cache_own, start_marks, given[:, distance * local_len :])
        else:
            outgoing = (cache_own, start_marks)
        incoming = jax.tree.map(
            lambda part, own: part.astype(own.dtype),
            from_behind(shortened(outgoing), "tm", distance),
            outgoing,
        )
        memory_slots[hops_total - distance] = jnp.where(
            open_flag, incoming[0], memory_slots[hops_total - distance]
        )
        arrived = jnp.logical_and(open_flag, (incoming[1] > 0)[:, None, None])
        if distance < hops_total:
            for position in range(hops_total - distance):
                portion = incoming[2][:, position * local_len : (position + 1) * local_len]
                memory_slots[position] = jnp.where(arrived, portion, memory_slots[position])
        open_flag = jnp.logical_and(open_flag, jnp.logical_not(arrived))
    assembled = jnp.concatenate(memory_slots, axis=1)
    return jnp.where(starts[:, None, None], given, assembled)


def on_device(
    tokens,
    cotangent,
    given_cache,
    value_routes,
    output_routes,
    valid_counts,
    doc_starts,
    norm1_gain,
    norm1_shift,
    qk_weight,
    router_weight,
    value_weight,
    output_weight,
    rel_bias,
    norm2_gain,
    norm2_shift,
    ffn_in,
    ffn_out,
):
    batches, unused_row, local_len, model_width = tokens.shape
    row_count = batches * local_len
    inner_width = HEADS * HEAD_DIM
    head_experts = HEADS * EXPERTS
    full_weights = (
        lax.all_gather(norm1_gain, ("doc", "tm"), axis=0, tiled=True),
        lax.all_gather(norm1_shift, ("doc", "tm"), axis=0, tiled=True),
        lax.all_gather(qk_weight, ("doc", "tm"), axis=0, tiled=True),
        lax.all_gather(router_weight, ("doc", "tm"), axis=0, tiled=True),
        lax.all_gather(value_weight, ("doc", "tm"), axis=0, tiled=True),
        lax.all_gather(output_weight, ("doc", "tm"), axis=1, tiled=True),
        lax.all_gather(rel_bias, ("doc", "tm"), axis=1, tiled=True),
        lax.all_gather(norm2_gain, ("doc", "tm"), axis=0, tiled=True),
        lax.all_gather(norm2_shift, ("doc", "tm"), axis=0, tiled=True),
        lax.all_gather(ffn_in, ("doc", "tm"), axis=0, tiled=True),
        lax.all_gather(ffn_out, ("doc", "tm"), axis=0, tiled=True),
    )
    (
        gain_one,
        shift_one,
        w_qk,
        w_router,
        w_value,
        w_output,
        table_bf,
        gain_two,
        shift_two,
        w_in,
        w_out,
    ) = full_weights
    gain_one = gain_one.astype(jnp.float32)
    shift_one = shift_one.astype(jnp.float32)
    gain_two = gain_two.astype(jnp.float32)
    shift_two = shift_two.astype(jnp.float32)
    table = table_bf.astype(jnp.float32)
    router_f = w_router.astype(jnp.float32)
    inputs = tokens.reshape(row_count, model_width).astype(jnp.float32)
    counts = valid_counts.reshape(batches)
    starts = doc_starts.reshape(batches) > 0
    token_mask = (
        (jnp.arange(local_len, dtype=jnp.int32)[None, :] < counts[:, None])
        .astype(jnp.float32)
        .reshape(row_count, 1)
    )
    value_pick = selection(value_routes.reshape(row_count, HEADS, TOPK))
    output_pick = selection(output_routes.reshape(row_count, HEADS, TOPK))
    normed_one, norm1_unit, norm1_inv = norm_forward(inputs, gain_one, shift_one)
    act_one = normed_one.astype(jnp.bfloat16)
    qk_vals = jnp.dot(act_one, w_qk, preferred_element_type=jnp.float32).astype(jnp.bfloat16)
    gates = jax.nn.sigmoid(jnp.dot(act_one, w_router, preferred_element_type=jnp.float32))
    gate_value = gates[:, :head_experts].reshape(row_count, HEADS, EXPERTS) * value_pick
    gate_output = gates[:, head_experts:].reshape(row_count, HEADS, EXPERTS) * output_pick
    value_gate_t = jnp.transpose(gate_value, (0, 2, 1))[..., None]
    output_gate_t = jnp.transpose(gate_output, (0, 2, 1))[..., None]
    parts = jnp.dot(act_one, w_value, preferred_element_type=jnp.float32).reshape(
        row_count, EXPERTS, HEADS, HEAD_DIM
    )
    values = (
        jnp.sum(value_gate_t * parts, axis=1).reshape(row_count, inner_width).astype(jnp.bfloat16)
    )
    cache_own = jnp.concatenate([qk_vals[:, inner_width:], values], axis=1).reshape(
        batches, local_len, 2 * inner_width
    )
    given = given_cache.reshape(batches, MEM, 2 * inner_width)
    memory = memory_by_hops(cache_own, given, starts, local_len)
    queries = qk_vals[:, :inner_width].reshape(batches, local_len, HEADS, HEAD_DIM)
    keys = jnp.concatenate([memory[:, :, :inner_width], cache_own[:, :, :inner_width]], axis=1)
    keys = keys.reshape(batches, MEM + local_len, HEADS, HEAD_DIM)
    vals = jnp.concatenate([memory[:, :, inner_width:], cache_own[:, :, inner_width:]], axis=1)
    vals = vals.reshape(batches, MEM + local_len, HEADS, HEAD_DIM)
    scores, valid = attention_scores(queries, keys, table, counts)
    top = jnp.max(scores, axis=-1, keepdims=True)
    expo = jnp.exp(scores - top)
    denom = jnp.sum(expo, axis=-1, keepdims=True)
    log_total = top + jnp.log(denom)
    probs_b = (expo / denom).astype(jnp.bfloat16)
    attended = jnp.einsum("bhqk,bkhd->bqhd", probs_b, vals, preferred_element_type=jnp.float32)
    attended = attended.reshape(row_count, inner_width).astype(jnp.bfloat16)
    attended_f = attended.astype(jnp.float32).reshape(row_count, 1, HEADS, HEAD_DIM)
    mixed = (
        (output_gate_t * attended_f).reshape(row_count, EXPERTS * inner_width).astype(jnp.bfloat16)
    )
    hidden = inputs + jnp.dot(mixed, w_output, preferred_element_type=jnp.float32)
    normed_two, norm2_unit, norm2_inv = norm_forward(hidden, gain_two, shift_two)
    act_two = normed_two.astype(jnp.bfloat16)
    pre_act = jnp.dot(act_two, w_in, preferred_element_type=jnp.float32)
    activated = jax.nn.gelu(pre_act, approximate=False).astype(jnp.bfloat16)
    ffn_result = jnp.dot(activated, w_out, preferred_element_type=jnp.float32)
    layer_out = (token_mask * (hidden + ffn_result)).astype(jnp.bfloat16).reshape(tokens.shape)
    upstream = cotangent.reshape(row_count, model_width).astype(jnp.float32) * token_mask
    upstream_b = upstream.astype(jnp.bfloat16)
    d_out_w = jnp.einsum("nf,nd->fd", activated, upstream_b, preferred_element_type=jnp.float32)
    d_act = jnp.einsum("nd,fd->nf", upstream_b, w_out, preferred_element_type=jnp.float32)
    d_pre = (d_act * gelu_slope(pre_act)).astype(jnp.bfloat16)
    d_in_w = jnp.einsum("nd,nf->df", act_two, d_pre, preferred_element_type=jnp.float32)
    d_norm_two = jnp.einsum("nf,df->nd", d_pre, w_in, preferred_element_type=jnp.float32)
    d_from_two, d_gain_two, d_shift_two = norm_backward(d_norm_two, norm2_unit, norm2_inv, gain_two)
    d_hidden = upstream + d_from_two
    ffn_width = d_in_w.shape[1]
    d_branch = d_hidden.astype(jnp.bfloat16)
    d_output_t = jnp.einsum("nd,nk->dk", d_branch, mixed, preferred_element_type=jnp.float32)
    d_mixed = jnp.einsum(
        "nd,kd->nk", d_branch, w_output, preferred_element_type=jnp.float32
    ).astype(jnp.bfloat16)
    d_mixed = d_mixed.astype(jnp.float32).reshape(row_count, EXPERTS, HEADS, HEAD_DIM)
    d_gate_out = jnp.sum(d_mixed * attended_f, axis=-1)
    d_attended = (
        jnp.sum(d_mixed * output_gate_t, axis=1)
        .astype(jnp.bfloat16)
        .reshape(batches, local_len, HEADS, HEAD_DIM)
    )
    probs = jnp.where(valid, jnp.exp(scores - log_total), 0.0)
    d_probs = jnp.einsum("bqhd,bkhd->bhqk", d_attended, vals, preferred_element_type=jnp.float32)
    delta = jnp.sum(d_probs * probs, axis=-1, keepdims=True)
    d_scores = probs * (d_probs - delta)
    score_sum = jnp.sum(d_scores, axis=0)
    d_table = bias_backward(score_sum, local_len)
    d_scores_b = d_scores.astype(jnp.bfloat16)
    scale = HEAD_DIM ** (-0.5)
    d_queries = (
        jnp.einsum("bhqk,bkhd->bqhd", d_scores_b, keys, preferred_element_type=jnp.float32) * scale
    )
    d_keys = (
        jnp.einsum(
            "bhqk,bqhd->bkhd", d_scores_b[..., MEM:], queries, preferred_element_type=jnp.float32
        )
        * scale
    )
    d_vals = jnp.einsum(
        "bhqk,bqhd->bkhd", probs_b[..., MEM:], d_attended, preferred_element_type=jnp.float32
    )
    d_qk = jnp.concatenate(
        [d_queries.reshape(row_count, inner_width), d_keys.reshape(row_count, inner_width)], axis=1
    ).astype(jnp.bfloat16)
    d_values = (
        d_vals.reshape(row_count, 1, HEADS, HEAD_DIM).astype(jnp.bfloat16).astype(jnp.float32)
    )
    d_gate_val = jnp.sum(parts * d_values, axis=-1)
    d_parts = (
        (value_gate_t * d_values).reshape(row_count, EXPERTS * inner_width).astype(jnp.bfloat16)
    )
    d_gates = jnp.concatenate(
        [
            jnp.transpose(d_gate_val, (0, 2, 1)).reshape(row_count, head_experts)
            * value_pick.reshape(row_count, head_experts),
            jnp.transpose(d_gate_out, (0, 2, 1)).reshape(row_count, head_experts)
            * output_pick.reshape(row_count, head_experts),
        ],
        axis=1,
    )
    d_logits = d_gates * gates * (1.0 - gates)
    d_qk_w = jnp.einsum("nd,nk->dk", act_one, d_qk, preferred_element_type=jnp.float32)
    d_value_w = jnp.einsum("nd,nk->dk", act_one, d_parts, preferred_element_type=jnp.float32)
    d_router_w = jnp.einsum("nd,nk->dk", act_one.astype(jnp.float32), d_logits, precision=HIGH)
    d_norm_one = jnp.einsum("nk,dk->nd", d_qk, w_qk, preferred_element_type=jnp.float32)
    d_norm_one = d_norm_one + jnp.einsum(
        "nk,dk->nd", d_parts, w_value, preferred_element_type=jnp.float32
    )
    d_norm_one = d_norm_one + jnp.einsum("nk,dk->nd", d_logits, router_f, precision=HIGH)
    d_from_one, d_gain_one, d_shift_one = norm_backward(d_norm_one, norm1_unit, norm1_inv, gain_one)
    input_grad = (d_hidden + d_from_one).reshape(tokens.shape)
    shares = (
        lax.psum_scatter(d_gain_one, ("doc", "tm"), scatter_dimension=0, tiled=True),
        lax.psum_scatter(d_shift_one, ("doc", "tm"), scatter_dimension=0, tiled=True),
        lax.psum_scatter(flatten(d_qk_w), ("doc", "tm"), scatter_dimension=0, tiled=True),
        lax.psum_scatter(flatten(d_router_w), ("doc", "tm"), scatter_dimension=0, tiled=True),
        lax.psum_scatter(flatten(d_value_w), ("doc", "tm"), scatter_dimension=0, tiled=True),
        lax.psum_scatter(flatten(d_output_t), ("doc", "tm"), scatter_dimension=0, tiled=True),
        lax.psum_scatter(d_table, ("doc", "tm"), scatter_dimension=1, tiled=True),
        lax.psum_scatter(d_gain_two, ("doc", "tm"), scatter_dimension=0, tiled=True),
        lax.psum_scatter(d_shift_two, ("doc", "tm"), scatter_dimension=0, tiled=True),
        lax.psum_scatter(flatten(d_in_w), ("doc", "tm"), scatter_dimension=0, tiled=True),
        lax.psum_scatter(flatten(d_out_w), ("doc", "tm"), scatter_dimension=0, tiled=True),
    )
    qk_share = shares[2].reshape(-1, 2 * inner_width)
    router_share = shares[3].reshape(-1, 2 * head_experts)
    value_share = shares[4].reshape(-1, EXPERTS * inner_width)
    output_share = shares[5].reshape(-1, EXPERTS * inner_width).T
    in_share = shares[9].reshape(-1, ffn_width)
    out_share = shares[10].reshape(-1, model_width)
    return (
        layer_out,
        input_grad,
        shares[0],
        shares[1],
        qk_share,
        router_share,
        value_share,
        output_share,
        shares[6],
        shares[7],
        shares[8],
        in_share,
        out_share,
    )


MESH = pl.DeviceIdType.MESH
PAD = 128
SIDE = 2
HALF_HEADS = HEADS // SIDE
W_QK = 2 * HALF_HEADS * PAD
W_VAL = EXPERTS * HALF_HEADS * PAD
W_MISC = 128
W_A = W_QK + W_VAL + W_MISC
W_O = EXPERTS * HALF_HEADS * PAD
MISC = W_QK + W_VAL
N_ROUTE = 2 * HALF_HEADS * EXPERTS
COL_NORM = N_ROUTE
COL_BIAS = N_ROUTE + 4
VMEM_BYTES = 63 * 1024 * 1024
SCALE = HEAD_DIM ** (-0.5)


def pad_last(a, width):
    return jnp.pad(a, [(0, 0)] * (a.ndim - 1) + [(0, width - a.shape[-1])])


def neighbours(count):
    d, t = lax.axis_index("doc"), lax.axis_index("tm")
    z, c = t // 2, t % 2
    return dict(
        c=(d, z * 2 + 1 - c),
        x=(d + 1 - 2 * (d % 2), t),
        y=((d + 2) % 4, t),
        up=(d, jnp.minimum(t + 2, count - 1)),
        down=(d, jnp.maximum(t - 2, 0)),
    )


def enter(nb, z, levels):
    barrier = pltpu.get_barrier_semaphore()
    for name in ("c", "x", "y"):
        pl.semaphore_signal(barrier, inc=1, device_id=nb[name], device_id_type=MESH)

    @pl.when(z < levels - 1)
    def _():
        pl.semaphore_signal(barrier, inc=1, device_id=nb["up"], device_id_type=MESH)

    @pl.when(z > 0)
    def _():
        pl.semaphore_signal(barrier, inc=1, device_id=nb["down"], device_id_type=MESH)

    ends = jnp.where(z < levels - 1, 1, 0) + jnp.where(z > 0, 1, 0)
    pl.semaphore_wait(barrier, 3 + ends)


class Gather:
    def __init__(self, ref, sems, nb, d, z, levels):
        self.ref, self.nb, self.d, self.z, self.levels = ref, nb, d, z, levels
        self.send, self.recv = sems
        self.half = ref.shape[2] // 2

    def copy(self, part, slot, to):
        return pltpu.make_async_remote_copy(
            src_ref=part, dst_ref=part, send_sem=self.send.at[slot], recv_sem=self.recv.at[slot],
            device_id=self.nb[to], device_id_type=MESH)

    def along(self, level, distance, to):
        base = 0 if to == "up" else self.levels
        return self.copy(self.ref.at[self.d, level], base + distance, to)

    def across(self, level, to, column=None):
        base = (2 if to == "x" else 3) * self.levels
        column = self.d if column is None else column
        return self.copy(self.ref.at[column, level], base + level, to)

    def corner(self, level, to, column):
        base = (4 if to == "x" else 5) * self.levels
        rows = pl.ds(self.half, self.half) if to == "x" else pl.ds(0, self.half)
        return self.copy(self.ref.at[column, level, rows], base + level, to)

    def begin(self):
        z, levels = self.z, self.levels

        @pl.when(z < levels - 1)
        def _():
            self.along(z, 1, "up").start()

        @pl.when(z > 0)
        def _():
            self.along(z, 1, "down").start()

        self.across(z, "x").start()
        self.across(z, "y").start()

    def line(self, k):
        z, levels = self.z, self.levels

        @pl.when(z >= k)
        def _():
            self.along(z - k, k, "up").wait_recv()

            @pl.when(z < levels - 1)
            def _():
                self.along(z - k, k + 1, "up").start()

            self.across(z - k, "x").start()
            self.across(z - k, "y").start()

        @pl.when(z + k < levels)
        def _():
            self.along(z + k, k, "down").wait_recv()

            @pl.when(z > 0)
            def _():
                self.along(z + k, k + 1, "down").start()

            self.across(z + k, "x").start()
            self.across(z + k, "y").start()

    def turn(self, k):
        z, levels, d = self.z, self.levels, self.d
        by_x, by_y = d + 1 - 2 * (d % 2), (d + 2) % 4

        def one(level):
            self.across(level, "x").wait_recv()
            self.corner(level, "y", by_x).start()
            self.across(level, "y").wait_recv()
            self.corner(level, "x", by_y).start()

        if k == 0:
            one(z)
        else:
            pl.when(z >= k)(lambda: one(z - k))
            pl.when(z + k < levels)(lambda: one(z + k))

    def finish(self, k):
        z, levels, d = self.z, self.levels, self.d
        by_x, by_y = d + 1 - 2 * (d % 2), (d + 2) % 4

        def one(level):
            self.corner(level, "x", by_y).wait_recv()
            self.corner(level, "y", by_x).wait_recv()

        if k == 0:
            one(z)
        else:
            pl.when(z >= k)(lambda: one(z - k))
            pl.when(z + k < levels)(lambda: one(z + k))

    def drain(self):
        z, levels, d = self.z, self.levels, self.d
        by_x, by_y = d + 1 - 2 * (d % 2), (d + 2) % 4
        for level in range(levels):
            self.across(level, "x").wait_send()
            self.across(level, "y").wait_send()
            self.corner(level, "x", by_y).wait_send()
            self.corner(level, "y", by_x).wait_send()
        for k in range(1, levels):

            @pl.when(jnp.logical_and(z >= k - 1, z < levels - 1))
            def _():
                self.along(z - k + 1, k, "up").wait_send()

            @pl.when(jnp.logical_and(z + k - 1 < levels, z > 0))
            def _():
                self.along(z + k - 1, k, "down").wait_send()


def selector(side):
    inner = HEADS * HEAD_DIM
    wide = HALF_HEADS * PAD
    src = lax.broadcasted_iota(jnp.int32, (2 * inner, 2 * wide), 0)
    dst = lax.broadcasted_iota(jnp.int32, (2 * inner, 2 * wide), 1)
    kind, head, feature = dst // wide, (dst // PAD) % HALF_HEADS, dst % PAD
    wanted = kind * inner + (side * HALF_HEADS + head) * HEAD_DIM + feature
    hit = jnp.logical_and(src == wanted, feature < HEAD_DIM)
    return jnp.where(hit, 1.0, 0.0).astype(jnp.bfloat16)


def table_by_offset(w_a, per_device, shard, local_len, spread):
    distance = MEM + local_len - 1 - lax.broadcasted_iota(jnp.int32, (1, spread), 1)
    bucket = bucket_index(distance)
    wanted = (bucket // per_device) * shard + bucket % per_device
    step = 128

    def body(i, total):
        at = pl.ds(pl.multiple_of(i * step, step), step)
        ids = lax.broadcasted_iota(jnp.int32, (step, spread), 0) + i * step
        one_hot = jnp.where(ids == wanted, 1.0, 0.0).astype(jnp.bfloat16)
        return total + dot_f32(w_a[at, MISC:W_A], one_hot, TN)

    return lax.fori_loop(0, w_a.shape[0] // step, body, jnp.zeros((W_MISC, spread), jnp.float32))


NT = (((1,), (1,)), ((), ()))
TN = (((0,), (0,)), ((), ()))


def dot_f32(a, b, dims=(((1,), (0,)), ((), ()))):
    return lax.dot_general(a, b, dims, preferred_element_type=jnp.float32)


def forward_kernel(
    levels, batches, local_len, per_device,
    a_in, o_in, i_in, f_in, x_in, g_in,
    a_out, o_out, i_out, f_all, xs_out, act_out, front_out, gates_out, win_out, probs_out, att_out,
    mixed_out, hidden_out, n2_out, vec_out, ffn_out, slope_out,
    a_all, o_all, i_all, xs, graw, win, cr, sel, unit, act, front, gates, vec, bias, probs, att, mixed,
    arrived, hidden, n2, ffn, slope,
    send, recv, csend, crecv, lsem, gsend, grecv, msend, mrecv, esend, erecv, osem, psem,
):
    bf16, f32 = jnp.bfloat16, jnp.float32
    d, t = lax.axis_index("doc"), lax.axis_index("tm")
    z, c = t // 2, t % 2
    nb = neighbours(2 * levels)
    shard = a_in.shape[1]
    width = f_in.shape[1]
    rows = batches * local_len
    both = 2 * rows
    wide = HALF_HEADS * PAD
    own = pl.ds(pl.multiple_of(c * shard, 16), shard)
    reach = cr.shape[0]

    def local(src, dst, index):
        cp = pltpu.make_async_copy(src, dst, lsem.at[index])
        cp.start()
        return cp

    def sibling(src, dst, index):
        return pltpu.make_async_remote_copy(
            src_ref=src, dst_ref=dst, send_sem=csend.at[index], recv_sem=crecv.at[index],
            device_id=nb["c"], device_id_type=MESH)

    loc_a = local(a_in.at[c], a_all.at[d, z, own], 0)
    loc_x = local(x_in, xs.at[c], 1)
    loc_g = local(g_in, graw.at[c], 2)
    loc_o = local(o_in.at[c], o_all.at[d, z, own], 3)
    loc_i = local(i_in.at[c], i_all.at[d, z, own], 4)
    loc_f = local(f_in, f_all.at[d, z], 5)
    enter(nb, z, levels)
    rem_a = sibling(a_in.at[1 - c], a_all.at[d, z, own], 0)
    rem_x = sibling(x_in, xs.at[c], 1)
    rem_g = sibling(g_in, graw.at[c], 2)
    rem_o = sibling(o_in.at[1 - c], o_all.at[d, z, own], 3)
    rem_i = sibling(i_in.at[1 - c], i_all.at[d, z, own], 4)
    for cp in (rem_a, rem_x, rem_g, rem_o, rem_i):
        cp.start()
    ga, go, gi, gf = [
        Gather(ref, (send.at[i], recv.at[i]), nb, d, z, levels)
        for i, ref in enumerate((a_all, o_all, i_all, f_all))
    ]
    loc_a.wait()
    rem_a.wait()
    ga.begin()
    sel[...] = selector(c)

    loc_x.wait()
    rem_x.wait()
    step = 64

    def stats(i, carry):
        at = pl.ds(pl.multiple_of((i % (rows // step)) * step, step), step)
        block = i // (rows // step)
        values = xs[block, at, :width].astype(f32)
        centered = values - jnp.mean(values, axis=-1, keepdims=True)
        inverse = lax.rsqrt(jnp.mean(centered * centered, axis=-1, keepdims=True) + EPS)
        unit[pl.ds(pl.multiple_of(i * step, step), step)] = centered * inverse
        return carry

    lax.fori_loop(0, both // step, stats, 0)
    ga.line(1)

    def slot(s):
        return pl.ds(s * local_len, local_len)

    def starts_of(block, batch):
        column = xs[block, pl.ds(batch * local_len, local_len), 2 * width : 2 * width + 128]
        return column[:, 40:41].astype(f32)

    def place(block, s, follow):
        for batch in range(batches):
            at = block * batches + batch
            mine = dot_f32(graw[block, batch, slot(s)], sel[...]).astype(bf16)
            if follow:
                moved = win[at, slot(s)] if block == 0 else win[batch, slot(s + 1)]
                first = jnp.broadcast_to(starts_of(block, batch), mine.shape) > 0.5
                mine = jnp.where(first, mine.astype(f32), moved.astype(f32)).astype(bf16)
            win[at, slot(s)] = mine

    slots = MEM // local_len

    def chain(k):
        count = min(2, slots - 1 - 2 * k)
        top = slots - 2 * k
        src = win.at[pl.ds(batches, batches), pl.ds((top - count) * local_len, count * local_len)]
        dst = win.at[pl.ds(0, batches), pl.ds((top - count - 1) * local_len, count * local_len)]
        return pltpu.make_async_remote_copy(
            src_ref=src, dst_ref=dst, send_sem=gsend.at[k], recv_sem=grecv.at[k],
            device_id=nb["up"], device_id_type=MESH)

    rounds = slots // 2
    has_up, has_down = z < levels - 1, z > 0

    def chain_start(k):
        pl.when(has_up)(lambda: chain(k).start())

    def chain_round(k):
        pl.when(has_down)(lambda: chain(k).wait_recv())
        for s in (slots - 2 - 2 * k, slots - 3 - 2 * k):
            if s >= 0:
                place(0, s, True)
        for s in (slots - 3 - 2 * k, slots - 4 - 2 * k):
            if s >= 0:
                place(1, s, True)
        if k + 1 < rounds:
            chain_start(k + 1)

    loc_g.wait()
    rem_g.wait()
    place(0, slots - 1, False)
    place(1, slots - 1, False)
    place(1, slots - 2, True)
    chain_start(0)
    ga.turn(0)
    ga.line(2)
    ga.turn(1)
    chain_round(0)
    ga.line(3) if levels > 3 else None
    for k in range(4, levels):
        ga.line(k)
    loc_o.wait()
    rem_o.wait()
    go.begin()
    for k in range(2, levels):
        ga.turn(k)
    chain_round(1)
    for k in range(levels):
        ga.finish(k)
    out_a = pltpu.make_async_copy(a_all, a_out, osem.at[0])
    out_a.start()
    go.line(1)

    w_a = a_all.reshape(4 * levels * 2 * shard, W_A)
    vec[...] = w_a[:, MISC:W_A].astype(f32).T

    def norm(i, carry):
        at = pl.ds(pl.multiple_of(i * step, step), step)
        act[at] = (unit[at] * vec[COL_NORM : COL_NORM + 1] + vec[COL_NORM + 1 : COL_NORM + 2]).astype(bf16)
        return carry

    lax.fori_loop(0, both // step, norm, 0)

    def project(i, carry):
        at = pl.ds(pl.multiple_of(i * 256, 256), 256)
        front[:, at] = dot_f32(act[...], w_a[:, at])
        return carry

    lax.fori_loop(0, MISC // 256, project, 0)
    front[:, MISC:W_A] = dot_f32(act[...], w_a[:, MISC:W_A])
    go.line(2)
    go.turn(0)
    meta_at = pl.ds(pl.multiple_of(2 * width + c * 128, 128), 128)

    def gate(i, carry):
        at = pl.ds(pl.multiple_of(i * local_len, local_len), local_len)
        gated = jax.nn.sigmoid(front[at, MISC:W_A])
        gates[at] = gated
        picks = xs[i // batches, pl.ds(pl.multiple_of((i % batches) * local_len, local_len), local_len), meta_at]
        gated = gated * picks.astype(f32)
        for h in range(HALF_HEADS):
            total = jnp.zeros((local_len, PAD), f32)
            for e in range(EXPERTS):
                lane = h * EXPERTS + e
                col = W_QK + (e * HALF_HEADS + h) * PAD
                total = total + gated[:, lane : lane + 1] * front[at, col : col + PAD]
            win[i, pl.ds(MEM, local_len), wide + h * PAD : wide + (h + 1) * PAD] = total.astype(bf16)
        win[i, pl.ds(MEM, local_len), :wide] = front[at, wide : 2 * wide].astype(bf16)
        return carry

    lax.fori_loop(0, 2 * batches, gate, 0)

    def hop(k):
        src = win.at[:, pl.ds(MEM, local_len)] if k == 1 else cr.at[k - 2]
        return pltpu.make_async_remote_copy(
            src_ref=src, dst_ref=cr.at[k - 1], send_sem=msend.at[k - 1], recv_sem=mrecv.at[k - 1],
            device_id=nb["up"], device_id_type=MESH)

    def hop_start(k):
        pl.when(jnp.logical_and(has_up, z >= k - 1))(lambda: hop(k).start())

    def hop_arrived(k):
        pl.when(z >= k)(lambda: hop(k).wait_recv())

    hop_start(1)
    go.line(3) if levels > 3 else None
    for k in range(4, levels):
        go.line(k)
    go.turn(1)
    chain_round(2)
    chain_round(3)
    for k in range(4, rounds):
        chain_round(k)

    spread = MEM + 2 * local_len
    table = table_by_offset(w_a, per_device, shard, local_len, spread)
    for h in range(HALF_HEADS):
        line = jnp.broadcast_to(table[COL_BIAS + h : COL_BIAS + h + 1], (local_len, spread))
        turned = pltpu.roll(line, spread - local_len + 1, 1, stride=1, stride_axis=0)
        bias[h] = turned[:, : MEM + local_len]
    loc_i.wait()
    rem_i.wait()
    gi.begin()
    for k in range(2, levels):
        go.turn(k)
    for k in range(1, reach + 1):
        hop_arrived(k)
        if k < reach:
            hop_start(k + 1)
    gi.line(1)

    for k in range(rounds):
        pl.when(has_up)(lambda: chain(k).wait_send())
    for batch in range(batches):
        seen = []
        for back in range(slots + 1):
            block = jnp.maximum(t - c + 1 - back, 0) + d * 2 * levels
            tile = w_a[pl.ds(pl.multiple_of(block * shard, 16), 16), MISC:W_A].astype(f32)
            col = COL_BIAS + HALF_HEADS + batch
            seen.append(tile[0:1, col : col + 1])
        for block in range(2):
            stopped = jnp.zeros((1, 1), f32)
            for n in range(1, slots + 1):
                stopped = jnp.maximum(stopped, seen[n - 1 if block else n])
                if block:
                    k, which = n // 2, 1 - n % 2
                else:
                    k, which = (n + 1) // 2, n % 2
                if k > reach:
                    continue
                at = which * batches + batch
                source = win[at, pl.ds(MEM, local_len)] if k == 0 else cr[k - 1, at]
                into = block * batches + batch
                held = win[into, slot(slots - n)]
                stop = jnp.broadcast_to(stopped, held.shape) > 0.5
                win[into, slot(slots - n)] = jnp.where(stop, held.astype(f32), source.astype(f32)).astype(bf16)
    out_w = pltpu.make_async_copy(win, win_out, osem.at[1])
    out_w.start()

    key_ids = lax.broadcasted_iota(jnp.int32, (local_len, local_len), 1)
    row_ids = lax.broadcasted_iota(jnp.int32, (local_len, local_len), 0)

    def probs_copy(i, slot_of):
        return pltpu.make_async_copy(probs.at[slot_of], probs_out.at[i], psem.at[slot_of])

    def attend(i, carry):
        at = pl.ds(pl.multiple_of(i * local_len, local_len), local_len)
        block, batch = i // batches, i % batches
        rows_at = pl.ds(pl.multiple_of(batch * local_len, local_len), local_len)
        count = xs[block, rows_at, 2 * width : 2 * width + 128][:, 41:42].astype(f32)
        seen = jnp.logical_and(key_ids <= row_ids, key_ids.astype(f32) < count)
        picks = xs[block, rows_at, meta_at].astype(f32) * gates[at]
        slot_of = lax.rem(i, 2)
        pl.when(i >= 2)(lambda: probs_copy(i - 2, slot_of).wait())
        for h in range(HALF_HEADS):
            cols = slice(h * PAD, (h + 1) * PAD)
            q = front[at, cols].astype(bf16)
            s = dot_f32(q, win[i, :, cols], NT) * SCALE + bias[h]
            s = jnp.concatenate([s[:, :MEM], jnp.where(seen, s[:, MEM:], NEG)], axis=1)
            top = jnp.max(s, axis=-1, keepdims=True)
            expo = jnp.exp(s - top)
            p = expo * (1.0 / jnp.sum(expo, axis=-1, keepdims=True))
            probs[slot_of, h] = p
            p = p.astype(bf16)
            got = dot_f32(p, win[i, :, wide + h * PAD : wide + (h + 1) * PAD]).astype(bf16)
            att[at, cols] = got
            got = got.astype(f32)
            for e in range(EXPERTS):
                lane = HALF_HEADS * EXPERTS + h * EXPERTS + e
                col = (e * HALF_HEADS + h) * PAD
                mixed[at, col : col + PAD] = (picks[:, lane : lane + 1] * got).astype(bf16)
        probs_copy(i, slot_of).start()
        return carry

    lax.fori_loop(0, 2 * batches, attend, 0)
    for i in range(2 * batches - 2, 2 * batches):
        probs_copy(i, i % 2).wait()
    gi.line(2)
    gi.turn(0)
    for k in range(levels):
        go.finish(k)

    w_o = o_all.reshape(4 * levels * 2 * shard, W_O)
    branch = unit
    far = pl.ds(pl.multiple_of((1 - c) * rows, rows), rows)
    near = pl.ds(pl.multiple_of(c * rows, rows), rows)

    def out_project(at):
        def body(i, carry):
            cols = pl.ds(pl.multiple_of(i * 256, 256), 256)
            branch[at, cols] = dot_f32(mixed[at], w_o[cols], NT)
            return carry

        lax.fori_loop(0, width // 256, body, 0)

    def exchange(src, dst, index):
        return pltpu.make_async_remote_copy(
            src_ref=src, dst_ref=dst, send_sem=esend.at[index], recv_sem=erecv.at[index],
            device_id=nb["c"], device_id_type=MESH)

    out_project(far)
    give = exchange(branch.at[far], arrived, 0)
    give.start()
    out_project(near)
    out_o = pltpu.make_async_copy(o_all, o_out, osem.at[2])
    out_o.start()
    give.wait_recv()

    def second(i, carry):
        at = pl.ds(pl.multiple_of(i * step, step), step)
        total_at = pl.ds(pl.multiple_of(c * rows + i * step, step), step)
        values = xs[c, at, :width].astype(f32) + branch[total_at] + arrived[at]
        hidden[at] = values
        centered = values - jnp.mean(values, axis=-1, keepdims=True)
        inverse = lax.rsqrt(jnp.mean(centered * centered, axis=-1, keepdims=True) + EPS)
        normed = centered * inverse * vec[COL_NORM + 2 : COL_NORM + 3] + vec[COL_NORM + 3 : COL_NORM + 4]
        n2[total_at] = normed.astype(bf16)
        return carry

    lax.fori_loop(0, rows // step, second, 0)
    pair = exchange(n2.at[near], n2.at[near], 1)
    pair.start()
    gi.line(3) if levels > 3 else None
    for k in range(4, levels):
        gi.line(k)
    loc_f.wait()
    gf.begin()
    for k in range(1, levels):
        gi.turn(k)
        gf.line(k)
    gf.turn(0)
    pair.wait_recv()
    outs = [
        pltpu.make_async_copy(src, dst, osem.at[3 + i])
        for i, (src, dst) in enumerate((
            (xs, xs_out), (act, act_out), (front, front_out), (gates, gates_out),
            (att, att_out), (mixed, mixed_out), (hidden, hidden_out), (n2, n2_out), (vec, vec_out)))
    ]
    for cp in outs:
        cp.start()
    for k in range(levels):
        gi.finish(k)
    out_i = pltpu.make_async_copy(i_all, i_out, osem.at[13])
    out_i.start()

    w_i = i_all.reshape(4 * levels * 2 * shard, i_all.shape[3])

    def activate(i, carry):
        at = pl.ds(pl.multiple_of(i * 256, 256), 256)
        pre = dot_f32(n2[...], w_i[:, at])
        below = 0.5 * (1.0 + lax.erf(pre * 0.7071067811865476))
        ffn[:, at] = (pre * below).astype(bf16)
        slope[:, at] = (below + pre * jnp.exp(-0.5 * pre * pre) * 0.3989422804014327).astype(bf16)
        return carry

    steps = ffn.shape[1] // 256
    lax.fori_loop(0, steps // 2, activate, 0)
    gf.turn(1)
    lax.fori_loop(steps // 2, steps, activate, 0)
    outs += [pltpu.make_async_copy(ffn, ffn_out, osem.at[14]), pltpu.make_async_copy(slope, slope_out, osem.at[15])]
    outs[-2].start()
    outs[-1].start()
    for k in range(2, levels):
        gf.turn(k)
    for k in range(levels):
        gf.finish(k)
    for group in (ga, go, gi, gf):
        group.drain()
    for cp in (give, pair):
        cp.wait_send()
    for k in range(1, reach + 1):
        pl.when(jnp.logical_and(has_up, z >= k - 1))(lambda: hop(k).wait_send())
    out_a.wait()
    out_w.wait()
    out_o.wait()
    out_i.wait()
    for cp in outs:
        cp.wait()


def forward(levels, batches, local_len, per_device, packs):
    a, o, i, f, x, g = packs
    bf16, f32 = jnp.bfloat16, jnp.float32
    width = f.shape[1]
    rows = batches * local_len
    both = 2 * rows
    wide = HALF_HEADS * PAD
    two = lambda v: (4, levels, 2 * v.shape[1], v.shape[2])
    window = (2 * batches, MEM + local_len, 2 * wide)
    probs = (2 * batches, HALF_HEADS, local_len, MEM + local_len)
    outs = [
        (two(a), bf16), (two(o), bf16), (two(i), bf16), ((4, levels) + f.shape, bf16),
        ((2,) + x.shape, bf16), ((both, width), bf16), ((both, W_A), f32), ((both, W_MISC), f32),
        (window, bf16), (probs, f32), ((both, wide), bf16), ((both, W_O), bf16),
        ((rows, width), f32), ((both, width), bf16), ((W_MISC, width), f32), ((both, i.shape[2]), bf16),
        ((both, i.shape[2]), bf16),
    ]
    reach = min(MEM // local_len // 2, levels - 1)
    scratch = [
        (two(a), bf16), (two(o), bf16), (two(i), bf16), ((2,) + x.shape, bf16), ((2,) + g.shape, bf16),
        (window, bf16), ((reach, 2 * batches, local_len, 2 * wide), bf16), ((g.shape[2], 2 * wide), bf16),
        ((both, width), f32), ((both, width), bf16), ((both, W_A), f32), ((both, W_MISC), f32),
        ((W_MISC, width), f32), ((HALF_HEADS, local_len, MEM + local_len), f32), ((2,) + probs[1:], f32),
        ((both, wide), bf16), ((both, W_O), bf16), ((rows, width), f32),
        ((rows, width), f32), ((both, width), bf16), ((both, i.shape[2]), bf16), ((both, i.shape[2]), bf16),
    ]
    rounds = MEM // local_len // 2
    sems = [(4, 6 * levels), (4, 6 * levels), (6,), (6,), (6,), (rounds,), (rounds,), (reach,), (reach,), (2,), (2,), (16,), (2,)]
    hbm = pl.BlockSpec(memory_space=pl.ANY)
    return pl.pallas_call(
        functools.partial(forward_kernel, levels, batches, local_len, per_device),
        out_shape=[jax.ShapeDtypeStruct(s, k) for s, k in outs],
        in_specs=[hbm] * 6,
        out_specs=[hbm] * len(outs),
        scratch_shapes=[pltpu.VMEM(s, k) for s, k in scratch] + [pltpu.SemaphoreType.DMA(s) for s in sems],
        compiler_params=pltpu.CompilerParams(
            collective_id=1, has_side_effects=True, vmem_limit_bytes=VMEM_BYTES),
    )(a, o, i, f, x, g)


def add_rows(dst, terms):
    rows, width = dst.shape
    step = 16

    def body(i, carry):
        at = pl.ds(pl.multiple_of(i * step, step), step)
        total = terms[0][at].astype(jnp.float32)
        for term in terms[1:]:
            total = total + term[at].astype(jnp.float32)
        dst[at] = total.astype(dst.dtype)
        return carry

    lax.fori_loop(0, rows // step, body, 0)


class Scatter:
    def __init__(self, src, view, sems, nb, d, z, levels, total):
        self.src, self.view, self.nb, self.d, self.z, self.levels = src, view, nb, d, z, levels
        self.send, self.recv = sems
        self.sum = total
        self.half = src.shape[2] // 2
        self.by_x, self.by_y = d + 1 - 2 * (d % 2), (d + 2) % 4
        self.low, self.high = pl.ds(0, self.half), pl.ds(self.half, self.half)

    def copy(self, src, dst, slot, to):
        return pltpu.make_async_remote_copy(
            src_ref=src, dst_ref=dst, send_sem=self.send.at[slot], recv_sem=self.recv.at[slot],
            device_id=self.nb[to], device_id_type=MESH)

    def corner(self, j, to):
        part, name, base = (self.low, "cx", 0) if to == "x" else (self.high, "cy", self.levels)
        return self.copy(self.src.at[3 - self.d, j, part], self.view(name, j), base + j, to)

    def direct(self, j, to):
        if to == "x":
            column, part, name, base = self.by_x, self.low, "rx", 2 * self.levels
        else:
            column, part, name, base = self.by_y, self.high, "ry", 3 * self.levels
        return self.copy(self.src.at[column, j, part], self.view(name, j).at[part], base + j, to)

    def relay(self, j, to):
        if to == "x":
            held, part, name, base = "cy", self.high, "rx", 4 * self.levels
        else:
            held, part, name, base = "cx", self.low, "ry", 5 * self.levels
        return self.copy(self.view(held, j), self.view(name, j).at[part], base + j, to)

    def along(self, j, to, first=False):
        base = (6 if to == "up" else 7) * self.levels
        return self.copy(self.view("rx" if first else to, j), self.view(to, j), base + j, to)

    def issue(self, j):
        self.corner(j, "x").start()
        self.corner(j, "y").start()
        self.direct(j, "x").start()
        self.direct(j, "y").start()

    def turn(self, j):
        self.corner(j, "x").wait_recv()
        add_rows(self.view("cx", j), [self.view("cx", j), self.src.at[self.by_y, j, self.low]])
        self.relay(j, "y").start()
        self.corner(j, "y").wait_recv()
        add_rows(self.view("cy", j), [self.view("cy", j), self.src.at[self.by_x, j, self.high]])
        self.relay(j, "x").start()

    def column(self, j):
        for to in ("x", "y"):
            self.direct(j, to).wait_recv()
            self.relay(j, to).wait_recv()
        add_rows(self.view("rx", j), [self.view("rx", j), self.view("ry", j), self.src.at[self.d, j]])

    def lift(self, j, stage):
        def hop(to):
            if stage:
                self.along(j, to).wait_recv()
                add_rows(self.view(to, j), [self.view(to, j), self.view("rx", j)])
            self.along(j, to, first=stage == 0).start()

        if stage < j:
            pl.when(self.z == stage)(lambda: hop("up"))
        if self.levels - 1 - stage > j:
            pl.when(self.z == self.levels - 1 - stage)(lambda: hop("down"))

    def total(self, j):
        @pl.when(self.z == j)
        def _():
            terms = [self.view("rx", j)]
            for to, there in (("up", j > 0), ("down", j < self.levels - 1)):
                if there:
                    self.along(j, to).wait_recv()
                    terms.append(self.view(to, j))
            add_rows(self.sum, terms)

    def drain(self):
        for j in range(self.levels):
            for to in ("x", "y"):
                self.corner(j, to).wait_send()
                self.direct(j, to).wait_send()
                self.relay(j, to).wait_send()
            pl.when(self.z < j)(lambda: self.along(j, "up").wait_send())
            pl.when(self.z > j)(lambda: self.along(j, "down").wait_send())


class Pipeline:
    def __init__(self, units, levels, ahead):
        self.units, self.levels, self.ahead, self.now = units, levels, ahead, 0

    def each(self, n, act):
        if 0 <= n < len(self.units):
            for scatter, j in self.units[n]:
                act(scatter, j)

    def begin(self):
        for n in range(self.ahead):
            self.each(n, lambda s, j: s.issue(j))

    def step(self):
        n = self.now
        self.each(n, lambda s, j: s.turn(j))
        self.each(n + self.ahead, lambda s, j: s.issue(j))
        self.each(n - 1, lambda s, j: s.column(j))
        for stage in range(self.levels - 1):
            self.each(n - 2 - stage, lambda s, j: s.lift(j, stage))
        self.each(n - 1 - self.levels, lambda s, j: s.total(j))
        self.now += 1

    def finish(self):
        while self.now < len(self.units) + self.levels + 1:
            self.step()


def norm_rows(values):
    centered = values - jnp.mean(values, axis=-1, keepdims=True)
    inverse = lax.rsqrt(jnp.mean(centered * centered, axis=-1, keepdims=True) + EPS)
    return centered * inverse, inverse


def norm_rows_backward(upstream, normed, inverse, gain):
    scaled = upstream * gain
    inside = (
        scaled
        - jnp.mean(scaled, axis=-1, keepdims=True)
        - normed * jnp.mean(scaled * normed, axis=-1, keepdims=True)
    )
    return inside * inverse


VEC_ROW = COL_NORM // 8 * 8
VEC_GAIN = COL_NORM - VEC_ROW


def backward_kernel(
    levels, batches, local_len, per_device, shard,
    wf_in, wi_in, wo_in, wa_in, ffn_in, slope_in, xs_in, n2_in, hidden_in, vec_in, att_in, gates_in, front_in,
    win_in, probs_in, mixed_in, act_in,
    f_out, i_out, o_out, a_out, m_out, layer_out, grad_out,
    w_f, w_i, ffn, slope, grad, meta, n2, hidden, vec, att, gates, front, win, probs,
    branch, arrived, dhid, db, dmix, dfront, dsum, norms,
    f_total, i_total, o_total, a_total, m_total, *rest,
):
    bf16, f32 = jnp.bfloat16, jnp.float32
    f_bufs, i_bufs, m_bufs = rest[:7], rest[7:14], rest[14:21]
    o_src, o_cx, o_cy, a_src, a_cx, a_cy = rest[21:27]
    send, recv, lsem, tsem, esend, erecv, osem, ready, freed = rest[27:]
    d, t = lax.axis_index("doc"), lax.axis_index("tm")
    z, c = t // 2, t % 2
    nb = neighbours(2 * levels)
    width = w_f.shape[1]
    rows = batches * local_len
    both = 2 * rows
    wide = HALF_HEADS * PAD
    ff = ffn.shape[1]
    far = pl.ds(pl.multiple_of((1 - c) * rows, rows), rows)
    near = pl.ds(pl.multiple_of(c * rows, rows), rows)

    def load(src, dst, index):
        cp = pltpu.make_async_copy(src, dst, lsem.at[index])
        cp.start()
        return cp

    meta_at = pl.ds(pl.multiple_of(2 * width + c * 128, 128), 128)
    l_ffn = load(ffn_in, ffn, 0)
    l_grad = load(xs_in.at[:, :, pl.ds(width, width)], grad, 1)
    l_wf = load(wf_in, w_f, 2)
    l_slope = load(slope_in, slope, 3)
    l_n2 = load(n2_in, n2, 4)
    l_wi = load(wi_in, w_i, 5)
    l_hid = load(hidden_in, hidden, 6)
    l_vec = load(vec_in.at[pl.ds(VEC_ROW, 8)], vec, 7)
    l_mixed = load(mixed_in, dmix, 8)
    l_meta = load(xs_in.at[:, :, meta_at], meta, 9)
    l_att = load(att_in, att, 10)
    l_gates = load(gates_in, gates, 11)
    w_o = a_src.at[:, :, :, pl.ds(0, W_O)]
    l_wo = load(wo_in, w_o, 12)

    def tiles(i):
        at = pl.ds(i * local_len, local_len)
        return [
            pltpu.make_async_copy(win_in.at[i], win.at[i % 2], tsem.at[0, i % 2]),
            pltpu.make_async_copy(probs_in.at[i], probs.at[i % 2], tsem.at[1, i % 2]),
            pltpu.make_async_copy(front_in.at[at, pl.ds(0, MISC)], front.at[i % 2], tsem.at[2, i % 2]),
        ]

    for cp in tiles(0):
        cp.start()
    enter(nb, z, levels)

    names = ("cx", "cy", "rx", "ry", "up", "down")

    def plain(bufs):
        return lambda name, j: bufs[1 + names.index(name)].at[j]

    block_rows = shard * SIDE

    def within(held, cx, cy, cols):
        def view(name, j):
            if name in ("cx", "cy"):
                return (cx if name == "cx" else cy).at[j]
            ref, base = held[name]
            return ref.at[pl.ds(base + j * block_rows, block_rows), pl.ds(0, cols)]

        return view

    span = levels * block_rows
    o_view = within(dict(rx=(ffn, 0), ry=(ffn, span), up=(slope, 0), down=(slope, span)), o_cx, o_cy, W_O)
    a_view = within(dict(rx=(w_i, 0), ry=(w_i, span), up=(w_i, 2 * span), down=(w_i, 3 * span)), a_cx, a_cy, MISC)
    sums = [
        Scatter(src, view, (send.at[i], recv.at[i]), nb, d, z, levels, total)
        for i, (src, view, total) in enumerate((
            (f_bufs[0], plain(f_bufs), f_total), (i_bufs[0], plain(i_bufs), i_total),
            (o_src, o_view, o_total), (a_src, a_view, a_total), (m_bufs[0], plain(m_bufs), m_total)))
    ]
    sf, si, so, sa, sm = sums
    order = []
    for k in range((levels + 1) // 2):
        order += [levels - 1 - k, k] if levels - 1 - k != k else [k]
    units = [[(s, j)] for s in (sf, si, so, sa) for j in order]
    units[-1] = units[-1] + [(sm, j) for j in order]
    line = Pipeline(units, levels, 2)

    def exchange(src, dst, index):
        return pltpu.make_async_remote_copy(
            src_ref=src, dst_ref=dst, send_sem=esend.at[index], recv_sem=erecv.at[index],
            device_id=nb["c"], device_id_type=MESH)

    def weight_grad(dst, left, right, chunk, total, column):
        at = pl.ds(pl.multiple_of(column * span, span), span)

        def body(i, carry):
            cols = pl.ds(pl.multiple_of(i * chunk, chunk), chunk)
            got = dot_f32(left[:, at], right[:, cols], TN).astype(bf16)
            dst[column, :, :, cols] = got.reshape(levels, block_rows, chunk)
            return carry

        lax.fori_loop(0, total // chunk, body, 0)

    l_ffn.wait()
    l_grad.wait()
    g_all = grad.reshape(both, width)
    f_rows = f_bufs[0].shape[2]
    f_span = levels * f_rows
    for column in (3 - d, sf.by_x, sf.by_y, d):
        at = pl.ds(pl.multiple_of(column * f_span, f_span), f_span)
        f_bufs[0][column] = dot_f32(ffn[:, at], g_all[...], TN).astype(bf16).reshape(levels, f_rows, width)
    line.begin()

    l_wf.wait()
    l_slope.wait()

    def back(i, carry):
        at = pl.ds(pl.multiple_of(i * 256, 256), 256)
        slope[:, at] = (dot_f32(g_all[...], w_f[at], NT) * slope[:, at].astype(f32)).astype(bf16)
        return carry

    lax.fori_loop(0, ff // 256, back, 0)
    l_n2.wait()
    for column in range(4):
        weight_grad(i_bufs[0], n2, slope, 512, ff, column)
    line.step()

    l_wi.wait()

    def times(src, weights, dims):
        def run(at):
            def body(i, carry):
                cols = pl.ds(pl.multiple_of(i * 256, 256), 256)
                branch[at, cols] = dot_f32(src[at], weights(cols), dims)
                return carry

            lax.fori_loop(0, width // 256, body, 0)

        return run

    through_in = times(slope, lambda cols: w_i[cols], NT)
    through_in(far)
    give = exchange(branch.at[far], arrived, 0)
    give.start()
    through_in(near)
    line.step()
    l_hid.wait()
    l_vec.wait()
    give.wait()
    norms[...] = jnp.zeros_like(norms)
    step = 64

    def second(i, carry):
        at = pl.ds(pl.multiple_of(i * step, step), step)
        total_at = pl.ds(pl.multiple_of(c * rows + i * step, step), step)
        normed, inverse = norm_rows(hidden[at])
        up = branch[total_at] + arrived[at]
        norms[COL_NORM + 2 : COL_NORM + 3] += jnp.sum(up * normed, axis=0, keepdims=True)
        norms[COL_NORM + 3 : COL_NORM + 4] += jnp.sum(up, axis=0, keepdims=True)
        got = norm_rows_backward(up, normed, inverse, vec[VEC_GAIN + 2 : VEC_GAIN + 3])
        got = got + grad[c, at].astype(f32)
        dhid[at] = got
        db[total_at] = got.astype(bf16)
        return carry

    lax.fori_loop(0, rows // step, second, 0)
    pair = exchange(db.at[near], db.at[near], 1)
    pair.start()
    l_act = load(act_in, grad, 13)

    through_out = times(ffn, lambda cols: w_f[:, cols], (((1,), (0,)), ((), ())))
    through_out(far)
    pair.wait()
    last = exchange(branch.at[far], arrived, 2)
    last.start()
    line.step()
    through_out(near)

    for name in ("x", "y"):
        pl.semaphore_signal(ready, inc=1, device_id=nb[name], device_id_type=MESH)
    for name, there in (("up", z < levels - 1), ("down", z > 0)):

        @pl.when(there)
        def _():
            pl.semaphore_signal(ready, inc=1, device_id=nb[name], device_id_type=MESH)

    l_wa = [
        load(wa_in.at[:, pl.ds(0, width)], w_f.at[pl.ds(0, width)], 14),
        load(wa_in.at[:, pl.ds(width, W_A - width)], w_f.at[pl.ds(width, width), pl.ds(0, W_A - width)], 15),
    ]
    l_mixed.wait()
    for column in range(4):
        weight_grad(o_src, db, dmix, 640, W_O, column)
    line.step()
    l_wo.wait()

    def mix(i, carry):
        cols = pl.ds(pl.multiple_of(i * wide, wide), wide)
        dmix[:, cols] = dot_f32(db[...], a_src[:, :, :, cols].reshape(width, wide)).astype(bf16)
        return carry

    lax.fori_loop(0, EXPERTS, mix, 0)
    l_meta.wait()
    l_att.wait()
    l_gates.wait()
    dsum[...] = jnp.zeros_like(dsum)
    lanes = lax.broadcasted_iota(jnp.int32, (local_len, W_MISC), 1)

    def attend(i):
        slot = i % 2
        if i + 1 < 2 * batches:
            for cp in tiles(i + 1):
                cp.start()
        for cp in tiles(i):
            cp.wait()
        at = pl.ds(i * local_len, local_len)
        block, batch = i // batches, i % batches
        gate = gates[at]
        picks = meta[block, pl.ds(batch * local_len, local_len)].astype(f32)
        gated = gate * picks
        d_gates = jnp.zeros((local_len, W_MISC), f32)
        for h in range(HALF_HEADS):
            cols = slice(h * PAD, (h + 1) * PAD)
            v_cols = slice(wide + h * PAD, wide + (h + 1) * PAD)
            got = att[at, cols].astype(f32)
            d_att = jnp.zeros((local_len, PAD), f32)
            for e in range(EXPERTS):
                lane = HALF_HEADS * EXPERTS + h * EXPERTS + e
                col = (e * HALF_HEADS + h) * PAD
                part = dmix[at, col : col + PAD].astype(f32)
                d_att = d_att + gated[:, lane : lane + 1] * part
                d_gates = jnp.where(lanes == lane, jnp.sum(part * got, axis=-1, keepdims=True), d_gates)
            d_att = d_att.astype(bf16)
            p = probs[slot, h]
            d_p = dot_f32(d_att, win[slot, :, v_cols], NT)
            delta = jnp.sum(d_p * p, axis=-1, keepdims=True)
            d_s = p * (d_p - delta)
            dsum[h] += d_s
            d_s = d_s.astype(bf16)
            q = front[slot, :, cols].astype(bf16)
            d_q = dot_f32(d_s, win[slot, :, cols]) * SCALE
            d_k = dot_f32(d_s[:, MEM:], q, TN) * SCALE
            d_v = dot_f32(p[:, MEM:].astype(bf16), d_att, TN).astype(bf16).astype(f32)
            dfront[at, cols] = d_q.astype(bf16)
            dfront[at, wide + h * PAD : wide + (h + 1) * PAD] = d_k.astype(bf16)
            for e in range(EXPERTS):
                lane = h * EXPERTS + e
                col = W_QK + (e * HALF_HEADS + h) * PAD
                part = front[slot, :, col : col + PAD]
                d_gates = jnp.where(lanes == lane, jnp.sum(part * d_v, axis=-1, keepdims=True), d_gates)
                dfront[at, col : col + PAD] = (gated[:, lane : lane + 1] * d_v).astype(bf16)
        d_logits = jnp.where(lanes < N_ROUTE, d_gates * picks * gate * (1.0 - gate), 0.0)
        dfront[at, MISC:W_A] = d_logits.astype(bf16)

    for i in range(2 * batches):
        attend(i)
        if line.now + line.ahead == 2 * levels:
            ends = jnp.where(z < levels - 1, 1, 0) + jnp.where(z > 0, 1, 0)
            pl.semaphore_wait(ready, 2 + ends)
        line.step()
    last.wait()

    def final(i, carry):
        at = pl.ds(pl.multiple_of(i * step, step), step)
        total_at = pl.ds(pl.multiple_of(c * rows + i * step, step), step)
        tail = meta[c, at].astype(f32)
        position = lax.broadcasted_iota(jnp.int32, (step, 1), 0) + (i * step) % local_len
        keep = position.astype(f32) < tail[:, 41:42]
        total = hidden[at] + branch[total_at] + arrived[at]
        db[total_at] = jnp.where(keep, total, 0.0).astype(bf16)
        return carry

    lax.fori_loop(0, rows // step, final, 0)
    pl.semaphore_signal(freed, inc=1, device_id=nb["c"], device_id_type=MESH)
    outs = [pltpu.make_async_copy(db.at[near], layer_out, osem.at[0])]
    outs[0].start()

    l_act.wait()
    one_all = grad.reshape(both, width)
    for column in range(4):
        weight_grad(a_src, one_all, dfront, 896, MISC, column)
    line.step()
    for cp in l_wa:
        cp.wait()

    def through_front(at):
        def body(i, carry):
            cols = pl.ds(pl.multiple_of(i * 256, 256), 256)
            below = pl.ds(pl.multiple_of(width + i * 256, 256), 256)
            branch[at, cols] = (
                dot_f32(dfront[at, :width], w_f[cols], NT)
                + dot_f32(dfront[at, width:], w_f[below, : W_A - width], NT))
            return carry

        lax.fori_loop(0, width // 256, body, 0)

    through_front(far)
    hand = exchange(branch.at[far], arrived, 3)
    pl.semaphore_wait(freed, 1)
    hand.start()
    through_front(near)
    line.step()

    spread = MEM + 2 * local_len
    ids = lax.broadcasted_iota(jnp.int32, (local_len, 1), 0)
    lines = []
    for h in range(HALF_HEADS):
        turned = jnp.concatenate([dsum[h], jnp.zeros((local_len, local_len), f32)], axis=1)
        bit = 1
        while bit < local_len:
            moved = pltpu.roll(turned, bit, 1)
            turned = jnp.where(((local_len - 1 - ids) // bit) % 2 == 1, moved, turned)
            bit *= 2
        lines.append(jnp.sum(turned, axis=0, keepdims=True))
    row_of = lax.broadcasted_iota(jnp.int32, (W_MISC, spread), 0)
    table = jnp.zeros((W_MISC, spread), f32)
    for h in range(HALF_HEADS):
        table = jnp.where(row_of == COL_BIAS + h, lines[h], table)
    high = table.astype(bf16)
    low = (table - high.astype(f32)).astype(bf16)
    distance = MEM + local_len - 1 - lax.broadcasted_iota(jnp.int32, (1, spread), 1)
    bucket = bucket_index(distance)
    wanted = (bucket // per_device) * shard + bucket % per_device
    hand.wait()

    def first(i, carry):
        at = pl.ds(pl.multiple_of(i * step, step), step)
        total_at = pl.ds(pl.multiple_of(c * rows + i * step, step), step)
        normed, inverse = norm_rows(n2[at].astype(f32))
        up = branch[total_at] + arrived[at]
        norms[COL_NORM : COL_NORM + 1] += jnp.sum(up * normed, axis=0, keepdims=True)
        norms[COL_NORM + 1 : COL_NORM + 2] += jnp.sum(up, axis=0, keepdims=True)
        dhid[at] += norm_rows_backward(up, normed, inverse, vec[VEC_GAIN : VEC_GAIN + 1])
        return carry

    l_x = load(xs_in.at[c, :, pl.ds(0, width)], n2.at[pl.ds(0, rows)], 16)
    l_x.wait()
    lax.fori_loop(0, rows // step, first, 0)
    outs.append(pltpu.make_async_copy(dhid, grad_out, osem.at[1]))
    outs[1].start()
    line.step()
    columns = norms[...].T

    for column in range(4):
        at = pl.ds(column * span, span)
        row_ids = lax.broadcasted_iota(jnp.int32, (span, spread), 0) + column * span
        one_hot = jnp.where(row_ids == wanted, 1.0, 0.0).astype(bf16)
        misc = dot_f32(one_hot, high, NT) + dot_f32(one_hot, low, NT)
        misc = misc + dot_f32(one_all[:, at], dfront[:, MISC:W_A], TN) + columns[column * span : (column + 1) * span]
        m_bufs[0][column] = misc.astype(bf16).reshape(levels, block_rows, W_MISC)
    line.finish()
    outs.append(pltpu.make_async_copy(f_total, f_out, osem.at[2]))
    outs[2].start()
    mine, other = [pl.ds(pl.multiple_of(k * shard, 16), shard) for k in (c, 1 - c)]
    for i, (total, out) in enumerate(((i_total, i_out), (o_total, o_out), (a_total, a_out), (m_total, m_out))):
        outs.append(pltpu.make_async_copy(total.at[mine], out.at[c], osem.at[3 + i]))
        outs[-1].start()
        outs.append(exchange(total.at[other], out.at[c], 4 + i))
        outs[-1].start()
    for s in sums:
        s.drain()
    for cp in outs:
        cp.wait()


def backward(levels, batches, local_len, per_device, shard, ins):
    bf16, f32 = jnp.bfloat16, jnp.float32
    (w_f, w_i, w_o, w_a, ffn, slope, xs, n2, hidden, vec, att, gates, front, win, probs, mixed, act) = ins
    ff, width = w_f.shape
    rows = batches * local_len
    both = 2 * rows
    f_rows = ff // (4 * levels)
    b_rows = width // (4 * levels)
    outs = [((f_rows, width), f32)] + [((SIDE, shard, w), f32) for w in (ff, W_O, MISC, W_MISC)]
    outs += [((rows, width), bf16), ((rows, width), f32)]
    scratch = [(v.shape, v.dtype) for v in (w_f, w_i, ffn, slope)]
    scratch += [((2, rows, width), bf16), ((2, rows, 128), bf16)]
    scratch += [(n2.shape, bf16), (hidden.shape, f32), ((8, width), f32), (att.shape, bf16), (gates.shape, f32)]
    scratch += [((2, local_len, MISC), f32), ((2,) + win.shape[1:], bf16), ((2,) + probs.shape[1:], f32)]
    scratch += [
        ((both, width), f32), ((rows, width), f32), ((rows, width), f32), ((both, width), bf16),
        ((both, W_O), bf16), ((both, W_A), bf16), ((HALF_HEADS, local_len, MEM + local_len), f32),
        ((W_MISC, width), f32), ((f_rows, width), f32),
    ]
    scratch += [((b_rows, w), f32) for w in (ff, W_O, MISC, W_MISC)]
    for r, w in ((f_rows, width), (b_rows, ff), (b_rows, W_MISC)):
        scratch.append(((4, levels, r, w), bf16))
        scratch += [((levels, k, w), bf16) for k in (r // 2, r // 2, r, r, r, r)]
    for w in (W_O, MISC):
        scratch.append(((4, levels, b_rows, w), bf16))
        scratch += [((levels, b_rows // 2, w), bf16)] * 2
    sems = [(5, 8 * levels), (5, 8 * levels), (17,), (3, 2), (8,), (8,), (8,)]
    hbm = pl.BlockSpec(memory_space=pl.ANY)
    return pl.pallas_call(
        functools.partial(backward_kernel, levels, batches, local_len, per_device, shard),
        out_shape=[jax.ShapeDtypeStruct(s, k) for s, k in outs],
        in_specs=[hbm] * len(ins),
        out_specs=[hbm] * len(outs),
        scratch_shapes=[pltpu.VMEM(s, k) for s, k in scratch]
        + [pltpu.SemaphoreType.DMA(s) for s in sems]
        + [pltpu.SemaphoreType.REGULAR] * 2,
        compiler_params=pltpu.CompilerParams(
            collective_id=2, has_side_effects=True, vmem_limit_bytes=VMEM_BYTES),
    )(*ins)


def split_heads(a, lead):
    rows = a.shape[0]
    a = pad_last(a.reshape(rows, lead, SIDE, HALF_HEADS, HEAD_DIM), PAD)
    return jnp.transpose(a, (2, 0, 1, 3, 4)).reshape(SIDE, rows, lead * HALF_HEADS * PAD)


def join_heads(a, lead):
    rows = a.shape[1]
    a = a.reshape(SIDE, rows, lead, HALF_HEADS, PAD)[..., :HEAD_DIM]
    return jnp.transpose(a, (1, 2, 0, 3, 4)).reshape(rows, lead * HEADS * HEAD_DIM)


def on_chip(
    tokens, cotangent, given_cache, value_routes, output_routes, valid_counts, doc_starts,
    norm1_gain, norm1_shift, qk_weight, router_weight, value_weight, output_weight, rel_bias,
    norm2_gain, norm2_shift, ffn_in, ffn_out,
):
    batches, unused_row, local_len, width = tokens.shape
    count = lax.axis_size("tm")
    levels = count // 2
    side = lax.axis_index("tm") % 2
    rows = batches * local_len
    shard = qk_weight.shape[0]
    blocks = 4 * levels
    bf16, f32 = jnp.bfloat16, jnp.float32

    a_qk = split_heads(qk_weight, 2)
    a_v = split_heads(value_weight, EXPERTS)
    a_o = split_heads(output_weight.T, EXPERTS)
    route = jnp.transpose(
        router_weight.reshape(shard, 2, SIDE, HALF_HEADS * EXPERTS), (2, 0, 1, 3)
    ).reshape(SIDE, shard, N_ROUTE)
    norms = jnp.broadcast_to(
        jnp.stack([norm1_gain, norm1_shift, norm2_gain, norm2_shift], axis=1)[None], (SIDE, shard, 4))
    buckets = rel_bias.shape[1]
    bias_cols = jnp.pad(
        jnp.transpose(rel_bias.reshape(SIDE, HALF_HEADS, buckets), (0, 2, 1)),
        ((0, 0), (0, shard - buckets), (0, 0)))
    starts_cols = jnp.broadcast_to(
        doc_starts.reshape(1, 1, batches).astype(bf16), (SIDE, shard, batches))
    misc = pad_last(jnp.concatenate([route, norms, bias_cols, starts_cols], axis=2), W_MISC)
    a_pack = jnp.concatenate([a_qk, a_v, misc], axis=2)
    hidden_block = ffn_out.shape[0]
    i_pack = jnp.transpose(
        ffn_in.reshape(shard, blocks, SIDE, hidden_block), (2, 0, 1, 3)
    ).reshape(SIDE, shard, blocks * hidden_block)

    mask = (jnp.arange(local_len)[None, :] < valid_counts.reshape(batches, 1)).astype(f32).reshape(rows, 1)
    x_own = tokens.reshape(rows, width)
    grad_own = (cotangent.reshape(rows, width).astype(f32) * mask).astype(bf16)
    picks = [
        jnp.transpose(
            selection(r.reshape(rows, SIDE, HALF_HEADS, TOPK)).reshape(rows, SIDE, HALF_HEADS * EXPERTS), (1, 0, 2))
        for r in (value_routes, output_routes)
    ]
    starts_col = jnp.repeat(doc_starts.reshape(batches), local_len).reshape(rows, 1).astype(bf16)
    counts_col = jnp.repeat(valid_counts.reshape(batches), local_len).reshape(rows, 1).astype(bf16)
    metas = [
        pad_last(jnp.concatenate([picks[0][s], picks[1][s]], axis=1).astype(bf16), 40) for s in range(SIDE)]
    metas = [pad_last(jnp.concatenate([m, starts_col, counts_col], axis=1), 128) for m in metas]
    x_pack = jnp.concatenate([x_own, grad_own] + metas, axis=1)
    g_pack = given_cache.reshape(batches, MEM, 2 * HEADS * HEAD_DIM)

    (a_all, o_all, i_all, f_all, xs, act_one, front, gates, win, probs, attended, mixed, hidden, n2, vec, act,
     slope) = forward(levels, batches, local_len, buckets, (a_pack, a_o, i_pack, ffn_out, x_pack, g_pack))
    w_a = a_all.reshape(width, W_A)
    w_i = i_all.reshape(width, -1)
    w_f = f_all.reshape(-1, width)
    out_share, i_sides, o_sides, a_sides, misc, layer_out, input_grad = backward(
        levels, batches, local_len, buckets, shard,
        (w_f, w_i, o_all, w_a, act, slope, xs, n2, hidden, vec, attended, gates, front, win, probs, mixed,
         act_one.reshape(2, rows, width)))
    layer_out = layer_out.reshape(tokens.shape)
    input_grad = input_grad.reshape(tokens.shape)
    qk_share = join_heads(a_sides[:, :, :W_QK], 2)
    value_share = join_heads(a_sides[:, :, W_QK:], EXPERTS)
    output_share = join_heads(o_sides, EXPERTS).T
    router_share = jnp.transpose(
        misc[:, :, :N_ROUTE].reshape(SIDE, shard, 2, HALF_HEADS * EXPERTS), (1, 2, 0, 3)
    ).reshape(shard, 2 * HEADS * EXPERTS)
    norm_share = misc[0, :, COL_NORM : COL_NORM + 4] + misc[1, :, COL_NORM : COL_NORM + 4]
    bias_share = jnp.transpose(misc[:, :buckets, COL_BIAS : COL_BIAS + HALF_HEADS], (0, 2, 1)).reshape(HEADS, buckets)
    in_share = jnp.transpose(
        i_sides.reshape(SIDE, shard, blocks, hidden_block), (1, 2, 0, 3)
    ).reshape(shard, -1)
    return (
        layer_out, input_grad, norm_share[:, 0], norm_share[:, 1], qk_share, router_share, value_share,
        output_share, bias_share, norm_share[:, 2], norm_share[:, 3], in_share, out_share,
    )


def by_size(*args):
    thin = args[9].shape[0] % 16 != 0
    paired = lax.axis_size("doc") == 4 and lax.axis_size("tm") % 2 == 0
    return on_device(*args) if thin or not paired else on_chip(*args)


def solution(mesh):
    return jax.shard_map(
        by_size,
        mesh=mesh,
        in_specs=(
            P(None, "doc", "tm", None),
            P(None, "doc", "tm", None),
            P(None, "doc", "tm", None),
            P(None, "doc", "tm", None, None),
            P(None, "doc", "tm", None, None),
            P(None, "doc", "tm"),
            P(None, "doc", "tm"),
            P(("doc", "tm")),
            P(("doc", "tm")),
            P(("doc", "tm"), None),
            P(("doc", "tm"), None),
            P(("doc", "tm"), None),
            P(None, ("doc", "tm")),
            P(None, ("doc", "tm")),
            P(("doc", "tm")),
            P(("doc", "tm")),
            P(("doc", "tm"), None),
            P(("doc", "tm"), None),
        ),
        out_specs=(
            P(None, "doc", "tm", None),
            P(None, "doc", "tm", None),
            P(("doc", "tm")),
            P(("doc", "tm")),
            P(("doc", "tm"), None),
            P(("doc", "tm"), None),
            P(("doc", "tm"), None),
            P(None, ("doc", "tm")),
            P(None, ("doc", "tm")),
            P(("doc", "tm")),
            P(("doc", "tm")),
            P(("doc", "tm"), None),
            P(("doc", "tm"), None),
        ),
        check_vma=False,
    )
```

```python
import functools

import jax
import jax.numpy as jnp
from jax import lax
from jax.experimental import pallas as pl
from jax.experimental.pallas import tpu as pltpu
from jax.sharding import PartitionSpec as P

HEADS = 4
HEAD_DIM = 112
EXPERTS = 5
TOPK = 2
MEM = 1024
BUCKETS = 256
NEAR = 128
STEP = 16


EPS = 1e-05
NEG = -1e30
HIGH = lax.Precision.HIGHEST


def shortened(array):
    return jax.tree.map(lambda a: a.astype(jnp.bfloat16) if a.dtype == jnp.float32 else a, array)


def from_behind(value, axis, steps):
    count = lax.axis_size(axis)
    first, last = (max(0, -steps), min(count, count - steps))
    return lax.ppermute(value, axis, [(source, source + steps) for source in range(first, last)])


def norm_forward(values, gain, shift):
    center_mean = jnp.mean(values, axis=-1, keepdims=True)
    centered = values - center_mean
    inverse = lax.rsqrt(jnp.mean(centered * centered, axis=-1, keepdims=True) + EPS)
    normed = centered * inverse
    return (normed * gain + shift, normed, inverse)


def norm_backward(upstream, normed, inverse, gain):
    scaled = upstream * gain
    inside = (
        scaled
        - jnp.mean(scaled, axis=-1, keepdims=True)
        - normed * jnp.mean(scaled * normed, axis=-1, keepdims=True)
    )
    return (inside * inverse, jnp.sum(upstream * normed, axis=0), jnp.sum(upstream, axis=0))


def selection(routes):
    expert_ids = jnp.arange(EXPERTS, dtype=jnp.int32)
    return jnp.sum((routes[..., None] == expert_ids).astype(jnp.float32), axis=-2)


def bucket_index(distance):
    far_bucket = NEAR + (distance - NEAR) // STEP
    return jnp.clip(jnp.where(distance < NEAR, distance, far_bucket), 0, BUCKETS - 1)


def gelu_slope(pre_act):
    return (
        0.5 * (1.0 + lax.erf(pre_act * 0.7071067811865476))
        + pre_act * jnp.exp(-0.5 * pre_act * pre_act) * 0.3989422804014327
    )


def flatten(matrix):
    return matrix.reshape(-1)


def bucket_matrix(local_len):
    spread = MEM + 2 * local_len - 1
    distance = jnp.arange(spread, dtype=jnp.int32) - (local_len - 1)
    bucket_ids = jnp.arange(BUCKETS, dtype=jnp.int32)
    return (bucket_index(distance)[:, None] == bucket_ids[None, :]).astype(jnp.float32)


def bias_matrix(table, local_len):
    spread = MEM + 2 * local_len - 1
    window = MEM + local_len
    by_distance = jnp.einsum("hc,kc->hk", table, bucket_matrix(local_len), precision=HIGH)
    turned = jnp.concatenate([by_distance[:, ::-1], jnp.zeros((HEADS, 1), jnp.float32)], axis=1)
    tiled = jnp.tile(turned, (1, local_len))[:, : local_len * spread].reshape(
        HEADS, local_len, spread
    )
    return tiled[:, :, local_len - 1 : local_len - 1 + window]


def bias_backward(score_sum, local_len):
    spread = MEM + 2 * local_len - 1
    padded = jnp.pad(score_sum, ((0, 0), (0, 0), (local_len - 1, 0))).reshape(
        HEADS, local_len * spread
    )
    padded = jnp.pad(padded, ((0, 0), (0, local_len))).reshape(HEADS, local_len, spread + 1)
    by_distance = jnp.sum(padded, axis=1)[:, :spread][:, ::-1]
    return jnp.einsum("hk,kc->hc", by_distance, bucket_matrix(local_len), precision=HIGH)


def attention_scores(queries, keys, table, counts):
    local_len = queries.shape[1]
    window = keys.shape[1]
    raw = jnp.einsum(
        "bqhd,bkhd->bhqk", queries, keys, preferred_element_type=jnp.float32
    ) * HEAD_DIM ** (-0.5)
    row_ids = jnp.arange(local_len, dtype=jnp.int32)[:, None]
    col_ids = jnp.arange(window, dtype=jnp.int32)[None, :]
    bias = bias_matrix(table, local_len)
    own_ids = col_ids - MEM
    causal = (own_ids <= row_ids)[None, None]
    live = own_ids[None, None] < counts[:, None, None, None]
    valid = jnp.logical_or((col_ids < MEM)[None, None], jnp.logical_and(causal, live))
    return (jnp.where(valid, raw + bias[None], NEG), valid)


def memory_by_hops(cache_own, given, starts, local_len):
    hops_total = MEM // local_len
    open_flag = jnp.logical_not(starts)[:, None, None]
    memory_slots = [jnp.zeros_like(cache_own) for _ in range(hops_total)]
    start_marks = starts.astype(jnp.bfloat16)
    for distance in range(1, hops_total + 1):
        if distance < hops_total:
            outgoing = (cache_own, start_marks, given[:, distance * local_len :])
        else:
            outgoing = (cache_own, start_marks)
        incoming = jax.tree.map(
            lambda part, own: part.astype(own.dtype),
            from_behind(shortened(outgoing), "tm", distance),
            outgoing,
        )
        memory_slots[hops_total - distance] = jnp.where(
            open_flag, incoming[0], memory_slots[hops_total - distance]
        )
        arrived = jnp.logical_and(open_flag, (incoming[1] > 0)[:, None, None])
        if distance < hops_total:
            for position in range(hops_total - distance):
                portion = incoming[2][:, position * local_len : (position + 1) * local_len]
                memory_slots[position] = jnp.where(arrived, portion, memory_slots[position])
        open_flag = jnp.logical_and(open_flag, jnp.logical_not(arrived))
    assembled = jnp.concatenate(memory_slots, axis=1)
    return jnp.where(starts[:, None, None], given, assembled)


def on_device(
    tokens,
    cotangent,
    given_cache,
    value_routes,
    output_routes,
    valid_counts,
    doc_starts,
    norm1_gain,
    norm1_shift,
    qk_weight,
    router_weight,
    value_weight,
    output_weight,
    rel_bias,
    norm2_gain,
    norm2_shift,
    ffn_in,
    ffn_out,
):
    batches, unused_row, local_len, model_width = tokens.shape
    row_count = batches * local_len
    inner_width = HEADS * HEAD_DIM
    head_experts = HEADS * EXPERTS
    full_weights = (
        lax.all_gather(norm1_gain, ("doc", "tm"), axis=0, tiled=True),
        lax.all_gather(norm1_shift, ("doc", "tm"), axis=0, tiled=True),
        lax.all_gather(qk_weight, ("doc", "tm"), axis=0, tiled=True),
        lax.all_gather(router_weight, ("doc", "tm"), axis=0, tiled=True),
        lax.all_gather(value_weight, ("doc", "tm"), axis=0, tiled=True),
        lax.all_gather(output_weight, ("doc", "tm"), axis=1, tiled=True),
        lax.all_gather(rel_bias, ("doc", "tm"), axis=1, tiled=True),
        lax.all_gather(norm2_gain, ("doc", "tm"), axis=0, tiled=True),
        lax.all_gather(norm2_shift, ("doc", "tm"), axis=0, tiled=True),
        lax.all_gather(ffn_in, ("doc", "tm"), axis=0, tiled=True),
        lax.all_gather(ffn_out, ("doc", "tm"), axis=0, tiled=True),
    )
    (
        gain_one,
        shift_one,
        w_qk,
        w_router,
        w_value,
        w_output,
        table_bf,
        gain_two,
        shift_two,
        w_in,
        w_out,
    ) = full_weights
    gain_one = gain_one.astype(jnp.float32)
    shift_one = shift_one.astype(jnp.float32)
    gain_two = gain_two.astype(jnp.float32)
    shift_two = shift_two.astype(jnp.float32)
    table = table_bf.astype(jnp.float32)
    router_f = w_router.astype(jnp.float32)
    inputs = tokens.reshape(row_count, model_width).astype(jnp.float32)
    counts = valid_counts.reshape(batches)
    starts = doc_starts.reshape(batches) > 0
    token_mask = (
        (jnp.arange(local_len, dtype=jnp.int32)[None, :] < counts[:, None])
        .astype(jnp.float32)
        .reshape(row_count, 1)
    )
    value_pick = selection(value_routes.reshape(row_count, HEADS, TOPK))
    output_pick = selection(output_routes.reshape(row_count, HEADS, TOPK))
    normed_one, norm1_unit, norm1_inv = norm_forward(inputs, gain_one, shift_one)
    act_one = normed_one.astype(jnp.bfloat16)
    qk_vals = jnp.dot(act_one, w_qk, preferred_element_type=jnp.float32).astype(jnp.bfloat16)
    gates = jax.nn.sigmoid(jnp.dot(act_one, w_router, preferred_element_type=jnp.float32))
    gate_value = gates[:, :head_experts].reshape(row_count, HEADS, EXPERTS) * value_pick
    gate_output = gates[:, head_experts:].reshape(row_count, HEADS, EXPERTS) * output_pick
    value_gate_t = jnp.transpose(gate_value, (0, 2, 1))[..., None]
    output_gate_t = jnp.transpose(gate_output, (0, 2, 1))[..., None]
    parts = jnp.dot(act_one, w_value, preferred_element_type=jnp.float32).reshape(
        row_count, EXPERTS, HEADS, HEAD_DIM
    )
    values = (
        jnp.sum(value_gate_t * parts, axis=1).reshape(row_count, inner_width).astype(jnp.bfloat16)
    )
    cache_own = jnp.concatenate([qk_vals[:, inner_width:], values], axis=1).reshape(
        batches, local_len, 2 * inner_width
    )
    given = given_cache.reshape(batches, MEM, 2 * inner_width)
    memory = memory_by_hops(cache_own, given, starts, local_len)
    queries = qk_vals[:, :inner_width].reshape(batches, local_len, HEADS, HEAD_DIM)
    keys = jnp.concatenate([memory[:, :, :inner_width], cache_own[:, :, :inner_width]], axis=1)
    keys = keys.reshape(batches, MEM + local_len, HEADS, HEAD_DIM)
    vals = jnp.concatenate([memory[:, :, inner_width:], cache_own[:, :, inner_width:]], axis=1)
    vals = vals.reshape(batches, MEM + local_len, HEADS, HEAD_DIM)
    scores, valid = attention_scores(queries, keys, table, counts)
    top = jnp.max(scores, axis=-1, keepdims=True)
    expo = jnp.exp(scores - top)
    denom = jnp.sum(expo, axis=-1, keepdims=True)
    log_total = top + jnp.log(denom)
    probs_b = (expo / denom).astype(jnp.bfloat16)
    attended = jnp.einsum("bhqk,bkhd->bqhd", probs_b, vals, preferred_element_type=jnp.float32)
    attended = attended.reshape(row_count, inner_width).astype(jnp.bfloat16)
    attended_f = attended.astype(jnp.float32).reshape(row_count, 1, HEADS, HEAD_DIM)
    mixed = (
        (output_gate_t * attended_f).reshape(row_count, EXPERTS * inner_width).astype(jnp.bfloat16)
    )
    hidden = inputs + jnp.dot(mixed, w_output, preferred_element_type=jnp.float32)
    normed_two, norm2_unit, norm2_inv = norm_forward(hidden, gain_two, shift_two)
    act_two = normed_two.astype(jnp.bfloat16)
    pre_act = jnp.dot(act_two, w_in, preferred_element_type=jnp.float32)
    activated = jax.nn.gelu(pre_act, approximate=False).astype(jnp.bfloat16)
    ffn_result = jnp.dot(activated, w_out, preferred_element_type=jnp.float32)
    layer_out = (token_mask * (hidden + ffn_result)).astype(jnp.bfloat16).reshape(tokens.shape)
    upstream = cotangent.reshape(row_count, model_width).astype(jnp.float32) * token_mask
    upstream_b = upstream.astype(jnp.bfloat16)
    d_out_w = jnp.einsum("nf,nd->fd", activated, upstream_b, preferred_element_type=jnp.float32)
    d_act = jnp.einsum("nd,fd->nf", upstream_b, w_out, preferred_element_type=jnp.float32)
    d_pre = (d_act * gelu_slope(pre_act)).astype(jnp.bfloat16)
    d_in_w = jnp.einsum("nd,nf->df", act_two, d_pre, preferred_element_type=jnp.float32)
    d_norm_two = jnp.einsum("nf,df->nd", d_pre, w_in, preferred_element_type=jnp.float32)
    d_from_two, d_gain_two, d_shift_two = norm_backward(d_norm_two, norm2_unit, norm2_inv, gain_two)
    d_hidden = upstream + d_from_two
    ffn_width = d_in_w.shape[1]
    d_branch = d_hidden.astype(jnp.bfloat16)
    d_output_t = jnp.einsum("nd,nk->dk", d_branch, mixed, preferred_element_type=jnp.float32)
    d_mixed = jnp.einsum(
        "nd,kd->nk", d_branch, w_output, preferred_element_type=jnp.float32
    ).astype(jnp.bfloat16)
    d_mixed = d_mixed.astype(jnp.float32).reshape(row_count, EXPERTS, HEADS, HEAD_DIM)
    d_gate_out = jnp.sum(d_mixed * attended_f, axis=-1)
    d_attended = (
        jnp.sum(d_mixed * output_gate_t, axis=1)
        .astype(jnp.bfloat16)
        .reshape(batches, local_len, HEADS, HEAD_DIM)
    )
    probs = jnp.where(valid, jnp.exp(scores - log_total), 0.0)
    d_probs = jnp.einsum("bqhd,bkhd->bhqk", d_attended, vals, preferred_element_type=jnp.float32)
    delta = jnp.sum(d_probs * probs, axis=-1, keepdims=True)
    d_scores = probs * (d_probs - delta)
    score_sum = jnp.sum(d_scores, axis=0)
    d_table = bias_backward(score_sum, local_len)
    d_scores_b = d_scores.astype(jnp.bfloat16)
    scale = HEAD_DIM ** (-0.5)
    d_queries = (
        jnp.einsum("bhqk,bkhd->bqhd", d_scores_b, keys, preferred_element_type=jnp.float32) * scale
    )
    d_keys = (
        jnp.einsum(
            "bhqk,bqhd->bkhd", d_scores_b[..., MEM:], queries, preferred_element_type=jnp.float32
        )
        * scale
    )
    d_vals = jnp.einsum(
        "bhqk,bqhd->bkhd", probs_b[..., MEM:], d_attended, preferred_element_type=jnp.float32
    )
    d_qk = jnp.concatenate(
        [d_queries.reshape(row_count, inner_width), d_keys.reshape(row_count, inner_width)], axis=1
    ).astype(jnp.bfloat16)
    d_values = (
        d_vals.reshape(row_count, 1, HEADS, HEAD_DIM).astype(jnp.bfloat16).astype(jnp.float32)
    )
    d_gate_val = jnp.sum(parts * d_values, axis=-1)
    d_parts = (
        (value_gate_t * d_values).reshape(row_count, EXPERTS * inner_width).astype(jnp.bfloat16)
    )
    d_gates = jnp.concatenate(
        [
            jnp.transpose(d_gate_val, (0, 2, 1)).reshape(row_count, head_experts)
            * value_pick.reshape(row_count, head_experts),
            jnp.transpose(d_gate_out, (0, 2, 1)).reshape(row_count, head_experts)
            * output_pick.reshape(row_count, head_experts),
        ],
        axis=1,
    )
    d_logits = d_gates * gates * (1.0 - gates)
    d_qk_w = jnp.einsum("nd,nk->dk", act_one, d_qk, preferred_element_type=jnp.float32)
    d_value_w = jnp.einsum("nd,nk->dk", act_one, d_parts, preferred_element_type=jnp.float32)
    d_router_w = jnp.einsum("nd,nk->dk", act_one.astype(jnp.float32), d_logits, precision=HIGH)
    d_norm_one = jnp.einsum("nk,dk->nd", d_qk, w_qk, preferred_element_type=jnp.float32)
    d_norm_one = d_norm_one + jnp.einsum(
        "nk,dk->nd", d_parts, w_value, preferred_element_type=jnp.float32
    )
    d_norm_one = d_norm_one + jnp.einsum("nk,dk->nd", d_logits, router_f, precision=HIGH)
    d_from_one, d_gain_one, d_shift_one = norm_backward(d_norm_one, norm1_unit, norm1_inv, gain_one)
    input_grad = (d_hidden + d_from_one).reshape(tokens.shape)
    shares = (
        lax.psum_scatter(d_gain_one, ("doc", "tm"), scatter_dimension=0, tiled=True),
        lax.psum_scatter(d_shift_one, ("doc", "tm"), scatter_dimension=0, tiled=True),
        lax.psum_scatter(flatten(d_qk_w), ("doc", "tm"), scatter_dimension=0, tiled=True),
        lax.psum_scatter(flatten(d_router_w), ("doc", "tm"), scatter_dimension=0, tiled=True),
        lax.psum_scatter(flatten(d_value_w), ("doc", "tm"), scatter_dimension=0, tiled=True),
        lax.psum_scatter(flatten(d_output_t), ("doc", "tm"), scatter_dimension=0, tiled=True),
        lax.psum_scatter(d_table, ("doc", "tm"), scatter_dimension=1, tiled=True),
        lax.psum_scatter(d_gain_two, ("doc", "tm"), scatter_dimension=0, tiled=True),
        lax.psum_scatter(d_shift_two, ("doc", "tm"), scatter_dimension=0, tiled=True),
        lax.psum_scatter(flatten(d_in_w), ("doc", "tm"), scatter_dimension=0, tiled=True),
        lax.psum_scatter(flatten(d_out_w), ("doc", "tm"), scatter_dimension=0, tiled=True),
    )
    qk_share = shares[2].reshape(-1, 2 * inner_width)
    router_share = shares[3].reshape(-1, 2 * head_experts)
    value_share = shares[4].reshape(-1, EXPERTS * inner_width)
    output_share = shares[5].reshape(-1, EXPERTS * inner_width).T
    in_share = shares[9].reshape(-1, ffn_width)
    out_share = shares[10].reshape(-1, model_width)
    return (
        layer_out,
        input_grad,
        shares[0],
        shares[1],
        qk_share,
        router_share,
        value_share,
        output_share,
        shares[6],
        shares[7],
        shares[8],
        in_share,
        out_share,
    )


MESH = pl.DeviceIdType.MESH
PAD = 128
SIDE = 2
HALF_HEADS = HEADS // SIDE
W_QK = 2 * HALF_HEADS * PAD
W_VAL = EXPERTS * HALF_HEADS * PAD
W_MISC = 128
W_A = W_QK + W_VAL + W_MISC
W_O = EXPERTS * HALF_HEADS * PAD
MISC = W_QK + W_VAL
N_ROUTE = 2 * HALF_HEADS * EXPERTS
COL_NORM = N_ROUTE
COL_BIAS = N_ROUTE + 4
VMEM_BYTES = 63 * 1024 * 1024
SCALE = HEAD_DIM ** (-0.5)


def pad_last(a, width):
    return jnp.pad(a, [(0, 0)] * (a.ndim - 1) + [(0, width - a.shape[-1])])


def neighbours(count):
    d, t = lax.axis_index("doc"), lax.axis_index("tm")
    z, c = t // 2, t % 2
    return dict(
        c=(d, z * 2 + 1 - c),
        x=(d + 1 - 2 * (d % 2), t),
        y=((d + 2) % 4, t),
        up=(d, jnp.minimum(t + 2, count - 1)),
        down=(d, jnp.maximum(t - 2, 0)),
    )


def enter(nb, z, levels):
    barrier = pltpu.get_barrier_semaphore()
    for name in ("c", "x", "y"):
        pl.semaphore_signal(barrier, inc=1, device_id=nb[name], device_id_type=MESH)

    @pl.when(z < levels - 1)
    def _():
        pl.semaphore_signal(barrier, inc=1, device_id=nb["up"], device_id_type=MESH)

    @pl.when(z > 0)
    def _():
        pl.semaphore_signal(barrier, inc=1, device_id=nb["down"], device_id_type=MESH)

    ends = jnp.where(z < levels - 1, 1, 0) + jnp.where(z > 0, 1, 0)
    pl.semaphore_wait(barrier, 3 + ends)


class Gather:
    def __init__(self, ref, sems, nb, d, z, levels):
        self.ref, self.nb, self.d, self.z, self.levels = ref, nb, d, z, levels
        self.send, self.recv = sems
        self.half = ref.shape[2] // 2

    def copy(self, part, slot, to):
        return pltpu.make_async_remote_copy(
            src_ref=part, dst_ref=part, send_sem=self.send.at[slot], recv_sem=self.recv.at[slot],
            device_id=self.nb[to], device_id_type=MESH)

    def along(self, level, distance, to):
        base = 0 if to == "up" else self.levels
        return self.copy(self.ref.at[self.d, level], base + distance, to)

    def across(self, level, to, column=None):
        base = (2 if to == "x" else 3) * self.levels
        column = self.d if column is None else column
        return self.copy(self.ref.at[column, level], base + level, to)

    def corner(self, level, to, column):
        base = (4 if to == "x" else 5) * self.levels
        rows = pl.ds(self.half, self.half) if to == "x" else pl.ds(0, self.half)
        return self.copy(self.ref.at[column, level, rows], base + level, to)

    def begin(self):
        z, levels = self.z, self.levels

        @pl.when(z < levels - 1)
        def _():
            self.along(z, 1, "up").start()

        @pl.when(z > 0)
        def _():
            self.along(z, 1, "down").start()

        self.across(z, "x").start()
        self.across(z, "y").start()

    def line(self, k):
        z, levels = self.z, self.levels

        @pl.when(z >= k)
        def _():
            self.along(z - k, k, "up").wait_recv()

            @pl.when(z < levels - 1)
            def _():
                self.along(z - k, k + 1, "up").start()

            self.across(z - k, "x").start()
            self.across(z - k, "y").start()

        @pl.when(z + k < levels)
        def _():
            self.along(z + k, k, "down").wait_recv()

            @pl.when(z > 0)
            def _():
                self.along(z + k, k + 1, "down").start()

            self.across(z + k, "x").start()
            self.across(z + k, "y").start()

    def turn(self, k):
        z, levels, d = self.z, self.levels, self.d
        by_x, by_y = d + 1 - 2 * (d % 2), (d + 2) % 4

        def one(level):
            self.across(level, "x").wait_recv()
            self.corner(level, "y", by_x).start()
            self.across(level, "y").wait_recv()
            self.corner(level, "x", by_y).start()

        if k == 0:
            one(z)
        else:
            pl.when(z >= k)(lambda: one(z - k))
            pl.when(z + k < levels)(lambda: one(z + k))

    def finish(self, k):
        z, levels, d = self.z, self.levels, self.d
        by_x, by_y = d + 1 - 2 * (d % 2), (d + 2) % 4

        def one(level):
            self.corner(level, "x", by_y).wait_recv()
            self.corner(level, "y", by_x).wait_recv()

        if k == 0:
            one(z)
        else:
            pl.when(z >= k)(lambda: one(z - k))
            pl.when(z + k < levels)(lambda: one(z + k))

    def drain(self):
        z, levels, d = self.z, self.levels, self.d
        by_x, by_y = d + 1 - 2 * (d % 2), (d + 2) % 4
        for level in range(levels):
            self.across(level, "x").wait_send()
            self.across(level, "y").wait_send()
            self.corner(level, "x", by_y).wait_send()
            self.corner(level, "y", by_x).wait_send()
        for k in range(1, levels):

            @pl.when(jnp.logical_and(z >= k - 1, z < levels - 1))
            def _():
                self.along(z - k + 1, k, "up").wait_send()

            @pl.when(jnp.logical_and(z + k - 1 < levels, z > 0))
            def _():
                self.along(z + k - 1, k, "down").wait_send()


def selector(side):
    inner = HEADS * HEAD_DIM
    wide = HALF_HEADS * PAD
    src = lax.broadcasted_iota(jnp.int32, (2 * inner, 2 * wide), 0)
    dst = lax.broadcasted_iota(jnp.int32, (2 * inner, 2 * wide), 1)
    kind, head, feature = dst // wide, (dst // PAD) % HALF_HEADS, dst % PAD
    wanted = kind * inner + (side * HALF_HEADS + head) * HEAD_DIM + feature
    hit = jnp.logical_and(src == wanted, feature < HEAD_DIM)
    return jnp.where(hit, 1.0, 0.0).astype(jnp.bfloat16)


def table_by_offset(w_a, per_device, shard, local_len, spread):
    distance = MEM + local_len - 1 - lax.broadcasted_iota(jnp.int32, (1, spread), 1)
    bucket = bucket_index(distance)
    wanted = (bucket // per_device) * shard + bucket % per_device
    step = 128

    def body(i, total):
        at = pl.ds(pl.multiple_of(i * step, step), step)
        ids = lax.broadcasted_iota(jnp.int32, (step, spread), 0) + i * step
        one_hot = jnp.where(ids == wanted, 1.0, 0.0).astype(jnp.bfloat16)
        return total + dot_f32(w_a[at, MISC:W_A], one_hot, TN)

    return lax.fori_loop(0, w_a.shape[0] // step, body, jnp.zeros((W_MISC, spread), jnp.float32))


NT = (((1,), (1,)), ((), ()))
TN = (((0,), (0,)), ((), ()))


def dot_f32(a, b, dims=(((1,), (0,)), ((), ()))):
    return lax.dot_general(a, b, dims, preferred_element_type=jnp.float32)


def forward_kernel(
    levels, batches, local_len, per_device,
    qk_in, value_in, router_in, norm_in, bias_in, branch_in, up_in, f_in, token_in, cot_in, vr_in, or_in, start_in,
    count_in, g_in,
    a_out, o_out, i_out, f_all, xs_out, act_out, front_out, gates_out, win_out, probs_out, att_out,
    mixed_out, hidden_out, n2_out, vec_out, ffn_out, slope_out,
    a_all, o_all, i_all, xs, graw, win, rbuf, sel, unit, act, front, gates, vec, bias, probs, att, mixed,
    arrived, hidden, n2, ffn, slope,
    qk_raw, value_raw, router_raw, norm_raw, bias_raw, branch_raw, up_raw, vr_raw, or_raw, start_raw, count_raw, f_raw, a_pack, o_pack, i_pack,
    send, recv, csend, crecv, lsem, gsend, grecv, esend, erecv, osem, psem,
):
    bf16, f32 = jnp.bfloat16, jnp.float32
    d, t = lax.axis_index("doc"), lax.axis_index("tm")
    z, c = t // 2, t % 2
    nb = neighbours(2 * levels)
    shard = qk_in.shape[0]
    width = f_in.shape[1]
    rows = batches * local_len
    both = 2 * rows
    wide = HALF_HEADS * PAD
    own = pl.ds(pl.multiple_of(c * shard, 16), shard)

    def local(src, dst, index):
        cp = pltpu.make_async_copy(src, dst, lsem.at[index])
        cp.start()
        return cp

    def sibling(src, dst, index):
        return pltpu.make_async_remote_copy(
            src_ref=src, dst_ref=dst, send_sem=csend.at[index], recv_sem=crecv.at[index],
            device_id=nb["c"], device_id_type=MESH)

    raws = [
        local(src, dst, i)
        for i, (src, dst) in enumerate((
            (qk_in, qk_raw), (value_in, value_raw), (router_in, router_raw), (norm_in, norm_raw), (bias_in, bias_raw),
            (branch_in, branch_raw), (up_in, up_raw), (vr_in, vr_raw), (or_in, or_raw), (start_in, start_raw),
            (count_in, count_raw)))
    ]
    loc_f = local(f_in, f_raw, 11)
    x_parts = ((token_in, pl.ds(0, width)), (cot_in, pl.ds(width, width)))
    loc_x = [local(src, xs.at[c, :, cols], 12 + i) for i, (src, cols) in enumerate(x_parts)]
    enter(nb, z, levels)
    rem_x = [sibling(src, xs.at[c, :, cols], i) for i, (src, cols) in enumerate(x_parts)]
    for cp in rem_x:
        cp.start()
    ga, go, gi, gf = [
        Gather(ref, (send.at[i], recv.at[i]), nb, d, z, levels)
        for i, ref in enumerate((a_all, o_all, i_all, f_all))
    ]

    for cp in raws[:5]:
        cp.wait()
    a_pack[...] = jnp.zeros_like(a_pack)
    norm_columns = norm_raw[...].astype(f32).T
    for side in range(SIDE):
        for h in range(HALF_HEADS):
            at = (side * HALF_HEADS + h) * HEAD_DIM
            for kind in range(2):
                col, src = (kind * HALF_HEADS + h) * PAD, kind * HEADS * HEAD_DIM + at
                a_pack[side, :, col : col + HEAD_DIM] = qk_raw[:, src : src + HEAD_DIM]
            for e in range(EXPERTS):
                col, src = W_QK + (e * HALF_HEADS + h) * PAD, e * HEADS * HEAD_DIM + at
                a_pack[side, :, col : col + HEAD_DIM] = value_raw[:, src : src + HEAD_DIM]
        routes = HALF_HEADS * EXPERTS
        for kind in range(2):
            src = (kind * SIDE + side) * routes
            a_pack[side, :, MISC + kind * routes : MISC + (kind + 1) * routes] = router_raw[:, src : src + routes]
        a_pack[side, :, MISC + COL_NORM : MISC + COL_NORM + 4] = norm_columns.astype(bf16)
        heads = bias_raw[side * HALF_HEADS : (side + 1) * HALF_HEADS].astype(f32).T
        tail = jnp.concatenate([heads, jnp.zeros((shard - per_device, HALF_HEADS), f32)], axis=0)
        a_pack[side, :, MISC + COL_BIAS : MISC + COL_BIAS + HALF_HEADS] = tail.astype(bf16)
    loc_a = local(a_pack.at[c], a_all.at[d, z, own], 17)
    rem_a = sibling(a_pack.at[1 - c], a_all.at[d, z, own], 3)
    rem_a.start()
    for cp in raws[7:]:
        cp.wait()
    row_ids = lax.broadcasted_iota(jnp.int32, (W_MISC, local_len), 0)
    for batch in range(batches):
        flags = [
            jnp.broadcast_to(raw[:, batch : batch + 1].astype(f32), (W_MISC, local_len)) for raw in (start_raw, count_raw)]
        for side in range(SIDE):
            rows_of = jnp.where(row_ids == 40, flags[0], jnp.where(row_ids == 41, flags[1], 0.0))
            for kind, raw in enumerate((vr_raw, or_raw)):
                for h in range(HALF_HEADS):
                    chosen = raw[batch, side * HALF_HEADS + h]
                    first = (kind * HALF_HEADS + h) * EXPERTS
                    expert = row_ids - first
                    hit = expert == chosen[0:1]
                    for k in range(1, TOPK):
                        hit = jnp.logical_or(hit, expert == chosen[k : k + 1])
                    inside = jnp.logical_and(row_ids >= first, row_ids < first + EXPERTS)
                    rows_of = jnp.where(jnp.logical_and(hit, inside), 1.0, rows_of)
            cols = pl.ds(2 * width + side * 128, 128)
            xs[c, pl.ds(batch * local_len, local_len), cols] = rows_of.T.astype(bf16)
    meta_cols = xs.at[c, :, pl.ds(2 * width, SIDE * 128)]
    rem_x.append(sibling(meta_cols, meta_cols, 2))
    rem_x[-1].start()
    loc_g = local(g_in, graw.at[c], 14)
    rem_g = sibling(g_in, graw.at[c], 4)
    rem_g.start()
    loc_a.wait()
    rem_a.wait()
    ga.begin()
    sel[...] = selector(c)

    for cp in loc_x + rem_x:
        cp.wait()
    step = 64

    def stats(i, carry):
        at = pl.ds(pl.multiple_of((i % (rows // step)) * step, step), step)
        block = i // (rows // step)
        values = xs[block, at, :width].astype(f32)
        centered = values - jnp.mean(values, axis=-1, keepdims=True)
        inverse = lax.rsqrt(jnp.mean(centered * centered, axis=-1, keepdims=True) + EPS)
        unit[pl.ds(pl.multiple_of(i * step, step), step)] = centered * inverse
        counts = xs[block, at, 2 * width : 2 * width + 128][:, 41:42].astype(f32)
        position = lax.broadcasted_iota(jnp.int32, (step, 1), 0) + (i * step) % local_len
        gradient = xs[block, at, width : 2 * width].astype(f32)
        xs[block, at, width : 2 * width] = jnp.where(position.astype(f32) < counts, gradient, 0.0).astype(bf16)
        return carry

    lax.fori_loop(0, both // step, stats, 0)
    ga.line(1)
    raws[6].wait()
    for side in range(SIDE):
        for p in range(4 * levels):
            src = (p * SIDE + side) * PAD
            i_pack[side, :, p * PAD : (p + 1) * PAD] = up_raw[:, src : src + PAD]
    raws[5].wait()
    o_pack[...] = jnp.zeros_like(o_pack)
    for side in range(SIDE):
        for h in range(HALF_HEADS):
            for e in range(EXPERTS):
                src = e * HEADS * HEAD_DIM + (side * HALF_HEADS + h) * HEAD_DIM
                col = (e * HALF_HEADS + h) * PAD
                o_pack[side, :, col : col + HEAD_DIM] = branch_raw[:, src : src + HEAD_DIM]
    loc_o = local(o_pack.at[c], o_all.at[d, z, own], 15)
    rem_o = sibling(o_pack.at[1 - c], o_all.at[d, z, own], 5)
    loc_i = local(i_pack.at[c], i_all.at[d, z, own], 16)
    rem_i = sibling(i_pack.at[1 - c], i_all.at[d, z, own], 6)
    rem_o.start()
    rem_i.start()

    slots = MEM // local_len
    has_up, has_down = z < levels - 1, z > 0

    def slot(s):
        return pl.ds(s * local_len, local_len)

    def starts_of(block, batch):
        column = xs[block, pl.ds(batch * local_len, local_len), 2 * width : 2 * width + 128]
        return column[:, 40:41].astype(f32)

    def spread_given(i, carry):
        at = pl.ds(pl.multiple_of((i % slots) * local_len, local_len), local_len)
        pair = i // slots
        mine = dot_f32(graw[pair // batches, pair % batches, at], sel[...])
        win[pair, at] = mine.astype(bf16)
        return carry

    def keep_or(block, batch, s, moved):
        at = block * batches + batch
        held = win[at, slot(s)]
        first = jnp.broadcast_to(starts_of(block, batch), held.shape) > 0.5
        win[at, slot(s)] = jnp.where(first, held.astype(f32), moved.astype(f32)).astype(bf16)

    def message(m, batch):
        src = win.at[batches + batch, pl.ds((slots - 1 - 2 * m) * local_len, 2 * local_len)]
        return pltpu.make_async_remote_copy(
            src_ref=src, dst_ref=rbuf.at[m, batch], send_sem=gsend.at[m, batch], recv_sem=grecv.at[m, batch],
            device_id=nb["up"], device_id_type=MESH)

    rounds = slots // 2

    def send_message(m, batch):
        if m < rounds:
            pl.when(has_up)(lambda: message(m, batch).start())

    def take(m):
        for batch in range(batches):
            pl.when(has_down)(lambda: message(m, batch).wait_recv())
            for k in (0, 1):
                keep_or(0, batch, slots - 1 - 2 * m - k, rbuf[m, batch, slot(1 - k)])
            for s in (slots - 2 - 2 * m, slots - 3 - 2 * m):
                if s >= 0:
                    keep_or(1, batch, s, win[batch, slot(s + 1)])
            send_message(m + 1, batch)

    def early(m):
        pl.when(z <= m)(lambda: take(m))

    def late(m):
        pl.when(z > m)(lambda: take(m))

    loc_g.wait()
    rem_g.wait()
    lax.fori_loop(0, 2 * batches * slots, spread_given, 0)
    early(0)
    ga.turn(0)
    ga.line(2)
    ga.turn(1)
    early(1)
    for k in range(3, levels):
        ga.line(k)
    loc_o.wait()
    rem_o.wait()
    go.begin()
    for k in range(2, levels):
        ga.turn(k)
    go.line(1)
    early(2)
    for k in range(levels):
        ga.finish(k)
    out_a = pltpu.make_async_copy(a_all, a_out, osem.at[0])
    out_a.start()

    w_a = a_all.reshape(4 * levels * 2 * shard, W_A)
    vec[...] = w_a[:, MISC:W_A].astype(f32).T

    def norm(i, carry):
        at = pl.ds(pl.multiple_of(i * step, step), step)
        act[at] = (unit[at] * vec[COL_NORM : COL_NORM + 1] + vec[COL_NORM + 1 : COL_NORM + 2]).astype(bf16)
        return carry

    lax.fori_loop(0, both // step, norm, 0)

    def project(i, carry):
        at = pl.ds(pl.multiple_of(i * 256, 256), 256)
        front[:, at] = dot_f32(act[...], w_a[:, at])
        return carry

    lax.fori_loop(0, MISC // 256, project, 0)
    front[:, MISC:W_A] = dot_f32(act[...], w_a[:, MISC:W_A])
    go.turn(0)
    go.line(2)
    loc_i.wait()
    rem_i.wait()
    gi.begin()
    meta_at = pl.ds(pl.multiple_of(2 * width + c * 128, 128), 128)

    def gate(i, carry):
        at = pl.ds(pl.multiple_of(i * local_len, local_len), local_len)
        gated = jax.nn.sigmoid(front[at, MISC:W_A])
        gates[at] = gated
        picks = xs[i // batches, pl.ds(pl.multiple_of((i % batches) * local_len, local_len), local_len), meta_at]
        gated = gated * picks.astype(f32)
        for h in range(HALF_HEADS):
            total = jnp.zeros((local_len, PAD), f32)
            for e in range(EXPERTS):
                lane = h * EXPERTS + e
                col = W_QK + (e * HALF_HEADS + h) * PAD
                total = total + gated[:, lane : lane + 1] * front[at, col : col + PAD]
            win[i, pl.ds(MEM, local_len), wide + h * PAD : wide + (h + 1) * PAD] = total.astype(bf16)
        win[i, pl.ds(MEM, local_len), :wide] = front[at, wide : 2 * wide].astype(bf16)
        return carry

    lax.fori_loop(0, 2 * batches, gate, 0)

    for batch in range(batches):
        keep_or(1, batch, slots - 1, win[batch, pl.ds(MEM, local_len)])
        send_message(0, batch)
    go.turn(1)
    for k in range(3, levels):
        go.line(k)
    gi.line(1)
    for m in range(3, rounds):
        early(m)

    spread = MEM + 2 * local_len
    table = table_by_offset(w_a, per_device, shard, local_len, spread)
    for h in range(HALF_HEADS):
        line = jnp.broadcast_to(table[COL_BIAS + h : COL_BIAS + h + 1], (local_len, spread))
        turned = pltpu.roll(line, spread - local_len + 1, 1, stride=1, stride_axis=0)
        bias[h] = turned[:, : MEM + local_len]
    for k in range(2, levels):
        go.turn(k)
    late(0)
    gi.turn(0)
    gi.line(2)
    loc_f.wait()
    own_f = local(f_raw, f_all.at[d, z], 18)
    own_f.wait()
    gf.begin()
    late(1)
    gi.turn(1)
    for k in range(3, levels):
        gi.line(k)
    gf.line(1)
    late(2)
    for m in range(3, rounds):
        late(m)
    out_w = pltpu.make_async_copy(win, win_out, osem.at[1])
    out_w.start()

    key_ids = lax.broadcasted_iota(jnp.int32, (local_len, local_len), 1)
    row_ids = lax.broadcasted_iota(jnp.int32, (local_len, local_len), 0)

    def probs_copy(i, slot_of):
        return pltpu.make_async_copy(probs.at[slot_of], probs_out.at[i], psem.at[slot_of])

    def attend(i, carry):
        at = pl.ds(pl.multiple_of(i * local_len, local_len), local_len)
        block, batch = i // batches, i % batches
        rows_at = pl.ds(pl.multiple_of(batch * local_len, local_len), local_len)
        count = xs[block, rows_at, 2 * width : 2 * width + 128][:, 41:42].astype(f32)
        seen = jnp.logical_and(key_ids <= row_ids, key_ids.astype(f32) < count)
        picks = xs[block, rows_at, meta_at].astype(f32) * gates[at]
        slot_of = lax.rem(i, 2)
        pl.when(i >= 2)(lambda: probs_copy(i - 2, slot_of).wait())
        for h in range(HALF_HEADS):
            cols = slice(h * PAD, (h + 1) * PAD)
            q = front[at, cols].astype(bf16)
            s = dot_f32(q, win[i, :, cols], NT) * SCALE + bias[h]
            s = jnp.concatenate([s[:, :MEM], jnp.where(seen, s[:, MEM:], NEG)], axis=1)
            top = jnp.max(s, axis=-1, keepdims=True)
            expo = jnp.exp(s - top)
            p = expo * (1.0 / jnp.sum(expo, axis=-1, keepdims=True))
            probs[slot_of, h] = p
            p = p.astype(bf16)
            got = dot_f32(p, win[i, :, wide + h * PAD : wide + (h + 1) * PAD]).astype(bf16)
            att[at, cols] = got
            got = got.astype(f32)
            for e in range(EXPERTS):
                lane = HALF_HEADS * EXPERTS + h * EXPERTS + e
                col = (e * HALF_HEADS + h) * PAD
                mixed[at, col : col + PAD] = (picks[:, lane : lane + 1] * got).astype(bf16)
        probs_copy(i, slot_of).start()
        return carry

    lax.fori_loop(0, batches, attend, 0)
    gf.turn(0)
    for k in range(2, levels):
        gi.turn(k)
    gf.line(2)
    lax.fori_loop(batches, 2 * batches, attend, 0)
    for i in range(2 * batches - 2, 2 * batches):
        probs_copy(i, i % 2).wait()
    gf.turn(1)
    for k in range(3, levels):
        gf.line(k)
    for k in range(levels):
        go.finish(k)

    w_o = o_all.reshape(4 * levels * 2 * shard, W_O)
    branch = unit
    far = pl.ds(pl.multiple_of((1 - c) * rows, rows), rows)
    near = pl.ds(pl.multiple_of(c * rows, rows), rows)

    def out_project(at):
        def body(i, carry):
            cols = pl.ds(pl.multiple_of(i * 256, 256), 256)
            branch[at, cols] = dot_f32(mixed[at], w_o[cols], NT)
            return carry

        lax.fori_loop(0, width // 256, body, 0)

    def exchange(src, dst, index):
        return pltpu.make_async_remote_copy(
            src_ref=src, dst_ref=dst, send_sem=esend.at[index], recv_sem=erecv.at[index],
            device_id=nb["c"], device_id_type=MESH)

    out_project(far)
    give = exchange(branch.at[far], arrived, 0)
    give.start()
    out_project(near)
    out_o = pltpu.make_async_copy(o_all, o_out, osem.at[2])
    out_o.start()
    give.wait_recv()

    def second(i, carry):
        at = pl.ds(pl.multiple_of(i * step, step), step)
        total_at = pl.ds(pl.multiple_of(c * rows + i * step, step), step)
        values = xs[c, at, :width].astype(f32) + branch[total_at] + arrived[at]
        hidden[at] = values
        centered = values - jnp.mean(values, axis=-1, keepdims=True)
        inverse = lax.rsqrt(jnp.mean(centered * centered, axis=-1, keepdims=True) + EPS)
        normed = centered * inverse * vec[COL_NORM + 2 : COL_NORM + 3] + vec[COL_NORM + 3 : COL_NORM + 4]
        n2[total_at] = normed.astype(bf16)
        return carry

    lax.fori_loop(0, rows // step, second, 0)
    pair = exchange(n2.at[near], n2.at[near], 1)
    pair.start()
    for k in range(2, levels):
        gf.turn(k)
    pair.wait_recv()
    outs = [
        pltpu.make_async_copy(src, dst, osem.at[3 + i])
        for i, (src, dst) in enumerate((
            (xs, xs_out), (act, act_out), (front, front_out), (gates, gates_out),
            (att, att_out), (mixed, mixed_out), (hidden, hidden_out), (n2, n2_out), (vec, vec_out)))
    ]
    for cp in outs:
        cp.start()
    for k in range(levels):
        gi.finish(k)
    out_i = pltpu.make_async_copy(i_all, i_out, osem.at[13])
    out_i.start()

    w_i = i_all.reshape(4 * levels * 2 * shard, i_all.shape[3])

    def activate(i, carry):
        at = pl.ds(pl.multiple_of(i * 256, 256), 256)
        pre = dot_f32(n2[...], w_i[:, at])
        below = 0.5 * (1.0 + lax.erf(pre * 0.7071067811865476))
        ffn[:, at] = (pre * below).astype(bf16)
        slope[:, at] = (below + pre * jnp.exp(-0.5 * pre * pre) * 0.3989422804014327).astype(bf16)
        return carry

    steps = ffn.shape[1] // 256
    lax.fori_loop(0, steps, activate, 0)
    outs += [pltpu.make_async_copy(ffn, ffn_out, osem.at[14]), pltpu.make_async_copy(slope, slope_out, osem.at[15])]
    outs[-2].start()
    outs[-1].start()
    for k in range(levels):
        gf.finish(k)
    for group in (ga, go, gi, gf):
        group.drain()
    for cp in (give, pair):
        cp.wait_send()
    for m in range(rounds):
        for batch in range(batches):
            pl.when(has_up)(lambda: message(m, batch).wait_send())
    out_a.wait()
    out_w.wait()
    out_o.wait()
    out_i.wait()
    for cp in outs:
        cp.wait()


def forward(levels, batches, local_len, per_device, ins):
    bf16, f32 = jnp.bfloat16, jnp.float32
    shape = jax.ShapeDtypeStruct
    qk, value, router, norms, bias_in, branch, up, f, tokens, cot, vr, outr, start, count, g = ins
    shard, width = qk.shape[0], f.shape[1]
    a, o, i = [shape((SIDE, shard, w), bf16) for w in (W_A, W_O, up.shape[1] // SIDE)]
    x = shape((tokens.shape[0], 2 * width + SIDE * 128), bf16)
    rows = batches * local_len
    both = 2 * rows
    wide = HALF_HEADS * PAD
    two = lambda v: (4, levels, 2 * v.shape[1], v.shape[2])
    window = (2 * batches, MEM + local_len, 2 * wide)
    probs = (2 * batches, HALF_HEADS, local_len, MEM + local_len)
    outs = [
        (two(a), bf16), (two(o), bf16), (two(i), bf16), ((4, levels) + f.shape, bf16),
        ((2,) + x.shape, bf16), ((both, width), bf16), ((both, W_A), f32), ((both, W_MISC), f32),
        (window, bf16), (probs, f32), ((both, wide), bf16), ((both, W_O), bf16),
        ((rows, width), f32), ((both, width), bf16), ((W_MISC, width), f32), ((both, i.shape[2]), bf16),
        ((both, i.shape[2]), bf16),
    ]
    rounds = MEM // local_len // 2
    scratch = [
        (two(a), bf16), (two(o), bf16), (two(i), bf16), ((2,) + x.shape, bf16), ((2,) + g.shape, bf16),
        (window, bf16), ((rounds, batches, 2 * local_len, 2 * wide), bf16), ((g.shape[2], 2 * wide), bf16),
        ((both, width), f32), ((both, width), bf16), ((both, W_A), f32), ((both, W_MISC), f32),
        ((W_MISC, width), f32), ((HALF_HEADS, local_len, MEM + local_len), f32), ((2,) + probs[1:], f32),
        ((both, wide), bf16), ((both, W_O), bf16), ((rows, width), f32),
        ((rows, width), f32), ((both, width), bf16), ((both, i.shape[2]), bf16), ((both, i.shape[2]), bf16),
    ]
    rounds = MEM // local_len // 2
    scratch += [(w.shape, w.dtype) for w in (qk, value, router, norms, bias_in, branch, up, vr, outr, start, count, f, a, o, i)]
    sems = [(4, 6 * levels), (4, 6 * levels), (7,), (7,), (19,), (rounds, batches), (rounds, batches), (2,), (2,), (16,), (2,)]
    hbm = pl.BlockSpec(memory_space=pl.ANY)
    return pl.pallas_call(
        functools.partial(forward_kernel, levels, batches, local_len, per_device),
        out_shape=[jax.ShapeDtypeStruct(s, k) for s, k in outs],
        in_specs=[hbm] * len(ins),
        out_specs=[hbm] * len(outs),
        scratch_shapes=[pltpu.VMEM(s, k) for s, k in scratch] + [pltpu.SemaphoreType.DMA(s) for s in sems],
        compiler_params=pltpu.CompilerParams(
            collective_id=1, has_side_effects=True, vmem_limit_bytes=VMEM_BYTES),
    )(*ins)


def add_rows(dst, terms):
    rows, width = dst.shape
    step = 16

    def body(i, carry):
        at = pl.ds(pl.multiple_of(i * step, step), step)
        total = terms[0][at].astype(jnp.float32)
        for term in terms[1:]:
            total = total + term[at].astype(jnp.float32)
        dst[at] = total.astype(dst.dtype)
        return carry

    lax.fori_loop(0, rows // step, body, 0)


class Scatter:
    def __init__(self, src, view, sems, nb, d, z, levels, total):
        self.src, self.view, self.nb, self.d, self.z, self.levels = src, view, nb, d, z, levels
        self.send, self.recv = sems
        self.sum = total
        self.half = src.shape[2] // 2
        self.by_x, self.by_y = d + 1 - 2 * (d % 2), (d + 2) % 4
        self.low, self.high = pl.ds(0, self.half), pl.ds(self.half, self.half)

    def copy(self, src, dst, slot, to):
        return pltpu.make_async_remote_copy(
            src_ref=src, dst_ref=dst, send_sem=self.send.at[slot], recv_sem=self.recv.at[slot],
            device_id=self.nb[to], device_id_type=MESH)

    def corner(self, j, to):
        part, name, base = (self.low, "cx", 0) if to == "x" else (self.high, "cy", self.levels)
        return self.copy(self.src.at[3 - self.d, j, part], self.view(name, j), base + j, to)

    def direct(self, j, to):
        if to == "x":
            column, part, name, base = self.by_x, self.low, "rx", 2 * self.levels
        else:
            column, part, name, base = self.by_y, self.high, "ry", 3 * self.levels
        return self.copy(self.src.at[column, j, part], self.view(name, j).at[part], base + j, to)

    def relay(self, j, to):
        if to == "x":
            held, part, name, base = "cy", self.high, "rx", 4 * self.levels
        else:
            held, part, name, base = "cx", self.low, "ry", 5 * self.levels
        return self.copy(self.view(held, j), self.view(name, j).at[part], base + j, to)

    def along(self, j, to, first=False):
        base = (6 if to == "up" else 7) * self.levels
        there = self.view(to, j, self.z + (1 if to == "up" else -1))
        return self.copy(self.view("rx" if first else to, j), there, base + j, to)

    def issue(self, j):
        self.corner(j, "x").start()
        self.corner(j, "y").start()
        self.direct(j, "x").start()
        self.direct(j, "y").start()

    def turn(self, j):
        self.corner(j, "x").wait_recv()
        add_rows(self.view("cx", j), [self.view("cx", j), self.src.at[self.by_y, j, self.low]])
        self.relay(j, "y").start()
        self.corner(j, "y").wait_recv()
        add_rows(self.view("cy", j), [self.view("cy", j), self.src.at[self.by_x, j, self.high]])
        self.relay(j, "x").start()

    def column(self, j):
        for to in ("x", "y"):
            self.direct(j, to).wait_recv()
            self.relay(j, to).wait_recv()
        add_rows(self.view("rx", j), [self.view("rx", j), self.view("ry", j), self.src.at[self.d, j]])

    def lift(self, j, stage):
        def hop(to):
            if stage:
                self.along(j, to).wait_recv()
                add_rows(self.view(to, j), [self.view(to, j), self.view("rx", j)])
            self.along(j, to, first=stage == 0).start()

        if stage < j:
            pl.when(self.z == stage)(lambda: hop("up"))
        if self.levels - 1 - stage > j:
            pl.when(self.z == self.levels - 1 - stage)(lambda: hop("down"))

    def total(self, j):
        @pl.when(self.z == j)
        def _():
            terms = [self.view("rx", j)]
            for to, there in (("up", j > 0), ("down", j < self.levels - 1)):
                if there:
                    self.along(j, to).wait_recv()
                    terms.append(self.view(to, j))
            add_rows(self.sum, terms)

    def drain(self):
        for j in range(self.levels):
            for to in ("x", "y"):
                self.corner(j, to).wait_send()
                self.direct(j, to).wait_send()
                self.relay(j, to).wait_send()
            pl.when(self.z < j)(lambda: self.along(j, "up").wait_send())
            pl.when(self.z > j)(lambda: self.along(j, "down").wait_send())


class LineFirst:
    def __init__(self, src, view, bufs, sems, nb, d, z, levels, total):
        self.src, self.view, self.nb, self.d, self.z, self.levels = src, view, nb, d, z, levels
        self.cx, self.cy, self.rx, self.ry = bufs
        self.send, self.recv = sems
        self.sum = total
        half = src.shape[2] // 2
        self.by_x, self.by_y = d + 1 - 2 * (d % 2), (d + 2) % 4
        self.low, self.high = pl.ds(0, half), pl.ds(half, half)

    def copy(self, src, dst, slot, to):
        return pltpu.make_async_remote_copy(
            src_ref=src, dst_ref=dst, send_sem=self.send.at[slot], recv_sem=self.recv.at[slot],
            device_id=self.nb[to], device_id_type=MESH)

    def along(self, j, column, to, level, first=False):
        slot = (0 if to == "up" else 4 * self.levels) + 4 * j + column
        after = level + (1 if to == "up" else -1)
        src = self.src.at[column, j] if first else self.view(j, column)
        return self.copy(src, self.view(self.levels if to == "down" and after == j else j, column), slot, to)

    def lift(self, j, stage):
        def hop(to, level):
            for column in range(4):
                if stage:
                    before = level - (1 if to == "up" else -1)
                    self.along(j, column, to, before).wait_recv()
                    held = self.view(j, column)
                    add_rows(held, [held, self.src.at[column, j]])
                self.along(j, column, to, level, first=stage == 0).start()

        if stage < j:
            pl.when(self.z == stage)(lambda: hop("up", stage))
        if self.levels - 1 - stage > j:
            pl.when(self.z == self.levels - 1 - stage)(lambda: hop("down", self.levels - 1 - stage))

    def gathered(self, j):
        @pl.when(self.z == j)
        def _():
            for column in range(4):
                terms = [self.src.at[column, j]]
                if j > 0:
                    self.along(j, column, "up", j - 1).wait_recv()
                    terms.append(self.view(j, column))
                if j < self.levels - 1:
                    self.along(j, column, "down", j + 1).wait_recv()
                    terms.append(self.view(self.levels, column))
                add_rows(terms[0], terms)

    def plane(self, k):
        base = 8 * self.levels
        part = lambda column, rows: self.src.at[column, self.z, rows]
        return (
            self.copy(part(3 - self.d, self.low), self.cx, base, "x"),
            self.copy(part(3 - self.d, self.high), self.cy, base + 1, "y"),
            self.copy(part(self.by_x, self.low), self.rx.at[self.low], base + 2, "x"),
            self.copy(part(self.by_y, self.high), self.ry.at[self.high], base + 3, "y"),
            self.copy(self.cy, self.rx.at[self.high], base + 4, "x"),
            self.copy(self.cx, self.ry.at[self.low], base + 5, "y"),
        )[k]

    def issue(self):
        for k in range(4):
            self.plane(k).start()

    def turn(self):
        self.plane(0).wait_recv()
        add_rows(self.cx, [self.cx, self.src.at[self.by_y, self.z, self.low]])
        self.plane(5).start()
        self.plane(1).wait_recv()
        add_rows(self.cy, [self.cy, self.src.at[self.by_x, self.z, self.high]])
        self.plane(4).start()

    def column(self):
        for k in range(2, 6):
            self.plane(k).wait_recv()
        add_rows(self.sum, [self.rx, self.ry, self.src.at[self.d, self.z]])

    def drain(self):
        for k in range(6):
            self.plane(k).wait_send()
        for j in range(self.levels):
            for column in range(4):
                for level in range(self.levels):
                    if level < j:
                        pl.when(self.z == level)(lambda: self.along(j, column, "up", level).wait_send())
                    if level > j:
                        pl.when(self.z == level)(lambda: self.along(j, column, "down", level).wait_send())


A_PART = 896
AHEAD = 3


def LAGS(count):
    return [2] + [4 + 3 * k for k in range(count - 1)]


class Pipeline:
    def __init__(self, units, levels, ahead, lags):
        self.units, self.levels, self.ahead, self.now = units, levels, ahead, 0
        self.follow = [lambda s, j: s.column(j)]
        for stage in range(levels - 1):
            self.follow.append(lambda s, j, stage=stage: s.lift(j, stage))
        self.follow.append(lambda s, j: s.total(j))
        self.lags = lags(len(self.follow))
        self.done = [0] * len(units)

    def each(self, n, act):
        if 0 <= n < len(self.units):
            for scatter, j in self.units[n]:
                act(scatter, j)

    def begin(self):
        for n in range(self.ahead):
            self.each(n, lambda s, j: s.issue(j))

    def advance(self, n):
        self.each(n, self.follow[self.done[n]])
        self.done[n] += 1

    def step(self):
        n = self.now
        if n < len(self.units):
            self.each(n, lambda s, j: s.turn(j))
            self.each(n + self.ahead, lambda s, j: s.issue(j))
        for m in range(min(n + 1, len(self.units))):
            while self.done[m] < len(self.lags) and n - m >= self.lags[self.done[m]]:
                self.advance(m)
        self.now += 1

    def finish(self):
        while self.now < len(self.units):
            self.step()
        while min(self.done) < len(self.follow):
            for m in range(len(self.units)):
                if self.done[m] < len(self.follow):
                    self.advance(m)


def norm_rows(values):
    centered = values - jnp.mean(values, axis=-1, keepdims=True)
    inverse = lax.rsqrt(jnp.mean(centered * centered, axis=-1, keepdims=True) + EPS)
    return centered * inverse, inverse


def norm_rows_backward(upstream, normed, inverse, gain):
    scaled = upstream * gain
    inside = (
        scaled
        - jnp.mean(scaled, axis=-1, keepdims=True)
        - normed * jnp.mean(scaled * normed, axis=-1, keepdims=True)
    )
    return inside * inverse


VEC_ROW = COL_NORM // 8 * 8
VEC_GAIN = COL_NORM - VEC_ROW


def backward_kernel(
    levels, batches, local_len, per_device, shard,
    wf_in, wi_in, wo_in, wa_in, ffn_in, slope_in, xs_in, n2_in, hidden_in, vec_in, att_in, gates_in, front_in,
    win_in, probs_in, mixed_in, act_in,
    f_out, i_out, o_out, a_out, m_out, layer_out, grad_out,
    w_f, w_i, ffn, slope, grad, meta, n2, hidden, vec, att, gates, front, win, probs,
    branch, arrived, dhid, db, dmix, dfront, dsum, norms,
    f_total, i_total, o_total, a_total, m_total, *rest,
):
    bf16, f32 = jnp.bfloat16, jnp.float32
    f_bufs, i_bufs, m_bufs = rest[:6], rest[6:12], rest[12:18]
    a_src, a_cx, a_cy, o_src, o_line, o_cx, o_cy, o_rx, o_ry = rest[18:27]
    send, recv, osend, orecv, lsem, tsem, esend, erecv, osem, ready, freed = rest[27:]
    d, t = lax.axis_index("doc"), lax.axis_index("tm")
    z, c = t // 2, t % 2
    nb = neighbours(2 * levels)
    width = w_f.shape[1]
    rows = batches * local_len
    both = 2 * rows
    wide = HALF_HEADS * PAD
    ff = ffn.shape[1]
    far = pl.ds(pl.multiple_of((1 - c) * rows, rows), rows)
    near = pl.ds(pl.multiple_of(c * rows, rows), rows)

    def load(src, dst, index):
        cp = pltpu.make_async_copy(src, dst, lsem.at[index])
        cp.start()
        return cp

    meta_at = pl.ds(pl.multiple_of(2 * width + c * 128, 128), 128)
    l_ffn = load(ffn_in, ffn, 0)
    l_grad = load(xs_in.at[:, :, pl.ds(width, width)], grad, 1)
    enter(nb, z, levels)
    l_ffn.wait()
    l_grad.wait()
    l_wf = load(wf_in, w_f, 2)
    l_slope = load(slope_in, slope, 3)
    l_n2 = load(n2_in, n2, 4)
    l_wi = load(wi_in, w_i, 5)
    l_hid = load(hidden_in, hidden, 6)
    l_vec = load(vec_in.at[pl.ds(VEC_ROW, 8)], vec, 7)
    l_mixed = load(mixed_in, dmix, 8)
    l_meta = load(xs_in.at[:, :, meta_at], meta, 9)
    l_att = load(att_in, att, 10)
    l_gates = load(gates_in, gates, 11)
    w_o = a_src.at[:, :, :, pl.ds(0, W_O)]
    l_wo = load(wo_in, w_o, 12)

    def tiles(i):
        at = pl.ds(i * local_len, local_len)
        return [
            pltpu.make_async_copy(win_in.at[i], win.at[i % 2], tsem.at[0, i % 2]),
            pltpu.make_async_copy(front_in.at[at, pl.ds(0, wide)], front.at[i % 2, :, pl.ds(0, wide)], tsem.at[2, i % 2]),
            pltpu.make_async_copy(
                front_in.at[at, pl.ds(W_QK, W_VAL)], front.at[i % 2, :, pl.ds(wide, W_VAL)], tsem.at[3, i % 2]),
        ]

    def probs_tile(n):
        return pltpu.make_async_copy(probs_in.at[n // HALF_HEADS, n % HALF_HEADS], probs.at[n % 2], tsem.at[1, n % 2])

    for cp in tiles(0):
        cp.start()
    probs_tile(0).start()

    names = ("cx", "cy", "rx", "ry")

    def plain(bufs):
        def view(name, j, level=z):
            if name == "up":
                return bufs[5].at[j]
            if name == "down":
                return bufs[5].at[jnp.where(level == j, levels, j)]
            return bufs[1 + names.index(name)].at[j]

        return view

    block_rows = shard * SIDE

    def within(held, cx, cy, cols):
        def view(name, j, level=z):
            if name in ("cx", "cy"):
                return (cx if name == "cx" else cy).at[j, :, cols]
            ref, base = held[name]
            return ref.at[pl.ds(base + j * block_rows, block_rows), cols]

        return view

    span = levels * block_rows
    a_held = dict(rx=(w_i, 0), ry=(w_i, span), up=(w_i, 2 * span), down=(w_i, 3 * span))
    a_cols = [pl.ds(k * A_PART, A_PART) for k in range(MISC // A_PART)]
    sums = [
        Scatter(src, view, (send.at[i], recv.at[i]), nb, d, z, levels, total)
        for i, (src, view, total) in enumerate((
            (f_bufs[0], plain(f_bufs), f_total), (i_bufs[0], plain(i_bufs), i_total),
            (m_bufs[0], plain(m_bufs), m_total)) + tuple(
                (a_src.at[:, :, :, cols], within(a_held, a_cx, a_cy, cols), a_total.at[:, cols]) for cols in a_cols))
    ]
    sf, si, sm = sums[:3]
    held = []
    for ref in (ffn, slope):
        for base in range(0, ref.shape[0], 4 * block_rows):
            held.append((ref, base))
    held = held[:levels] + [(o_line, 0)]

    def o_view(slot, column):
        ref, base = held[slot]
        return ref.at[pl.ds(base + column * block_rows, block_rows), pl.ds(0, W_O)]

    so = LineFirst(o_src, o_view, (o_cx, o_cy, o_rx, o_ry), (osend, orecv), nb, d, z, levels, o_total)
    order = []
    for k in range((levels + 1) // 2):
        order += [levels - 1 - k, k] if levels - 1 - k != k else [k]
    units = [[(s, j)] for s in [sf, si] + sums[3:] for j in order]
    units[-1] = units[-1] + [(sm, j) for j in order]
    line = Pipeline(units, levels, AHEAD, LAGS)

    def exchange(src, dst, index):
        return pltpu.make_async_remote_copy(
            src_ref=src, dst_ref=dst, send_sem=esend.at[index], recv_sem=erecv.at[index],
            device_id=nb["c"], device_id_type=MESH)

    def weight_grad(dst, left, right, chunk, total, column):
        at = pl.ds(pl.multiple_of(column * span, span), span)

        def body(i, carry):
            cols = pl.ds(pl.multiple_of(i * chunk, chunk), chunk)
            got = dot_f32(left[:, at], right[:, cols], TN).astype(bf16)
            dst[column, :, :, cols] = got.reshape(levels, block_rows, chunk)
            return carry

        lax.fori_loop(0, total // chunk, body, 0)

    g_all = grad.reshape(both, width)
    f_rows = f_bufs[0].shape[2]
    f_span = levels * f_rows
    for column in (3 - d, sf.by_x, sf.by_y, d):
        at = pl.ds(pl.multiple_of(column * f_span, f_span), f_span)
        f_bufs[0][column] = dot_f32(ffn[:, at], g_all[...], TN).astype(bf16).reshape(levels, f_rows, width)
    line.begin()

    l_wf.wait()
    l_slope.wait()

    def back(i, carry):
        at = pl.ds(pl.multiple_of(i * 256, 256), 256)
        slope[:, at] = (dot_f32(g_all[...], w_f[at], NT) * slope[:, at].astype(f32)).astype(bf16)
        return carry

    lax.fori_loop(0, ff // 256, back, 0)
    l_n2.wait()
    for column in range(4):
        weight_grad(i_bufs[0], n2, slope, 512, ff, column)
    line.step()

    l_wi.wait()

    def times(src, weights, dims):
        def run(at):
            def body(i, carry):
                cols = pl.ds(pl.multiple_of(i * 256, 256), 256)
                branch[at, cols] = dot_f32(src[at], weights(cols), dims)
                return carry

            lax.fori_loop(0, width // 256, body, 0)

        return run

    through_in = times(slope, lambda cols: w_i[cols], NT)
    through_in(far)
    give = exchange(branch.at[far], arrived, 0)
    give.start()
    through_in(near)
    line.step()
    l_hid.wait()
    l_vec.wait()
    give.wait()
    norms[...] = jnp.zeros_like(norms)
    step = 64

    def second(i, carry):
        at = pl.ds(pl.multiple_of(i * step, step), step)
        total_at = pl.ds(pl.multiple_of(c * rows + i * step, step), step)
        normed, inverse = norm_rows(hidden[at])
        up = branch[total_at] + arrived[at]
        norms[COL_NORM + 2 : COL_NORM + 3] += jnp.sum(up * normed, axis=0, keepdims=True)
        norms[COL_NORM + 3 : COL_NORM + 4] += jnp.sum(up, axis=0, keepdims=True)
        got = norm_rows_backward(up, normed, inverse, vec[VEC_GAIN + 2 : VEC_GAIN + 3])
        got = got + grad[c, at].astype(f32)
        dhid[at] = got
        db[total_at] = got.astype(bf16)
        return carry

    lax.fori_loop(0, rows // step, second, 0)
    pair = exchange(db.at[near], db.at[near], 1)
    pair.start()
    l_act = load(act_in, grad, 13)

    through_out = times(ffn, lambda cols: w_f[:, cols], (((1,), (0,)), ((), ())))
    through_out(far)
    pair.wait()
    last = exchange(branch.at[far], arrived, 2)
    last.start()
    line.step()
    through_out(near)

    for name in ("x", "y"):
        pl.semaphore_signal(ready, inc=1, device_id=nb[name], device_id_type=MESH)
    for name, there in (("up", z < levels - 1), ("down", z > 0)):

        @pl.when(there)
        def _():
            pl.semaphore_signal(ready, inc=1, device_id=nb[name], device_id_type=MESH)

    l_wa = [
        load(wa_in.at[:, pl.ds(0, width)], w_f.at[pl.ds(0, width)], 14),
        load(wa_in.at[:, pl.ds(width, W_A - width)], w_f.at[pl.ds(width, width), pl.ds(0, W_A - width)], 15),
    ]
    l_mixed.wait()
    for column in range(4):
        weight_grad(o_src, db, dmix, 640, W_O, column)
    ends = jnp.where(z < levels - 1, 1, 0) + jnp.where(z > 0, 1, 0)
    pl.semaphore_wait(ready, 2 + ends)
    for j in order:
        so.lift(j, 0)
    l_wo.wait()

    def mix(i, carry):
        cols = pl.ds(pl.multiple_of(i * wide, wide), wide)
        dmix[:, cols] = dot_f32(db[...], a_src[:, :, :, cols].reshape(width, wide)).astype(bf16)
        return carry

    lax.fori_loop(0, EXPERTS, mix, 0)
    l_meta.wait()
    l_att.wait()
    l_gates.wait()
    dsum[...] = jnp.zeros_like(dsum)
    lanes = lax.broadcasted_iota(jnp.int32, (local_len, W_MISC), 1)

    def attend(i):
        slot = i % 2
        if i + 1 < 2 * batches:
            for cp in tiles(i + 1):
                cp.start()
        for cp in tiles(i):
            cp.wait()
        at = pl.ds(i * local_len, local_len)
        block, batch = i // batches, i % batches
        gate = gates[at]
        picks = meta[block, pl.ds(batch * local_len, local_len)].astype(f32)
        gated = gate * picks
        d_gates = jnp.zeros((local_len, W_MISC), f32)
        for h in range(HALF_HEADS):
            cols = slice(h * PAD, (h + 1) * PAD)
            v_cols = slice(wide + h * PAD, wide + (h + 1) * PAD)
            got = att[at, cols].astype(f32)
            d_att = jnp.zeros((local_len, PAD), f32)
            for e in range(EXPERTS):
                lane = HALF_HEADS * EXPERTS + h * EXPERTS + e
                col = (e * HALF_HEADS + h) * PAD
                part = dmix[at, col : col + PAD].astype(f32)
                d_att = d_att + gated[:, lane : lane + 1] * part
                d_gates = jnp.where(lanes == lane, jnp.sum(part * got, axis=-1, keepdims=True), d_gates)
            d_att = d_att.astype(bf16)
            n = i * HALF_HEADS + h
            if n + 1 < 2 * batches * HALF_HEADS:
                probs_tile(n + 1).start()
            probs_tile(n).wait()
            p = probs[n % 2]
            d_p = dot_f32(d_att, win[slot, :, v_cols], NT)
            delta = jnp.sum(d_p * p, axis=-1, keepdims=True)
            d_s = p * (d_p - delta)
            dsum[h] += d_s
            d_s = d_s.astype(bf16)
            q = front[slot, :, cols].astype(bf16)
            d_q = dot_f32(d_s, win[slot, :, cols]) * SCALE
            d_k = dot_f32(d_s[:, MEM:], q, TN) * SCALE
            d_v = dot_f32(p[:, MEM:].astype(bf16), d_att, TN).astype(bf16).astype(f32)
            dfront[at, cols] = d_q.astype(bf16)
            dfront[at, wide + h * PAD : wide + (h + 1) * PAD] = d_k.astype(bf16)
            for e in range(EXPERTS):
                lane = h * EXPERTS + e
                col = W_QK + (e * HALF_HEADS + h) * PAD
                part = front[slot, :, col - W_QK + wide : col - W_QK + wide + PAD]
                d_gates = jnp.where(lanes == lane, jnp.sum(part * d_v, axis=-1, keepdims=True), d_gates)
                dfront[at, col : col + PAD] = (gated[:, lane : lane + 1] * d_v).astype(bf16)
        d_logits = jnp.where(lanes < N_ROUTE, d_gates * picks * gate * (1.0 - gate), 0.0)
        dfront[at, MISC:W_A] = d_logits.astype(bf16)

    def o_stage(stage, part):
        for j in part:
            so.lift(j, stage)

    outer, inner_levels = order[:2], order[2:]
    attend(0)
    line.step()
    attend(1)
    o_stage(1, outer)
    line.step()
    for i in range(2, 2 * batches):
        attend(i)
    l_act.wait()
    one_all = grad.reshape(both, width)
    for column in range(4):
        weight_grad(a_src, one_all, dfront, 896, MISC, column)
    line.step()
    o_stage(1, inner_levels)
    last.wait()

    def final(i, carry):
        at = pl.ds(pl.multiple_of(i * step, step), step)
        total_at = pl.ds(pl.multiple_of(c * rows + i * step, step), step)
        tail = meta[c, at].astype(f32)
        position = lax.broadcasted_iota(jnp.int32, (step, 1), 0) + (i * step) % local_len
        keep = position.astype(f32) < tail[:, 41:42]
        total = hidden[at] + branch[total_at] + arrived[at]
        db[total_at] = jnp.where(keep, total, 0.0).astype(bf16)
        return carry

    lax.fori_loop(0, rows // step, final, 0)
    pl.semaphore_signal(freed, inc=1, device_id=nb["c"], device_id_type=MESH)
    outs = [pltpu.make_async_copy(db.at[near], layer_out, osem.at[0])]
    outs[0].start()

    line.step()
    for stage in range(2, levels - 1):
        o_stage(stage, order)
    for cp in l_wa:
        cp.wait()

    def through_front(at):
        def body(i, carry):
            cols = pl.ds(pl.multiple_of(i * 256, 256), 256)
            below = pl.ds(pl.multiple_of(width + i * 256, 256), 256)
            branch[at, cols] = (
                dot_f32(dfront[at, :width], w_f[cols], NT)
                + dot_f32(dfront[at, width:], w_f[below, : W_A - width], NT))
            return carry

        lax.fori_loop(0, width // 256, body, 0)

    through_front(far)
    hand = exchange(branch.at[far], arrived, 3)
    pl.semaphore_wait(freed, 1)
    hand.start()
    through_front(near)
    line.step()
    for j in order:
        so.gathered(j)
    so.issue()

    spread = MEM + 2 * local_len
    ids = lax.broadcasted_iota(jnp.int32, (local_len, 1), 0)
    lines = []
    for h in range(HALF_HEADS):
        turned = jnp.concatenate([dsum[h], jnp.zeros((local_len, local_len), f32)], axis=1)
        bit = 1
        while bit < local_len:
            moved = pltpu.roll(turned, bit, 1)
            turned = jnp.where(((local_len - 1 - ids) // bit) % 2 == 1, moved, turned)
            bit *= 2
        lines.append(jnp.sum(turned, axis=0, keepdims=True))
    row_of = lax.broadcasted_iota(jnp.int32, (W_MISC, spread), 0)
    table = jnp.zeros((W_MISC, spread), f32)
    for h in range(HALF_HEADS):
        table = jnp.where(row_of == COL_BIAS + h, lines[h], table)
    high = table.astype(bf16)
    low = (table - high.astype(f32)).astype(bf16)
    distance = MEM + local_len - 1 - lax.broadcasted_iota(jnp.int32, (1, spread), 1)
    bucket = bucket_index(distance)
    wanted = (bucket // per_device) * shard + bucket % per_device
    hand.wait()

    def first(i, carry):
        at = pl.ds(pl.multiple_of(i * step, step), step)
        total_at = pl.ds(pl.multiple_of(c * rows + i * step, step), step)
        normed, inverse = norm_rows(n2[at].astype(f32))
        up = branch[total_at] + arrived[at]
        norms[COL_NORM : COL_NORM + 1] += jnp.sum(up * normed, axis=0, keepdims=True)
        norms[COL_NORM + 1 : COL_NORM + 2] += jnp.sum(up, axis=0, keepdims=True)
        dhid[at] += norm_rows_backward(up, normed, inverse, vec[VEC_GAIN : VEC_GAIN + 1])
        return carry

    l_x = load(xs_in.at[c, :, pl.ds(0, width)], n2.at[pl.ds(0, rows)], 16)
    l_x.wait()
    lax.fori_loop(0, rows // step, first, 0)
    outs.append(pltpu.make_async_copy(dhid, grad_out, osem.at[1]))
    outs[1].start()
    columns = norms[...].T

    for column in range(4):
        at = pl.ds(column * span, span)
        row_ids = lax.broadcasted_iota(jnp.int32, (span, spread), 0) + column * span
        one_hot = jnp.where(row_ids == wanted, 1.0, 0.0).astype(bf16)
        misc = dot_f32(one_hot, high, NT) + dot_f32(one_hot, low, NT)
        misc = misc + dot_f32(one_all[:, at], dfront[:, MISC:W_A], TN) + columns[column * span : (column + 1) * span]
        m_bufs[0][column] = misc.astype(bf16).reshape(levels, block_rows, W_MISC)
    line.step()
    line.step()
    so.turn()
    line.step()
    line.step()
    so.column()
    line.finish()
    outs.append(pltpu.make_async_copy(f_total, f_out, osem.at[2]))
    outs[2].start()
    mine, other = [pl.ds(pl.multiple_of(k * shard, 16), shard) for k in (c, 1 - c)]
    for i, (total, out) in enumerate(((i_total, i_out), (o_total, o_out), (a_total, a_out), (m_total, m_out))):
        outs.append(exchange(total.at[other], out.at[c], 4 + i))
        outs[-1].start()
        outs.append(pltpu.make_async_copy(total.at[mine], out.at[c], osem.at[3 + i]))
        outs[-1].start()
    for s in sums + [so]:
        s.drain()
    for cp in outs:
        cp.wait()


def backward(levels, batches, local_len, per_device, shard, ins):
    bf16, f32 = jnp.bfloat16, jnp.float32
    (w_f, w_i, w_o, w_a, ffn, slope, xs, n2, hidden, vec, att, gates, front, win, probs, mixed, act) = ins
    ff, width = w_f.shape
    rows = batches * local_len
    both = 2 * rows
    f_rows = ff // (4 * levels)
    b_rows = width // (4 * levels)
    wide = HALF_HEADS * PAD
    outs = [((f_rows, width), f32)] + [((SIDE, shard, w), f32) for w in (ff, W_O, MISC, W_MISC)]
    outs += [((rows, width), bf16), ((rows, width), f32)]
    scratch = [(v.shape, v.dtype) for v in (w_f, w_i, ffn, slope)]
    scratch += [((2, rows, width), bf16), ((2, rows, 128), bf16)]
    scratch += [(n2.shape, bf16), (hidden.shape, f32), ((8, width), f32), (att.shape, bf16), (gates.shape, f32)]
    scratch += [((2, local_len, wide + W_VAL), f32), ((2,) + win.shape[1:], bf16), ((2,) + probs.shape[2:], f32)]
    scratch += [
        ((both, width), f32), ((rows, width), f32), ((rows, width), f32), ((both, width), bf16),
        ((both, W_O), bf16), ((both, W_A), bf16), ((HALF_HEADS, local_len, MEM + local_len), f32),
        ((W_MISC, width), f32), ((f_rows, width), f32),
    ]
    scratch += [((b_rows, w), f32) for w in (ff, W_O, MISC, W_MISC)]
    for r, w in ((f_rows, width), (b_rows, ff), (b_rows, W_MISC)):
        scratch.append(((4, levels, r, w), bf16))
        scratch += [((levels, k, w), bf16) for k in (r // 2, r // 2, r, r)]
        scratch.append(((levels + 1, r, w), bf16))
    scratch.append(((4, levels, b_rows, MISC), bf16))
    scratch += [((levels, b_rows // 2, MISC), bf16)] * 2
    scratch += [((4, levels, b_rows, W_O), bf16), ((4 * b_rows, W_O), bf16)]
    scratch += [((k, W_O), bf16) for k in (b_rows // 2, b_rows // 2, b_rows, b_rows)]
    sems = [(3 + MISC // A_PART, 8 * levels)] * 2 + [(8 * levels + 6,), (8 * levels + 6,), (17,), (4, 2), (8,), (8,), (10,)]
    hbm = pl.BlockSpec(memory_space=pl.ANY)
    return pl.pallas_call(
        functools.partial(backward_kernel, levels, batches, local_len, per_device, shard),
        out_shape=[jax.ShapeDtypeStruct(s, k) for s, k in outs],
        in_specs=[hbm] * len(ins),
        out_specs=[hbm] * len(outs),
        scratch_shapes=[pltpu.VMEM(s, k) for s, k in scratch]
        + [pltpu.SemaphoreType.DMA(s) for s in sems]
        + [pltpu.SemaphoreType.REGULAR] * 2,
        compiler_params=pltpu.CompilerParams(
            collective_id=2, has_side_effects=True, vmem_limit_bytes=VMEM_BYTES),
    )(*ins)


def share_kernel(
    per_device, f_in, i_in, o_in, a_in, m_in, layer_in, grad_in,
    f_out, in_out, branch_out, value_out, qk_out, router_out, gain1, shift1, gain2, shift2, bias_out, layer_out, grad_out,
    f_hold, layer_hold, grad_hold, sems,
):
    big = ((f_in, f_hold, f_out), (layer_in, layer_hold, layer_out), (grad_in, grad_hold, grad_out))
    there = [pltpu.make_async_copy(src, held, sems.at[i]) for i, (src, held, unused) in enumerate(big)]
    back = [pltpu.make_async_copy(held, dst, sems.at[3 + i]) for i, (unused, held, dst) in enumerate(big)]
    for cp in there:
        cp.start()
    for side in range(SIDE):
        for p in range(i_in.shape[2] // PAD):
            col = (p * SIDE + side) * PAD
            in_out[:, col : col + PAD] = i_in[side, :, p * PAD : (p + 1) * PAD]
        for h in range(HALF_HEADS):
            at = (side * HALF_HEADS + h) * HEAD_DIM
            for e in range(EXPERTS):
                col, dst = (e * HALF_HEADS + h) * PAD, e * HEADS * HEAD_DIM + at
                value_out[:, dst : dst + HEAD_DIM] = a_in[side, :, W_QK + col : W_QK + col + HEAD_DIM]
                branch_out[:, dst : dst + HEAD_DIM] = o_in[side, :, col : col + HEAD_DIM]
            for kind in range(2):
                col, dst = (kind * HALF_HEADS + h) * PAD, kind * HEADS * HEAD_DIM + at
                qk_out[:, dst : dst + HEAD_DIM] = a_in[side, :, col : col + HEAD_DIM]
        routes = HALF_HEADS * EXPERTS
        for kind in range(2):
            dst = (kind * SIDE + side) * routes
            router_out[:, dst : dst + routes] = m_in[side, :, kind * routes : (kind + 1) * routes]
        turned = m_in[side].T
        bias_out[side * HALF_HEADS : (side + 1) * HALF_HEADS] = turned[COL_BIAS : COL_BIAS + HALF_HEADS, :per_device]
    turned = (m_in[0] + m_in[1]).T
    for i, out in enumerate((gain1, shift1, gain2, shift2)):
        out[...] = turned[COL_NORM + i : COL_NORM + i + 1]
    for cp, after in zip(there, back):
        cp.wait()
        after.start()
    for cp in back:
        cp.wait()


def shares_of(per_device, ins):
    f, i, o, a, m, layer, grad = ins
    shard = i.shape[1]
    inner = HEADS * HEAD_DIM
    f32 = jnp.float32
    shapes = [
        (f.shape, f32), ((shard, SIDE * i.shape[2]), f32), ((shard, EXPERTS * inner), f32),
        ((shard, EXPERTS * inner), f32), ((shard, 2 * inner), f32), ((shard, 2 * HEADS * EXPERTS), f32)]
    shapes += [((1, shard), f32)] * 4 + [((HEADS, per_device), f32), (layer.shape, layer.dtype), (grad.shape, f32)]
    hbm, vmem = pl.BlockSpec(memory_space=pl.ANY), pl.BlockSpec(memory_space=pltpu.VMEM)
    return pl.pallas_call(
        functools.partial(share_kernel, per_device),
        out_shape=[jax.ShapeDtypeStruct(s, k) for s, k in shapes],
        in_specs=[hbm] + [vmem] * 4 + [hbm] * 2,
        out_specs=[hbm] + [vmem] * 10 + [hbm] * 2,
        scratch_shapes=[pltpu.VMEM(w.shape, w.dtype) for w in (f, layer, grad)] + [pltpu.SemaphoreType.DMA((6,))],
        compiler_params=pltpu.CompilerParams(vmem_limit_bytes=VMEM_BYTES),
    )(*ins)


def on_chip(
    tokens, cotangent, given_cache, value_routes, output_routes, valid_counts, doc_starts,
    norm1_gain, norm1_shift, qk_weight, router_weight, value_weight, output_weight, rel_bias,
    norm2_gain, norm2_shift, ffn_in, ffn_out,
):
    batches, unused_row, local_len, width = tokens.shape
    count = lax.axis_size("tm")
    levels = count // 2
    side = lax.axis_index("tm") % 2
    rows = batches * local_len
    shard = qk_weight.shape[0]
    blocks = 4 * levels
    bf16, f32 = jnp.bfloat16, jnp.float32

    norms = jnp.stack([norm1_gain, norm1_shift, norm2_gain, norm2_shift])
    routes = [
        jnp.transpose(r.reshape(batches, local_len, HEADS, TOPK), (0, 2, 3, 1)) for r in (value_routes, output_routes)]
    buckets = rel_bias.shape[1]
    (a_all, o_all, i_all, f_all, xs, act_one, front, gates, win, probs, attended, mixed, hidden, n2, vec, act,
     slope) = forward(
        levels, batches, local_len, buckets,
        (qk_weight, value_weight, router_weight, norms, rel_bias, output_weight.T, ffn_in, ffn_out,
         tokens.reshape(rows, width), cotangent.reshape(rows, width), routes[0], routes[1],
         doc_starts.reshape(1, batches), valid_counts.reshape(1, batches),
         given_cache.reshape(batches, MEM, 2 * HEADS * HEAD_DIM)))
    w_a = a_all.reshape(width, W_A)
    w_i = i_all.reshape(width, -1)
    w_f = f_all.reshape(-1, width)
    sums = backward(
        levels, batches, local_len, buckets, shard,
        (w_f, w_i, o_all, w_a, act, slope, xs, n2, hidden, vec, attended, gates, front, win, probs, mixed,
         act_one.reshape(2, rows, width)))
    (out_share, in_share, branch_share, value_share, qk_share, router_share, gain1, shift1, gain2, shift2, bias_share,
     layer_out, input_grad) = shares_of(buckets, sums)
    gain1, shift1, gain2, shift2 = [v.reshape(shard) for v in (gain1, shift1, gain2, shift2)]
    return (
        layer_out.reshape(tokens.shape), input_grad.reshape(tokens.shape), gain1, shift1, qk_share, router_share,
        value_share, branch_share.T, bias_share, gain2, shift2, in_share, out_share,
    )


def by_size(*args):
    thin = args[9].shape[0] % 16 != 0
    paired = lax.axis_size("doc") == 4 and lax.axis_size("tm") % 2 == 0
    return on_device(*args) if thin or not paired else on_chip(*args)


def solution(mesh):
    return jax.shard_map(
        by_size,
        mesh=mesh,
        in_specs=(
            P(None, "doc", "tm", None),
            P(None, "doc", "tm", None),
            P(None, "doc", "tm", None),
            P(None, "doc", "tm", None, None),
            P(None, "doc", "tm", None, None),
            P(None, "doc", "tm"),
            P(None, "doc", "tm"),
            P(("doc", "tm")),
            P(("doc", "tm")),
            P(("doc", "tm"), None),
            P(("doc", "tm"), None),
            P(("doc", "tm"), None),
            P(None, ("doc", "tm")),
            P(None, ("doc", "tm")),
            P(("doc", "tm")),
            P(("doc", "tm")),
            P(("doc", "tm"), None),
            P(("doc", "tm"), None),
        ),
        out_specs=(
            P(None, "doc", "tm", None),
            P(None, "doc", "tm", None),
            P(("doc", "tm")),
            P(("doc", "tm")),
            P(("doc", "tm"), None),
            P(("doc", "tm"), None),
            P(("doc", "tm"), None),
            P(None, ("doc", "tm")),
            P(None, ("doc", "tm")),
            P(("doc", "tm")),
            P(("doc", "tm")),
            P(("doc", "tm"), None),
            P(("doc", "tm"), None),
        ),
        check_vma=False,
    )
```

```python
import functools

import jax
import jax.numpy as jnp
from jax import lax
from jax.experimental import pallas as pl
from jax.experimental.pallas import tpu as pltpu
from jax.sharding import PartitionSpec as P

HEADS = 4
HEAD_DIM = 112
EXPERTS = 5
TOPK = 2
MEM = 1024
BUCKETS = 256
NEAR = 128
STEP = 16


EPS = 1e-05
NEG = -1e30
HIGH = lax.Precision.HIGHEST


def shortened(array):
    return jax.tree.map(lambda a: a.astype(jnp.bfloat16) if a.dtype == jnp.float32 else a, array)


def from_behind(value, axis, steps):
    count = lax.axis_size(axis)
    first, last = (max(0, -steps), min(count, count - steps))
    return lax.ppermute(value, axis, [(source, source + steps) for source in range(first, last)])


def norm_forward(values, gain, shift):
    center_mean = jnp.mean(values, axis=-1, keepdims=True)
    centered = values - center_mean
    inverse = lax.rsqrt(jnp.mean(centered * centered, axis=-1, keepdims=True) + EPS)
    normed = centered * inverse
    return (normed * gain + shift, normed, inverse)


def norm_backward(upstream, normed, inverse, gain):
    scaled = upstream * gain
    inside = (
        scaled
        - jnp.mean(scaled, axis=-1, keepdims=True)
        - normed * jnp.mean(scaled * normed, axis=-1, keepdims=True)
    )
    return (inside * inverse, jnp.sum(upstream * normed, axis=0), jnp.sum(upstream, axis=0))


def selection(routes):
    expert_ids = jnp.arange(EXPERTS, dtype=jnp.int32)
    return jnp.sum((routes[..., None] == expert_ids).astype(jnp.float32), axis=-2)


def bucket_index(distance):
    far_bucket = NEAR + (distance - NEAR) // STEP
    return jnp.clip(jnp.where(distance < NEAR, distance, far_bucket), 0, BUCKETS - 1)


def gelu_slope(pre_act):
    return (
        0.5 * (1.0 + lax.erf(pre_act * 0.7071067811865476))
        + pre_act * jnp.exp(-0.5 * pre_act * pre_act) * 0.3989422804014327
    )


def flatten(matrix):
    return matrix.reshape(-1)


def bucket_matrix(local_len):
    spread = MEM + 2 * local_len - 1
    distance = jnp.arange(spread, dtype=jnp.int32) - (local_len - 1)
    bucket_ids = jnp.arange(BUCKETS, dtype=jnp.int32)
    return (bucket_index(distance)[:, None] == bucket_ids[None, :]).astype(jnp.float32)


def bias_matrix(table, local_len):
    spread = MEM + 2 * local_len - 1
    window = MEM + local_len
    by_distance = jnp.einsum("hc,kc->hk", table, bucket_matrix(local_len), precision=HIGH)
    turned = jnp.concatenate([by_distance[:, ::-1], jnp.zeros((HEADS, 1), jnp.float32)], axis=1)
    tiled = jnp.tile(turned, (1, local_len))[:, : local_len * spread].reshape(
        HEADS, local_len, spread
    )
    return tiled[:, :, local_len - 1 : local_len - 1 + window]


def bias_backward(score_sum, local_len):
    spread = MEM + 2 * local_len - 1
    padded = jnp.pad(score_sum, ((0, 0), (0, 0), (local_len - 1, 0))).reshape(
        HEADS, local_len * spread
    )
    padded = jnp.pad(padded, ((0, 0), (0, local_len))).reshape(HEADS, local_len, spread + 1)
    by_distance = jnp.sum(padded, axis=1)[:, :spread][:, ::-1]
    return jnp.einsum("hk,kc->hc", by_distance, bucket_matrix(local_len), precision=HIGH)


def attention_scores(queries, keys, table, counts):
    local_len = queries.shape[1]
    window = keys.shape[1]
    raw = jnp.einsum(
        "bqhd,bkhd->bhqk", queries, keys, preferred_element_type=jnp.float32
    ) * HEAD_DIM ** (-0.5)
    row_ids = jnp.arange(local_len, dtype=jnp.int32)[:, None]
    col_ids = jnp.arange(window, dtype=jnp.int32)[None, :]
    bias = bias_matrix(table, local_len)
    own_ids = col_ids - MEM
    causal = (own_ids <= row_ids)[None, None]
    live = own_ids[None, None] < counts[:, None, None, None]
    valid = jnp.logical_or((col_ids < MEM)[None, None], jnp.logical_and(causal, live))
    return (jnp.where(valid, raw + bias[None], NEG), valid)


def memory_by_hops(cache_own, given, starts, local_len):
    hops_total = MEM // local_len
    open_flag = jnp.logical_not(starts)[:, None, None]
    memory_slots = [jnp.zeros_like(cache_own) for _ in range(hops_total)]
    start_marks = starts.astype(jnp.bfloat16)
    for distance in range(1, hops_total + 1):
        if distance < hops_total:
            outgoing = (cache_own, start_marks, given[:, distance * local_len :])
        else:
            outgoing = (cache_own, start_marks)
        incoming = jax.tree.map(
            lambda part, own: part.astype(own.dtype),
            from_behind(shortened(outgoing), "tm", distance),
            outgoing,
        )
        memory_slots[hops_total - distance] = jnp.where(
            open_flag, incoming[0], memory_slots[hops_total - distance]
        )
        arrived = jnp.logical_and(open_flag, (incoming[1] > 0)[:, None, None])
        if distance < hops_total:
            for position in range(hops_total - distance):
                portion = incoming[2][:, position * local_len : (position + 1) * local_len]
                memory_slots[position] = jnp.where(arrived, portion, memory_slots[position])
        open_flag = jnp.logical_and(open_flag, jnp.logical_not(arrived))
    assembled = jnp.concatenate(memory_slots, axis=1)
    return jnp.where(starts[:, None, None], given, assembled)


def on_device(
    tokens,
    cotangent,
    given_cache,
    value_routes,
    output_routes,
    valid_counts,
    doc_starts,
    norm1_gain,
    norm1_shift,
    qk_weight,
    router_weight,
    value_weight,
    output_weight,
    rel_bias,
    norm2_gain,
    norm2_shift,
    ffn_in,
    ffn_out,
):
    batches, unused_row, local_len, model_width = tokens.shape
    row_count = batches * local_len
    inner_width = HEADS * HEAD_DIM
    head_experts = HEADS * EXPERTS
    full_weights = (
        lax.all_gather(norm1_gain, ("doc", "tm"), axis=0, tiled=True),
        lax.all_gather(norm1_shift, ("doc", "tm"), axis=0, tiled=True),
        lax.all_gather(qk_weight, ("doc", "tm"), axis=0, tiled=True),
        lax.all_gather(router_weight, ("doc", "tm"), axis=0, tiled=True),
        lax.all_gather(value_weight, ("doc", "tm"), axis=0, tiled=True),
        lax.all_gather(output_weight, ("doc", "tm"), axis=1, tiled=True),
        lax.all_gather(rel_bias, ("doc", "tm"), axis=1, tiled=True),
        lax.all_gather(norm2_gain, ("doc", "tm"), axis=0, tiled=True),
        lax.all_gather(norm2_shift, ("doc", "tm"), axis=0, tiled=True),
        lax.all_gather(ffn_in, ("doc", "tm"), axis=0, tiled=True),
        lax.all_gather(ffn_out, ("doc", "tm"), axis=0, tiled=True),
    )
    (
        gain_one,
        shift_one,
        w_qk,
        w_router,
        w_value,
        w_output,
        table_bf,
        gain_two,
        shift_two,
        w_in,
        w_out,
    ) = full_weights
    gain_one = gain_one.astype(jnp.float32)
    shift_one = shift_one.astype(jnp.float32)
    gain_two = gain_two.astype(jnp.float32)
    shift_two = shift_two.astype(jnp.float32)
    table = table_bf.astype(jnp.float32)
    router_f = w_router.astype(jnp.float32)
    inputs = tokens.reshape(row_count, model_width).astype(jnp.float32)
    counts = valid_counts.reshape(batches)
    starts = doc_starts.reshape(batches) > 0
    token_mask = (
        (jnp.arange(local_len, dtype=jnp.int32)[None, :] < counts[:, None])
        .astype(jnp.float32)
        .reshape(row_count, 1)
    )
    value_pick = selection(value_routes.reshape(row_count, HEADS, TOPK))
    output_pick = selection(output_routes.reshape(row_count, HEADS, TOPK))
    normed_one, norm1_unit, norm1_inv = norm_forward(inputs, gain_one, shift_one)
    act_one = normed_one.astype(jnp.bfloat16)
    qk_vals = jnp.dot(act_one, w_qk, preferred_element_type=jnp.float32).astype(jnp.bfloat16)
    gates = jax.nn.sigmoid(jnp.dot(act_one, w_router, preferred_element_type=jnp.float32))
    gate_value = gates[:, :head_experts].reshape(row_count, HEADS, EXPERTS) * value_pick
    gate_output = gates[:, head_experts:].reshape(row_count, HEADS, EXPERTS) * output_pick
    value_gate_t = jnp.transpose(gate_value, (0, 2, 1))[..., None]
    output_gate_t = jnp.transpose(gate_output, (0, 2, 1))[..., None]
    parts = jnp.dot(act_one, w_value, preferred_element_type=jnp.float32).reshape(
        row_count, EXPERTS, HEADS, HEAD_DIM
    )
    values = (
        jnp.sum(value_gate_t * parts, axis=1).reshape(row_count, inner_width).astype(jnp.bfloat16)
    )
    cache_own = jnp.concatenate([qk_vals[:, inner_width:], values], axis=1).reshape(
        batches, local_len, 2 * inner_width
    )
    given = given_cache.reshape(batches, MEM, 2 * inner_width)
    memory = memory_by_hops(cache_own, given, starts, local_len)
    queries = qk_vals[:, :inner_width].reshape(batches, local_len, HEADS, HEAD_DIM)
    keys = jnp.concatenate([memory[:, :, :inner_width], cache_own[:, :, :inner_width]], axis=1)
    keys = keys.reshape(batches, MEM + local_len, HEADS, HEAD_DIM)
    vals = jnp.concatenate([memory[:, :, inner_width:], cache_own[:, :, inner_width:]], axis=1)
    vals = vals.reshape(batches, MEM + local_len, HEADS, HEAD_DIM)
    scores, valid = attention_scores(queries, keys, table, counts)
    top = jnp.max(scores, axis=-1, keepdims=True)
    expo = jnp.exp(scores - top)
    denom = jnp.sum(expo, axis=-1, keepdims=True)
    log_total = top + jnp.log(denom)
    probs_b = (expo / denom).astype(jnp.bfloat16)
    attended = jnp.einsum("bhqk,bkhd->bqhd", probs_b, vals, preferred_element_type=jnp.float32)
    attended = attended.reshape(row_count, inner_width).astype(jnp.bfloat16)
    attended_f = attended.astype(jnp.float32).reshape(row_count, 1, HEADS, HEAD_DIM)
    mixed = (
        (output_gate_t * attended_f).reshape(row_count, EXPERTS * inner_width).astype(jnp.bfloat16)
    )
    hidden = inputs + jnp.dot(mixed, w_output, preferred_element_type=jnp.float32)
    normed_two, norm2_unit, norm2_inv = norm_forward(hidden, gain_two, shift_two)
    act_two = normed_two.astype(jnp.bfloat16)
    pre_act = jnp.dot(act_two, w_in, preferred_element_type=jnp.float32)
    activated = jax.nn.gelu(pre_act, approximate=False).astype(jnp.bfloat16)
    ffn_result = jnp.dot(activated, w_out, preferred_element_type=jnp.float32)
    layer_out = (token_mask * (hidden + ffn_result)).astype(jnp.bfloat16).reshape(tokens.shape)
    upstream = cotangent.reshape(row_count, model_width).astype(jnp.float32) * token_mask
    upstream_b = upstream.astype(jnp.bfloat16)
    d_out_w = jnp.einsum("nf,nd->fd", activated, upstream_b, preferred_element_type=jnp.float32)
    d_act = jnp.einsum("nd,fd->nf", upstream_b, w_out, preferred_element_type=jnp.float32)
    d_pre = (d_act * gelu_slope(pre_act)).astype(jnp.bfloat16)
    d_in_w = jnp.einsum("nd,nf->df", act_two, d_pre, preferred_element_type=jnp.float32)
    d_norm_two = jnp.einsum("nf,df->nd", d_pre, w_in, preferred_element_type=jnp.float32)
    d_from_two, d_gain_two, d_shift_two = norm_backward(d_norm_two, norm2_unit, norm2_inv, gain_two)
    d_hidden = upstream + d_from_two
    ffn_width = d_in_w.shape[1]
    d_branch = d_hidden.astype(jnp.bfloat16)
    d_output_t = jnp.einsum("nd,nk->dk", d_branch, mixed, preferred_element_type=jnp.float32)
    d_mixed = jnp.einsum(
        "nd,kd->nk", d_branch, w_output, preferred_element_type=jnp.float32
    ).astype(jnp.bfloat16)
    d_mixed = d_mixed.astype(jnp.float32).reshape(row_count, EXPERTS, HEADS, HEAD_DIM)
    d_gate_out = jnp.sum(d_mixed * attended_f, axis=-1)
    d_attended = (
        jnp.sum(d_mixed * output_gate_t, axis=1)
        .astype(jnp.bfloat16)
        .reshape(batches, local_len, HEADS, HEAD_DIM)
    )
    probs = jnp.where(valid, jnp.exp(scores - log_total), 0.0)
    d_probs = jnp.einsum("bqhd,bkhd->bhqk", d_attended, vals, preferred_element_type=jnp.float32)
    delta = jnp.sum(d_probs * probs, axis=-1, keepdims=True)
    d_scores = probs * (d_probs - delta)
    score_sum = jnp.sum(d_scores, axis=0)
    d_table = bias_backward(score_sum, local_len)
    d_scores_b = d_scores.astype(jnp.bfloat16)
    scale = HEAD_DIM ** (-0.5)
    d_queries = (
        jnp.einsum("bhqk,bkhd->bqhd", d_scores_b, keys, preferred_element_type=jnp.float32) * scale
    )
    d_keys = (
        jnp.einsum(
            "bhqk,bqhd->bkhd", d_scores_b[..., MEM:], queries, preferred_element_type=jnp.float32
        )
        * scale
    )
    d_vals = jnp.einsum(
        "bhqk,bqhd->bkhd", probs_b[..., MEM:], d_attended, preferred_element_type=jnp.float32
    )
    d_qk = jnp.concatenate(
        [d_queries.reshape(row_count, inner_width), d_keys.reshape(row_count, inner_width)], axis=1
    ).astype(jnp.bfloat16)
    d_values = (
        d_vals.reshape(row_count, 1, HEADS, HEAD_DIM).astype(jnp.bfloat16).astype(jnp.float32)
    )
    d_gate_val = jnp.sum(parts * d_values, axis=-1)
    d_parts = (
        (value_gate_t * d_values).reshape(row_count, EXPERTS * inner_width).astype(jnp.bfloat16)
    )
    d_gates = jnp.concatenate(
        [
            jnp.transpose(d_gate_val, (0, 2, 1)).reshape(row_count, head_experts)
            * value_pick.reshape(row_count, head_experts),
            jnp.transpose(d_gate_out, (0, 2, 1)).reshape(row_count, head_experts)
            * output_pick.reshape(row_count, head_experts),
        ],
        axis=1,
    )
    d_logits = d_gates * gates * (1.0 - gates)
    d_qk_w = jnp.einsum("nd,nk->dk", act_one, d_qk, preferred_element_type=jnp.float32)
    d_value_w = jnp.einsum("nd,nk->dk", act_one, d_parts, preferred_element_type=jnp.float32)
    d_router_w = jnp.einsum("nd,nk->dk", act_one.astype(jnp.float32), d_logits, precision=HIGH)
    d_norm_one = jnp.einsum("nk,dk->nd", d_qk, w_qk, preferred_element_type=jnp.float32)
    d_norm_one = d_norm_one + jnp.einsum(
        "nk,dk->nd", d_parts, w_value, preferred_element_type=jnp.float32
    )
    d_norm_one = d_norm_one + jnp.einsum("nk,dk->nd", d_logits, router_f, precision=HIGH)
    d_from_one, d_gain_one, d_shift_one = norm_backward(d_norm_one, norm1_unit, norm1_inv, gain_one)
    input_grad = (d_hidden + d_from_one).reshape(tokens.shape)
    shares = (
        lax.psum_scatter(d_gain_one, ("doc", "tm"), scatter_dimension=0, tiled=True),
        lax.psum_scatter(d_shift_one, ("doc", "tm"), scatter_dimension=0, tiled=True),
        lax.psum_scatter(flatten(d_qk_w), ("doc", "tm"), scatter_dimension=0, tiled=True),
        lax.psum_scatter(flatten(d_router_w), ("doc", "tm"), scatter_dimension=0, tiled=True),
        lax.psum_scatter(flatten(d_value_w), ("doc", "tm"), scatter_dimension=0, tiled=True),
        lax.psum_scatter(flatten(d_output_t), ("doc", "tm"), scatter_dimension=0, tiled=True),
        lax.psum_scatter(d_table, ("doc", "tm"), scatter_dimension=1, tiled=True),
        lax.psum_scatter(d_gain_two, ("doc", "tm"), scatter_dimension=0, tiled=True),
        lax.psum_scatter(d_shift_two, ("doc", "tm"), scatter_dimension=0, tiled=True),
        lax.psum_scatter(flatten(d_in_w), ("doc", "tm"), scatter_dimension=0, tiled=True),
        lax.psum_scatter(flatten(d_out_w), ("doc", "tm"), scatter_dimension=0, tiled=True),
    )
    qk_share = shares[2].reshape(-1, 2 * inner_width)
    router_share = shares[3].reshape(-1, 2 * head_experts)
    value_share = shares[4].reshape(-1, EXPERTS * inner_width)
    output_share = shares[5].reshape(-1, EXPERTS * inner_width).T
    in_share = shares[9].reshape(-1, ffn_width)
    out_share = shares[10].reshape(-1, model_width)
    return (
        layer_out,
        input_grad,
        shares[0],
        shares[1],
        qk_share,
        router_share,
        value_share,
        output_share,
        shares[6],
        shares[7],
        shares[8],
        in_share,
        out_share,
    )


MESH = pl.DeviceIdType.MESH
PAD = 128
SIDE = 2
HALF_HEADS = HEADS // SIDE
W_QK = 2 * HALF_HEADS * PAD
W_VAL = EXPERTS * HALF_HEADS * PAD
W_MISC = 128
W_A = W_QK + W_VAL + W_MISC
W_O = EXPERTS * HALF_HEADS * PAD
MISC = W_QK + W_VAL
N_ROUTE = 2 * HALF_HEADS * EXPERTS
COL_NORM = N_ROUTE
COL_BIAS = N_ROUTE + 4
VMEM_BYTES = 63 * 1024 * 1024
SCALE = HEAD_DIM ** (-0.5)


def pad_last(a, width):
    return jnp.pad(a, [(0, 0)] * (a.ndim - 1) + [(0, width - a.shape[-1])])


def neighbours(count):
    d, t = lax.axis_index("doc"), lax.axis_index("tm")
    z, c = t // 2, t % 2
    return dict(
        c=(d, z * 2 + 1 - c),
        x=(d + 1 - 2 * (d % 2), t),
        y=((d + 2) % 4, t),
        up=(d, jnp.minimum(t + 2, count - 1)),
        down=(d, jnp.maximum(t - 2, 0)),
    )


def enter(nb, z, levels):
    barrier = pltpu.get_barrier_semaphore()
    for name in ("c", "x", "y"):
        pl.semaphore_signal(barrier, inc=1, device_id=nb[name], device_id_type=MESH)

    @pl.when(z < levels - 1)
    def _():
        pl.semaphore_signal(barrier, inc=1, device_id=nb["up"], device_id_type=MESH)

    @pl.when(z > 0)
    def _():
        pl.semaphore_signal(barrier, inc=1, device_id=nb["down"], device_id_type=MESH)

    ends = jnp.where(z < levels - 1, 1, 0) + jnp.where(z > 0, 1, 0)
    pl.semaphore_wait(barrier, 3 + ends)


class Gather:
    def __init__(self, ref, sems, nb, d, z, levels):
        self.ref, self.nb, self.d, self.z, self.levels = ref, nb, d, z, levels
        self.send, self.recv = sems
        self.half = ref.shape[2] // 2

    def copy(self, part, slot, to):
        return pltpu.make_async_remote_copy(
            src_ref=part, dst_ref=part, send_sem=self.send.at[slot], recv_sem=self.recv.at[slot],
            device_id=self.nb[to], device_id_type=MESH)

    def along(self, level, distance, to):
        base = 0 if to == "up" else self.levels
        return self.copy(self.ref.at[self.d, level], base + distance, to)

    def across(self, level, to, column=None):
        base = (2 if to == "x" else 3) * self.levels
        column = self.d if column is None else column
        return self.copy(self.ref.at[column, level], base + level, to)

    def corner(self, level, to, column):
        base = (4 if to == "x" else 5) * self.levels
        rows = pl.ds(self.half, self.half) if to == "x" else pl.ds(0, self.half)
        return self.copy(self.ref.at[column, level, rows], base + level, to)

    def begin(self):
        z, levels = self.z, self.levels

        @pl.when(z < levels - 1)
        def _():
            self.along(z, 1, "up").start()

        @pl.when(z > 0)
        def _():
            self.along(z, 1, "down").start()

        self.across(z, "x").start()
        self.across(z, "y").start()

    def line(self, k):
        z, levels = self.z, self.levels

        @pl.when(z >= k)
        def _():
            self.along(z - k, k, "up").wait_recv()

            @pl.when(z < levels - 1)
            def _():
                self.along(z - k, k + 1, "up").start()

            self.across(z - k, "x").start()
            self.across(z - k, "y").start()

        @pl.when(z + k < levels)
        def _():
            self.along(z + k, k, "down").wait_recv()

            @pl.when(z > 0)
            def _():
                self.along(z + k, k + 1, "down").start()

            self.across(z + k, "x").start()
            self.across(z + k, "y").start()

    def turn(self, k):
        z, levels, d = self.z, self.levels, self.d
        by_x, by_y = d + 1 - 2 * (d % 2), (d + 2) % 4

        def one(level):
            self.across(level, "x").wait_recv()
            self.corner(level, "y", by_x).start()
            self.across(level, "y").wait_recv()
            self.corner(level, "x", by_y).start()

        if k == 0:
            one(z)
        else:
            pl.when(z >= k)(lambda: one(z - k))
            pl.when(z + k < levels)(lambda: one(z + k))

    def finish(self, k):
        z, levels, d = self.z, self.levels, self.d
        by_x, by_y = d + 1 - 2 * (d % 2), (d + 2) % 4

        def one(level):
            self.corner(level, "x", by_y).wait_recv()
            self.corner(level, "y", by_x).wait_recv()

        if k == 0:
            one(z)
        else:
            pl.when(z >= k)(lambda: one(z - k))
            pl.when(z + k < levels)(lambda: one(z + k))

    def drain(self):
        z, levels, d = self.z, self.levels, self.d
        by_x, by_y = d + 1 - 2 * (d % 2), (d + 2) % 4
        for level in range(levels):
            self.across(level, "x").wait_send()
            self.across(level, "y").wait_send()
            self.corner(level, "x", by_y).wait_send()
            self.corner(level, "y", by_x).wait_send()
        for k in range(1, levels):

            @pl.when(jnp.logical_and(z >= k - 1, z < levels - 1))
            def _():
                self.along(z - k + 1, k, "up").wait_send()

            @pl.when(jnp.logical_and(z + k - 1 < levels, z > 0))
            def _():
                self.along(z + k - 1, k, "down").wait_send()


def selector(side):
    inner = HEADS * HEAD_DIM
    wide = HALF_HEADS * PAD
    src = lax.broadcasted_iota(jnp.int32, (2 * inner, 2 * wide), 0)
    dst = lax.broadcasted_iota(jnp.int32, (2 * inner, 2 * wide), 1)
    kind, head, feature = dst // wide, (dst // PAD) % HALF_HEADS, dst % PAD
    wanted = kind * inner + (side * HALF_HEADS + head) * HEAD_DIM + feature
    hit = jnp.logical_and(src == wanted, feature < HEAD_DIM)
    return jnp.where(hit, 1.0, 0.0).astype(jnp.bfloat16)


def table_by_offset(w_a, per_device, shard, local_len, spread):
    distance = MEM + local_len - 1 - lax.broadcasted_iota(jnp.int32, (1, spread), 1)
    bucket = bucket_index(distance)
    wanted = (bucket // per_device) * shard + bucket % per_device
    step = 128

    def body(i, total):
        at = pl.ds(pl.multiple_of(i * step, step), step)
        ids = lax.broadcasted_iota(jnp.int32, (step, spread), 0) + i * step
        one_hot = jnp.where(ids == wanted, 1.0, 0.0).astype(jnp.bfloat16)
        return total + dot_f32(w_a[at, MISC:W_A], one_hot, TN)

    return lax.fori_loop(0, w_a.shape[0] // step, body, jnp.zeros((W_MISC, spread), jnp.float32))


NT = (((1,), (1,)), ((), ()))
TN = (((0,), (0,)), ((), ()))


def dot_f32(a, b, dims=(((1,), (0,)), ((), ()))):
    return lax.dot_general(a, b, dims, preferred_element_type=jnp.float32)


def steps_of(text):
    return [(w.split(".")[0], w.split(".")[1][:-1], int(w[-1])) for w in text.split()]


EVENTS = {point: steps_of(text) for point, text in dict(
    f="f.begin0",
    a="a.begin0",
    stats="a.line1",
    packs="",
    given="m.early0 a.turn0 a.line2 a.turn1 a.line3 a.turn2 o.begin0 m.early1 a.turn3 o.line1 m.early2",
    front="o.turn0 o.line2 i.begin0",
    cache="o.turn1 o.line3 i.line1 f.line1 m.early3",
    memory="o.turn2 o.turn3 i.line2 f.line2 m0.late0 i.turn0 i.line3 f.line3 m0.late1 i.turn1 m0.late2",
    half="m1.late0 m1.late1 f.turn0 i.turn2 i.turn3 m1.late2",
    attended="f.turn1",
    far="",
    pair="f.turn2 f.turn3",
    activated="",
).items()}


def forward_kernel(
    levels, batches, local_len, per_device,
    qk_in, value_in, router_in, norm_in, bias_in, branch_in, up_in, f_in, token_in, cot_in, vr_in, or_in, start_in,
    count_in, g_in,
    a_out, o_out, i_out, f_all, xs_out, act_out, front_out, gates_out, win_out, probs_out, att_out,
    mixed_out, hidden_out, n2_out, vec_out, ffn_out, slope_out, fgrad_out,
    a_all, o_all, i_all, xs, graw, win, rbuf, sel, unit, act, front, gates, vec, bias, probs, att, mixed,
    arrived, hidden, n2, ffn, slope,
    qk_raw, value_raw, router_raw, norm_raw, bias_raw, branch_raw, up_raw, vr_raw, or_raw, start_raw, count_raw, f_raw, a_pack, o_pack, i_pack,
    send, recv, csend, crecv, lsem, gsend, grecv, esend, erecv, osem, psem,
):
    bf16, f32 = jnp.bfloat16, jnp.float32
    d, t = lax.axis_index("doc"), lax.axis_index("tm")
    z, c = t // 2, t % 2
    nb = neighbours(2 * levels)
    shard = qk_in.shape[0]
    width = f_in.shape[1]
    rows = batches * local_len
    both = 2 * rows
    wide = HALF_HEADS * PAD
    own = pl.ds(pl.multiple_of(c * shard, 16), shard)

    def local(src, dst, index):
        cp = pltpu.make_async_copy(src, dst, lsem.at[index])
        cp.start()
        return cp

    def sibling(src, dst, index):
        return pltpu.make_async_remote_copy(
            src_ref=src, dst_ref=dst, send_sem=csend.at[index], recv_sem=crecv.at[index],
            device_id=nb["c"], device_id_type=MESH)

    raws = [
        local(src, dst, i)
        for i, (src, dst) in enumerate((
            (qk_in, qk_raw), (value_in, value_raw), (router_in, router_raw), (norm_in, norm_raw), (bias_in, bias_raw),
            (branch_in, branch_raw), (up_in, up_raw), (vr_in, vr_raw), (or_in, or_raw), (start_in, start_raw),
            (count_in, count_raw)))
    ]
    loc_f = local(f_in, f_raw, 11)
    x_parts = ((token_in, pl.ds(0, width)), (cot_in, pl.ds(width, width)))
    loc_x = [local(src, xs.at[c, :, cols], 12 + i) for i, (src, cols) in enumerate(x_parts)]
    enter(nb, z, levels)
    rem_x = [sibling(src, xs.at[c, :, cols], i) for i, (src, cols) in enumerate(x_parts)]
    for cp in rem_x:
        cp.start()
    ga, go, gi, gf = [
        Gather(ref, (send.at[i], recv.at[i]), nb, d, z, levels)
        for i, ref in enumerate((a_all, o_all, i_all, f_all))
    ]

    loc_f.wait()
    own_f = local(f_raw, f_all.at[d, z], 18)
    own_f.wait()
    groups = dict(a=ga, o=go, i=gi, f=gf)
    left = [
        (name, what, k) for name in groups for what, first in (("begin", 0), ("line", 1), ("turn", 0), ("finish", 0))
        for k in range(first, 1 if what == "begin" else levels)]
    left += [("m", "early", k) for k in range(MEM // local_len // 2)]
    left += [("m%d" % batch, "late", k) for batch in range(batches) for k in range(MEM // local_len // 2)]

    def do(name, what, k):
        if (name, what, k) not in left:
            return
        left.remove((name, what, k))
        if what == "early":
            early(k)
            return
        if what == "late":
            late(k, int(name[1:]))
            return
        group = groups[name]
        if what == "begin":
            for cp in placed[name]:
                cp.wait()
            group.begin()
        else:
            dict(line=group.line, turn=group.turn, finish=group.finish)[what](k)

    def run(point):
        for event in EVENTS[point]:
            do(*event)

    def complete(name):
        for event in [e for e in left if e[0] == name]:
            do(*event)

    placed = dict(f=[])
    run("f")

    for cp in raws[:5]:
        cp.wait()
    a_pack[...] = jnp.zeros_like(a_pack)
    norm_columns = norm_raw[...].astype(f32).T
    for side in range(SIDE):
        for h in range(HALF_HEADS):
            at = (side * HALF_HEADS + h) * HEAD_DIM
            for kind in range(2):
                col, src = (kind * HALF_HEADS + h) * PAD, kind * HEADS * HEAD_DIM + at
                a_pack[side, :, col : col + HEAD_DIM] = qk_raw[:, src : src + HEAD_DIM]
            for e in range(EXPERTS):
                col, src = W_QK + (e * HALF_HEADS + h) * PAD, e * HEADS * HEAD_DIM + at
                a_pack[side, :, col : col + HEAD_DIM] = value_raw[:, src : src + HEAD_DIM]
        routes = HALF_HEADS * EXPERTS
        for kind in range(2):
            src = (kind * SIDE + side) * routes
            a_pack[side, :, MISC + kind * routes : MISC + (kind + 1) * routes] = router_raw[:, src : src + routes]
        a_pack[side, :, MISC + COL_NORM : MISC + COL_NORM + 4] = norm_columns.astype(bf16)
        heads = bias_raw[side * HALF_HEADS : (side + 1) * HALF_HEADS].astype(f32).T
        tail = jnp.concatenate([heads, jnp.zeros((shard - per_device, HALF_HEADS), f32)], axis=0)
        a_pack[side, :, MISC + COL_BIAS : MISC + COL_BIAS + HALF_HEADS] = tail.astype(bf16)
    loc_a = local(a_pack.at[c], a_all.at[d, z, own], 17)
    rem_a = sibling(a_pack.at[1 - c], a_all.at[d, z, own], 3)
    rem_a.start()
    for cp in raws[7:]:
        cp.wait()
    row_ids = lax.broadcasted_iota(jnp.int32, (W_MISC, local_len), 0)
    for batch in range(batches):
        flags = [
            jnp.broadcast_to(raw[:, batch : batch + 1].astype(f32), (W_MISC, local_len)) for raw in (start_raw, count_raw)]
        for side in range(SIDE):
            rows_of = jnp.where(row_ids == 40, flags[0], jnp.where(row_ids == 41, flags[1], 0.0))
            for kind, raw in enumerate((vr_raw, or_raw)):
                for h in range(HALF_HEADS):
                    chosen = raw[batch, side * HALF_HEADS + h]
                    first = (kind * HALF_HEADS + h) * EXPERTS
                    expert = row_ids - first
                    hit = expert == chosen[0:1]
                    for k in range(1, TOPK):
                        hit = jnp.logical_or(hit, expert == chosen[k : k + 1])
                    inside = jnp.logical_and(row_ids >= first, row_ids < first + EXPERTS)
                    rows_of = jnp.where(jnp.logical_and(hit, inside), 1.0, rows_of)
            cols = pl.ds(2 * width + side * 128, 128)
            xs[c, pl.ds(batch * local_len, local_len), cols] = rows_of.T.astype(bf16)
    meta_cols = xs.at[c, :, pl.ds(2 * width, SIDE * 128)]
    rem_x.append(sibling(meta_cols, meta_cols, 2))
    rem_x[-1].start()
    loc_g = local(g_in, graw.at[c], 14)
    rem_g = sibling(g_in, graw.at[c], 4)
    rem_g.start()
    placed["a"] = (loc_a, rem_a)
    run("a")
    sel[...] = selector(c)

    for cp in loc_x + rem_x:
        cp.wait()
    step = 64

    def stats(i, carry):
        at = pl.ds(pl.multiple_of((i % (rows // step)) * step, step), step)
        block = i // (rows // step)
        values = xs[block, at, :width].astype(f32)
        centered = values - jnp.mean(values, axis=-1, keepdims=True)
        inverse = lax.rsqrt(jnp.mean(centered * centered, axis=-1, keepdims=True) + EPS)
        unit[pl.ds(pl.multiple_of(i * step, step), step)] = centered * inverse
        counts = xs[block, at, 2 * width : 2 * width + 128][:, 41:42].astype(f32)
        position = lax.broadcasted_iota(jnp.int32, (step, 1), 0) + (i * step) % local_len
        gradient = xs[block, at, width : 2 * width].astype(f32)
        xs[block, at, width : 2 * width] = jnp.where(position.astype(f32) < counts, gradient, 0.0).astype(bf16)
        return carry

    lax.fori_loop(0, both // step, stats, 0)
    run("stats")
    raws[6].wait()
    for side in range(SIDE):
        for p in range(4 * levels):
            src = (p * SIDE + side) * PAD
            i_pack[side, :, p * PAD : (p + 1) * PAD] = up_raw[:, src : src + PAD]
    raws[5].wait()
    o_pack[...] = jnp.zeros_like(o_pack)
    for side in range(SIDE):
        for h in range(HALF_HEADS):
            for e in range(EXPERTS):
                src = e * HEADS * HEAD_DIM + (side * HALF_HEADS + h) * HEAD_DIM
                col = (e * HALF_HEADS + h) * PAD
                o_pack[side, :, col : col + HEAD_DIM] = branch_raw[:, src : src + HEAD_DIM]
    loc_o = local(o_pack.at[c], o_all.at[d, z, own], 15)
    rem_o = sibling(o_pack.at[1 - c], o_all.at[d, z, own], 5)
    loc_i = local(i_pack.at[c], i_all.at[d, z, own], 16)
    rem_i = sibling(i_pack.at[1 - c], i_all.at[d, z, own], 6)
    rem_o.start()
    rem_i.start()
    placed["o"], placed["i"] = (loc_o, rem_o), (loc_i, rem_i)
    run("packs")

    slots = MEM // local_len
    has_up, has_down = z < levels - 1, z > 0

    def slot(s):
        return pl.ds(s * local_len, local_len)

    def starts_of(block, batch):
        column = xs[block, pl.ds(batch * local_len, local_len), 2 * width : 2 * width + 128]
        return column[:, 40:41].astype(f32)

    def spread_given(i, carry):
        at = pl.ds(pl.multiple_of((i % slots) * local_len, local_len), local_len)
        pair = i // slots
        mine = dot_f32(graw[pair // batches, pair % batches, at], sel[...])
        win[pair, at] = mine.astype(bf16)
        return carry

    def keep_or(block, batch, s, moved):
        at = block * batches + batch
        held = win[at, slot(s)]
        first = jnp.broadcast_to(starts_of(block, batch), held.shape) > 0.5
        win[at, slot(s)] = jnp.where(first, held.astype(f32), moved.astype(f32)).astype(bf16)

    def message(m, batch):
        src = win.at[batches + batch, pl.ds((slots - 1 - 2 * m) * local_len, 2 * local_len)]
        return pltpu.make_async_remote_copy(
            src_ref=src, dst_ref=rbuf.at[m, batch], send_sem=gsend.at[m, batch], recv_sem=grecv.at[m, batch],
            device_id=nb["up"], device_id_type=MESH)

    rounds = slots // 2

    def send_message(m, batch):
        if m < rounds:
            pl.when(has_up)(lambda: message(m, batch).start())

    def take(m, some):
        for batch in some:
            pl.when(has_down)(lambda: message(m, batch).wait_recv())
            for k in (0, 1):
                keep_or(0, batch, slots - 1 - 2 * m - k, rbuf[m, batch, slot(1 - k)])
            for s in (slots - 2 - 2 * m, slots - 3 - 2 * m):
                if s >= 0:
                    keep_or(1, batch, s, win[batch, slot(s + 1)])
            send_message(m + 1, batch)

    def early(m):
        pl.when(z <= m)(lambda: take(m, range(batches)))

    def late(m, batch):
        pl.when(z > m)(lambda: take(m, (batch,)))

    loc_g.wait()
    rem_g.wait()
    lax.fori_loop(0, 2 * batches * slots, spread_given, 0)
    run("given")
    complete("a")
    out_a = pltpu.make_async_copy(a_all, a_out, osem.at[0])
    out_a.start()

    w_a = a_all.reshape(4 * levels * 2 * shard, W_A)
    vec[...] = w_a[:, MISC:W_A].astype(f32).T

    def norm(i, carry):
        at = pl.ds(pl.multiple_of(i * step, step), step)
        act[at] = (unit[at] * vec[COL_NORM : COL_NORM + 1] + vec[COL_NORM + 1 : COL_NORM + 2]).astype(bf16)
        return carry

    lax.fori_loop(0, both // step, norm, 0)

    def project(i, carry):
        at = pl.ds(pl.multiple_of(i * 256, 256), 256)
        front[:, at] = dot_f32(act[...], w_a[:, at])
        return carry

    lax.fori_loop(0, MISC // 256, project, 0)
    front[:, MISC:W_A] = dot_f32(act[...], w_a[:, MISC:W_A])
    run("front")
    meta_at = pl.ds(pl.multiple_of(2 * width + c * 128, 128), 128)

    def gate(i, carry):
        at = pl.ds(pl.multiple_of(i * local_len, local_len), local_len)
        gated = jax.nn.sigmoid(front[at, MISC:W_A])
        gates[at] = gated
        picks = xs[i // batches, pl.ds(pl.multiple_of((i % batches) * local_len, local_len), local_len), meta_at]
        gated = gated * picks.astype(f32)
        for h in range(HALF_HEADS):
            total = jnp.zeros((local_len, PAD), f32)
            for e in range(EXPERTS):
                lane = h * EXPERTS + e
                col = W_QK + (e * HALF_HEADS + h) * PAD
                total = total + gated[:, lane : lane + 1] * front[at, col : col + PAD]
            win[i, pl.ds(MEM, local_len), wide + h * PAD : wide + (h + 1) * PAD] = total.astype(bf16)
        win[i, pl.ds(MEM, local_len), :wide] = front[at, wide : 2 * wide].astype(bf16)
        return carry

    lax.fori_loop(0, 2 * batches, gate, 0)

    for batch in range(batches):
        keep_or(1, batch, slots - 1, win[batch, pl.ds(MEM, local_len)])
        send_message(0, batch)
    run("cache")

    spread = MEM + 2 * local_len
    table = table_by_offset(w_a, per_device, shard, local_len, spread)
    for h in range(HALF_HEADS):
        line = jnp.broadcast_to(table[COL_BIAS + h : COL_BIAS + h + 1], (local_len, spread))
        turned = pltpu.roll(line, spread - local_len + 1, 1, stride=1, stride_axis=0)
        bias[h] = turned[:, : MEM + local_len]
    run("memory")
    complete("m")
    complete("m0")

    key_ids = lax.broadcasted_iota(jnp.int32, (local_len, local_len), 1)
    row_ids = lax.broadcasted_iota(jnp.int32, (local_len, local_len), 0)

    def probs_copy(i, slot_of):
        return pltpu.make_async_copy(probs.at[slot_of], probs_out.at[i], psem.at[slot_of])

    def pair_of(n):
        return (n % 2) * batches + n // 2

    def attend(n, carry):
        i = pair_of(n)
        at = pl.ds(pl.multiple_of(i * local_len, local_len), local_len)
        block, batch = i // batches, i % batches
        rows_at = pl.ds(pl.multiple_of(batch * local_len, local_len), local_len)
        count = xs[block, rows_at, 2 * width : 2 * width + 128][:, 41:42].astype(f32)
        seen = jnp.logical_and(key_ids <= row_ids, key_ids.astype(f32) < count)
        picks = xs[block, rows_at, meta_at].astype(f32) * gates[at]
        slot_of = lax.rem(n, 2)
        pl.when(n >= 2)(lambda: probs_copy(pair_of(n - 2), slot_of).wait())
        for h in range(HALF_HEADS):
            cols = slice(h * PAD, (h + 1) * PAD)
            q = front[at, cols].astype(bf16)
            s = dot_f32(q, win[i, :, cols], NT) * SCALE + bias[h]
            s = jnp.concatenate([s[:, :MEM], jnp.where(seen, s[:, MEM:], NEG)], axis=1)
            top = jnp.max(s, axis=-1, keepdims=True)
            expo = jnp.exp(s - top)
            p = expo * (1.0 / jnp.sum(expo, axis=-1, keepdims=True))
            probs[slot_of, h] = p
            p = p.astype(bf16)
            got = dot_f32(p, win[i, :, wide + h * PAD : wide + (h + 1) * PAD]).astype(bf16)
            att[at, cols] = got
            got = got.astype(f32)
            for e in range(EXPERTS):
                lane = HALF_HEADS * EXPERTS + h * EXPERTS + e
                col = (e * HALF_HEADS + h) * PAD
                mixed[at, col : col + PAD] = (picks[:, lane : lane + 1] * got).astype(bf16)
        probs_copy(i, slot_of).start()
        return carry

    lax.fori_loop(0, 2, attend, 0)
    run("half")
    for batch in range(1, batches):
        complete("m%d" % batch)
    out_w = pltpu.make_async_copy(win, win_out, osem.at[1])
    out_w.start()
    lax.fori_loop(2, 2 * batches, attend, 0)
    for n in range(2 * batches - 2, 2 * batches):
        probs_copy(pair_of(n), n % 2).wait()
    run("attended")
    complete("o")

    w_o = o_all.reshape(4 * levels * 2 * shard, W_O)
    branch = unit
    far = pl.ds(pl.multiple_of((1 - c) * rows, rows), rows)
    near = pl.ds(pl.multiple_of(c * rows, rows), rows)

    def out_project(at):
        def body(i, carry):
            cols = pl.ds(pl.multiple_of(i * 256, 256), 256)
            branch[at, cols] = dot_f32(mixed[at], w_o[cols], NT)
            return carry

        lax.fori_loop(0, width // 256, body, 0)

    def exchange(src, dst, index):
        return pltpu.make_async_remote_copy(
            src_ref=src, dst_ref=dst, send_sem=esend.at[index], recv_sem=erecv.at[index],
            device_id=nb["c"], device_id_type=MESH)

    out_project(far)
    give = exchange(branch.at[far], arrived, 0)
    give.start()
    run("far")
    out_project(near)
    out_o = pltpu.make_async_copy(o_all, o_out, osem.at[2])
    out_o.start()
    give.wait_recv()

    def second(i, carry):
        at = pl.ds(pl.multiple_of(i * step, step), step)
        total_at = pl.ds(pl.multiple_of(c * rows + i * step, step), step)
        values = xs[c, at, :width].astype(f32) + branch[total_at] + arrived[at]
        hidden[at] = values
        centered = values - jnp.mean(values, axis=-1, keepdims=True)
        inverse = lax.rsqrt(jnp.mean(centered * centered, axis=-1, keepdims=True) + EPS)
        normed = centered * inverse * vec[COL_NORM + 2 : COL_NORM + 3] + vec[COL_NORM + 3 : COL_NORM + 4]
        n2[total_at] = normed.astype(bf16)
        return carry

    lax.fori_loop(0, rows // step, second, 0)
    pair = exchange(n2.at[near], n2.at[near], 1)
    pair.start()
    run("pair")
    pair.wait_recv()
    outs = [
        pltpu.make_async_copy(src, dst, osem.at[3 + i])
        for i, (src, dst) in enumerate((
            (xs, xs_out), (act, act_out), (front, front_out), (gates, gates_out),
            (att, att_out), (mixed, mixed_out), (hidden, hidden_out), (n2, n2_out), (vec, vec_out)))
    ]
    for cp in outs:
        cp.start()
    complete("i")
    out_i = pltpu.make_async_copy(i_all, i_out, osem.at[13])
    out_i.start()

    w_i = i_all.reshape(4 * levels * 2 * shard, i_all.shape[3])

    def activate(i, carry):
        at = pl.ds(pl.multiple_of(i * 256, 256), 256)
        pre = dot_f32(n2[...], w_i[:, at])
        below = 0.5 * (1.0 + lax.erf(pre * 0.7071067811865476))
        ffn[:, at] = (pre * below).astype(bf16)
        slope[:, at] = (below + pre * jnp.exp(-0.5 * pre * pre) * 0.3989422804014327).astype(bf16)
        return carry

    steps = ffn.shape[1] // 256
    lax.fori_loop(0, steps, activate, 0)
    run("activated")
    outs += [pltpu.make_async_copy(ffn, ffn_out, osem.at[14]), pltpu.make_async_copy(slope, slope_out, osem.at[15])]
    outs[-2].start()
    outs[-1].start()

    for m in range(rounds):
        for batch in range(batches):
            pl.when(has_up)(lambda: message(m, batch).wait_send())
    out_w.wait()
    span = ffn.shape[1] // 4
    half = width // 2

    def ffn_grad(i, carry):
        at = pl.ds(pl.multiple_of(i * span, span), span)
        for side in range(2):
            cols = slice(width + side * half, width + (side + 1) * half)
            left = jnp.concatenate([xs[0, :, cols], xs[1, :, cols]], axis=0)
            win[i, side * span : (side + 1) * span] = dot_f32(ffn[:, at], left, TN).astype(bf16)
        return carry

    lax.fori_loop(0, 4, ffn_grad, 0)
    for column in range(4):
        for side in range(2):
            outs.append(pltpu.make_async_copy(
                win.at[column, pl.ds(side * span, span)],
                fgrad_out.at[column, :, pl.ds(side * half, half)], osem.at[16 + 2 * column + side]))
            outs[-1].start()
    complete("f")
    for group in (ga, go, gi, gf):
        group.drain()
    for cp in (give, pair):
        cp.wait_send()
    out_a.wait()
    out_o.wait()
    out_i.wait()
    for cp in outs:
        cp.wait()


def forward(levels, batches, local_len, per_device, ins):
    bf16, f32 = jnp.bfloat16, jnp.float32
    shape = jax.ShapeDtypeStruct
    qk, value, router, norms, bias_in, branch, up, f, tokens, cot, vr, outr, start, count, g = ins
    shard, width = qk.shape[0], f.shape[1]
    a, o, i = [shape((SIDE, shard, w), bf16) for w in (W_A, W_O, up.shape[1] // SIDE)]
    x = shape((tokens.shape[0], 2 * width + SIDE * 128), bf16)
    rows = batches * local_len
    both = 2 * rows
    wide = HALF_HEADS * PAD
    two = lambda v: (4, levels, 2 * v.shape[1], v.shape[2])
    window = (2 * batches, MEM + local_len, 2 * wide)
    probs = (2 * batches, HALF_HEADS, local_len, MEM + local_len)
    outs = [
        (two(a), bf16), (two(o), bf16), (two(i), bf16), ((4, levels) + f.shape, bf16),
        ((2,) + x.shape, bf16), ((both, width), bf16), ((both, W_A), f32), ((both, W_MISC), f32),
        (window, bf16), (probs, f32), ((both, wide), bf16), ((both, W_O), bf16),
        ((rows, width), f32), ((both, width), bf16), ((W_MISC, width), f32), ((both, i.shape[2]), bf16),
        ((both, i.shape[2]), bf16), ((4, i.shape[2] // 4, width), bf16),
    ]
    rounds = MEM // local_len // 2
    scratch = [
        (two(a), bf16), (two(o), bf16), (two(i), bf16), ((2,) + x.shape, bf16), ((2,) + g.shape, bf16),
        (window, bf16), ((rounds, batches, 2 * local_len, 2 * wide), bf16), ((g.shape[2], 2 * wide), bf16),
        ((both, width), f32), ((both, width), bf16), ((both, W_A), f32), ((both, W_MISC), f32),
        ((W_MISC, width), f32), ((HALF_HEADS, local_len, MEM + local_len), f32), ((2,) + probs[1:], f32),
        ((both, wide), bf16), ((both, W_O), bf16), ((rows, width), f32),
        ((rows, width), f32), ((both, width), bf16), ((both, i.shape[2]), bf16), ((both, i.shape[2]), bf16),
    ]
    rounds = MEM // local_len // 2
    scratch += [(w.shape, w.dtype) for w in (qk, value, router, norms, bias_in, branch, up, vr, outr, start, count, f, a, o, i)]
    sems = [(4, 6 * levels), (4, 6 * levels), (7,), (7,), (19,), (rounds, batches), (rounds, batches), (2,), (2,), (24,), (2,)]
    hbm = pl.BlockSpec(memory_space=pl.ANY)
    return pl.pallas_call(
        functools.partial(forward_kernel, levels, batches, local_len, per_device),
        out_shape=[jax.ShapeDtypeStruct(s, k) for s, k in outs],
        in_specs=[hbm] * len(ins),
        out_specs=[hbm] * len(outs),
        scratch_shapes=[pltpu.VMEM(s, k) for s, k in scratch] + [pltpu.SemaphoreType.DMA(s) for s in sems],
        compiler_params=pltpu.CompilerParams(
            collective_id=1, has_side_effects=True, vmem_limit_bytes=VMEM_BYTES),
    )(*ins)


def add_rows(dst, terms):
    rows, width = dst.shape
    step = 16

    def body(i, carry):
        at = pl.ds(pl.multiple_of(i * step, step), step)
        total = terms[0][at].astype(jnp.float32)
        for term in terms[1:]:
            total = total + term[at].astype(jnp.float32)
        dst[at] = total.astype(dst.dtype)
        return carry

    lax.fori_loop(0, rows // step, body, 0)


class Scatter:
    def __init__(self, src, view, sems, nb, d, z, levels, total):
        self.src, self.view, self.nb, self.d, self.z, self.levels = src, view, nb, d, z, levels
        self.send, self.recv = sems
        self.sum = total
        self.half = src.shape[2] // 2
        self.by_x, self.by_y = d + 1 - 2 * (d % 2), (d + 2) % 4
        self.low, self.high = pl.ds(0, self.half), pl.ds(self.half, self.half)

    def copy(self, src, dst, slot, to):
        return pltpu.make_async_remote_copy(
            src_ref=src, dst_ref=dst, send_sem=self.send.at[slot], recv_sem=self.recv.at[slot],
            device_id=self.nb[to], device_id_type=MESH)

    def corner(self, j, to):
        part, name, base = (self.low, "cx", 0) if to == "x" else (self.high, "cy", self.levels)
        return self.copy(self.src.at[3 - self.d, j, part], self.view(name, j), base + j, to)

    def direct(self, j, to):
        if to == "x":
            column, part, name, base = self.by_x, self.low, "rx", 2 * self.levels
        else:
            column, part, name, base = self.by_y, self.high, "ry", 3 * self.levels
        return self.copy(self.src.at[column, j, part], self.view(name, j).at[part], base + j, to)

    def relay(self, j, to):
        if to == "x":
            held, part, name, base = "cy", self.high, "rx", 4 * self.levels
        else:
            held, part, name, base = "cx", self.low, "ry", 5 * self.levels
        return self.copy(self.view(held, j), self.view(name, j).at[part], base + j, to)

    def along(self, j, to, first=False):
        base = (6 if to == "up" else 7) * self.levels
        there = self.view(to, j, self.z + (1 if to == "up" else -1))
        return self.copy(self.view("rx" if first else to, j), there, base + j, to)

    def issue(self, j):
        self.corner(j, "x").start()
        self.corner(j, "y").start()
        self.direct(j, "x").start()
        self.direct(j, "y").start()

    def turn(self, j):
        self.corner(j, "x").wait_recv()
        add_rows(self.view("cx", j), [self.view("cx", j), self.src.at[self.by_y, j, self.low]])
        self.relay(j, "y").start()
        self.corner(j, "y").wait_recv()
        add_rows(self.view("cy", j), [self.view("cy", j), self.src.at[self.by_x, j, self.high]])
        self.relay(j, "x").start()

    def column(self, j):
        for to in ("x", "y"):
            self.direct(j, to).wait_recv()
            self.relay(j, to).wait_recv()
        add_rows(self.view("rx", j), [self.view("rx", j), self.view("ry", j), self.src.at[self.d, j]])

    def lift(self, j, stage):
        def hop(to):
            if stage:
                self.along(j, to).wait_recv()
                add_rows(self.view(to, j), [self.view(to, j), self.view("rx", j)])
            self.along(j, to, first=stage == 0).start()

        if stage < j:
            pl.when(self.z == stage)(lambda: hop("up"))
        if self.levels - 1 - stage > j:
            pl.when(self.z == self.levels - 1 - stage)(lambda: hop("down"))

    def total(self, j):
        @pl.when(self.z == j)
        def _():
            terms = [self.view("rx", j)]
            for to, there in (("up", j > 0), ("down", j < self.levels - 1)):
                if there:
                    self.along(j, to).wait_recv()
                    terms.append(self.view(to, j))
            add_rows(self.sum, terms)

    def drain(self):
        for j in range(self.levels):
            for to in ("x", "y"):
                self.corner(j, to).wait_send()
                self.direct(j, to).wait_send()
                self.relay(j, to).wait_send()
            pl.when(self.z < j)(lambda: self.along(j, "up").wait_send())
            pl.when(self.z > j)(lambda: self.along(j, "down").wait_send())


class LineFirst:
    def __init__(self, src, view, bufs, sems, nb, d, z, levels, total):
        self.src, self.view, self.nb, self.d, self.z, self.levels = src, view, nb, d, z, levels
        self.cx, self.cy, self.rx, self.ry = bufs
        self.send, self.recv = sems
        self.sum = total
        half = src.shape[2] // 2
        self.by_x, self.by_y = d + 1 - 2 * (d % 2), (d + 2) % 4
        self.low, self.high = pl.ds(0, half), pl.ds(half, half)

    def copy(self, src, dst, slot, to):
        return pltpu.make_async_remote_copy(
            src_ref=src, dst_ref=dst, send_sem=self.send.at[slot], recv_sem=self.recv.at[slot],
            device_id=self.nb[to], device_id_type=MESH)

    def along(self, j, column, to, level, first=False):
        slot = (0 if to == "up" else 4 * self.levels) + 4 * j + column
        after = level + (1 if to == "up" else -1)
        src = self.src.at[column, j] if first else self.view(j, column)
        return self.copy(src, self.view(self.levels if to == "down" and after == j else j, column), slot, to)

    def lift(self, j, stage):
        def hop(to, level):
            for column in range(4):
                if stage:
                    before = level - (1 if to == "up" else -1)
                    self.along(j, column, to, before).wait_recv()
                    held = self.view(j, column)
                    add_rows(held, [held, self.src.at[column, j]])
                self.along(j, column, to, level, first=stage == 0).start()

        if stage < j:
            pl.when(self.z == stage)(lambda: hop("up", stage))
        if self.levels - 1 - stage > j:
            pl.when(self.z == self.levels - 1 - stage)(lambda: hop("down", self.levels - 1 - stage))

    def gathered(self, j):
        @pl.when(self.z == j)
        def _():
            for column in range(4):
                terms = [self.src.at[column, j]]
                if j > 0:
                    self.along(j, column, "up", j - 1).wait_recv()
                    terms.append(self.view(j, column))
                if j < self.levels - 1:
                    self.along(j, column, "down", j + 1).wait_recv()
                    terms.append(self.view(self.levels, column))
                add_rows(terms[0], terms)

    def plane(self, k):
        base = 8 * self.levels
        part = lambda column, rows: self.src.at[column, self.z, rows]
        return (
            self.copy(part(3 - self.d, self.low), self.cx, base, "x"),
            self.copy(part(3 - self.d, self.high), self.cy, base + 1, "y"),
            self.copy(part(self.by_x, self.low), self.rx.at[self.low], base + 2, "x"),
            self.copy(part(self.by_y, self.high), self.ry.at[self.high], base + 3, "y"),
            self.copy(self.cy, self.rx.at[self.high], base + 4, "x"),
            self.copy(self.cx, self.ry.at[self.low], base + 5, "y"),
        )[k]

    def issue(self):
        for k in range(4):
            self.plane(k).start()

    def turn(self):
        self.plane(0).wait_recv()
        add_rows(self.cx, [self.cx, self.src.at[self.by_y, self.z, self.low]])
        self.plane(5).start()
        self.plane(1).wait_recv()
        add_rows(self.cy, [self.cy, self.src.at[self.by_x, self.z, self.high]])
        self.plane(4).start()

    def column(self):
        for k in range(2, 6):
            self.plane(k).wait_recv()
        add_rows(self.sum, [self.rx, self.ry, self.src.at[self.d, self.z]])

    def drain(self):
        for k in range(6):
            self.plane(k).wait_send()
        for j in range(self.levels):
            for column in range(4):
                for level in range(self.levels):
                    if level < j:
                        pl.when(self.z == level)(lambda: self.along(j, column, "up", level).wait_send())
                    if level > j:
                        pl.when(self.z == level)(lambda: self.along(j, column, "down", level).wait_send())


M_UNIT = 13
A_PARTS = (768, 640, 384)
AHEAD = 3


def LAGS(count):
    return [2] + [4 + 3 * k for k in range(count - 1)]


class Pipeline:
    def __init__(self, units, levels, ahead, lags):
        self.units, self.levels, self.ahead, self.now = units, levels, ahead, 0
        self.follow = [lambda s, j: s.column(j)]
        for stage in range(levels - 1):
            self.follow.append(lambda s, j, stage=stage: s.lift(j, stage))
        self.follow.append(lambda s, j: s.total(j))
        self.lags = lags(len(self.follow))
        self.done = [0] * len(units)

    def each(self, n, act):
        if 0 <= n < len(self.units):
            for scatter, j in self.units[n]:
                act(scatter, j)

    def begin(self):
        for n in range(self.ahead):
            self.each(n, lambda s, j: s.issue(j))

    def advance(self, n):
        self.each(n, self.follow[self.done[n]])
        self.done[n] += 1

    def step(self):
        n = self.now
        if n < len(self.units):
            self.each(n, lambda s, j: s.turn(j))
            self.each(n + self.ahead, lambda s, j: s.issue(j))
        for m in range(min(n + 1, len(self.units))):
            while self.done[m] < len(self.lags) and n - m >= self.lags[self.done[m]]:
                self.advance(m)
        self.now += 1

    def turns(self):
        while self.now < len(self.units):
            self.step()

    def round(self):
        for m in range(len(self.units)):
            if self.done[m] < len(self.follow):
                self.advance(m)

    def finish(self):
        while min(self.done) < len(self.follow):
            self.round()


def norm_rows(values):
    centered = values - jnp.mean(values, axis=-1, keepdims=True)
    inverse = lax.rsqrt(jnp.mean(centered * centered, axis=-1, keepdims=True) + EPS)
    return centered * inverse, inverse


def norm_rows_backward(upstream, normed, inverse, gain):
    scaled = upstream * gain
    inside = (
        scaled
        - jnp.mean(scaled, axis=-1, keepdims=True)
        - normed * jnp.mean(scaled * normed, axis=-1, keepdims=True)
    )
    return inside * inverse


VEC_ROW = COL_NORM // 8 * 8
VEC_GAIN = COL_NORM - VEC_ROW


def backward_kernel(
    levels, batches, local_len, per_device, shard,
    fgrad_in, wf_in, wi_in, wo_in, wa_in, ffn_in, slope_in, xs_in, n2_in, hidden_in, vec_in, att_in, gates_in, front_in,
    win_in, probs_in, mixed_in, act_in,
    f_out, i_out, o_out, a_out, m_out, layer_out, grad_out,
    w_f, w_i, ffn, slope, grad, meta, n2, hidden, vec, att, gates, front, win, probs,
    branch, arrived, dhid, db, dmix, dfront, dsum, norms,
    f_total, i_total, o_total, a_total, m_total, *rest,
):
    bf16, f32 = jnp.bfloat16, jnp.float32
    f_bufs, i_bufs, m_bufs = rest[:6], rest[6:12], rest[12:18]
    a_src, a_cx, a_cy, o_src, o_line, o_cx, o_cy, o_rx, o_ry = rest[18:27]
    send, recv, osend, orecv, lsem, tsem, esend, erecv, osem, ready, freed = rest[27:]
    d, t = lax.axis_index("doc"), lax.axis_index("tm")
    z, c = t // 2, t % 2
    nb = neighbours(2 * levels)
    width = w_f.shape[1]
    rows = batches * local_len
    both = 2 * rows
    wide = HALF_HEADS * PAD
    ff = ffn.shape[1]
    far = pl.ds(pl.multiple_of((1 - c) * rows, rows), rows)
    near = pl.ds(pl.multiple_of(c * rows, rows), rows)

    def load(src, dst, index):
        cp = pltpu.make_async_copy(src, dst, lsem.at[index])
        cp.start()
        return cp

    meta_at = pl.ds(pl.multiple_of(2 * width + c * 128, 128), 128)
    l_first = load(fgrad_in, f_bufs[0], 17)
    l_grad = load(xs_in.at[:, :, pl.ds(width, width)], grad, 1)
    l_wf = load(wf_in, w_f, 2)
    enter(nb, z, levels)
    l_first.wait()
    l_slope = load(slope_in, slope, 3)
    l_ffn = load(ffn_in, ffn, 0)
    l_n2 = load(n2_in, n2, 4)
    l_wi = load(wi_in, w_i, 5)
    l_hid = load(hidden_in, hidden, 6)
    l_vec = load(vec_in.at[pl.ds(VEC_ROW, 8)], vec, 7)
    l_mixed = load(mixed_in, dmix, 8)
    l_meta = load(xs_in.at[:, :, meta_at], meta, 9)
    l_att = load(att_in, att, 10)
    l_gates = load(gates_in, gates, 11)
    w_o = a_src.at[:, :, :, pl.ds(0, W_O)]
    l_wo = load(wo_in, w_o, 12)

    def tiles(i):
        at = pl.ds(i * local_len, local_len)
        return [
            pltpu.make_async_copy(win_in.at[i], win.at[i % 2], tsem.at[0, i % 2]),
            pltpu.make_async_copy(front_in.at[at, pl.ds(0, wide)], front.at[i % 2, :, pl.ds(0, wide)], tsem.at[2, i % 2]),
            pltpu.make_async_copy(
                front_in.at[at, pl.ds(W_QK, W_VAL)], front.at[i % 2, :, pl.ds(wide, W_VAL)], tsem.at[3, i % 2]),
        ]

    def probs_tile(n):
        return pltpu.make_async_copy(probs_in.at[n // HALF_HEADS, n % HALF_HEADS], probs.at[n % 2], tsem.at[1, n % 2])

    for cp in tiles(0):
        cp.start()
    probs_tile(0).start()

    names = ("cx", "cy", "rx", "ry")

    def plain(bufs):
        def view(name, j, level=z):
            if name == "up":
                return bufs[5].at[j]
            if name == "down":
                return bufs[5].at[jnp.where(level == j, levels, j)]
            return bufs[1 + names.index(name)].at[j]

        return view

    block_rows = shard * SIDE

    def within(held, cx, cy, cols):
        def view(name, j, level=z):
            if name in ("cx", "cy"):
                return (cx if name == "cx" else cy).at[j, :, cols]
            ref, base = held[name]
            return ref.at[pl.ds(base + j * block_rows, block_rows), cols]

        return view

    span = levels * block_rows
    a_held = dict(rx=(w_i, 0), ry=(w_i, span), up=(w_i, 2 * span), down=(w_i, 3 * span))
    a_cols = [pl.ds(sum(A_PARTS[:k]), A_PARTS[k]) for k in range(len(A_PARTS))]
    sums = [
        Scatter(src, view, (send.at[i], recv.at[i]), nb, d, z, levels, total)
        for i, (src, view, total) in enumerate((
            (f_bufs[0], plain(f_bufs), f_total), (i_bufs[0], plain(i_bufs), i_total),
            (m_bufs[0], plain(m_bufs), m_total)) + tuple(
                (a_src.at[:, :, :, cols], within(a_held, a_cx, a_cy, cols), a_total.at[:, cols]) for cols in a_cols))
    ]
    sf, si, sm = sums[:3]
    held = []
    for ref in (ffn, slope):
        for base in range(0, ref.shape[0], 4 * block_rows):
            held.append((ref, base))
    held = held[:levels] + [(o_line, 0)]

    def o_view(slot, column):
        ref, base = held[slot]
        return ref.at[pl.ds(base + column * block_rows, block_rows), pl.ds(0, W_O)]

    so = LineFirst(o_src, o_view, (o_cx, o_cy, o_rx, o_ry), (osend, orecv), nb, d, z, levels, o_total)
    order = []
    for k in range((levels + 1) // 2):
        order += [levels - 1 - k, k] if levels - 1 - k != k else [k]
    units = [[(s, j)] for s in [sf, si] + sums[3:] for j in order]
    units[M_UNIT] = units[M_UNIT] + [(sm, j) for j in order]
    line = Pipeline(units, levels, AHEAD, LAGS)

    def exchange(src, dst, index):
        return pltpu.make_async_remote_copy(
            src_ref=src, dst_ref=dst, send_sem=esend.at[index], recv_sem=erecv.at[index],
            device_id=nb["c"], device_id_type=MESH)

    def weight_grad(dst, left, right, chunk, total, column):
        at = pl.ds(pl.multiple_of(column * span, span), span)

        def body(i, carry):
            cols = pl.ds(pl.multiple_of(i * chunk, chunk), chunk)
            got = dot_f32(left[:, at], right[:, cols], TN).astype(bf16)
            dst[column, :, :, cols] = got.reshape(levels, block_rows, chunk)
            return carry

        lax.fori_loop(0, total // chunk, body, 0)

    line.begin()

    l_wf.wait()
    l_slope.wait()
    l_grad.wait()
    g_all = grad.reshape(both, width)

    def back(i, carry):
        at = pl.ds(pl.multiple_of(i * 256, 256), 256)
        slope[:, at] = (dot_f32(g_all[...], w_f[at], NT) * slope[:, at].astype(f32)).astype(bf16)
        return carry

    lax.fori_loop(0, ff // 256, back, 0)
    l_n2.wait()
    for column in range(4):
        weight_grad(i_bufs[0], n2, slope, 512, ff, column)
    line.step()

    l_wi.wait()

    def times(src, weights, dims):
        def run(at):
            def body(i, carry):
                cols = pl.ds(pl.multiple_of(i * 256, 256), 256)
                branch[at, cols] = dot_f32(src[at], weights(cols), dims)
                return carry

            lax.fori_loop(0, width // 256, body, 0)

        return run

    through_in = times(slope, lambda cols: w_i[cols], NT)
    through_in(far)
    give = exchange(branch.at[far], arrived, 0)
    give.start()
    through_in(near)
    line.step()
    l_hid.wait()
    l_vec.wait()
    give.wait()
    norms[...] = jnp.zeros_like(norms)
    step = 64

    def second(i, carry):
        at = pl.ds(pl.multiple_of(i * step, step), step)
        total_at = pl.ds(pl.multiple_of(c * rows + i * step, step), step)
        normed, inverse = norm_rows(hidden[at])
        up = branch[total_at] + arrived[at]
        norms[COL_NORM + 2 : COL_NORM + 3] += jnp.sum(up * normed, axis=0, keepdims=True)
        norms[COL_NORM + 3 : COL_NORM + 4] += jnp.sum(up, axis=0, keepdims=True)
        got = norm_rows_backward(up, normed, inverse, vec[VEC_GAIN + 2 : VEC_GAIN + 3])
        got = got + grad[c, at].astype(f32)
        dhid[at] = got
        db[total_at] = got.astype(bf16)
        return carry

    lax.fori_loop(0, rows // step, second, 0)
    pair = exchange(db.at[near], db.at[near], 1)
    pair.start()
    l_act = load(act_in, grad, 13)

    through_out = times(ffn, lambda cols: w_f[:, cols], (((1,), (0,)), ((), ())))
    l_ffn.wait()
    through_out(far)
    pair.wait()
    last = exchange(branch.at[far], arrived, 2)
    last.start()
    line.step()
    through_out(near)

    for name in ("x", "y"):
        pl.semaphore_signal(ready, inc=1, device_id=nb[name], device_id_type=MESH)
    for name, there in (("up", z < levels - 1), ("down", z > 0)):

        @pl.when(there)
        def _():
            pl.semaphore_signal(ready, inc=1, device_id=nb[name], device_id_type=MESH)

    l_wa = [
        load(wa_in.at[:, pl.ds(0, width)], w_f.at[pl.ds(0, width)], 14),
        load(wa_in.at[:, pl.ds(width, W_A - width)], w_f.at[pl.ds(width, width), pl.ds(0, W_A - width)], 15),
    ]
    l_mixed.wait()
    for column in range(4):
        weight_grad(o_src, db, dmix, 640, W_O, column)
    ends = jnp.where(z < levels - 1, 1, 0) + jnp.where(z > 0, 1, 0)
    pl.semaphore_wait(ready, 2 + ends)
    for j in order:
        so.lift(j, 0)
    l_wo.wait()

    def mix(i, carry):
        cols = pl.ds(pl.multiple_of(i * wide, wide), wide)
        dmix[:, cols] = dot_f32(db[...], a_src[:, :, :, cols].reshape(width, wide)).astype(bf16)
        return carry

    lax.fori_loop(0, EXPERTS, mix, 0)
    l_meta.wait()
    l_att.wait()
    l_gates.wait()
    dsum[...] = jnp.zeros_like(dsum)
    lanes = lax.broadcasted_iota(jnp.int32, (local_len, W_MISC), 1)

    def attend(i):
        slot = i % 2
        if i + 1 < 2 * batches:
            for cp in tiles(i + 1):
                cp.start()
        for cp in tiles(i):
            cp.wait()
        at = pl.ds(i * local_len, local_len)
        block, batch = i // batches, i % batches
        gate = gates[at]
        picks = meta[block, pl.ds(batch * local_len, local_len)].astype(f32)
        gated = gate * picks
        d_gates = jnp.zeros((local_len, W_MISC), f32)
        for h in range(HALF_HEADS):
            cols = slice(h * PAD, (h + 1) * PAD)
            v_cols = slice(wide + h * PAD, wide + (h + 1) * PAD)
            got = att[at, cols].astype(f32)
            d_att = jnp.zeros((local_len, PAD), f32)
            for e in range(EXPERTS):
                lane = HALF_HEADS * EXPERTS + h * EXPERTS + e
                col = (e * HALF_HEADS + h) * PAD
                part = dmix[at, col : col + PAD].astype(f32)
                d_att = d_att + gated[:, lane : lane + 1] * part
                d_gates = jnp.where(lanes == lane, jnp.sum(part * got, axis=-1, keepdims=True), d_gates)
            d_att = d_att.astype(bf16)
            n = i * HALF_HEADS + h
            if n + 1 < 2 * batches * HALF_HEADS:
                probs_tile(n + 1).start()
            probs_tile(n).wait()
            p = probs[n % 2]
            d_p = dot_f32(d_att, win[slot, :, v_cols], NT)
            delta = jnp.sum(d_p * p, axis=-1, keepdims=True)
            d_s = p * (d_p - delta)
            dsum[h] += d_s
            d_s = d_s.astype(bf16)
            q = front[slot, :, cols].astype(bf16)
            d_q = dot_f32(d_s, win[slot, :, cols]) * SCALE
            d_k = dot_f32(d_s[:, MEM:], q, TN) * SCALE
            d_v = dot_f32(p[:, MEM:].astype(bf16), d_att, TN).astype(bf16).astype(f32)
            dfront[at, cols] = d_q.astype(bf16)
            dfront[at, wide + h * PAD : wide + (h + 1) * PAD] = d_k.astype(bf16)
            for e in range(EXPERTS):
                lane = h * EXPERTS + e
                col = W_QK + (e * HALF_HEADS + h) * PAD
                part = front[slot, :, col - W_QK + wide : col - W_QK + wide + PAD]
                d_gates = jnp.where(lanes == lane, jnp.sum(part * d_v, axis=-1, keepdims=True), d_gates)
                dfront[at, col : col + PAD] = (gated[:, lane : lane + 1] * d_v).astype(bf16)
        d_logits = jnp.where(lanes < N_ROUTE, d_gates * picks * gate * (1.0 - gate), 0.0)
        dfront[at, MISC:W_A] = d_logits.astype(bf16)

    def o_stage(stage, part):
        for j in part:
            so.lift(j, stage)

    outer, inner_levels = order[:2], order[2:]
    attend(0)
    line.step()
    attend(1)
    o_stage(1, outer)
    line.step()
    for i in range(2, 2 * batches):
        attend(i)
    l_act.wait()
    one_all = grad.reshape(both, width)
    for column in range(4):
        weight_grad(a_src, one_all, dfront, 896, MISC, column)
    line.step()
    o_stage(1, inner_levels)
    last.wait()

    def final(i, carry):
        at = pl.ds(pl.multiple_of(i * step, step), step)
        total_at = pl.ds(pl.multiple_of(c * rows + i * step, step), step)
        tail = meta[c, at].astype(f32)
        position = lax.broadcasted_iota(jnp.int32, (step, 1), 0) + (i * step) % local_len
        keep = position.astype(f32) < tail[:, 41:42]
        total = hidden[at] + branch[total_at] + arrived[at]
        db[total_at] = jnp.where(keep, total, 0.0).astype(bf16)
        return carry

    lax.fori_loop(0, rows // step, final, 0)
    pl.semaphore_signal(freed, inc=1, device_id=nb["c"], device_id_type=MESH)
    outs = [pltpu.make_async_copy(db.at[near], layer_out, osem.at[0])]
    outs[0].start()

    line.step()
    for stage in range(2, levels - 1):
        o_stage(stage, order)
    for cp in l_wa:
        cp.wait()

    def through_front(at):
        def body(i, carry):
            cols = pl.ds(pl.multiple_of(i * 256, 256), 256)
            below = pl.ds(pl.multiple_of(width + i * 256, 256), 256)
            branch[at, cols] = (
                dot_f32(dfront[at, :width], w_f[cols], NT)
                + dot_f32(dfront[at, width:], w_f[below, : W_A - width], NT))
            return carry

        lax.fori_loop(0, width // 256, body, 0)

    through_front(far)
    hand = exchange(branch.at[far], arrived, 3)
    pl.semaphore_wait(freed, 1)
    hand.start()
    through_front(near)
    line.step()

    spread = MEM + 2 * local_len
    ids = lax.broadcasted_iota(jnp.int32, (local_len, 1), 0)
    lines = []
    for h in range(HALF_HEADS):
        turned = jnp.concatenate([dsum[h], jnp.zeros((local_len, local_len), f32)], axis=1)
        bit = 1
        while bit < local_len:
            moved = pltpu.roll(turned, bit, 1)
            turned = jnp.where(((local_len - 1 - ids) // bit) % 2 == 1, moved, turned)
            bit *= 2
        lines.append(jnp.sum(turned, axis=0, keepdims=True))
    row_of = lax.broadcasted_iota(jnp.int32, (W_MISC, spread), 0)
    table = jnp.zeros((W_MISC, spread), f32)
    for h in range(HALF_HEADS):
        table = jnp.where(row_of == COL_BIAS + h, lines[h], table)
    high = table.astype(bf16)
    low = (table - high.astype(f32)).astype(bf16)
    distance = MEM + local_len - 1 - lax.broadcasted_iota(jnp.int32, (1, spread), 1)
    bucket = bucket_index(distance)
    wanted = (bucket // per_device) * shard + bucket % per_device
    hand.wait()

    def first(i, carry):
        at = pl.ds(pl.multiple_of(i * step, step), step)
        total_at = pl.ds(pl.multiple_of(c * rows + i * step, step), step)
        normed, inverse = norm_rows(n2[at].astype(f32))
        up = branch[total_at] + arrived[at]
        norms[COL_NORM : COL_NORM + 1] += jnp.sum(up * normed, axis=0, keepdims=True)
        norms[COL_NORM + 1 : COL_NORM + 2] += jnp.sum(up, axis=0, keepdims=True)
        dhid[at] += norm_rows_backward(up, normed, inverse, vec[VEC_GAIN : VEC_GAIN + 1])
        return carry

    l_x = load(xs_in.at[c, :, pl.ds(0, width)], n2.at[pl.ds(0, rows)], 16)
    l_x.wait()
    lax.fori_loop(0, rows // step, first, 0)
    outs.append(pltpu.make_async_copy(dhid, grad_out, osem.at[1]))
    outs[1].start()
    columns = norms[...].T

    for column in range(4):
        at = pl.ds(column * span, span)
        row_ids = lax.broadcasted_iota(jnp.int32, (span, spread), 0) + column * span
        one_hot = jnp.where(row_ids == wanted, 1.0, 0.0).astype(bf16)
        misc = dot_f32(one_hot, high, NT) + dot_f32(one_hot, low, NT)
        misc = misc + dot_f32(one_all[:, at], dfront[:, MISC:W_A], TN) + columns[column * span : (column + 1) * span]
        m_bufs[0][column] = misc.astype(bf16).reshape(levels, block_rows, W_MISC)
    line.step()
    line.step()
    for j in order:
        so.gathered(j)
    line.turns()
    so.issue()
    line.round()
    so.turn()
    line.round()
    so.column()
    line.finish()
    outs.append(pltpu.make_async_copy(f_total, f_out, osem.at[2]))
    outs[2].start()
    mine, other = [pl.ds(pl.multiple_of(k * shard, 16), shard) for k in (c, 1 - c)]
    for i, (total, out) in enumerate(((i_total, i_out), (o_total, o_out), (a_total, a_out), (m_total, m_out))):
        outs.append(exchange(total.at[other], out.at[c], 4 + i))
        outs[-1].start()
        outs.append(pltpu.make_async_copy(total.at[mine], out.at[c], osem.at[3 + i]))
        outs[-1].start()
    for s in sums + [so]:
        s.drain()
    for cp in outs:
        cp.wait()


def backward(levels, batches, local_len, per_device, shard, ins):
    bf16, f32 = jnp.bfloat16, jnp.float32
    (unused, w_f, w_i, w_o, w_a, ffn, slope, xs, n2, hidden, vec, att, gates, front, win, probs, mixed, act) = ins
    ff, width = w_f.shape
    rows = batches * local_len
    both = 2 * rows
    f_rows = ff // (4 * levels)
    b_rows = width // (4 * levels)
    wide = HALF_HEADS * PAD
    outs = [((f_rows, width), f32)] + [((SIDE, shard, w), f32) for w in (ff, W_O, MISC, W_MISC)]
    outs += [((rows, width), bf16), ((rows, width), f32)]
    scratch = [(v.shape, v.dtype) for v in (w_f, w_i, ffn, slope)]
    scratch += [((2, rows, width), bf16), ((2, rows, 128), bf16)]
    scratch += [(n2.shape, bf16), (hidden.shape, f32), ((8, width), f32), (att.shape, bf16), (gates.shape, f32)]
    scratch += [((2, local_len, wide + W_VAL), f32), ((2,) + win.shape[1:], bf16), ((2,) + probs.shape[2:], f32)]
    scratch += [
        ((both, width), f32), ((rows, width), f32), ((rows, width), f32), ((both, width), bf16),
        ((both, W_O), bf16), ((both, W_A), bf16), ((HALF_HEADS, local_len, MEM + local_len), f32),
        ((W_MISC, width), f32), ((f_rows, width), f32),
    ]
    scratch += [((b_rows, w), f32) for w in (ff, W_O, MISC, W_MISC)]
    for r, w in ((f_rows, width), (b_rows, ff), (b_rows, W_MISC)):
        scratch.append(((4, levels, r, w), bf16))
        scratch += [((levels, k, w), bf16) for k in (r // 2, r // 2, r, r)]
        scratch.append(((levels + 1, r, w), bf16))
    scratch.append(((4, levels, b_rows, MISC), bf16))
    scratch += [((levels, b_rows // 2, MISC), bf16)] * 2
    scratch += [((4, levels, b_rows, W_O), bf16), ((4 * b_rows, W_O), bf16)]
    scratch += [((k, W_O), bf16) for k in (b_rows // 2, b_rows // 2, b_rows, b_rows)]
    sems = [(3 + len(A_PARTS), 8 * levels)] * 2 + [(8 * levels + 6,), (8 * levels + 6,), (18,), (4, 2), (8,), (8,), (10,)]
    hbm = pl.BlockSpec(memory_space=pl.ANY)
    return pl.pallas_call(
        functools.partial(backward_kernel, levels, batches, local_len, per_device, shard),
        out_shape=[jax.ShapeDtypeStruct(s, k) for s, k in outs],
        in_specs=[hbm] * len(ins),
        out_specs=[hbm] * len(outs),
        scratch_shapes=[pltpu.VMEM(s, k) for s, k in scratch]
        + [pltpu.SemaphoreType.DMA(s) for s in sems]
        + [pltpu.SemaphoreType.REGULAR] * 2,
        compiler_params=pltpu.CompilerParams(
            collective_id=2, has_side_effects=True, vmem_limit_bytes=VMEM_BYTES),
    )(*ins)


def share_kernel(
    per_device, f_in, i_in, o_in, a_in, m_in, layer_in, grad_in,
    f_out, in_out, branch_out, value_out, qk_out, router_out, gain1, shift1, gain2, shift2, bias_out, layer_out, grad_out,
    f_hold, layer_hold, grad_hold, sems,
):
    big = ((f_in, f_hold, f_out), (layer_in, layer_hold, layer_out), (grad_in, grad_hold, grad_out))
    there = [pltpu.make_async_copy(src, held, sems.at[i]) for i, (src, held, unused) in enumerate(big)]
    back = [pltpu.make_async_copy(held, dst, sems.at[3 + i]) for i, (unused, held, dst) in enumerate(big)]
    for cp in there:
        cp.start()
    for side in range(SIDE):
        for p in range(i_in.shape[2] // PAD):
            col = (p * SIDE + side) * PAD
            in_out[:, col : col + PAD] = i_in[side, :, p * PAD : (p + 1) * PAD]
        for h in range(HALF_HEADS):
            at = (side * HALF_HEADS + h) * HEAD_DIM
            for e in range(EXPERTS):
                col, dst = (e * HALF_HEADS + h) * PAD, e * HEADS * HEAD_DIM + at
                value_out[:, dst : dst + HEAD_DIM] = a_in[side, :, W_QK + col : W_QK + col + HEAD_DIM]
                branch_out[:, dst : dst + HEAD_DIM] = o_in[side, :, col : col + HEAD_DIM]
            for kind in range(2):
                col, dst = (kind * HALF_HEADS + h) * PAD, kind * HEADS * HEAD_DIM + at
                qk_out[:, dst : dst + HEAD_DIM] = a_in[side, :, col : col + HEAD_DIM]
        routes = HALF_HEADS * EXPERTS
        for kind in range(2):
            dst = (kind * SIDE + side) * routes
            router_out[:, dst : dst + routes] = m_in[side, :, kind * routes : (kind + 1) * routes]
        turned = m_in[side].T
        bias_out[side * HALF_HEADS : (side + 1) * HALF_HEADS] = turned[COL_BIAS : COL_BIAS + HALF_HEADS, :per_device]
    turned = (m_in[0] + m_in[1]).T
    for i, out in enumerate((gain1, shift1, gain2, shift2)):
        out[...] = turned[COL_NORM + i : COL_NORM + i + 1]
    for cp, after in zip(there, back):
        cp.wait()
        after.start()
    for cp in back:
        cp.wait()


def shares_of(per_device, ins):
    f, i, o, a, m, layer, grad = ins
    shard = i.shape[1]
    inner = HEADS * HEAD_DIM
    f32 = jnp.float32
    shapes = [
        (f.shape, f32), ((shard, SIDE * i.shape[2]), f32), ((shard, EXPERTS * inner), f32),
        ((shard, EXPERTS * inner), f32), ((shard, 2 * inner), f32), ((shard, 2 * HEADS * EXPERTS), f32)]
    shapes += [((1, shard), f32)] * 4 + [((HEADS, per_device), f32), (layer.shape, layer.dtype), (grad.shape, f32)]
    hbm, vmem = pl.BlockSpec(memory_space=pl.ANY), pl.BlockSpec(memory_space=pltpu.VMEM)
    return pl.pallas_call(
        functools.partial(share_kernel, per_device),
        out_shape=[jax.ShapeDtypeStruct(s, k) for s, k in shapes],
        in_specs=[hbm] + [vmem] * 4 + [hbm] * 2,
        out_specs=[hbm] + [vmem] * 10 + [hbm] * 2,
        scratch_shapes=[pltpu.VMEM(w.shape, w.dtype) for w in (f, layer, grad)] + [pltpu.SemaphoreType.DMA((6,))],
        compiler_params=pltpu.CompilerParams(vmem_limit_bytes=VMEM_BYTES),
    )(*ins)


def on_chip(
    tokens, cotangent, given_cache, value_routes, output_routes, valid_counts, doc_starts,
    norm1_gain, norm1_shift, qk_weight, router_weight, value_weight, output_weight, rel_bias,
    norm2_gain, norm2_shift, ffn_in, ffn_out,
):
    batches, unused_row, local_len, width = tokens.shape
    count = lax.axis_size("tm")
    levels = count // 2
    side = lax.axis_index("tm") % 2
    rows = batches * local_len
    shard = qk_weight.shape[0]
    blocks = 4 * levels
    bf16, f32 = jnp.bfloat16, jnp.float32

    norms = jnp.stack([norm1_gain, norm1_shift, norm2_gain, norm2_shift])
    routes = [
        jnp.transpose(r.reshape(batches, local_len, HEADS, TOPK), (0, 2, 3, 1)) for r in (value_routes, output_routes)]
    buckets = rel_bias.shape[1]
    hidden_block = ffn_out.shape[0]
    (a_all, o_all, i_all, f_all, xs, act_one, front, gates, win, probs, attended, mixed, hidden, n2, vec, act,
     slope, f_grad) = forward(
        levels, batches, local_len, buckets,
        (qk_weight, value_weight, router_weight, norms, rel_bias, output_weight.T, ffn_in, ffn_out,
         tokens.reshape(rows, width), cotangent.reshape(rows, width), routes[0], routes[1],
         doc_starts.reshape(1, batches), valid_counts.reshape(1, batches),
         given_cache.reshape(batches, MEM, 2 * HEADS * HEAD_DIM)))
    w_a = a_all.reshape(width, W_A)
    w_i = i_all.reshape(width, -1)
    w_f = f_all.reshape(-1, width)
    sums = backward(
        levels, batches, local_len, buckets, shard,
        (f_grad.reshape(4, levels, hidden_block, width), w_f, w_i, o_all, w_a, act, slope, xs, n2, hidden, vec, attended, gates, front, win, probs, mixed,
         act_one.reshape(2, rows, width)))
    (out_share, in_share, branch_share, value_share, qk_share, router_share, gain1, shift1, gain2, shift2, bias_share,
     layer_out, input_grad) = shares_of(buckets, sums)
    gain1, shift1, gain2, shift2 = [v.reshape(shard) for v in (gain1, shift1, gain2, shift2)]
    return (
        layer_out.reshape(tokens.shape), input_grad.reshape(tokens.shape), gain1, shift1, qk_share, router_share,
        value_share, branch_share.T, bias_share, gain2, shift2, in_share, out_share,
    )


def by_size(*args):
    thin = args[9].shape[0] % 16 != 0
    paired = lax.axis_size("doc") == 4 and lax.axis_size("tm") % 2 == 0
    return on_device(*args) if thin or not paired else on_chip(*args)


def solution(mesh):
    return jax.shard_map(
        by_size,
        mesh=mesh,
        in_specs=(
            P(None, "doc", "tm", None),
            P(None, "doc", "tm", None),
            P(None, "doc", "tm", None),
            P(None, "doc", "tm", None, None),
            P(None, "doc", "tm", None, None),
            P(None, "doc", "tm"),
            P(None, "doc", "tm"),
            P(("doc", "tm")),
            P(("doc", "tm")),
            P(("doc", "tm"), None),
            P(("doc", "tm"), None),
            P(("doc", "tm"), None),
            P(None, ("doc", "tm")),
            P(None, ("doc", "tm")),
            P(("doc", "tm")),
            P(("doc", "tm")),
            P(("doc", "tm"), None),
            P(("doc", "tm"), None),
        ),
        out_specs=(
            P(None, "doc", "tm", None),
            P(None, "doc", "tm", None),
            P(("doc", "tm")),
            P(("doc", "tm")),
            P(("doc", "tm"), None),
            P(("doc", "tm"), None),
            P(("doc", "tm"), None),
            P(None, ("doc", "tm")),
            P(None, ("doc", "tm")),
            P(("doc", "tm")),
            P(("doc", "tm")),
            P(("doc", "tm"), None),
            P(("doc", "tm"), None),
        ),
        check_vma=False,
    )
```

```python
import functools

import jax
import jax.numpy as jnp
from jax import lax
from jax.experimental import pallas as pl
from jax.experimental.pallas import tpu as pltpu
from jax.sharding import PartitionSpec as P

HEADS = 4
HEAD_DIM = 112
EXPERTS = 5
TOPK = 2
MEM = 1024
BUCKETS = 256
NEAR = 128
STEP = 16


EPS = 1e-05
NEG = -1e30
HIGH = lax.Precision.HIGHEST


def shortened(array):
    return jax.tree.map(lambda a: a.astype(jnp.bfloat16) if a.dtype == jnp.float32 else a, array)


def from_behind(value, axis, steps):
    count = lax.axis_size(axis)
    first, last = (max(0, -steps), min(count, count - steps))
    return lax.ppermute(value, axis, [(source, source + steps) for source in range(first, last)])


def norm_forward(values, gain, shift):
    center_mean = jnp.mean(values, axis=-1, keepdims=True)
    centered = values - center_mean
    inverse = lax.rsqrt(jnp.mean(centered * centered, axis=-1, keepdims=True) + EPS)
    normed = centered * inverse
    return (normed * gain + shift, normed, inverse)


def norm_backward(upstream, normed, inverse, gain):
    scaled = upstream * gain
    inside = (
        scaled
        - jnp.mean(scaled, axis=-1, keepdims=True)
        - normed * jnp.mean(scaled * normed, axis=-1, keepdims=True)
    )
    return (inside * inverse, jnp.sum(upstream * normed, axis=0), jnp.sum(upstream, axis=0))


def selection(routes):
    expert_ids = jnp.arange(EXPERTS, dtype=jnp.int32)
    return jnp.sum((routes[..., None] == expert_ids).astype(jnp.float32), axis=-2)


def bucket_index(distance):
    far_bucket = NEAR + (distance - NEAR) // STEP
    return jnp.clip(jnp.where(distance < NEAR, distance, far_bucket), 0, BUCKETS - 1)


def gelu_slope(pre_act):
    return (
        0.5 * (1.0 + lax.erf(pre_act * 0.7071067811865476))
        + pre_act * jnp.exp(-0.5 * pre_act * pre_act) * 0.3989422804014327
    )


def flatten(matrix):
    return matrix.reshape(-1)


def bucket_matrix(local_len):
    spread = MEM + 2 * local_len - 1
    distance = jnp.arange(spread, dtype=jnp.int32) - (local_len - 1)
    bucket_ids = jnp.arange(BUCKETS, dtype=jnp.int32)
    return (bucket_index(distance)[:, None] == bucket_ids[None, :]).astype(jnp.float32)


def bias_matrix(table, local_len):
    spread = MEM + 2 * local_len - 1
    window = MEM + local_len
    by_distance = jnp.einsum("hc,kc->hk", table, bucket_matrix(local_len), precision=HIGH)
    turned = jnp.concatenate([by_distance[:, ::-1], jnp.zeros((HEADS, 1), jnp.float32)], axis=1)
    tiled = jnp.tile(turned, (1, local_len))[:, : local_len * spread].reshape(
        HEADS, local_len, spread
    )
    return tiled[:, :, local_len - 1 : local_len - 1 + window]


def bias_backward(score_sum, local_len):
    spread = MEM + 2 * local_len - 1
    padded = jnp.pad(score_sum, ((0, 0), (0, 0), (local_len - 1, 0))).reshape(
        HEADS, local_len * spread
    )
    padded = jnp.pad(padded, ((0, 0), (0, local_len))).reshape(HEADS, local_len, spread + 1)
    by_distance = jnp.sum(padded, axis=1)[:, :spread][:, ::-1]
    return jnp.einsum("hk,kc->hc", by_distance, bucket_matrix(local_len), precision=HIGH)


def attention_scores(queries, keys, table, counts):
    local_len = queries.shape[1]
    window = keys.shape[1]
    raw = jnp.einsum(
        "bqhd,bkhd->bhqk", queries, keys, preferred_element_type=jnp.float32
    ) * HEAD_DIM ** (-0.5)
    row_ids = jnp.arange(local_len, dtype=jnp.int32)[:, None]
    col_ids = jnp.arange(window, dtype=jnp.int32)[None, :]
    bias = bias_matrix(table, local_len)
    own_ids = col_ids - MEM
    causal = (own_ids <= row_ids)[None, None]
    live = own_ids[None, None] < counts[:, None, None, None]
    valid = jnp.logical_or((col_ids < MEM)[None, None], jnp.logical_and(causal, live))
    return (jnp.where(valid, raw + bias[None], NEG), valid)


def memory_by_hops(cache_own, given, starts, local_len):
    hops_total = MEM // local_len
    open_flag = jnp.logical_not(starts)[:, None, None]
    memory_slots = [jnp.zeros_like(cache_own) for _ in range(hops_total)]
    start_marks = starts.astype(jnp.bfloat16)
    for distance in range(1, hops_total + 1):
        if distance < hops_total:
            outgoing = (cache_own, start_marks, given[:, distance * local_len :])
        else:
            outgoing = (cache_own, start_marks)
        incoming = jax.tree.map(
            lambda part, own: part.astype(own.dtype),
            from_behind(shortened(outgoing), "tm", distance),
            outgoing,
        )
        memory_slots[hops_total - distance] = jnp.where(
            open_flag, incoming[0], memory_slots[hops_total - distance]
        )
        arrived = jnp.logical_and(open_flag, (incoming[1] > 0)[:, None, None])
        if distance < hops_total:
            for position in range(hops_total - distance):
                portion = incoming[2][:, position * local_len : (position + 1) * local_len]
                memory_slots[position] = jnp.where(arrived, portion, memory_slots[position])
        open_flag = jnp.logical_and(open_flag, jnp.logical_not(arrived))
    assembled = jnp.concatenate(memory_slots, axis=1)
    return jnp.where(starts[:, None, None], given, assembled)


def on_device(
    tokens,
    cotangent,
    given_cache,
    value_routes,
    output_routes,
    valid_counts,
    doc_starts,
    norm1_gain,
    norm1_shift,
    qk_weight,
    router_weight,
    value_weight,
    output_weight,
    rel_bias,
    norm2_gain,
    norm2_shift,
    ffn_in,
    ffn_out,
):
    batches, unused_row, local_len, model_width = tokens.shape
    row_count = batches * local_len
    inner_width = HEADS * HEAD_DIM
    head_experts = HEADS * EXPERTS
    full_weights = (
        lax.all_gather(norm1_gain, ("doc", "tm"), axis=0, tiled=True),
        lax.all_gather(norm1_shift, ("doc", "tm"), axis=0, tiled=True),
        lax.all_gather(qk_weight, ("doc", "tm"), axis=0, tiled=True),
        lax.all_gather(router_weight, ("doc", "tm"), axis=0, tiled=True),
        lax.all_gather(value_weight, ("doc", "tm"), axis=0, tiled=True),
        lax.all_gather(output_weight, ("doc", "tm"), axis=1, tiled=True),
        lax.all_gather(rel_bias, ("doc", "tm"), axis=1, tiled=True),
        lax.all_gather(norm2_gain, ("doc", "tm"), axis=0, tiled=True),
        lax.all_gather(norm2_shift, ("doc", "tm"), axis=0, tiled=True),
        lax.all_gather(ffn_in, ("doc", "tm"), axis=0, tiled=True),
        lax.all_gather(ffn_out, ("doc", "tm"), axis=0, tiled=True),
    )
    (
        gain_one,
        shift_one,
        w_qk,
        w_router,
        w_value,
        w_output,
        table_bf,
        gain_two,
        shift_two,
        w_in,
        w_out,
    ) = full_weights
    gain_one = gain_one.astype(jnp.float32)
    shift_one = shift_one.astype(jnp.float32)
    gain_two = gain_two.astype(jnp.float32)
    shift_two = shift_two.astype(jnp.float32)
    table = table_bf.astype(jnp.float32)
    router_f = w_router.astype(jnp.float32)
    inputs = tokens.reshape(row_count, model_width).astype(jnp.float32)
    counts = valid_counts.reshape(batches)
    starts = doc_starts.reshape(batches) > 0
    token_mask = (
        (jnp.arange(local_len, dtype=jnp.int32)[None, :] < counts[:, None])
        .astype(jnp.float32)
        .reshape(row_count, 1)
    )
    value_pick = selection(value_routes.reshape(row_count, HEADS, TOPK))
    output_pick = selection(output_routes.reshape(row_count, HEADS, TOPK))
    normed_one, norm1_unit, norm1_inv = norm_forward(inputs, gain_one, shift_one)
    act_one = normed_one.astype(jnp.bfloat16)
    qk_vals = jnp.dot(act_one, w_qk, preferred_element_type=jnp.float32).astype(jnp.bfloat16)
    gates = jax.nn.sigmoid(jnp.dot(act_one, w_router, preferred_element_type=jnp.float32))
    gate_value = gates[:, :head_experts].reshape(row_count, HEADS, EXPERTS) * value_pick
    gate_output = gates[:, head_experts:].reshape(row_count, HEADS, EXPERTS) * output_pick
    value_gate_t = jnp.transpose(gate_value, (0, 2, 1))[..., None]
    output_gate_t = jnp.transpose(gate_output, (0, 2, 1))[..., None]
    parts = jnp.dot(act_one, w_value, preferred_element_type=jnp.float32).reshape(
        row_count, EXPERTS, HEADS, HEAD_DIM
    )
    values = (
        jnp.sum(value_gate_t * parts, axis=1).reshape(row_count, inner_width).astype(jnp.bfloat16)
    )
    cache_own = jnp.concatenate([qk_vals[:, inner_width:], values], axis=1).reshape(
        batches, local_len, 2 * inner_width
    )
    given = given_cache.reshape(batches, MEM, 2 * inner_width)
    memory = memory_by_hops(cache_own, given, starts, local_len)
    queries = qk_vals[:, :inner_width].reshape(batches, local_len, HEADS, HEAD_DIM)
    keys = jnp.concatenate([memory[:, :, :inner_width], cache_own[:, :, :inner_width]], axis=1)
    keys = keys.reshape(batches, MEM + local_len, HEADS, HEAD_DIM)
    vals = jnp.concatenate([memory[:, :, inner_width:], cache_own[:, :, inner_width:]], axis=1)
    vals = vals.reshape(batches, MEM + local_len, HEADS, HEAD_DIM)
    scores, valid = attention_scores(queries, keys, table, counts)
    top = jnp.max(scores, axis=-1, keepdims=True)
    expo = jnp.exp(scores - top)
    denom = jnp.sum(expo, axis=-1, keepdims=True)
    log_total = top + jnp.log(denom)
    probs_b = (expo / denom).astype(jnp.bfloat16)
    attended = jnp.einsum("bhqk,bkhd->bqhd", probs_b, vals, preferred_element_type=jnp.float32)
    attended = attended.reshape(row_count, inner_width).astype(jnp.bfloat16)
    attended_f = attended.astype(jnp.float32).reshape(row_count, 1, HEADS, HEAD_DIM)
    mixed = (
        (output_gate_t * attended_f).reshape(row_count, EXPERTS * inner_width).astype(jnp.bfloat16)
    )
    hidden = inputs + jnp.dot(mixed, w_output, preferred_element_type=jnp.float32)
    normed_two, norm2_unit, norm2_inv = norm_forward(hidden, gain_two, shift_two)
    act_two = normed_two.astype(jnp.bfloat16)
    pre_act = jnp.dot(act_two, w_in, preferred_element_type=jnp.float32)
    activated = jax.nn.gelu(pre_act, approximate=False).astype(jnp.bfloat16)
    ffn_result = jnp.dot(activated, w_out, preferred_element_type=jnp.float32)
    layer_out = (token_mask * (hidden + ffn_result)).astype(jnp.bfloat16).reshape(tokens.shape)
    upstream = cotangent.reshape(row_count, model_width).astype(jnp.float32) * token_mask
    upstream_b = upstream.astype(jnp.bfloat16)
    d_out_w = jnp.einsum("nf,nd->fd", activated, upstream_b, preferred_element_type=jnp.float32)
    d_act = jnp.einsum("nd,fd->nf", upstream_b, w_out, preferred_element_type=jnp.float32)
    d_pre = (d_act * gelu_slope(pre_act)).astype(jnp.bfloat16)
    d_in_w = jnp.einsum("nd,nf->df", act_two, d_pre, preferred_element_type=jnp.float32)
    d_norm_two = jnp.einsum("nf,df->nd", d_pre, w_in, preferred_element_type=jnp.float32)
    d_from_two, d_gain_two, d_shift_two = norm_backward(d_norm_two, norm2_unit, norm2_inv, gain_two)
    d_hidden = upstream + d_from_two
    ffn_width = d_in_w.shape[1]
    d_branch = d_hidden.astype(jnp.bfloat16)
    d_output_t = jnp.einsum("nd,nk->dk", d_branch, mixed, preferred_element_type=jnp.float32)
    d_mixed = jnp.einsum(
        "nd,kd->nk", d_branch, w_output, preferred_element_type=jnp.float32
    ).astype(jnp.bfloat16)
    d_mixed = d_mixed.astype(jnp.float32).reshape(row_count, EXPERTS, HEADS, HEAD_DIM)
    d_gate_out = jnp.sum(d_mixed * attended_f, axis=-1)
    d_attended = (
        jnp.sum(d_mixed * output_gate_t, axis=1)
        .astype(jnp.bfloat16)
        .reshape(batches, local_len, HEADS, HEAD_DIM)
    )
    probs = jnp.where(valid, jnp.exp(scores - log_total), 0.0)
    d_probs = jnp.einsum("bqhd,bkhd->bhqk", d_attended, vals, preferred_element_type=jnp.float32)
    delta = jnp.sum(d_probs * probs, axis=-1, keepdims=True)
    d_scores = probs * (d_probs - delta)
    score_sum = jnp.sum(d_scores, axis=0)
    d_table = bias_backward(score_sum, local_len)
    d_scores_b = d_scores.astype(jnp.bfloat16)
    scale = HEAD_DIM ** (-0.5)
    d_queries = (
        jnp.einsum("bhqk,bkhd->bqhd", d_scores_b, keys, preferred_element_type=jnp.float32) * scale
    )
    d_keys = (
        jnp.einsum(
            "bhqk,bqhd->bkhd", d_scores_b[..., MEM:], queries, preferred_element_type=jnp.float32
        )
        * scale
    )
    d_vals = jnp.einsum(
        "bhqk,bqhd->bkhd", probs_b[..., MEM:], d_attended, preferred_element_type=jnp.float32
    )
    d_qk = jnp.concatenate(
        [d_queries.reshape(row_count, inner_width), d_keys.reshape(row_count, inner_width)], axis=1
    ).astype(jnp.bfloat16)
    d_values = (
        d_vals.reshape(row_count, 1, HEADS, HEAD_DIM).astype(jnp.bfloat16).astype(jnp.float32)
    )
    d_gate_val = jnp.sum(parts * d_values, axis=-1)
    d_parts = (
        (value_gate_t * d_values).reshape(row_count, EXPERTS * inner_width).astype(jnp.bfloat16)
    )
    d_gates = jnp.concatenate(
        [
            jnp.transpose(d_gate_val, (0, 2, 1)).reshape(row_count, head_experts)
            * value_pick.reshape(row_count, head_experts),
            jnp.transpose(d_gate_out, (0, 2, 1)).reshape(row_count, head_experts)
            * output_pick.reshape(row_count, head_experts),
        ],
        axis=1,
    )
    d_logits = d_gates * gates * (1.0 - gates)
    d_qk_w = jnp.einsum("nd,nk->dk", act_one, d_qk, preferred_element_type=jnp.float32)
    d_value_w = jnp.einsum("nd,nk->dk", act_one, d_parts, preferred_element_type=jnp.float32)
    d_router_w = jnp.einsum("nd,nk->dk", act_one.astype(jnp.float32), d_logits, precision=HIGH)
    d_norm_one = jnp.einsum("nk,dk->nd", d_qk, w_qk, preferred_element_type=jnp.float32)
    d_norm_one = d_norm_one + jnp.einsum(
        "nk,dk->nd", d_parts, w_value, preferred_element_type=jnp.float32
    )
    d_norm_one = d_norm_one + jnp.einsum("nk,dk->nd", d_logits, router_f, precision=HIGH)
    d_from_one, d_gain_one, d_shift_one = norm_backward(d_norm_one, norm1_unit, norm1_inv, gain_one)
    input_grad = (d_hidden + d_from_one).reshape(tokens.shape)
    shares = (
        lax.psum_scatter(d_gain_one, ("doc", "tm"), scatter_dimension=0, tiled=True),
        lax.psum_scatter(d_shift_one, ("doc", "tm"), scatter_dimension=0, tiled=True),
        lax.psum_scatter(flatten(d_qk_w), ("doc", "tm"), scatter_dimension=0, tiled=True),
        lax.psum_scatter(flatten(d_router_w), ("doc", "tm"), scatter_dimension=0, tiled=True),
        lax.psum_scatter(flatten(d_value_w), ("doc", "tm"), scatter_dimension=0, tiled=True),
        lax.psum_scatter(flatten(d_output_t), ("doc", "tm"), scatter_dimension=0, tiled=True),
        lax.psum_scatter(d_table, ("doc", "tm"), scatter_dimension=1, tiled=True),
        lax.psum_scatter(d_gain_two, ("doc", "tm"), scatter_dimension=0, tiled=True),
        lax.psum_scatter(d_shift_two, ("doc", "tm"), scatter_dimension=0, tiled=True),
        lax.psum_scatter(flatten(d_in_w), ("doc", "tm"), scatter_dimension=0, tiled=True),
        lax.psum_scatter(flatten(d_out_w), ("doc", "tm"), scatter_dimension=0, tiled=True),
    )
    qk_share = shares[2].reshape(-1, 2 * inner_width)
    router_share = shares[3].reshape(-1, 2 * head_experts)
    value_share = shares[4].reshape(-1, EXPERTS * inner_width)
    output_share = shares[5].reshape(-1, EXPERTS * inner_width).T
    in_share = shares[9].reshape(-1, ffn_width)
    out_share = shares[10].reshape(-1, model_width)
    return (
        layer_out,
        input_grad,
        shares[0],
        shares[1],
        qk_share,
        router_share,
        value_share,
        output_share,
        shares[6],
        shares[7],
        shares[8],
        in_share,
        out_share,
    )


MESH = pl.DeviceIdType.MESH
PAD = 128
SIDE = 2
HALF_HEADS = HEADS // SIDE
W_QK = 2 * HALF_HEADS * PAD
W_VAL = EXPERTS * HALF_HEADS * PAD
W_MISC = 128
W_A = W_QK + W_VAL + W_MISC
W_O = EXPERTS * HALF_HEADS * PAD
MISC = W_QK + W_VAL
N_ROUTE = 2 * HALF_HEADS * EXPERTS
COL_NORM = N_ROUTE
COL_BIAS = N_ROUTE + 4
VMEM_BYTES = 63 * 1024 * 1024
SCALE = HEAD_DIM ** (-0.5)


def pad_last(a, width):
    return jnp.pad(a, [(0, 0)] * (a.ndim - 1) + [(0, width - a.shape[-1])])


def neighbours(count):
    d, t = lax.axis_index("doc"), lax.axis_index("tm")
    z, c = t // 2, t % 2
    return dict(
        c=(d, z * 2 + 1 - c),
        x=(d + 1 - 2 * (d % 2), t),
        y=((d + 2) % 4, t),
        up=(d, jnp.minimum(t + 2, count - 1)),
        down=(d, jnp.maximum(t - 2, 0)),
    )


def enter(nb, z, levels):
    barrier = pltpu.get_barrier_semaphore()
    for name in ("c", "x", "y"):
        pl.semaphore_signal(barrier, inc=1, device_id=nb[name], device_id_type=MESH)

    @pl.when(z < levels - 1)
    def _():
        pl.semaphore_signal(barrier, inc=1, device_id=nb["up"], device_id_type=MESH)

    @pl.when(z > 0)
    def _():
        pl.semaphore_signal(barrier, inc=1, device_id=nb["down"], device_id_type=MESH)

    ends = jnp.where(z < levels - 1, 1, 0) + jnp.where(z > 0, 1, 0)
    pl.semaphore_wait(barrier, 3 + ends)


class Gather:
    def __init__(self, ref, sems, nb, d, z, levels):
        self.ref, self.nb, self.d, self.z, self.levels = ref, nb, d, z, levels
        self.send, self.recv = sems
        self.half = ref.shape[2] // 2

    def copy(self, part, slot, to):
        return pltpu.make_async_remote_copy(
            src_ref=part, dst_ref=part, send_sem=self.send.at[slot], recv_sem=self.recv.at[slot],
            device_id=self.nb[to], device_id_type=MESH)

    def along(self, level, distance, to):
        base = 0 if to == "up" else self.levels
        return self.copy(self.ref.at[self.d, level], base + distance, to)

    def across(self, level, to, column=None):
        base = (2 if to == "x" else 3) * self.levels
        column = self.d if column is None else column
        return self.copy(self.ref.at[column, level], base + level, to)

    def corner(self, level, to, column):
        base = (4 if to == "x" else 5) * self.levels
        rows = pl.ds(self.half, self.half) if to == "x" else pl.ds(0, self.half)
        return self.copy(self.ref.at[column, level, rows], base + level, to)

    def begin(self):
        z, levels = self.z, self.levels

        @pl.when(z < levels - 1)
        def _():
            self.along(z, 1, "up").start()

        @pl.when(z > 0)
        def _():
            self.along(z, 1, "down").start()

        self.across(z, "x").start()
        self.across(z, "y").start()

    def line(self, k):
        z, levels = self.z, self.levels

        @pl.when(z >= k)
        def _():
            self.along(z - k, k, "up").wait_recv()

            @pl.when(z < levels - 1)
            def _():
                self.along(z - k, k + 1, "up").start()

            self.across(z - k, "x").start()
            self.across(z - k, "y").start()

        @pl.when(z + k < levels)
        def _():
            self.along(z + k, k, "down").wait_recv()

            @pl.when(z > 0)
            def _():
                self.along(z + k, k + 1, "down").start()

            self.across(z + k, "x").start()
            self.across(z + k, "y").start()

    def turn(self, k):
        z, levels, d = self.z, self.levels, self.d
        by_x, by_y = d + 1 - 2 * (d % 2), (d + 2) % 4

        def one(level):
            self.across(level, "x").wait_recv()
            self.corner(level, "y", by_x).start()
            self.across(level, "y").wait_recv()
            self.corner(level, "x", by_y).start()

        if k == 0:
            one(z)
        else:
            pl.when(z >= k)(lambda: one(z - k))
            pl.when(z + k < levels)(lambda: one(z + k))

    def finish(self, k):
        z, levels, d = self.z, self.levels, self.d
        by_x, by_y = d + 1 - 2 * (d % 2), (d + 2) % 4

        def one(level):
            self.corner(level, "x", by_y).wait_recv()
            self.corner(level, "y", by_x).wait_recv()

        if k == 0:
            one(z)
        else:
            pl.when(z >= k)(lambda: one(z - k))
            pl.when(z + k < levels)(lambda: one(z + k))

    def drain(self):
        z, levels, d = self.z, self.levels, self.d
        by_x, by_y = d + 1 - 2 * (d % 2), (d + 2) % 4
        for level in range(levels):
            self.across(level, "x").wait_send()
            self.across(level, "y").wait_send()
            self.corner(level, "x", by_y).wait_send()
            self.corner(level, "y", by_x).wait_send()
        for k in range(1, levels):

            @pl.when(jnp.logical_and(z >= k - 1, z < levels - 1))
            def _():
                self.along(z - k + 1, k, "up").wait_send()

            @pl.when(jnp.logical_and(z + k - 1 < levels, z > 0))
            def _():
                self.along(z + k - 1, k, "down").wait_send()


def selector(side):
    inner = HEADS * HEAD_DIM
    wide = HALF_HEADS * PAD
    src = lax.broadcasted_iota(jnp.int32, (2 * inner, 2 * wide), 0)
    dst = lax.broadcasted_iota(jnp.int32, (2 * inner, 2 * wide), 1)
    kind, head, feature = dst // wide, (dst // PAD) % HALF_HEADS, dst % PAD
    wanted = kind * inner + (side * HALF_HEADS + head) * HEAD_DIM + feature
    hit = jnp.logical_and(src == wanted, feature < HEAD_DIM)
    return jnp.where(hit, 1.0, 0.0).astype(jnp.bfloat16)


def table_by_offset(w_a, per_device, shard, local_len, spread):
    distance = MEM + local_len - 1 - lax.broadcasted_iota(jnp.int32, (1, spread), 1)
    bucket = bucket_index(distance)
    wanted = (bucket // per_device) * shard + bucket % per_device
    step = 128

    def body(i, total):
        at = pl.ds(pl.multiple_of(i * step, step), step)
        ids = lax.broadcasted_iota(jnp.int32, (step, spread), 0) + i * step
        one_hot = jnp.where(ids == wanted, 1.0, 0.0).astype(jnp.bfloat16)
        return total + dot_f32(w_a[at, MISC:W_A], one_hot, TN)

    return lax.fori_loop(0, w_a.shape[0] // step, body, jnp.zeros((W_MISC, spread), jnp.float32))


NT = (((1,), (1,)), ((), ()))
TN = (((0,), (0,)), ((), ()))


def dot_f32(a, b, dims=(((1,), (0,)), ((), ()))):
    return lax.dot_general(a, b, dims, preferred_element_type=jnp.float32)


def steps_of(text):
    return [(w.split(".")[0], w.split(".")[1][:-1], int(w[-1])) for w in text.split()]


EVENTS = {point: steps_of(text) for point, text in dict(
    f="f.begin0",
    a="a.begin0",
    stats="a.line1",
    packs="",
    given="m.early0 a.turn0 a.line2 a.turn1 a.line3 a.turn2 o.begin0 m.early1 a.turn3 o.line1 m.early2",
    front="o.turn0 o.line2 i.begin0",
    cache="o.turn1 o.line3 i.line1 f.line1 m.early3",
    memory="o.turn2 o.turn3 i.line2 f.line2 m0.late0 i.turn0 i.line3 f.line3 m0.late1 i.turn1 m0.late2",
    half="m1.late0 m1.late1 f.turn0 i.turn2 i.turn3 m1.late2",
    attended="f.turn1",
    far="",
    pair="f.turn2 f.turn3",
    activated="",
).items()}


def forward_kernel(
    levels, batches, local_len, per_device,
    qk_in, value_in, router_in, norm_in, bias_in, branch_in, up_in, f_in, token_in, cot_in, vr_in, or_in, start_in,
    count_in, g_in,
    a_out, o_out, i_out, f_all, xs_out, act_out, front_out, gates_out, win_out, probs_out, att_out,
    mixed_out, hidden_out, n2_out, vec_out, ffn_out, slope_out, fgrad_out,
    a_all, o_all, i_all, xs, graw, win, rbuf, sel, unit, act, front, gates, vec, bias, probs, att, mixed,
    arrived, hidden, n2, ffn, slope,
    qk_raw, value_raw, router_raw, norm_raw, bias_raw, branch_raw, up_raw, vr_raw, or_raw, start_raw, count_raw, f_raw, a_pack, o_pack, i_pack,
    send, recv, csend, crecv, lsem, gsend, grecv, esend, erecv, osem, psem,
):
    bf16, f32 = jnp.bfloat16, jnp.float32
    d, t = lax.axis_index("doc"), lax.axis_index("tm")
    z, c = t // 2, t % 2
    nb = neighbours(2 * levels)
    shard = qk_in.shape[0]
    width = f_in.shape[1]
    rows = batches * local_len
    both = 2 * rows
    wide = HALF_HEADS * PAD
    own = pl.ds(pl.multiple_of(c * shard, 16), shard)

    def local(src, dst, index):
        cp = pltpu.make_async_copy(src, dst, lsem.at[index])
        cp.start()
        return cp

    def sibling(src, dst, index):
        return pltpu.make_async_remote_copy(
            src_ref=src, dst_ref=dst, send_sem=csend.at[index], recv_sem=crecv.at[index],
            device_id=nb["c"], device_id_type=MESH)

    raws = [
        local(src, dst, i)
        for i, (src, dst) in enumerate((
            (qk_in, qk_raw), (value_in, value_raw), (router_in, router_raw), (norm_in, norm_raw), (bias_in, bias_raw),
            (branch_in, branch_raw), (up_in, up_raw), (vr_in, vr_raw), (or_in, or_raw), (start_in, start_raw),
            (count_in, count_raw)))
    ]
    loc_f = local(f_in, f_raw, 11)
    x_parts = ((token_in, pl.ds(0, width)), (cot_in, pl.ds(width, width)))
    loc_x = [local(src, xs.at[c, :, cols], 12 + i) for i, (src, cols) in enumerate(x_parts)]
    enter(nb, z, levels)
    rem_x = [sibling(src, xs.at[c, :, cols], i) for i, (src, cols) in enumerate(x_parts)]
    for cp in rem_x:
        cp.start()
    ga, go, gi, gf = [
        Gather(ref, (send.at[i], recv.at[i]), nb, d, z, levels)
        for i, ref in enumerate((a_all, o_all, i_all, f_all))
    ]

    loc_f.wait()
    own_f = local(f_raw, f_all.at[d, z], 18)
    own_f.wait()
    groups = dict(a=ga, o=go, i=gi, f=gf)
    left = [
        (name, what, k) for name in groups for what, first in (("begin", 0), ("line", 1), ("turn", 0), ("finish", 0))
        for k in range(first, 1 if what == "begin" else levels)]
    left += [("m", "early", k) for k in range(MEM // local_len // 2)]
    left += [("m%d" % batch, "late", k) for batch in range(batches) for k in range(MEM // local_len // 2)]

    def do(name, what, k):
        if (name, what, k) not in left:
            return
        left.remove((name, what, k))
        if what == "early":
            early(k)
            return
        if what == "late":
            late(k, int(name[1:]))
            return
        group = groups[name]
        if what == "begin":
            for cp in placed[name]:
                cp.wait()
            group.begin()
        else:
            dict(line=group.line, turn=group.turn, finish=group.finish)[what](k)

    def run(point):
        for event in EVENTS[point]:
            do(*event)

    def complete(name):
        for event in [e for e in left if e[0] == name]:
            do(*event)

    placed = dict(f=[])
    run("f")

    for cp in raws[:5]:
        cp.wait()
    a_pack[...] = jnp.zeros_like(a_pack)
    norm_columns = norm_raw[...].astype(f32).T
    for side in range(SIDE):
        for h in range(HALF_HEADS):
            at = (side * HALF_HEADS + h) * HEAD_DIM
            for kind in range(2):
                col, src = (kind * HALF_HEADS + h) * PAD, kind * HEADS * HEAD_DIM + at
                a_pack[side, :, col : col + HEAD_DIM] = qk_raw[:, src : src + HEAD_DIM]
            for e in range(EXPERTS):
                col, src = W_QK + (e * HALF_HEADS + h) * PAD, e * HEADS * HEAD_DIM + at
                a_pack[side, :, col : col + HEAD_DIM] = value_raw[:, src : src + HEAD_DIM]
        routes = HALF_HEADS * EXPERTS
        for kind in range(2):
            src = (kind * SIDE + side) * routes
            a_pack[side, :, MISC + kind * routes : MISC + (kind + 1) * routes] = router_raw[:, src : src + routes]
        a_pack[side, :, MISC + COL_NORM : MISC + COL_NORM + 4] = norm_columns.astype(bf16)
        heads = bias_raw[side * HALF_HEADS : (side + 1) * HALF_HEADS].astype(f32).T
        tail = jnp.concatenate([heads, jnp.zeros((shard - per_device, HALF_HEADS), f32)], axis=0)
        a_pack[side, :, MISC + COL_BIAS : MISC + COL_BIAS + HALF_HEADS] = tail.astype(bf16)
    loc_a = local(a_pack.at[c], a_all.at[d, z, own], 17)
    rem_a = sibling(a_pack.at[1 - c], a_all.at[d, z, own], 3)
    rem_a.start()
    for cp in raws[7:]:
        cp.wait()
    row_ids = lax.broadcasted_iota(jnp.int32, (W_MISC, local_len), 0)
    for batch in range(batches):
        flags = [
            jnp.broadcast_to(raw[:, batch : batch + 1].astype(f32), (W_MISC, local_len)) for raw in (start_raw, count_raw)]
        for side in range(SIDE):
            rows_of = jnp.where(row_ids == 40, flags[0], jnp.where(row_ids == 41, flags[1], 0.0))
            for kind, raw in enumerate((vr_raw, or_raw)):
                for h in range(HALF_HEADS):
                    chosen = raw[batch, side * HALF_HEADS + h]
                    first = (kind * HALF_HEADS + h) * EXPERTS
                    expert = row_ids - first
                    hit = expert == chosen[0:1]
                    for k in range(1, TOPK):
                        hit = jnp.logical_or(hit, expert == chosen[k : k + 1])
                    inside = jnp.logical_and(row_ids >= first, row_ids < first + EXPERTS)
                    rows_of = jnp.where(jnp.logical_and(hit, inside), 1.0, rows_of)
            cols = pl.ds(2 * width + side * 128, 128)
            xs[c, pl.ds(batch * local_len, local_len), cols] = rows_of.T.astype(bf16)
    meta_cols = xs.at[c, :, pl.ds(2 * width, SIDE * 128)]
    rem_x.append(sibling(meta_cols, meta_cols, 2))
    rem_x[-1].start()
    loc_g = local(g_in, graw.at[c], 14)
    rem_g = sibling(g_in, graw.at[c], 4)
    rem_g.start()
    placed["a"] = (loc_a, rem_a)
    run("a")
    sel[...] = selector(c)

    for cp in loc_x + rem_x:
        cp.wait()
    step = 64

    def stats(i, carry):
        at = pl.ds(pl.multiple_of((i % (rows // step)) * step, step), step)
        block = i // (rows // step)
        values = xs[block, at, :width].astype(f32)
        centered = values - jnp.mean(values, axis=-1, keepdims=True)
        inverse = lax.rsqrt(jnp.mean(centered * centered, axis=-1, keepdims=True) + EPS)
        unit[pl.ds(pl.multiple_of(i * step, step), step)] = centered * inverse
        counts = xs[block, at, 2 * width : 2 * width + 128][:, 41:42].astype(f32)
        position = lax.broadcasted_iota(jnp.int32, (step, 1), 0) + (i * step) % local_len
        gradient = xs[block, at, width : 2 * width].astype(f32)
        xs[block, at, width : 2 * width] = jnp.where(position.astype(f32) < counts, gradient, 0.0).astype(bf16)
        return carry

    lax.fori_loop(0, both // step, stats, 0)
    run("stats")
    raws[6].wait()
    for side in range(SIDE):
        for p in range(4 * levels):
            src = (p * SIDE + side) * PAD
            i_pack[side, :, p * PAD : (p + 1) * PAD] = up_raw[:, src : src + PAD]
    raws[5].wait()
    o_pack[...] = jnp.zeros_like(o_pack)
    for side in range(SIDE):
        for h in range(HALF_HEADS):
            for e in range(EXPERTS):
                src = e * HEADS * HEAD_DIM + (side * HALF_HEADS + h) * HEAD_DIM
                col = (e * HALF_HEADS + h) * PAD
                o_pack[side, :, col : col + HEAD_DIM] = branch_raw[:, src : src + HEAD_DIM]
    loc_o = local(o_pack.at[c], o_all.at[d, z, own], 15)
    rem_o = sibling(o_pack.at[1 - c], o_all.at[d, z, own], 5)
    loc_i = local(i_pack.at[c], i_all.at[d, z, own], 16)
    rem_i = sibling(i_pack.at[1 - c], i_all.at[d, z, own], 6)
    rem_o.start()
    rem_i.start()
    placed["o"], placed["i"] = (loc_o, rem_o), (loc_i, rem_i)
    run("packs")

    slots = MEM // local_len
    has_up, has_down = z < levels - 1, z > 0

    def slot(s):
        return pl.ds(s * local_len, local_len)

    def starts_of(block, batch):
        column = xs[block, pl.ds(batch * local_len, local_len), 2 * width : 2 * width + 128]
        return column[:, 40:41].astype(f32)

    def spread_given(i, carry):
        at = pl.ds(pl.multiple_of((i % slots) * local_len, local_len), local_len)
        pair = i // slots
        mine = dot_f32(graw[pair // batches, pair % batches, at], sel[...])
        win[pair, at] = mine.astype(bf16)
        return carry

    def keep_or(block, batch, s, moved):
        at = block * batches + batch
        held = win[at, slot(s)]
        first = jnp.broadcast_to(starts_of(block, batch), held.shape) > 0.5
        win[at, slot(s)] = jnp.where(first, held.astype(f32), moved.astype(f32)).astype(bf16)

    def message(m, batch):
        src = win.at[batches + batch, pl.ds((slots - 1 - 2 * m) * local_len, 2 * local_len)]
        return pltpu.make_async_remote_copy(
            src_ref=src, dst_ref=rbuf.at[m, batch], send_sem=gsend.at[m, batch], recv_sem=grecv.at[m, batch],
            device_id=nb["up"], device_id_type=MESH)

    rounds = slots // 2

    def send_message(m, batch):
        if m < rounds:
            pl.when(has_up)(lambda: message(m, batch).start())

    def take(m, some):
        for batch in some:
            pl.when(has_down)(lambda: message(m, batch).wait_recv())
            for k in (0, 1):
                keep_or(0, batch, slots - 1 - 2 * m - k, rbuf[m, batch, slot(1 - k)])
            for s in (slots - 2 - 2 * m, slots - 3 - 2 * m):
                if s >= 0:
                    keep_or(1, batch, s, win[batch, slot(s + 1)])
            send_message(m + 1, batch)

    def early(m):
        pl.when(z <= m)(lambda: take(m, range(batches)))

    def late(m, batch):
        pl.when(z > m)(lambda: take(m, (batch,)))

    loc_g.wait()
    rem_g.wait()
    lax.fori_loop(0, 2 * batches * slots, spread_given, 0)
    run("given")
    complete("a")
    out_a = pltpu.make_async_copy(a_all, a_out, osem.at[0])
    out_a.start()

    w_a = a_all.reshape(4 * levels * 2 * shard, W_A)
    vec[...] = w_a[:, MISC:W_A].astype(f32).T

    def norm(i, carry):
        at = pl.ds(pl.multiple_of(i * step, step), step)
        act[at] = (unit[at] * vec[COL_NORM : COL_NORM + 1] + vec[COL_NORM + 1 : COL_NORM + 2]).astype(bf16)
        return carry

    lax.fori_loop(0, both // step, norm, 0)

    def project(i, carry):
        at = pl.ds(pl.multiple_of(i * 256, 256), 256)
        front[:, at] = dot_f32(act[...], w_a[:, at])
        return carry

    lax.fori_loop(0, MISC // 256, project, 0)
    front[:, MISC:W_A] = dot_f32(act[...], w_a[:, MISC:W_A])
    run("front")
    meta_at = pl.ds(pl.multiple_of(2 * width + c * 128, 128), 128)

    def gate(i, carry):
        at = pl.ds(pl.multiple_of(i * local_len, local_len), local_len)
        gated = jax.nn.sigmoid(front[at, MISC:W_A])
        gates[at] = gated
        picks = xs[i // batches, pl.ds(pl.multiple_of((i % batches) * local_len, local_len), local_len), meta_at]
        gated = gated * picks.astype(f32)
        for h in range(HALF_HEADS):
            total = jnp.zeros((local_len, PAD), f32)
            for e in range(EXPERTS):
                lane = h * EXPERTS + e
                col = W_QK + (e * HALF_HEADS + h) * PAD
                total = total + gated[:, lane : lane + 1] * front[at, col : col + PAD]
            win[i, pl.ds(MEM, local_len), wide + h * PAD : wide + (h + 1) * PAD] = total.astype(bf16)
        win[i, pl.ds(MEM, local_len), :wide] = front[at, wide : 2 * wide].astype(bf16)
        return carry

    lax.fori_loop(0, 2 * batches, gate, 0)

    for batch in range(batches):
        keep_or(1, batch, slots - 1, win[batch, pl.ds(MEM, local_len)])
        send_message(0, batch)
    run("cache")

    spread = MEM + 2 * local_len
    table = table_by_offset(w_a, per_device, shard, local_len, spread)
    for h in range(HALF_HEADS):
        line = jnp.broadcast_to(table[COL_BIAS + h : COL_BIAS + h + 1], (local_len, spread))
        turned = pltpu.roll(line, spread - local_len + 1, 1, stride=1, stride_axis=0)
        bias[h] = turned[:, : MEM + local_len]
    run("memory")
    complete("m")
    complete("m0")

    key_ids = lax.broadcasted_iota(jnp.int32, (local_len, local_len), 1)
    row_ids = lax.broadcasted_iota(jnp.int32, (local_len, local_len), 0)

    def probs_copy(i, slot_of):
        return pltpu.make_async_copy(probs.at[slot_of], probs_out.at[i], psem.at[slot_of])

    def pair_of(n):
        return (n % 2) * batches + n // 2

    def attend(n, carry):
        i = pair_of(n)
        at = pl.ds(pl.multiple_of(i * local_len, local_len), local_len)
        block, batch = i // batches, i % batches
        rows_at = pl.ds(pl.multiple_of(batch * local_len, local_len), local_len)
        count = xs[block, rows_at, 2 * width : 2 * width + 128][:, 41:42].astype(f32)
        seen = jnp.logical_and(key_ids <= row_ids, key_ids.astype(f32) < count)
        picks = xs[block, rows_at, meta_at].astype(f32) * gates[at]
        slot_of = lax.rem(n, 2)
        pl.when(n >= 2)(lambda: probs_copy(pair_of(n - 2), slot_of).wait())
        for h in range(HALF_HEADS):
            cols = slice(h * PAD, (h + 1) * PAD)
            q = front[at, cols].astype(bf16)
            s = dot_f32(q, win[i, :, cols], NT) * SCALE + bias[h]
            s = jnp.concatenate([s[:, :MEM], jnp.where(seen, s[:, MEM:], NEG)], axis=1)
            top = jnp.max(s, axis=-1, keepdims=True)
            expo = jnp.exp(s - top)
            p = expo * (1.0 / jnp.sum(expo, axis=-1, keepdims=True))
            probs[slot_of, h] = p
            p = p.astype(bf16)
            got = dot_f32(p, win[i, :, wide + h * PAD : wide + (h + 1) * PAD]).astype(bf16)
            att[at, cols] = got
            got = got.astype(f32)
            for e in range(EXPERTS):
                lane = HALF_HEADS * EXPERTS + h * EXPERTS + e
                col = (e * HALF_HEADS + h) * PAD
                mixed[at, col : col + PAD] = (picks[:, lane : lane + 1] * got).astype(bf16)
        probs_copy(i, slot_of).start()
        return carry

    lax.fori_loop(0, 2, attend, 0)
    run("half")
    for batch in range(1, batches):
        complete("m%d" % batch)
    out_w = pltpu.make_async_copy(win, win_out, osem.at[1])
    out_w.start()
    lax.fori_loop(2, 2 * batches, attend, 0)
    for n in range(2 * batches - 2, 2 * batches):
        probs_copy(pair_of(n), n % 2).wait()
    run("attended")
    complete("o")

    w_o = o_all.reshape(4 * levels * 2 * shard, W_O)
    branch = unit
    far = pl.ds(pl.multiple_of((1 - c) * rows, rows), rows)
    near = pl.ds(pl.multiple_of(c * rows, rows), rows)

    def out_project(at):
        def body(i, carry):
            cols = pl.ds(pl.multiple_of(i * 256, 256), 256)
            branch[at, cols] = dot_f32(mixed[at], w_o[cols], NT)
            return carry

        lax.fori_loop(0, width // 256, body, 0)

    def exchange(src, dst, index):
        return pltpu.make_async_remote_copy(
            src_ref=src, dst_ref=dst, send_sem=esend.at[index], recv_sem=erecv.at[index],
            device_id=nb["c"], device_id_type=MESH)

    out_project(far)
    give = exchange(branch.at[far], arrived, 0)
    give.start()
    run("far")
    out_project(near)
    out_o = pltpu.make_async_copy(o_all, o_out, osem.at[2])
    out_o.start()
    give.wait_recv()

    def second(i, carry):
        at = pl.ds(pl.multiple_of(i * step, step), step)
        total_at = pl.ds(pl.multiple_of(c * rows + i * step, step), step)
        values = xs[c, at, :width].astype(f32) + branch[total_at] + arrived[at]
        hidden[at] = values
        centered = values - jnp.mean(values, axis=-1, keepdims=True)
        inverse = lax.rsqrt(jnp.mean(centered * centered, axis=-1, keepdims=True) + EPS)
        normed = centered * inverse * vec[COL_NORM + 2 : COL_NORM + 3] + vec[COL_NORM + 3 : COL_NORM + 4]
        n2[total_at] = normed.astype(bf16)
        return carry

    lax.fori_loop(0, rows // step, second, 0)
    pair = exchange(n2.at[near], n2.at[near], 1)
    pair.start()
    run("pair")
    pair.wait_recv()
    outs = [
        pltpu.make_async_copy(src, dst, osem.at[3 + i])
        for i, (src, dst) in enumerate((
            (xs, xs_out), (act, act_out), (front, front_out), (gates, gates_out),
            (att, att_out), (mixed, mixed_out), (hidden, hidden_out), (n2, n2_out), (vec, vec_out)))
    ]
    for cp in outs:
        cp.start()
    complete("i")
    out_i = pltpu.make_async_copy(i_all, i_out, osem.at[13])
    out_i.start()

    w_i = i_all.reshape(4 * levels * 2 * shard, i_all.shape[3])

    def activate(i, carry):
        at = pl.ds(pl.multiple_of(i * 256, 256), 256)
        pre = dot_f32(n2[...], w_i[:, at])
        below = 0.5 * (1.0 + lax.erf(pre * 0.7071067811865476))
        ffn[:, at] = (pre * below).astype(bf16)
        slope[:, at] = (below + pre * jnp.exp(-0.5 * pre * pre) * 0.3989422804014327).astype(bf16)
        return carry

    steps = ffn.shape[1] // 256
    lax.fori_loop(0, steps, activate, 0)
    run("activated")
    outs += [pltpu.make_async_copy(ffn, ffn_out, osem.at[14]), pltpu.make_async_copy(slope, slope_out, osem.at[15])]
    outs[-2].start()
    outs[-1].start()

    for m in range(rounds):
        for batch in range(batches):
            pl.when(has_up)(lambda: message(m, batch).wait_send())
    out_w.wait()
    span = ffn.shape[1] // 4
    half = width // 2

    def ffn_grad(i, carry):
        at = pl.ds(pl.multiple_of(i * span, span), span)
        for side in range(2):
            cols = slice(width + side * half, width + (side + 1) * half)
            left = jnp.concatenate([xs[0, :, cols], xs[1, :, cols]], axis=0)
            win[i, side * span : (side + 1) * span] = dot_f32(ffn[:, at], left, TN).astype(bf16)
        return carry

    lax.fori_loop(0, 4, ffn_grad, 0)
    for column in range(4):
        for side in range(2):
            outs.append(pltpu.make_async_copy(
                win.at[column, pl.ds(side * span, span)],
                fgrad_out.at[column, :, pl.ds(side * half, half)], osem.at[16 + 2 * column + side]))
            outs[-1].start()
    complete("f")
    for group in (ga, go, gi, gf):
        group.drain()
    for cp in (give, pair):
        cp.wait_send()
    out_a.wait()
    out_o.wait()
    out_i.wait()
    for cp in outs:
        cp.wait()


def forward(levels, batches, local_len, per_device, ins):
    bf16, f32 = jnp.bfloat16, jnp.float32
    shape = jax.ShapeDtypeStruct
    qk, value, router, norms, bias_in, branch, up, f, tokens, cot, vr, outr, start, count, g = ins
    shard, width = qk.shape[0], f.shape[1]
    a, o, i = [shape((SIDE, shard, w), bf16) for w in (W_A, W_O, up.shape[1] // SIDE)]
    x = shape((tokens.shape[0], 2 * width + SIDE * 128), bf16)
    rows = batches * local_len
    both = 2 * rows
    wide = HALF_HEADS * PAD
    two = lambda v: (4, levels, 2 * v.shape[1], v.shape[2])
    window = (2 * batches, MEM + local_len, 2 * wide)
    probs = (2 * batches, HALF_HEADS, local_len, MEM + local_len)
    outs = [
        (two(a), bf16), (two(o), bf16), (two(i), bf16), ((4, levels) + f.shape, bf16),
        ((2,) + x.shape, bf16), ((both, width), bf16), ((both, W_A), f32), ((both, W_MISC), f32),
        (window, bf16), (probs, f32), ((both, wide), bf16), ((both, W_O), bf16),
        ((rows, width), f32), ((both, width), bf16), ((W_MISC, width), f32), ((both, i.shape[2]), bf16),
        ((both, i.shape[2]), bf16), ((4, i.shape[2] // 4, width), bf16),
    ]
    rounds = MEM // local_len // 2
    scratch = [
        (two(a), bf16), (two(o), bf16), (two(i), bf16), ((2,) + x.shape, bf16), ((2,) + g.shape, bf16),
        (window, bf16), ((rounds, batches, 2 * local_len, 2 * wide), bf16), ((g.shape[2], 2 * wide), bf16),
        ((both, width), f32), ((both, width), bf16), ((both, W_A), f32), ((both, W_MISC), f32),
        ((W_MISC, width), f32), ((HALF_HEADS, local_len, MEM + local_len), f32), ((2,) + probs[1:], f32),
        ((both, wide), bf16), ((both, W_O), bf16), ((rows, width), f32),
        ((rows, width), f32), ((both, width), bf16), ((both, i.shape[2]), bf16), ((both, i.shape[2]), bf16),
    ]
    rounds = MEM // local_len // 2
    scratch += [(w.shape, w.dtype) for w in (qk, value, router, norms, bias_in, branch, up, vr, outr, start, count, f, a, o, i)]
    sems = [(4, 6 * levels), (4, 6 * levels), (7,), (7,), (19,), (rounds, batches), (rounds, batches), (2,), (2,), (24,), (2,)]
    hbm = pl.BlockSpec(memory_space=pl.ANY)
    return pl.pallas_call(
        functools.partial(forward_kernel, levels, batches, local_len, per_device),
        out_shape=[jax.ShapeDtypeStruct(s, k) for s, k in outs],
        in_specs=[hbm] * len(ins),
        out_specs=[hbm] * len(outs),
        scratch_shapes=[pltpu.VMEM(s, k) for s, k in scratch] + [pltpu.SemaphoreType.DMA(s) for s in sems],
        compiler_params=pltpu.CompilerParams(
            collective_id=1, has_side_effects=True, vmem_limit_bytes=VMEM_BYTES),
    )(*ins)


def add_rows(dst, terms):
    rows, width = dst.shape
    step = 16

    def body(i, carry):
        at = pl.ds(pl.multiple_of(i * step, step), step)
        total = terms[0][at].astype(jnp.float32)
        for term in terms[1:]:
            total = total + term[at].astype(jnp.float32)
        dst[at] = total.astype(dst.dtype)
        return carry

    lax.fori_loop(0, rows // step, body, 0)


class Scatter:
    def __init__(self, src, view, sems, nb, d, z, levels, total):
        self.src, self.view, self.nb, self.d, self.z, self.levels = src, view, nb, d, z, levels
        self.send, self.recv = sems
        self.sum = total
        self.half = src.shape[2] // 2
        self.by_x, self.by_y = d + 1 - 2 * (d % 2), (d + 2) % 4
        self.low, self.high = pl.ds(0, self.half), pl.ds(self.half, self.half)

    def copy(self, src, dst, slot, to):
        return pltpu.make_async_remote_copy(
            src_ref=src, dst_ref=dst, send_sem=self.send.at[slot], recv_sem=self.recv.at[slot],
            device_id=self.nb[to], device_id_type=MESH)

    def corner(self, j, to):
        part, name, base = (self.low, "cx", 0) if to == "x" else (self.high, "cy", self.levels)
        return self.copy(self.src.at[3 - self.d, j, part], self.view(name, j), base + j, to)

    def direct(self, j, to):
        if to == "x":
            column, part, name, base = self.by_x, self.low, "rx", 2 * self.levels
        else:
            column, part, name, base = self.by_y, self.high, "ry", 3 * self.levels
        return self.copy(self.src.at[column, j, part], self.view(name, j).at[part], base + j, to)

    def relay(self, j, to):
        if to == "x":
            held, part, name, base = "cy", self.high, "rx", 4 * self.levels
        else:
            held, part, name, base = "cx", self.low, "ry", 5 * self.levels
        return self.copy(self.view(held, j), self.view(name, j).at[part], base + j, to)

    def along(self, j, to, first=False):
        base = (6 if to == "up" else 7) * self.levels
        there = self.view(to, j, self.z + (1 if to == "up" else -1))
        return self.copy(self.view("rx" if first else to, j), there, base + j, to)

    def issue(self, j):
        self.corner(j, "x").start()
        self.corner(j, "y").start()
        self.direct(j, "x").start()
        self.direct(j, "y").start()

    def turn(self, j):
        self.corner(j, "x").wait_recv()
        add_rows(self.view("cx", j), [self.view("cx", j), self.src.at[self.by_y, j, self.low]])
        self.relay(j, "y").start()
        self.corner(j, "y").wait_recv()
        add_rows(self.view("cy", j), [self.view("cy", j), self.src.at[self.by_x, j, self.high]])
        self.relay(j, "x").start()

    def column(self, j):
        for to in ("x", "y"):
            self.direct(j, to).wait_recv()
            self.relay(j, to).wait_recv()
        add_rows(self.view("rx", j), [self.view("rx", j), self.view("ry", j), self.src.at[self.d, j]])

    def lift(self, j, stage):
        def hop(to):
            if stage:
                self.along(j, to).wait_recv()
                add_rows(self.view(to, j), [self.view(to, j), self.view("rx", j)])
            self.along(j, to, first=stage == 0).start()

        if stage < j:
            pl.when(self.z == stage)(lambda: hop("up"))
        if self.levels - 1 - stage > j:
            pl.when(self.z == self.levels - 1 - stage)(lambda: hop("down"))

    def total(self, j):
        @pl.when(self.z == j)
        def _():
            terms = [self.view("rx", j)]
            for to, there in (("up", j > 0), ("down", j < self.levels - 1)):
                if there:
                    self.along(j, to).wait_recv()
                    terms.append(self.view(to, j))
            add_rows(self.sum, terms)

    def drain(self):
        for j in range(self.levels):
            for to in ("x", "y"):
                self.corner(j, to).wait_send()
                self.direct(j, to).wait_send()
                self.relay(j, to).wait_send()
            pl.when(self.z < j)(lambda: self.along(j, "up").wait_send())
            pl.when(self.z > j)(lambda: self.along(j, "down").wait_send())


class LineFirst:
    def __init__(self, src, view, bufs, sems, nb, d, z, levels, total):
        self.src, self.view, self.nb, self.d, self.z, self.levels = src, view, nb, d, z, levels
        self.cx, self.cy, self.rx, self.ry = bufs
        self.send, self.recv = sems
        self.sum = total
        half = src.shape[2] // 2
        self.by_x, self.by_y = d + 1 - 2 * (d % 2), (d + 2) % 4
        self.low, self.high = pl.ds(0, half), pl.ds(half, half)

    def copy(self, src, dst, slot, to):
        return pltpu.make_async_remote_copy(
            src_ref=src, dst_ref=dst, send_sem=self.send.at[slot], recv_sem=self.recv.at[slot],
            device_id=self.nb[to], device_id_type=MESH)

    def along(self, j, column, to, level, first=False):
        slot = (0 if to == "up" else 4 * self.levels) + 4 * j + column
        after = level + (1 if to == "up" else -1)
        src = self.src.at[column, j] if first else self.view(j, column)
        return self.copy(src, self.view(self.levels if to == "down" and after == j else j, column), slot, to)

    def lift(self, j, stage):
        def hop(to, level):
            for column in range(4):
                if stage:
                    before = level - (1 if to == "up" else -1)
                    self.along(j, column, to, before).wait_recv()
                    held = self.view(j, column)
                    add_rows(held, [held, self.src.at[column, j]])
                self.along(j, column, to, level, first=stage == 0).start()

        if stage < j:
            pl.when(self.z == stage)(lambda: hop("up", stage))
        if self.levels - 1 - stage > j:
            pl.when(self.z == self.levels - 1 - stage)(lambda: hop("down", self.levels - 1 - stage))

    def gathered(self, j):
        @pl.when(self.z == j)
        def _():
            for column in range(4):
                terms = [self.src.at[column, j]]
                if j > 0:
                    self.along(j, column, "up", j - 1).wait_recv()
                    terms.append(self.view(j, column))
                if j < self.levels - 1:
                    self.along(j, column, "down", j + 1).wait_recv()
                    terms.append(self.view(self.levels, column))
                add_rows(terms[0], terms)

    def plane(self, k):
        base = 8 * self.levels
        part = lambda column, rows: self.src.at[column, self.z, rows]
        return (
            self.copy(part(3 - self.d, self.low), self.cx, base, "x"),
            self.copy(part(3 - self.d, self.high), self.cy, base + 1, "y"),
            self.copy(part(self.by_x, self.low), self.rx.at[self.low], base + 2, "x"),
            self.copy(part(self.by_y, self.high), self.ry.at[self.high], base + 3, "y"),
            self.copy(self.cy, self.rx.at[self.high], base + 4, "x"),
            self.copy(self.cx, self.ry.at[self.low], base + 5, "y"),
        )[k]

    def issue(self):
        for k in range(4):
            self.plane(k).start()

    def turn(self):
        self.plane(0).wait_recv()
        add_rows(self.cx, [self.cx, self.src.at[self.by_y, self.z, self.low]])
        self.plane(5).start()
        self.plane(1).wait_recv()
        add_rows(self.cy, [self.cy, self.src.at[self.by_x, self.z, self.high]])
        self.plane(4).start()

    def column(self):
        for k in range(2, 6):
            self.plane(k).wait_recv()
        add_rows(self.sum, [self.rx, self.ry, self.src.at[self.d, self.z]])

    def drain(self):
        for k in range(6):
            self.plane(k).wait_send()
        for j in range(self.levels):
            for column in range(4):
                for level in range(self.levels):
                    if level < j:
                        pl.when(self.z == level)(lambda: self.along(j, column, "up", level).wait_send())
                    if level > j:
                        pl.when(self.z == level)(lambda: self.along(j, column, "down", level).wait_send())


A_PARTS = (1024, 768)
AHEAD = 3


def LAGS(unit, k, levels):
    return 2 + 3 * k if unit < 3 * levels else 1 + k


O_STEPS = {4: ((0, 1), (1, 0)), 6: ((1, 1),), 7: ((2, 0), (2, 1))}


class Pipeline:
    def __init__(self, units, levels, ahead, lags):
        self.units, self.levels, self.ahead, self.now = units, levels, ahead, 0
        self.follow = [lambda s, j: s.column(j)]
        for stage in range(levels - 1):
            self.follow.append(lambda s, j, stage=stage: s.lift(j, stage))
        self.follow.append(lambda s, j: s.total(j))
        self.lags = lags
        self.done = [0] * len(units)

    def each(self, n, act):
        if 0 <= n < len(self.units):
            for scatter, j in self.units[n]:
                act(scatter, j)

    def begin(self):
        for n in range(self.ahead):
            self.each(n, lambda s, j: s.issue(j))

    def advance(self, n):
        self.each(n, self.follow[self.done[n]])
        self.done[n] += 1

    def step(self):
        n = self.now
        if n < len(self.units):
            self.each(n, lambda s, j: s.turn(j))
            self.each(n + self.ahead, lambda s, j: s.issue(j))
        for m in range(min(n + 1, len(self.units))):
            while self.done[m] < len(self.follow) and n - m >= self.lags(m, self.done[m], self.levels):
                self.advance(m)
        self.now += 1

    def turns(self):
        while self.now < len(self.units):
            self.step()

    def round(self):
        for m in range(len(self.units)):
            if self.done[m] < len(self.follow):
                self.advance(m)

    def finish(self):
        while min(self.done) < len(self.follow):
            self.round()


def norm_rows(values):
    centered = values - jnp.mean(values, axis=-1, keepdims=True)
    inverse = lax.rsqrt(jnp.mean(centered * centered, axis=-1, keepdims=True) + EPS)
    return centered * inverse, inverse


def norm_rows_backward(upstream, normed, inverse, gain):
    scaled = upstream * gain
    inside = (
        scaled
        - jnp.mean(scaled, axis=-1, keepdims=True)
        - normed * jnp.mean(scaled * normed, axis=-1, keepdims=True)
    )
    return inside * inverse


VEC_ROW = COL_NORM // 8 * 8
VEC_GAIN = COL_NORM - VEC_ROW


def backward_kernel(
    levels, batches, local_len, per_device, shard,
    fgrad_in, wf_in, wi_in, wo_in, wa_in, ffn_in, slope_in, xs_in, n2_in, hidden_in, vec_in, att_in, gates_in, front_in,
    win_in, probs_in, mixed_in, act_in,
    f_out, i_out, o_out, a_out, m_out, layer_out, grad_out,
    w_f, w_i, ffn, slope, grad, meta, n2, hidden, vec, att, gates, front, win, probs,
    branch, arrived, dhid, db, dmix, dfront, dsum, norms,
    f_total, i_total, o_total, a_total, m_total, *rest,
):
    bf16, f32 = jnp.bfloat16, jnp.float32
    f_bufs, i_bufs, m_bufs = rest[:6], rest[6:12], rest[12:18]
    a_src, a_cx, a_cy, o_src, o_line, o_cx, o_cy, o_rx, o_ry = rest[18:27]
    send, recv, osend, orecv, lsem, tsem, esend, erecv, osem, ready, freed = rest[27:]
    d, t = lax.axis_index("doc"), lax.axis_index("tm")
    z, c = t // 2, t % 2
    nb = neighbours(2 * levels)
    width = w_f.shape[1]
    rows = batches * local_len
    both = 2 * rows
    wide = HALF_HEADS * PAD
    ff = ffn.shape[1]
    far = pl.ds(pl.multiple_of((1 - c) * rows, rows), rows)
    near = pl.ds(pl.multiple_of(c * rows, rows), rows)

    def load(src, dst, index):
        cp = pltpu.make_async_copy(src, dst, lsem.at[index])
        cp.start()
        return cp

    meta_at = pl.ds(pl.multiple_of(2 * width + c * 128, 128), 128)
    l_first = load(fgrad_in, f_bufs[0], 17)
    l_grad = load(xs_in.at[:, :, pl.ds(width, width)], grad, 1)
    l_wf = load(wf_in, w_f, 2)
    enter(nb, z, levels)
    l_first.wait()
    l_slope = load(slope_in, slope, 3)
    l_ffn = load(ffn_in, ffn, 0)
    l_n2 = load(n2_in, n2, 4)
    l_wi = load(wi_in, w_i, 5)
    l_hid = load(hidden_in, hidden, 6)
    l_vec = load(vec_in.at[pl.ds(VEC_ROW, 8)], vec, 7)
    l_mixed = load(mixed_in, dmix, 8)
    l_meta = load(xs_in.at[:, :, meta_at], meta, 9)
    l_att = load(att_in, att, 10)
    l_gates = load(gates_in, gates, 11)
    w_o = a_src.at[:, :, :, pl.ds(0, W_O)]
    l_wo = load(wo_in, w_o, 12)

    def tiles(i):
        at = pl.ds(i * local_len, local_len)
        return [
            pltpu.make_async_copy(win_in.at[i], win.at[i % 2], tsem.at[0, i % 2]),
            pltpu.make_async_copy(front_in.at[at, pl.ds(0, wide)], front.at[i % 2, :, pl.ds(0, wide)], tsem.at[2, i % 2]),
            pltpu.make_async_copy(
                front_in.at[at, pl.ds(W_QK, W_VAL)], front.at[i % 2, :, pl.ds(wide, W_VAL)], tsem.at[3, i % 2]),
        ]

    def probs_tile(n):
        return pltpu.make_async_copy(probs_in.at[n // HALF_HEADS, n % HALF_HEADS], probs.at[n % 2], tsem.at[1, n % 2])

    for cp in tiles(0):
        cp.start()
    probs_tile(0).start()

    names = ("cx", "cy", "rx", "ry")

    def plain(bufs):
        def view(name, j, level=z):
            if name == "up":
                return bufs[5].at[j]
            if name == "down":
                return bufs[5].at[jnp.where(level == j, levels, j)]
            return bufs[1 + names.index(name)].at[j]

        return view

    block_rows = shard * SIDE

    def within(held, cx, cy, cols):
        def view(name, j, level=z):
            if name in ("cx", "cy"):
                return (cx if name == "cx" else cy).at[j, :, cols]
            ref, base = held[name]
            return ref.at[pl.ds(base + j * block_rows, block_rows), cols]

        return view

    span = levels * block_rows
    a_held = dict(rx=(w_i, 0), ry=(w_i, span), up=(w_i, 2 * span), down=(w_i, 3 * span))
    a_cols = [pl.ds(sum(A_PARTS[:k]), A_PARTS[k]) for k in range(len(A_PARTS))]
    sums = [
        Scatter(src, view, (send.at[i], recv.at[i]), nb, d, z, levels, total)
        for i, (src, view, total) in enumerate((
            (f_bufs[0], plain(f_bufs), f_total), (i_bufs[0], plain(i_bufs), i_total),
            (m_bufs[0], plain(m_bufs), m_total)) + tuple(
                (a_src.at[:, :, :, cols], within(a_held, a_cx, a_cy, cols), a_total.at[:, cols]) for cols in a_cols))
    ]
    sf, si, sm = sums[:3]
    held = []
    for ref in (ffn, slope):
        for base in range(0, ref.shape[0], 4 * block_rows):
            held.append((ref, base))
    held = held[:levels] + [(o_line, 0)]

    def o_view(slot, column):
        ref, base = held[slot]
        return ref.at[pl.ds(base + column * block_rows, block_rows), pl.ds(0, W_O)]

    so = LineFirst(o_src, o_view, (o_cx, o_cy, o_rx, o_ry), (osend, orecv), nb, d, z, levels, o_total)
    order = []
    for k in range((levels + 1) // 2):
        order += [levels - 1 - k, k] if levels - 1 - k != k else [k]
    units = [[(s, j)] for s in [sf, si] + sums[3:] for j in order]
    units[3 * levels + 1] = units[3 * levels + 1] + [(sm, j) for j in order]
    line = Pipeline(units, levels, AHEAD, LAGS)

    def exchange(src, dst, index):
        return pltpu.make_async_remote_copy(
            src_ref=src, dst_ref=dst, send_sem=esend.at[index], recv_sem=erecv.at[index],
            device_id=nb["c"], device_id_type=MESH)

    def weight_grad(dst, left, right, chunk, total, column):
        at = pl.ds(pl.multiple_of(column * span, span), span)

        def body(i, carry):
            cols = pl.ds(pl.multiple_of(i * chunk, chunk), chunk)
            got = dot_f32(left[:, at], right[:, cols], TN).astype(bf16)
            dst[column, :, :, cols] = got.reshape(levels, block_rows, chunk)
            return carry

        lax.fori_loop(0, total // chunk, body, 0)

    line.begin()

    l_wf.wait()
    l_slope.wait()
    l_grad.wait()
    g_all = grad.reshape(both, width)

    def back(i, carry):
        at = pl.ds(pl.multiple_of(i * 256, 256), 256)
        slope[:, at] = (dot_f32(g_all[...], w_f[at], NT) * slope[:, at].astype(f32)).astype(bf16)
        return carry

    lax.fori_loop(0, ff // 256, back, 0)
    l_n2.wait()
    for column in range(4):
        weight_grad(i_bufs[0], n2, slope, 512, ff, column)
    line.step()

    l_wi.wait()

    def times(src, weights, dims):
        def run(at):
            def body(i, carry):
                cols = pl.ds(pl.multiple_of(i * 256, 256), 256)
                branch[at, cols] = dot_f32(src[at], weights(cols), dims)
                return carry

            lax.fori_loop(0, width // 256, body, 0)

        return run

    through_in = times(slope, lambda cols: w_i[cols], NT)
    through_in(far)
    give = exchange(branch.at[far], arrived, 0)
    give.start()
    through_in(near)
    line.step()
    l_hid.wait()
    l_vec.wait()
    give.wait()
    norms[...] = jnp.zeros_like(norms)
    step = 64

    def second(i, carry):
        at = pl.ds(pl.multiple_of(i * step, step), step)
        total_at = pl.ds(pl.multiple_of(c * rows + i * step, step), step)
        normed, inverse = norm_rows(hidden[at])
        up = branch[total_at] + arrived[at]
        norms[COL_NORM + 2 : COL_NORM + 3] += jnp.sum(up * normed, axis=0, keepdims=True)
        norms[COL_NORM + 3 : COL_NORM + 4] += jnp.sum(up, axis=0, keepdims=True)
        got = norm_rows_backward(up, normed, inverse, vec[VEC_GAIN + 2 : VEC_GAIN + 3])
        got = got + grad[c, at].astype(f32)
        dhid[at] = got
        db[total_at] = got.astype(bf16)
        return carry

    lax.fori_loop(0, rows // step, second, 0)
    pair = exchange(db.at[near], db.at[near], 1)
    pair.start()
    l_act = load(act_in, grad, 13)

    through_out = times(ffn, lambda cols: w_f[:, cols], (((1,), (0,)), ((), ())))
    l_ffn.wait()
    through_out(far)
    pair.wait()
    last = exchange(branch.at[far], arrived, 2)
    last.start()
    line.step()
    through_out(near)

    for name in ("x", "y"):
        pl.semaphore_signal(ready, inc=1, device_id=nb[name], device_id_type=MESH)
    for name, there in (("up", z < levels - 1), ("down", z > 0)):

        @pl.when(there)
        def _():
            pl.semaphore_signal(ready, inc=1, device_id=nb[name], device_id_type=MESH)

    l_wa = [
        load(wa_in.at[:, pl.ds(0, width)], w_f.at[pl.ds(0, width)], 14),
        load(wa_in.at[:, pl.ds(width, W_A - width)], w_f.at[pl.ds(width, width), pl.ds(0, W_A - width)], 15),
    ]
    l_mixed.wait()
    for column in range(4):
        weight_grad(o_src, db, dmix, 640, W_O, column)
    ends = jnp.where(z < levels - 1, 1, 0) + jnp.where(z > 0, 1, 0)
    pl.semaphore_wait(ready, 2 + ends)
    outer, inner_levels = order[:2], order[2:]

    def o_stage(stage, part):
        for j in part:
            so.lift(j, stage)

    def tick():
        for stage, part in O_STEPS.get(line.now, ()):
            if stage < levels - 1:
                o_stage(stage, outer if part == 0 else inner_levels)
        line.step()

    o_stage(0, outer)
    l_wo.wait()

    def mix(i, carry):
        cols = pl.ds(pl.multiple_of(i * wide, wide), wide)
        dmix[:, cols] = dot_f32(db[...], a_src[:, :, :, cols].reshape(width, wide)).astype(bf16)
        return carry

    lax.fori_loop(0, EXPERTS, mix, 0)
    l_meta.wait()
    l_att.wait()
    l_gates.wait()
    dsum[...] = jnp.zeros_like(dsum)
    lanes = lax.broadcasted_iota(jnp.int32, (local_len, W_MISC), 1)

    def attend(i):
        slot = i % 2
        if i + 1 < 2 * batches:
            for cp in tiles(i + 1):
                cp.start()
        for cp in tiles(i):
            cp.wait()
        at = pl.ds(i * local_len, local_len)
        block, batch = i // batches, i % batches
        gate = gates[at]
        picks = meta[block, pl.ds(batch * local_len, local_len)].astype(f32)
        gated = gate * picks
        d_gates = jnp.zeros((local_len, W_MISC), f32)
        for h in range(HALF_HEADS):
            cols = slice(h * PAD, (h + 1) * PAD)
            v_cols = slice(wide + h * PAD, wide + (h + 1) * PAD)
            got = att[at, cols].astype(f32)
            d_att = jnp.zeros((local_len, PAD), f32)
            for e in range(EXPERTS):
                lane = HALF_HEADS * EXPERTS + h * EXPERTS + e
                col = (e * HALF_HEADS + h) * PAD
                part = dmix[at, col : col + PAD].astype(f32)
                d_att = d_att + gated[:, lane : lane + 1] * part
                d_gates = jnp.where(lanes == lane, jnp.sum(part * got, axis=-1, keepdims=True), d_gates)
            d_att = d_att.astype(bf16)
            n = i * HALF_HEADS + h
            if n + 1 < 2 * batches * HALF_HEADS:
                probs_tile(n + 1).start()
            probs_tile(n).wait()
            p = probs[n % 2]
            d_p = dot_f32(d_att, win[slot, :, v_cols], NT)
            delta = jnp.sum(d_p * p, axis=-1, keepdims=True)
            d_s = p * (d_p - delta)
            dsum[h] += d_s
            d_s = d_s.astype(bf16)
            q = front[slot, :, cols].astype(bf16)
            d_q = dot_f32(d_s, win[slot, :, cols]) * SCALE
            d_k = dot_f32(d_s[:, MEM:], q, TN) * SCALE
            d_v = dot_f32(p[:, MEM:].astype(bf16), d_att, TN).astype(bf16).astype(f32)
            dfront[at, cols] = d_q.astype(bf16)
            dfront[at, wide + h * PAD : wide + (h + 1) * PAD] = d_k.astype(bf16)
            for e in range(EXPERTS):
                lane = h * EXPERTS + e
                col = W_QK + (e * HALF_HEADS + h) * PAD
                part = front[slot, :, col - W_QK + wide : col - W_QK + wide + PAD]
                d_gates = jnp.where(lanes == lane, jnp.sum(part * d_v, axis=-1, keepdims=True), d_gates)
                dfront[at, col : col + PAD] = (gated[:, lane : lane + 1] * d_v).astype(bf16)
        d_logits = jnp.where(lanes < N_ROUTE, d_gates * picks * gate * (1.0 - gate), 0.0)
        dfront[at, MISC:W_A] = d_logits.astype(bf16)

    attend(0)
    tick()
    attend(1)
    tick()
    for i in range(2, 2 * batches):
        attend(i)
    l_act.wait()
    one_all = grad.reshape(both, width)
    for column in range(4):
        weight_grad(a_src, one_all, dfront, 896, MISC, column)
    tick()
    last.wait()

    def final(i, carry):
        at = pl.ds(pl.multiple_of(i * step, step), step)
        total_at = pl.ds(pl.multiple_of(c * rows + i * step, step), step)
        tail = meta[c, at].astype(f32)
        position = lax.broadcasted_iota(jnp.int32, (step, 1), 0) + (i * step) % local_len
        keep = position.astype(f32) < tail[:, 41:42]
        total = hidden[at] + branch[total_at] + arrived[at]
        db[total_at] = jnp.where(keep, total, 0.0).astype(bf16)
        return carry

    lax.fori_loop(0, rows // step, final, 0)
    pl.semaphore_signal(freed, inc=1, device_id=nb["c"], device_id_type=MESH)
    outs = [pltpu.make_async_copy(db.at[near], layer_out, osem.at[0])]
    outs[0].start()

    tick()
    for cp in l_wa:
        cp.wait()

    def through_front(at):
        def body(i, carry):
            cols = pl.ds(pl.multiple_of(i * 256, 256), 256)
            below = pl.ds(pl.multiple_of(width + i * 256, 256), 256)
            branch[at, cols] = (
                dot_f32(dfront[at, :width], w_f[cols], NT)
                + dot_f32(dfront[at, width:], w_f[below, : W_A - width], NT))
            return carry

        lax.fori_loop(0, width // 256, body, 0)

    through_front(far)
    hand = exchange(branch.at[far], arrived, 3)
    pl.semaphore_wait(freed, 1)
    hand.start()
    through_front(near)
    tick()

    spread = MEM + 2 * local_len
    ids = lax.broadcasted_iota(jnp.int32, (local_len, 1), 0)
    lines = []
    for h in range(HALF_HEADS):
        turned = jnp.concatenate([dsum[h], jnp.zeros((local_len, local_len), f32)], axis=1)
        bit = 1
        while bit < local_len:
            moved = pltpu.roll(turned, bit, 1)
            turned = jnp.where(((local_len - 1 - ids) // bit) % 2 == 1, moved, turned)
            bit *= 2
        lines.append(jnp.sum(turned, axis=0, keepdims=True))
    row_of = lax.broadcasted_iota(jnp.int32, (W_MISC, spread), 0)
    table = jnp.zeros((W_MISC, spread), f32)
    for h in range(HALF_HEADS):
        table = jnp.where(row_of == COL_BIAS + h, lines[h], table)
    high = table.astype(bf16)
    low = (table - high.astype(f32)).astype(bf16)
    distance = MEM + local_len - 1 - lax.broadcasted_iota(jnp.int32, (1, spread), 1)
    bucket = bucket_index(distance)
    wanted = (bucket // per_device) * shard + bucket % per_device
    hand.wait()

    def first(i, carry):
        at = pl.ds(pl.multiple_of(i * step, step), step)
        total_at = pl.ds(pl.multiple_of(c * rows + i * step, step), step)
        normed, inverse = norm_rows(n2[at].astype(f32))
        up = branch[total_at] + arrived[at]
        norms[COL_NORM : COL_NORM + 1] += jnp.sum(up * normed, axis=0, keepdims=True)
        norms[COL_NORM + 1 : COL_NORM + 2] += jnp.sum(up, axis=0, keepdims=True)
        dhid[at] += norm_rows_backward(up, normed, inverse, vec[VEC_GAIN : VEC_GAIN + 1])
        return carry

    l_x = load(xs_in.at[c, :, pl.ds(0, width)], n2.at[pl.ds(0, rows)], 16)
    l_x.wait()
    lax.fori_loop(0, rows // step, first, 0)
    outs.append(pltpu.make_async_copy(dhid, grad_out, osem.at[1]))
    outs[1].start()
    columns = norms[...].T

    for column in range(4):
        at = pl.ds(column * span, span)
        row_ids = lax.broadcasted_iota(jnp.int32, (span, spread), 0) + column * span
        one_hot = jnp.where(row_ids == wanted, 1.0, 0.0).astype(bf16)
        misc = dot_f32(one_hot, high, NT) + dot_f32(one_hot, low, NT)
        misc = misc + dot_f32(one_all[:, at], dfront[:, MISC:W_A], TN) + columns[column * span : (column + 1) * span]
        m_bufs[0][column] = misc.astype(bf16).reshape(levels, block_rows, W_MISC)
    while line.now < len(units):
        tick()
    for stage in range(3, levels - 1):
        o_stage(stage, order)
    for j in order:
        so.gathered(j)
    so.issue()
    line.round()
    so.turn()
    line.round()
    so.column()
    line.finish()
    outs.append(pltpu.make_async_copy(f_total, f_out, osem.at[2]))
    outs[2].start()
    mine, other = [pl.ds(pl.multiple_of(k * shard, 16), shard) for k in (c, 1 - c)]
    for i, (total, out) in enumerate(((i_total, i_out), (o_total, o_out), (a_total, a_out), (m_total, m_out))):
        outs.append(exchange(total.at[other], out.at[c], 4 + i))
        outs[-1].start()
        outs.append(pltpu.make_async_copy(total.at[mine], out.at[c], osem.at[3 + i]))
        outs[-1].start()
    for s in sums + [so]:
        s.drain()
    for cp in outs:
        cp.wait()


def backward(levels, batches, local_len, per_device, shard, ins):
    bf16, f32 = jnp.bfloat16, jnp.float32
    (unused, w_f, w_i, w_o, w_a, ffn, slope, xs, n2, hidden, vec, att, gates, front, win, probs, mixed, act) = ins
    ff, width = w_f.shape
    rows = batches * local_len
    both = 2 * rows
    f_rows = ff // (4 * levels)
    b_rows = width // (4 * levels)
    wide = HALF_HEADS * PAD
    outs = [((f_rows, width), f32)] + [((SIDE, shard, w), f32) for w in (ff, W_O, MISC, W_MISC)]
    outs += [((rows, width), bf16), ((rows, width), f32)]
    scratch = [(v.shape, v.dtype) for v in (w_f, w_i, ffn, slope)]
    scratch += [((2, rows, width), bf16), ((2, rows, 128), bf16)]
    scratch += [(n2.shape, bf16), (hidden.shape, f32), ((8, width), f32), (att.shape, bf16), (gates.shape, f32)]
    scratch += [((2, local_len, wide + W_VAL), f32), ((2,) + win.shape[1:], bf16), ((2,) + probs.shape[2:], f32)]
    scratch += [
        ((both, width), f32), ((rows, width), f32), ((rows, width), f32), ((both, width), bf16),
        ((both, W_O), bf16), ((both, W_A), bf16), ((HALF_HEADS, local_len, MEM + local_len), f32),
        ((W_MISC, width), f32), ((f_rows, width), f32),
    ]
    scratch += [((b_rows, w), f32) for w in (ff, W_O, MISC, W_MISC)]
    for r, w in ((f_rows, width), (b_rows, ff), (b_rows, W_MISC)):
        scratch.append(((4, levels, r, w), bf16))
        scratch += [((levels, k, w), bf16) for k in (r // 2, r // 2, r, r)]
        scratch.append(((levels + 1, r, w), bf16))
    scratch.append(((4, levels, b_rows, MISC), bf16))
    scratch += [((levels, b_rows // 2, MISC), bf16)] * 2
    scratch += [((4, levels, b_rows, W_O), bf16), ((4 * b_rows, W_O), bf16)]
    scratch += [((k, W_O), bf16) for k in (b_rows // 2, b_rows // 2, b_rows, b_rows)]
    sems = [(3 + len(A_PARTS), 8 * levels)] * 2 + [(8 * levels + 6,), (8 * levels + 6,), (18,), (4, 2), (8,), (8,), (10,)]
    hbm = pl.BlockSpec(memory_space=pl.ANY)
    return pl.pallas_call(
        functools.partial(backward_kernel, levels, batches, local_len, per_device, shard),
        out_shape=[jax.ShapeDtypeStruct(s, k) for s, k in outs],
        in_specs=[hbm] * len(ins),
        out_specs=[hbm] * len(outs),
        scratch_shapes=[pltpu.VMEM(s, k) for s, k in scratch]
        + [pltpu.SemaphoreType.DMA(s) for s in sems]
        + [pltpu.SemaphoreType.REGULAR] * 2,
        compiler_params=pltpu.CompilerParams(
            collective_id=2, has_side_effects=True, vmem_limit_bytes=VMEM_BYTES),
    )(*ins)


def share_kernel(
    per_device, f_in, i_in, o_in, a_in, m_in, layer_in, grad_in,
    f_out, in_out, branch_out, value_out, qk_out, router_out, gain1, shift1, gain2, shift2, bias_out, layer_out, grad_out,
    f_hold, layer_hold, grad_hold, sems,
):
    big = ((f_in, f_hold, f_out), (layer_in, layer_hold, layer_out), (grad_in, grad_hold, grad_out))
    there = [pltpu.make_async_copy(src, held, sems.at[i]) for i, (src, held, unused) in enumerate(big)]
    back = [pltpu.make_async_copy(held, dst, sems.at[3 + i]) for i, (unused, held, dst) in enumerate(big)]
    for cp in there:
        cp.start()
    for side in range(SIDE):
        for p in range(i_in.shape[2] // PAD):
            col = (p * SIDE + side) * PAD
            in_out[:, col : col + PAD] = i_in[side, :, p * PAD : (p + 1) * PAD]
        for h in range(HALF_HEADS):
            at = (side * HALF_HEADS + h) * HEAD_DIM
            for e in range(EXPERTS):
                col, dst = (e * HALF_HEADS + h) * PAD, e * HEADS * HEAD_DIM + at
                value_out[:, dst : dst + HEAD_DIM] = a_in[side, :, W_QK + col : W_QK + col + HEAD_DIM]
                branch_out[:, dst : dst + HEAD_DIM] = o_in[side, :, col : col + HEAD_DIM]
            for kind in range(2):
                col, dst = (kind * HALF_HEADS + h) * PAD, kind * HEADS * HEAD_DIM + at
                qk_out[:, dst : dst + HEAD_DIM] = a_in[side, :, col : col + HEAD_DIM]
        routes = HALF_HEADS * EXPERTS
        for kind in range(2):
            dst = (kind * SIDE + side) * routes
            router_out[:, dst : dst + routes] = m_in[side, :, kind * routes : (kind + 1) * routes]
        turned = m_in[side].T
        bias_out[side * HALF_HEADS : (side + 1) * HALF_HEADS] = turned[COL_BIAS : COL_BIAS + HALF_HEADS, :per_device]
    turned = (m_in[0] + m_in[1]).T
    for i, out in enumerate((gain1, shift1, gain2, shift2)):
        out[...] = turned[COL_NORM + i : COL_NORM + i + 1]
    for cp, after in zip(there, back):
        cp.wait()
        after.start()
    for cp in back:
        cp.wait()


def shares_of(per_device, ins):
    f, i, o, a, m, layer, grad = ins
    shard = i.shape[1]
    inner = HEADS * HEAD_DIM
    f32 = jnp.float32
    shapes = [
        (f.shape, f32), ((shard, SIDE * i.shape[2]), f32), ((shard, EXPERTS * inner), f32),
        ((shard, EXPERTS * inner), f32), ((shard, 2 * inner), f32), ((shard, 2 * HEADS * EXPERTS), f32)]
    shapes += [((1, shard), f32)] * 4 + [((HEADS, per_device), f32), (layer.shape, layer.dtype), (grad.shape, f32)]
    hbm, vmem = pl.BlockSpec(memory_space=pl.ANY), pl.BlockSpec(memory_space=pltpu.VMEM)
    return pl.pallas_call(
        functools.partial(share_kernel, per_device),
        out_shape=[jax.ShapeDtypeStruct(s, k) for s, k in shapes],
        in_specs=[hbm] + [vmem] * 4 + [hbm] * 2,
        out_specs=[hbm] + [vmem] * 10 + [hbm] * 2,
        scratch_shapes=[pltpu.VMEM(w.shape, w.dtype) for w in (f, layer, grad)] + [pltpu.SemaphoreType.DMA((6,))],
        compiler_params=pltpu.CompilerParams(vmem_limit_bytes=VMEM_BYTES),
    )(*ins)


def on_chip(
    tokens, cotangent, given_cache, value_routes, output_routes, valid_counts, doc_starts,
    norm1_gain, norm1_shift, qk_weight, router_weight, value_weight, output_weight, rel_bias,
    norm2_gain, norm2_shift, ffn_in, ffn_out,
):
    batches, unused_row, local_len, width = tokens.shape
    count = lax.axis_size("tm")
    levels = count // 2
    side = lax.axis_index("tm") % 2
    rows = batches * local_len
    shard = qk_weight.shape[0]
    blocks = 4 * levels
    bf16, f32 = jnp.bfloat16, jnp.float32

    norms = jnp.stack([norm1_gain, norm1_shift, norm2_gain, norm2_shift])
    routes = [
        jnp.transpose(r.reshape(batches, local_len, HEADS, TOPK), (0, 2, 3, 1)) for r in (value_routes, output_routes)]
    buckets = rel_bias.shape[1]
    hidden_block = ffn_out.shape[0]
    (a_all, o_all, i_all, f_all, xs, act_one, front, gates, win, probs, attended, mixed, hidden, n2, vec, act,
     slope, f_grad) = forward(
        levels, batches, local_len, buckets,
        (qk_weight, value_weight, router_weight, norms, rel_bias, output_weight.T, ffn_in, ffn_out,
         tokens.reshape(rows, width), cotangent.reshape(rows, width), routes[0], routes[1],
         doc_starts.reshape(1, batches), valid_counts.reshape(1, batches),
         given_cache.reshape(batches, MEM, 2 * HEADS * HEAD_DIM)))
    w_a = a_all.reshape(width, W_A)
    w_i = i_all.reshape(width, -1)
    w_f = f_all.reshape(-1, width)
    sums = backward(
        levels, batches, local_len, buckets, shard,
        (f_grad.reshape(4, levels, hidden_block, width), w_f, w_i, o_all, w_a, act, slope, xs, n2, hidden, vec, attended, gates, front, win, probs, mixed,
         act_one.reshape(2, rows, width)))
    (out_share, in_share, branch_share, value_share, qk_share, router_share, gain1, shift1, gain2, shift2, bias_share,
     layer_out, input_grad) = shares_of(buckets, sums)
    gain1, shift1, gain2, shift2 = [v.reshape(shard) for v in (gain1, shift1, gain2, shift2)]
    return (
        layer_out.reshape(tokens.shape), input_grad.reshape(tokens.shape), gain1, shift1, qk_share, router_share,
        value_share, branch_share.T, bias_share, gain2, shift2, in_share, out_share,
    )


def by_size(*args):
    thin = args[9].shape[0] % 16 != 0
    paired = lax.axis_size("doc") == 4 and lax.axis_size("tm") % 2 == 0 and lax.axis_size("tm") >= 8
    return on_device(*args) if thin or not paired else on_chip(*args)


def solution(mesh):
    return jax.shard_map(
        by_size,
        mesh=mesh,
        in_specs=(
            P(None, "doc", "tm", None),
            P(None, "doc", "tm", None),
            P(None, "doc", "tm", None),
            P(None, "doc", "tm", None, None),
            P(None, "doc", "tm", None, None),
            P(None, "doc", "tm"),
            P(None, "doc", "tm"),
            P(("doc", "tm")),
            P(("doc", "tm")),
            P(("doc", "tm"), None),
            P(("doc", "tm"), None),
            P(("doc", "tm"), None),
            P(None, ("doc", "tm")),
            P(None, ("doc", "tm")),
            P(("doc", "tm")),
            P(("doc", "tm")),
            P(("doc", "tm"), None),
            P(("doc", "tm"), None),
        ),
        out_specs=(
            P(None, "doc", "tm", None),
            P(None, "doc", "tm", None),
            P(("doc", "tm")),
            P(("doc", "tm")),
            P(("doc", "tm"), None),
            P(("doc", "tm"), None),
            P(("doc", "tm"), None),
            P(None, ("doc", "tm")),
            P(None, ("doc", "tm")),
            P(("doc", "tm")),
            P(("doc", "tm")),
            P(("doc", "tm"), None),
            P(("doc", "tm"), None),
        ),
        check_vma=False,
    )
```

```python
import functools

import jax
import jax.numpy as jnp
from jax import lax
from jax.experimental import pallas as pl
from jax.experimental.pallas import tpu as pltpu
from jax.sharding import PartitionSpec as P

HEADS = 4
HEAD_DIM = 112
EXPERTS = 5
TOPK = 2
MEM = 1024
BUCKETS = 256
NEAR = 128
STEP = 16


EPS = 1e-05
NEG = -1e30
HIGH = lax.Precision.HIGHEST


def shortened(array):
    return jax.tree.map(lambda a: a.astype(jnp.bfloat16) if a.dtype == jnp.float32 else a, array)


def from_behind(value, axis, steps):
    count = lax.axis_size(axis)
    first, last = (max(0, -steps), min(count, count - steps))
    return lax.ppermute(value, axis, [(source, source + steps) for source in range(first, last)])


def norm_forward(values, gain, shift):
    center_mean = jnp.mean(values, axis=-1, keepdims=True)
    centered = values - center_mean
    inverse = lax.rsqrt(jnp.mean(centered * centered, axis=-1, keepdims=True) + EPS)
    normed = centered * inverse
    return (normed * gain + shift, normed, inverse)


def norm_backward(upstream, normed, inverse, gain):
    scaled = upstream * gain
    inside = (
        scaled
        - jnp.mean(scaled, axis=-1, keepdims=True)
        - normed * jnp.mean(scaled * normed, axis=-1, keepdims=True)
    )
    return (inside * inverse, jnp.sum(upstream * normed, axis=0), jnp.sum(upstream, axis=0))


def selection(routes):
    expert_ids = jnp.arange(EXPERTS, dtype=jnp.int32)
    return jnp.sum((routes[..., None] == expert_ids).astype(jnp.float32), axis=-2)


def bucket_index(distance):
    far_bucket = NEAR + (distance - NEAR) // STEP
    return jnp.clip(jnp.where(distance < NEAR, distance, far_bucket), 0, BUCKETS - 1)


def gelu_slope(pre_act):
    return (
        0.5 * (1.0 + lax.erf(pre_act * 0.7071067811865476))
        + pre_act * jnp.exp(-0.5 * pre_act * pre_act) * 0.3989422804014327
    )


def flatten(matrix):
    return matrix.reshape(-1)


def bucket_matrix(local_len):
    spread = MEM + 2 * local_len - 1
    distance = jnp.arange(spread, dtype=jnp.int32) - (local_len - 1)
    bucket_ids = jnp.arange(BUCKETS, dtype=jnp.int32)
    return (bucket_index(distance)[:, None] == bucket_ids[None, :]).astype(jnp.float32)


def bias_matrix(table, local_len):
    spread = MEM + 2 * local_len - 1
    window = MEM + local_len
    by_distance = jnp.einsum("hc,kc->hk", table, bucket_matrix(local_len), precision=HIGH)
    turned = jnp.concatenate([by_distance[:, ::-1], jnp.zeros((HEADS, 1), jnp.float32)], axis=1)
    tiled = jnp.tile(turned, (1, local_len))[:, : local_len * spread].reshape(
        HEADS, local_len, spread
    )
    return tiled[:, :, local_len - 1 : local_len - 1 + window]


def bias_backward(score_sum, local_len):
    spread = MEM + 2 * local_len - 1
    padded = jnp.pad(score_sum, ((0, 0), (0, 0), (local_len - 1, 0))).reshape(
        HEADS, local_len * spread
    )
    padded = jnp.pad(padded, ((0, 0), (0, local_len))).reshape(HEADS, local_len, spread + 1)
    by_distance = jnp.sum(padded, axis=1)[:, :spread][:, ::-1]
    return jnp.einsum("hk,kc->hc", by_distance, bucket_matrix(local_len), precision=HIGH)


def attention_scores(queries, keys, table, counts):
    local_len = queries.shape[1]
    window = keys.shape[1]
    raw = jnp.einsum(
        "bqhd,bkhd->bhqk", queries, keys, preferred_element_type=jnp.float32
    ) * HEAD_DIM ** (-0.5)
    row_ids = jnp.arange(local_len, dtype=jnp.int32)[:, None]
    col_ids = jnp.arange(window, dtype=jnp.int32)[None, :]
    bias = bias_matrix(table, local_len)
    own_ids = col_ids - MEM
    causal = (own_ids <= row_ids)[None, None]
    live = own_ids[None, None] < counts[:, None, None, None]
    valid = jnp.logical_or((col_ids < MEM)[None, None], jnp.logical_and(causal, live))
    return (jnp.where(valid, raw + bias[None], NEG), valid)


def memory_by_hops(cache_own, given, starts, local_len):
    hops_total = MEM // local_len
    open_flag = jnp.logical_not(starts)[:, None, None]
    memory_slots = [jnp.zeros_like(cache_own) for _ in range(hops_total)]
    start_marks = starts.astype(jnp.bfloat16)
    for distance in range(1, hops_total + 1):
        if distance < hops_total:
            outgoing = (cache_own, start_marks, given[:, distance * local_len :])
        else:
            outgoing = (cache_own, start_marks)
        incoming = jax.tree.map(
            lambda part, own: part.astype(own.dtype),
            from_behind(shortened(outgoing), "tm", distance),
            outgoing,
        )
        memory_slots[hops_total - distance] = jnp.where(
            open_flag, incoming[0], memory_slots[hops_total - distance]
        )
        arrived = jnp.logical_and(open_flag, (incoming[1] > 0)[:, None, None])
        if distance < hops_total:
            for position in range(hops_total - distance):
                portion = incoming[2][:, position * local_len : (position + 1) * local_len]
                memory_slots[position] = jnp.where(arrived, portion, memory_slots[position])
        open_flag = jnp.logical_and(open_flag, jnp.logical_not(arrived))
    assembled = jnp.concatenate(memory_slots, axis=1)
    return jnp.where(starts[:, None, None], given, assembled)


def on_device(
    tokens,
    cotangent,
    given_cache,
    value_routes,
    output_routes,
    valid_counts,
    doc_starts,
    norm1_gain,
    norm1_shift,
    qk_weight,
    router_weight,
    value_weight,
    output_weight,
    rel_bias,
    norm2_gain,
    norm2_shift,
    ffn_in,
    ffn_out,
):
    batches, unused_row, local_len, model_width = tokens.shape
    row_count = batches * local_len
    inner_width = HEADS * HEAD_DIM
    head_experts = HEADS * EXPERTS
    full_weights = (
        lax.all_gather(norm1_gain, ("doc", "tm"), axis=0, tiled=True),
        lax.all_gather(norm1_shift, ("doc", "tm"), axis=0, tiled=True),
        lax.all_gather(qk_weight, ("doc", "tm"), axis=0, tiled=True),
        lax.all_gather(router_weight, ("doc", "tm"), axis=0, tiled=True),
        lax.all_gather(value_weight, ("doc", "tm"), axis=0, tiled=True),
        lax.all_gather(output_weight, ("doc", "tm"), axis=1, tiled=True),
        lax.all_gather(rel_bias, ("doc", "tm"), axis=1, tiled=True),
        lax.all_gather(norm2_gain, ("doc", "tm"), axis=0, tiled=True),
        lax.all_gather(norm2_shift, ("doc", "tm"), axis=0, tiled=True),
        lax.all_gather(ffn_in, ("doc", "tm"), axis=0, tiled=True),
        lax.all_gather(ffn_out, ("doc", "tm"), axis=0, tiled=True),
    )
    (
        gain_one,
        shift_one,
        w_qk,
        w_router,
        w_value,
        w_output,
        table_bf,
        gain_two,
        shift_two,
        w_in,
        w_out,
    ) = full_weights
    gain_one = gain_one.astype(jnp.float32)
    shift_one = shift_one.astype(jnp.float32)
    gain_two = gain_two.astype(jnp.float32)
    shift_two = shift_two.astype(jnp.float32)
    table = table_bf.astype(jnp.float32)
    router_f = w_router.astype(jnp.float32)
    inputs = tokens.reshape(row_count, model_width).astype(jnp.float32)
    counts = valid_counts.reshape(batches)
    starts = doc_starts.reshape(batches) > 0
    token_mask = (
        (jnp.arange(local_len, dtype=jnp.int32)[None, :] < counts[:, None])
        .astype(jnp.float32)
        .reshape(row_count, 1)
    )
    value_pick = selection(value_routes.reshape(row_count, HEADS, TOPK))
    output_pick = selection(output_routes.reshape(row_count, HEADS, TOPK))
    normed_one, norm1_unit, norm1_inv = norm_forward(inputs, gain_one, shift_one)
    act_one = normed_one.astype(jnp.bfloat16)
    qk_vals = jnp.dot(act_one, w_qk, preferred_element_type=jnp.float32).astype(jnp.bfloat16)
    gates = jax.nn.sigmoid(jnp.dot(act_one, w_router, preferred_element_type=jnp.float32))
    gate_value = gates[:, :head_experts].reshape(row_count, HEADS, EXPERTS) * value_pick
    gate_output = gates[:, head_experts:].reshape(row_count, HEADS, EXPERTS) * output_pick
    value_gate_t = jnp.transpose(gate_value, (0, 2, 1))[..., None]
    output_gate_t = jnp.transpose(gate_output, (0, 2, 1))[..., None]
    parts = jnp.dot(act_one, w_value, preferred_element_type=jnp.float32).reshape(
        row_count, EXPERTS, HEADS, HEAD_DIM
    )
    values = (
        jnp.sum(value_gate_t * parts, axis=1).reshape(row_count, inner_width).astype(jnp.bfloat16)
    )
    cache_own = jnp.concatenate([qk_vals[:, inner_width:], values], axis=1).reshape(
        batches, local_len, 2 * inner_width
    )
    given = given_cache.reshape(batches, MEM, 2 * inner_width)
    memory = memory_by_hops(cache_own, given, starts, local_len)
    queries = qk_vals[:, :inner_width].reshape(batches, local_len, HEADS, HEAD_DIM)
    keys = jnp.concatenate([memory[:, :, :inner_width], cache_own[:, :, :inner_width]], axis=1)
    keys = keys.reshape(batches, MEM + local_len, HEADS, HEAD_DIM)
    vals = jnp.concatenate([memory[:, :, inner_width:], cache_own[:, :, inner_width:]], axis=1)
    vals = vals.reshape(batches, MEM + local_len, HEADS, HEAD_DIM)
    scores, valid = attention_scores(queries, keys, table, counts)
    top = jnp.max(scores, axis=-1, keepdims=True)
    expo = jnp.exp(scores - top)
    denom = jnp.sum(expo, axis=-1, keepdims=True)
    log_total = top + jnp.log(denom)
    probs_b = (expo / denom).astype(jnp.bfloat16)
    attended = jnp.einsum("bhqk,bkhd->bqhd", probs_b, vals, preferred_element_type=jnp.float32)
    attended = attended.reshape(row_count, inner_width).astype(jnp.bfloat16)
    attended_f = attended.astype(jnp.float32).reshape(row_count, 1, HEADS, HEAD_DIM)
    mixed = (
        (output_gate_t * attended_f).reshape(row_count, EXPERTS * inner_width).astype(jnp.bfloat16)
    )
    hidden = inputs + jnp.dot(mixed, w_output, preferred_element_type=jnp.float32)
    normed_two, norm2_unit, norm2_inv = norm_forward(hidden, gain_two, shift_two)
    act_two = normed_two.astype(jnp.bfloat16)
    pre_act = jnp.dot(act_two, w_in, preferred_element_type=jnp.float32)
    activated = jax.nn.gelu(pre_act, approximate=False).astype(jnp.bfloat16)
    ffn_result = jnp.dot(activated, w_out, preferred_element_type=jnp.float32)
    layer_out = (token_mask * (hidden + ffn_result)).astype(jnp.bfloat16).reshape(tokens.shape)
    upstream = cotangent.reshape(row_count, model_width).astype(jnp.float32) * token_mask
    upstream_b = upstream.astype(jnp.bfloat16)
    d_out_w = jnp.einsum("nf,nd->fd", activated, upstream_b, preferred_element_type=jnp.float32)
    d_act = jnp.einsum("nd,fd->nf", upstream_b, w_out, preferred_element_type=jnp.float32)
    d_pre = (d_act * gelu_slope(pre_act)).astype(jnp.bfloat16)
    d_in_w = jnp.einsum("nd,nf->df", act_two, d_pre, preferred_element_type=jnp.float32)
    d_norm_two = jnp.einsum("nf,df->nd", d_pre, w_in, preferred_element_type=jnp.float32)
    d_from_two, d_gain_two, d_shift_two = norm_backward(d_norm_two, norm2_unit, norm2_inv, gain_two)
    d_hidden = upstream + d_from_two
    ffn_width = d_in_w.shape[1]
    d_branch = d_hidden.astype(jnp.bfloat16)
    d_output_t = jnp.einsum("nd,nk->dk", d_branch, mixed, preferred_element_type=jnp.float32)
    d_mixed = jnp.einsum(
        "nd,kd->nk", d_branch, w_output, preferred_element_type=jnp.float32
    ).astype(jnp.bfloat16)
    d_mixed = d_mixed.astype(jnp.float32).reshape(row_count, EXPERTS, HEADS, HEAD_DIM)
    d_gate_out = jnp.sum(d_mixed * attended_f, axis=-1)
    d_attended = (
        jnp.sum(d_mixed * output_gate_t, axis=1)
        .astype(jnp.bfloat16)
        .reshape(batches, local_len, HEADS, HEAD_DIM)
    )
    probs = jnp.where(valid, jnp.exp(scores - log_total), 0.0)
    d_probs = jnp.einsum("bqhd,bkhd->bhqk", d_attended, vals, preferred_element_type=jnp.float32)
    delta = jnp.sum(d_probs * probs, axis=-1, keepdims=True)
    d_scores = probs * (d_probs - delta)
    score_sum = jnp.sum(d_scores, axis=0)
    d_table = bias_backward(score_sum, local_len)
    d_scores_b = d_scores.astype(jnp.bfloat16)
    scale = HEAD_DIM ** (-0.5)
    d_queries = (
        jnp.einsum("bhqk,bkhd->bqhd", d_scores_b, keys, preferred_element_type=jnp.float32) * scale
    )
    d_keys = (
        jnp.einsum(
            "bhqk,bqhd->bkhd", d_scores_b[..., MEM:], queries, preferred_element_type=jnp.float32
        )
        * scale
    )
    d_vals = jnp.einsum(
        "bhqk,bqhd->bkhd", probs_b[..., MEM:], d_attended, preferred_element_type=jnp.float32
    )
    d_qk = jnp.concatenate(
        [d_queries.reshape(row_count, inner_width), d_keys.reshape(row_count, inner_width)], axis=1
    ).astype(jnp.bfloat16)
    d_values = (
        d_vals.reshape(row_count, 1, HEADS, HEAD_DIM).astype(jnp.bfloat16).astype(jnp.float32)
    )
    d_gate_val = jnp.sum(parts * d_values, axis=-1)
    d_parts = (
        (value_gate_t * d_values).reshape(row_count, EXPERTS * inner_width).astype(jnp.bfloat16)
    )
    d_gates = jnp.concatenate(
        [
            jnp.transpose(d_gate_val, (0, 2, 1)).reshape(row_count, head_experts)
            * value_pick.reshape(row_count, head_experts),
            jnp.transpose(d_gate_out, (0, 2, 1)).reshape(row_count, head_experts)
            * output_pick.reshape(row_count, head_experts),
        ],
        axis=1,
    )
    d_logits = d_gates * gates * (1.0 - gates)
    d_qk_w = jnp.einsum("nd,nk->dk", act_one, d_qk, preferred_element_type=jnp.float32)
    d_value_w = jnp.einsum("nd,nk->dk", act_one, d_parts, preferred_element_type=jnp.float32)
    d_router_w = jnp.einsum("nd,nk->dk", act_one.astype(jnp.float32), d_logits, precision=HIGH)
    d_norm_one = jnp.einsum("nk,dk->nd", d_qk, w_qk, preferred_element_type=jnp.float32)
    d_norm_one = d_norm_one + jnp.einsum(
        "nk,dk->nd", d_parts, w_value, preferred_element_type=jnp.float32
    )
    d_norm_one = d_norm_one + jnp.einsum("nk,dk->nd", d_logits, router_f, precision=HIGH)
    d_from_one, d_gain_one, d_shift_one = norm_backward(d_norm_one, norm1_unit, norm1_inv, gain_one)
    input_grad = (d_hidden + d_from_one).reshape(tokens.shape)
    shares = (
        lax.psum_scatter(d_gain_one, ("doc", "tm"), scatter_dimension=0, tiled=True),
        lax.psum_scatter(d_shift_one, ("doc", "tm"), scatter_dimension=0, tiled=True),
        lax.psum_scatter(flatten(d_qk_w), ("doc", "tm"), scatter_dimension=0, tiled=True),
        lax.psum_scatter(flatten(d_router_w), ("doc", "tm"), scatter_dimension=0, tiled=True),
        lax.psum_scatter(flatten(d_value_w), ("doc", "tm"), scatter_dimension=0, tiled=True),
        lax.psum_scatter(flatten(d_output_t), ("doc", "tm"), scatter_dimension=0, tiled=True),
        lax.psum_scatter(d_table, ("doc", "tm"), scatter_dimension=1, tiled=True),
        lax.psum_scatter(d_gain_two, ("doc", "tm"), scatter_dimension=0, tiled=True),
        lax.psum_scatter(d_shift_two, ("doc", "tm"), scatter_dimension=0, tiled=True),
        lax.psum_scatter(flatten(d_in_w), ("doc", "tm"), scatter_dimension=0, tiled=True),
        lax.psum_scatter(flatten(d_out_w), ("doc", "tm"), scatter_dimension=0, tiled=True),
    )
    qk_share = shares[2].reshape(-1, 2 * inner_width)
    router_share = shares[3].reshape(-1, 2 * head_experts)
    value_share = shares[4].reshape(-1, EXPERTS * inner_width)
    output_share = shares[5].reshape(-1, EXPERTS * inner_width).T
    in_share = shares[9].reshape(-1, ffn_width)
    out_share = shares[10].reshape(-1, model_width)
    return (
        layer_out,
        input_grad,
        shares[0],
        shares[1],
        qk_share,
        router_share,
        value_share,
        output_share,
        shares[6],
        shares[7],
        shares[8],
        in_share,
        out_share,
    )


MESH = pl.DeviceIdType.MESH
PAD = 128
SIDE = 2
HALF_HEADS = HEADS // SIDE
W_QK = 2 * HALF_HEADS * PAD
W_VAL = EXPERTS * HALF_HEADS * PAD
W_MISC = 128
W_A = W_QK + W_VAL + W_MISC
W_O = EXPERTS * HALF_HEADS * PAD
MISC = W_QK + W_VAL
N_ROUTE = 2 * HALF_HEADS * EXPERTS
COL_NORM = N_ROUTE
COL_BIAS = N_ROUTE + 4
VMEM_BYTES = 63 * 1024 * 1024
SCALE = HEAD_DIM ** (-0.5)


def pad_last(a, width):
    return jnp.pad(a, [(0, 0)] * (a.ndim - 1) + [(0, width - a.shape[-1])])


def neighbours(count):
    d, t = lax.axis_index("doc"), lax.axis_index("tm")
    z, c = t // 2, t % 2
    return dict(
        c=(d, z * 2 + 1 - c),
        x=(d + 1 - 2 * (d % 2), t),
        y=((d + 2) % 4, t),
        up=(d, jnp.minimum(t + 2, count - 1)),
        down=(d, jnp.maximum(t - 2, 0)),
    )


def enter(nb, z, levels):
    barrier = pltpu.get_barrier_semaphore()
    for name in ("c", "x", "y"):
        pl.semaphore_signal(barrier, inc=1, device_id=nb[name], device_id_type=MESH)

    @pl.when(z < levels - 1)
    def _():
        pl.semaphore_signal(barrier, inc=1, device_id=nb["up"], device_id_type=MESH)

    @pl.when(z > 0)
    def _():
        pl.semaphore_signal(barrier, inc=1, device_id=nb["down"], device_id_type=MESH)

    ends = jnp.where(z < levels - 1, 1, 0) + jnp.where(z > 0, 1, 0)
    pl.semaphore_wait(barrier, 3 + ends)


class Gather:
    def __init__(self, ref, sems, nb, d, z, levels):
        self.ref, self.nb, self.d, self.z, self.levels = ref, nb, d, z, levels
        self.send, self.recv = sems
        self.half = ref.shape[2] // 2

    def copy(self, part, slot, to):
        return pltpu.make_async_remote_copy(
            src_ref=part, dst_ref=part, send_sem=self.send.at[slot], recv_sem=self.recv.at[slot],
            device_id=self.nb[to], device_id_type=MESH)

    def along(self, level, distance, to):
        base = 0 if to == "up" else self.levels
        return self.copy(self.ref.at[self.d, level], base + distance, to)

    def across(self, level, to, column=None):
        base = (2 if to == "x" else 3) * self.levels
        column = self.d if column is None else column
        return self.copy(self.ref.at[column, level], base + level, to)

    def corner(self, level, to, column):
        base = (4 if to == "x" else 5) * self.levels
        rows = pl.ds(self.half, self.half) if to == "x" else pl.ds(0, self.half)
        return self.copy(self.ref.at[column, level, rows], base + level, to)

    def begin(self):
        z, levels = self.z, self.levels

        @pl.when(z < levels - 1)
        def _():
            self.along(z, 1, "up").start()

        @pl.when(z > 0)
        def _():
            self.along(z, 1, "down").start()

        self.across(z, "x").start()
        self.across(z, "y").start()

    def line(self, k):
        z, levels = self.z, self.levels

        @pl.when(z >= k)
        def _():
            self.along(z - k, k, "up").wait_recv()

            @pl.when(z < levels - 1)
            def _():
                self.along(z - k, k + 1, "up").start()

            self.across(z - k, "x").start()
            self.across(z - k, "y").start()

        @pl.when(z + k < levels)
        def _():
            self.along(z + k, k, "down").wait_recv()

            @pl.when(z > 0)
            def _():
                self.along(z + k, k + 1, "down").start()

            self.across(z + k, "x").start()
            self.across(z + k, "y").start()

    def turn(self, k):
        z, levels, d = self.z, self.levels, self.d
        by_x, by_y = d + 1 - 2 * (d % 2), (d + 2) % 4

        def one(level):
            self.across(level, "x").wait_recv()
            self.corner(level, "y", by_x).start()
            self.across(level, "y").wait_recv()
            self.corner(level, "x", by_y).start()

        if k == 0:
            one(z)
        else:
            pl.when(z >= k)(lambda: one(z - k))
            pl.when(z + k < levels)(lambda: one(z + k))

    def finish(self, k):
        z, levels, d = self.z, self.levels, self.d
        by_x, by_y = d + 1 - 2 * (d % 2), (d + 2) % 4

        def one(level):
            self.corner(level, "x", by_y).wait_recv()
            self.corner(level, "y", by_x).wait_recv()

        if k == 0:
            one(z)
        else:
            pl.when(z >= k)(lambda: one(z - k))
            pl.when(z + k < levels)(lambda: one(z + k))

    def drain(self):
        z, levels, d = self.z, self.levels, self.d
        by_x, by_y = d + 1 - 2 * (d % 2), (d + 2) % 4
        for level in range(levels):
            self.across(level, "x").wait_send()
            self.across(level, "y").wait_send()
            self.corner(level, "x", by_y).wait_send()
            self.corner(level, "y", by_x).wait_send()
        for k in range(1, levels):

            @pl.when(jnp.logical_and(z >= k - 1, z < levels - 1))
            def _():
                self.along(z - k + 1, k, "up").wait_send()

            @pl.when(jnp.logical_and(z + k - 1 < levels, z > 0))
            def _():
                self.along(z + k - 1, k, "down").wait_send()


def selector(side):
    inner = HEADS * HEAD_DIM
    wide = HALF_HEADS * PAD
    src = lax.broadcasted_iota(jnp.int32, (2 * inner, 2 * wide), 0)
    dst = lax.broadcasted_iota(jnp.int32, (2 * inner, 2 * wide), 1)
    kind, head, feature = dst // wide, (dst // PAD) % HALF_HEADS, dst % PAD
    wanted = kind * inner + (side * HALF_HEADS + head) * HEAD_DIM + feature
    hit = jnp.logical_and(src == wanted, feature < HEAD_DIM)
    return jnp.where(hit, 1.0, 0.0).astype(jnp.bfloat16)


def table_by_offset(w_a, per_device, shard, local_len, spread):
    distance = MEM + local_len - 1 - lax.broadcasted_iota(jnp.int32, (1, spread), 1)
    bucket = bucket_index(distance)
    wanted = (bucket // per_device) * shard + bucket % per_device
    step = 128

    def body(i, total):
        at = pl.ds(pl.multiple_of(i * step, step), step)
        ids = lax.broadcasted_iota(jnp.int32, (step, spread), 0) + i * step
        one_hot = jnp.where(ids == wanted, 1.0, 0.0).astype(jnp.bfloat16)
        return total + dot_f32(w_a[at, MISC:W_A], one_hot, TN)

    return lax.fori_loop(0, w_a.shape[0] // step, body, jnp.zeros((W_MISC, spread), jnp.float32))


NT = (((1,), (1,)), ((), ()))
TN = (((0,), (0,)), ((), ()))


def dot_f32(a, b, dims=(((1,), (0,)), ((), ()))):
    return lax.dot_general(a, b, dims, preferred_element_type=jnp.float32)


def steps_of(words):
    return [(w[0], w[1], int(w[2])) for w in words]


EVENTS = {point: steps_of(words) for point, words in dict(
    f=("fb0",),
    a=("ab0",),
    stats=("al1", "at0",),
    packs=(),
    given=("me0", "al2", "at1", "al3", "at2", "ob0", "me1", "at3",
        "ol1", "me2",),
    front=("ot0", "ol2", "ib0",),
    cache=("ot1", "ol3", "il1", "fl1", "me3",),
    memory=("ot2", "ot3", "il2", "fl2", "0h0", "it0", "il3", "fl3",
        "0h1", "it1", "0h2",),
    half=("1h0", "1h1", "ft0", "it2", "it3", "1h2",),
    attended=("ft1",),
    far=(),
    pair=("ft2", "ft3",),
    activated=(),
).items()}


def forward_kernel(
    levels, batches, local_len, per_device,
    qk_in, value_in, router_in, norm_in, bias_in, branch_in, up_in, f_in, token_in, cot_in, vr_in, or_in, start_in,
    count_in, g_in,
    a_out, o_out, i_out, f_all, xs_out, act_out, front_out, gates_out, win_out, probs_out, att_out,
    mixed_out, hidden_out, n2_out, vec_out, ffn_out, slope_out, fgrad_out,
    a_all, o_all, i_all, xs, graw, win, rbuf, sel, unit, act, front, gates, vec, bias, probs, att, mixed,
    arrived, hidden, n2, ffn, slope,
    qk_raw, value_raw, router_raw, norm_raw, bias_raw, branch_raw, up_raw, vr_raw, or_raw, start_raw, count_raw, f_raw, a_pack, o_pack, i_pack,
    send, recv, csend, crecv, lsem, gsend, grecv, esend, erecv, osem, psem,
):
    bf16, f32 = jnp.bfloat16, jnp.float32
    d, t = lax.axis_index("doc"), lax.axis_index("tm")
    z, c = t // 2, t % 2
    nb = neighbours(2 * levels)
    shard = qk_in.shape[0]
    width = f_in.shape[1]
    rows = batches * local_len
    both = 2 * rows
    wide = HALF_HEADS * PAD
    own = pl.ds(pl.multiple_of(c * shard, 16), shard)

    def local(src, dst, index):
        cp = pltpu.make_async_copy(src, dst, lsem.at[index])
        cp.start()
        return cp

    def sibling(src, dst, index):
        return pltpu.make_async_remote_copy(
            src_ref=src, dst_ref=dst, send_sem=csend.at[index], recv_sem=crecv.at[index],
            device_id=nb["c"], device_id_type=MESH)

    raws = [
        local(src, dst, i)
        for i, (src, dst) in enumerate((
            (qk_in, qk_raw), (value_in, value_raw), (router_in, router_raw), (norm_in, norm_raw), (bias_in, bias_raw),
            (branch_in, branch_raw), (up_in, up_raw), (vr_in, vr_raw), (or_in, or_raw), (start_in, start_raw),
            (count_in, count_raw)))
    ]
    loc_f = local(f_in, f_raw, 11)
    x_parts = ((token_in, pl.ds(0, width)), (cot_in, pl.ds(width, width)))
    loc_x = [local(src, xs.at[c, :, cols], 12 + i) for i, (src, cols) in enumerate(x_parts)]
    enter(nb, z, levels)
    rem_x = [sibling(src, xs.at[c, :, cols], i) for i, (src, cols) in enumerate(x_parts)]
    for cp in rem_x:
        cp.start()
    ga, go, gi, gf = [
        Gather(ref, (send.at[i], recv.at[i]), nb, d, z, levels)
        for i, ref in enumerate((a_all, o_all, i_all, f_all))
    ]

    loc_f.wait()
    own_f = local(f_raw, f_all.at[d, z], 18)
    own_f.wait()
    groups = dict(a=ga, o=go, i=gi, f=gf)
    left = [
        (name, what, k) for name in groups for what, first in (("b", 0), ("l", 1), ("t", 0), ("f", 0))
        for k in range(first, 1 if what == "b" else levels)]
    left += [("m", "e", k) for k in range(MEM // local_len // 2)]
    left += [(str(batch), "h", k) for batch in range(batches) for k in range(MEM // local_len // 2)]

    def do(name, what, k):
        if (name, what, k) not in left:
            return
        left.remove((name, what, k))
        if what == "e":
            early(k)
            return
        if what == "h":
            late(k, int(name))
            return
        group = groups[name]
        if what == "b":
            for cp in placed[name]:
                cp.wait()
            group.begin()
        else:
            dict(l=group.line, t=group.turn, f=group.finish)[what](k)

    def run(point):
        for event in EVENTS[point]:
            do(*event)

    def complete(name):
        for event in [e for e in left if e[0] == name]:
            do(*event)

    placed = dict(f=[])
    run("f")

    for cp in raws[:5]:
        cp.wait()
    a_pack[...] = jnp.zeros_like(a_pack)
    norm_columns = norm_raw[...].astype(f32).T
    for side in range(SIDE):
        for h in range(HALF_HEADS):
            at = (side * HALF_HEADS + h) * HEAD_DIM
            for kind in range(2):
                col, src = (kind * HALF_HEADS + h) * PAD, kind * HEADS * HEAD_DIM + at
                a_pack[side, :, col : col + HEAD_DIM] = qk_raw[:, src : src + HEAD_DIM]
            for e in range(EXPERTS):
                col, src = W_QK + (e * HALF_HEADS + h) * PAD, e * HEADS * HEAD_DIM + at
                a_pack[side, :, col : col + HEAD_DIM] = value_raw[:, src : src + HEAD_DIM]
        routes = HALF_HEADS * EXPERTS
        for kind in range(2):
            src = (kind * SIDE + side) * routes
            a_pack[side, :, MISC + kind * routes : MISC + (kind + 1) * routes] = router_raw[:, src : src + routes]
        a_pack[side, :, MISC + COL_NORM : MISC + COL_NORM + 4] = norm_columns.astype(bf16)
        heads = bias_raw[side * HALF_HEADS : (side + 1) * HALF_HEADS].astype(f32).T
        tail = jnp.concatenate([heads, jnp.zeros((shard - per_device, HALF_HEADS), f32)], axis=0)
        a_pack[side, :, MISC + COL_BIAS : MISC + COL_BIAS + HALF_HEADS] = tail.astype(bf16)
    loc_a = local(a_pack.at[c], a_all.at[d, z, own], 17)
    rem_a = sibling(a_pack.at[1 - c], a_all.at[d, z, own], 3)
    rem_a.start()
    for cp in raws[7:]:
        cp.wait()
    row_ids = lax.broadcasted_iota(jnp.int32, (W_MISC, local_len), 0)
    for batch in range(batches):
        flags = [
            jnp.broadcast_to(raw[:, batch : batch + 1].astype(f32), (W_MISC, local_len)) for raw in (start_raw, count_raw)]
        for side in range(SIDE):
            rows_of = jnp.where(row_ids == 40, flags[0], jnp.where(row_ids == 41, flags[1], 0.0))
            for kind, raw in enumerate((vr_raw, or_raw)):
                for h in range(HALF_HEADS):
                    chosen = raw[batch, side * HALF_HEADS + h]
                    first = (kind * HALF_HEADS + h) * EXPERTS
                    expert = row_ids - first
                    hit = expert == chosen[0:1]
                    for k in range(1, TOPK):
                        hit = jnp.logical_or(hit, expert == chosen[k : k + 1])
                    inside = jnp.logical_and(row_ids >= first, row_ids < first + EXPERTS)
                    rows_of = jnp.where(jnp.logical_and(hit, inside), 1.0, rows_of)
            cols = pl.ds(2 * width + side * 128, 128)
            xs[c, pl.ds(batch * local_len, local_len), cols] = rows_of.T.astype(bf16)
    meta_cols = xs.at[c, :, pl.ds(2 * width, SIDE * 128)]
    rem_x.append(sibling(meta_cols, meta_cols, 2))
    rem_x[-1].start()
    loc_g = local(g_in, graw.at[c], 14)
    rem_g = sibling(g_in, graw.at[c], 4)
    rem_g.start()
    placed["a"] = (loc_a, rem_a)
    run("a")
    sel[...] = selector(c)

    for cp in loc_x + rem_x:
        cp.wait()
    step = 64

    def stats(i, carry):
        at = pl.ds(pl.multiple_of((i % (rows // step)) * step, step), step)
        block = i // (rows // step)
        values = xs[block, at, :width].astype(f32)
        centered = values - jnp.mean(values, axis=-1, keepdims=True)
        inverse = lax.rsqrt(jnp.mean(centered * centered, axis=-1, keepdims=True) + EPS)
        unit[pl.ds(pl.multiple_of(i * step, step), step)] = centered * inverse
        counts = xs[block, at, 2 * width : 2 * width + 128][:, 41:42].astype(f32)
        position = lax.broadcasted_iota(jnp.int32, (step, 1), 0) + (i * step) % local_len
        gradient = xs[block, at, width : 2 * width].astype(f32)
        xs[block, at, width : 2 * width] = jnp.where(position.astype(f32) < counts, gradient, 0.0).astype(bf16)
        return carry

    lax.fori_loop(0, both // step, stats, 0)
    run("stats")
    raws[6].wait()
    for side in range(SIDE):
        for p in range(4 * levels):
            src = (p * SIDE + side) * PAD
            i_pack[side, :, p * PAD : (p + 1) * PAD] = up_raw[:, src : src + PAD]
    raws[5].wait()
    o_pack[...] = jnp.zeros_like(o_pack)
    for side in range(SIDE):
        for h in range(HALF_HEADS):
            for e in range(EXPERTS):
                src = e * HEADS * HEAD_DIM + (side * HALF_HEADS + h) * HEAD_DIM
                col = (e * HALF_HEADS + h) * PAD
                o_pack[side, :, col : col + HEAD_DIM] = branch_raw[:, src : src + HEAD_DIM]
    loc_o = local(o_pack.at[c], o_all.at[d, z, own], 15)
    rem_o = sibling(o_pack.at[1 - c], o_all.at[d, z, own], 5)
    loc_i = local(i_pack.at[c], i_all.at[d, z, own], 16)
    rem_i = sibling(i_pack.at[1 - c], i_all.at[d, z, own], 6)
    rem_o.start()
    rem_i.start()
    placed["o"], placed["i"] = (loc_o, rem_o), (loc_i, rem_i)
    run("packs")

    slots = MEM // local_len
    has_up, has_down = z < levels - 1, z > 0

    def slot(s):
        return pl.ds(s * local_len, local_len)

    def starts_of(block, batch):
        column = xs[block, pl.ds(batch * local_len, local_len), 2 * width : 2 * width + 128]
        return column[:, 40:41].astype(f32)

    def spread_given(i, carry):
        at = pl.ds(pl.multiple_of((i % slots) * local_len, local_len), local_len)
        pair = i // slots
        mine = dot_f32(graw[pair // batches, pair % batches, at], sel[...])
        win[pair, at] = mine.astype(bf16)
        return carry

    def keep_or(block, batch, s, moved):
        at = block * batches + batch
        held = win[at, slot(s)]
        first = jnp.broadcast_to(starts_of(block, batch), held.shape) > 0.5
        win[at, slot(s)] = jnp.where(first, held.astype(f32), moved.astype(f32)).astype(bf16)

    def message(m, batch):
        src = win.at[batches + batch, pl.ds((slots - 1 - 2 * m) * local_len, 2 * local_len)]
        return pltpu.make_async_remote_copy(
            src_ref=src, dst_ref=rbuf.at[m, batch], send_sem=gsend.at[m, batch], recv_sem=grecv.at[m, batch],
            device_id=nb["up"], device_id_type=MESH)

    rounds = slots // 2

    def send_message(m, batch):
        if m < rounds:
            pl.when(has_up)(lambda: message(m, batch).start())

    def take(m, some):
        for batch in some:
            pl.when(has_down)(lambda: message(m, batch).wait_recv())
            for k in (0, 1):
                keep_or(0, batch, slots - 1 - 2 * m - k, rbuf[m, batch, slot(1 - k)])
            for s in (slots - 2 - 2 * m, slots - 3 - 2 * m):
                if s >= 0:
                    keep_or(1, batch, s, win[batch, slot(s + 1)])
            send_message(m + 1, batch)

    def early(m):
        pl.when(z <= m)(lambda: take(m, range(batches)))

    def late(m, batch):
        pl.when(z > m)(lambda: take(m, (batch,)))

    loc_g.wait()
    rem_g.wait()
    lax.fori_loop(0, 2 * batches * slots, spread_given, 0)
    run("given")
    complete("a")
    out_a = pltpu.make_async_copy(a_all, a_out, osem.at[0])
    out_a.start()

    w_a = a_all.reshape(4 * levels * 2 * shard, W_A)
    vec[...] = w_a[:, MISC:W_A].astype(f32).T

    def norm(i, carry):
        at = pl.ds(pl.multiple_of(i * step, step), step)
        act[at] = (unit[at] * vec[COL_NORM : COL_NORM + 1] + vec[COL_NORM + 1 : COL_NORM + 2]).astype(bf16)
        return carry

    lax.fori_loop(0, both // step, norm, 0)

    def project(i, carry):
        at = pl.ds(pl.multiple_of(i * 256, 256), 256)
        front[:, at] = dot_f32(act[...], w_a[:, at])
        return carry

    lax.fori_loop(0, MISC // 256, project, 0)
    front[:, MISC:W_A] = dot_f32(act[...], w_a[:, MISC:W_A])
    run("front")
    meta_at = pl.ds(pl.multiple_of(2 * width + c * 128, 128), 128)

    def gate(i, carry):
        at = pl.ds(pl.multiple_of(i * local_len, local_len), local_len)
        gated = jax.nn.sigmoid(front[at, MISC:W_A])
        gates[at] = gated
        picks = xs[i // batches, pl.ds(pl.multiple_of((i % batches) * local_len, local_len), local_len), meta_at]
        gated = gated * picks.astype(f32)
        for h in range(HALF_HEADS):
            total = jnp.zeros((local_len, PAD), f32)
            for e in range(EXPERTS):
                lane = h * EXPERTS + e
                col = W_QK + (e * HALF_HEADS + h) * PAD
                total = total + gated[:, lane : lane + 1] * front[at, col : col + PAD]
            win[i, pl.ds(MEM, local_len), wide + h * PAD : wide + (h + 1) * PAD] = total.astype(bf16)
        win[i, pl.ds(MEM, local_len), :wide] = front[at, wide : 2 * wide].astype(bf16)
        return carry

    lax.fori_loop(0, 2 * batches, gate, 0)

    for batch in range(batches):
        keep_or(1, batch, slots - 1, win[batch, pl.ds(MEM, local_len)])
        send_message(0, batch)
    run("cache")

    spread = MEM + 2 * local_len
    table = table_by_offset(w_a, per_device, shard, local_len, spread)
    for h in range(HALF_HEADS):
        line = jnp.broadcast_to(table[COL_BIAS + h : COL_BIAS + h + 1], (local_len, spread))
        turned = pltpu.roll(line, spread - local_len + 1, 1, stride=1, stride_axis=0)
        bias[h] = turned[:, : MEM + local_len]
    run("memory")
    complete("m")
    complete("0")

    key_ids = lax.broadcasted_iota(jnp.int32, (local_len, local_len), 1)
    row_ids = lax.broadcasted_iota(jnp.int32, (local_len, local_len), 0)

    def probs_copy(i, slot_of):
        return pltpu.make_async_copy(probs.at[slot_of], probs_out.at[i], psem.at[slot_of])

    def pair_of(n):
        return (n % 2) * batches + n // 2

    def attend(n, carry):
        i = pair_of(n)
        at = pl.ds(pl.multiple_of(i * local_len, local_len), local_len)
        block, batch = i // batches, i % batches
        rows_at = pl.ds(pl.multiple_of(batch * local_len, local_len), local_len)
        count = xs[block, rows_at, 2 * width : 2 * width + 128][:, 41:42].astype(f32)
        seen = jnp.logical_and(key_ids <= row_ids, key_ids.astype(f32) < count)
        picks = xs[block, rows_at, meta_at].astype(f32) * gates[at]
        slot_of = lax.rem(n, 2)
        pl.when(n >= 2)(lambda: probs_copy(pair_of(n - 2), slot_of).wait())
        for h in range(HALF_HEADS):
            cols = slice(h * PAD, (h + 1) * PAD)
            q = front[at, cols].astype(bf16)
            s = dot_f32(q, win[i, :, cols], NT) * SCALE + bias[h]
            s = jnp.concatenate([s[:, :MEM], jnp.where(seen, s[:, MEM:], NEG)], axis=1)
            top = jnp.max(s, axis=-1, keepdims=True)
            expo = jnp.exp(s - top)
            p = expo * (1.0 / jnp.sum(expo, axis=-1, keepdims=True))
            probs[slot_of, h] = p
            p = p.astype(bf16)
            got = dot_f32(p, win[i, :, wide + h * PAD : wide + (h + 1) * PAD]).astype(bf16)
            att[at, cols] = got
            got = got.astype(f32)
            for e in range(EXPERTS):
                lane = HALF_HEADS * EXPERTS + h * EXPERTS + e
                col = (e * HALF_HEADS + h) * PAD
                mixed[at, col : col + PAD] = (picks[:, lane : lane + 1] * got).astype(bf16)
        probs_copy(i, slot_of).start()
        return carry

    lax.fori_loop(0, 2, attend, 0)
    run("half")
    for batch in range(1, batches):
        complete(str(batch))
    out_w = pltpu.make_async_copy(win, win_out, osem.at[1])
    out_w.start()
    lax.fori_loop(2, 2 * batches, attend, 0)
    for n in range(2 * batches - 2, 2 * batches):
        probs_copy(pair_of(n), n % 2).wait()
    run("attended")
    complete("o")

    w_o = o_all.reshape(4 * levels * 2 * shard, W_O)
    branch = unit
    far = pl.ds(pl.multiple_of((1 - c) * rows, rows), rows)
    near = pl.ds(pl.multiple_of(c * rows, rows), rows)

    def out_project(at):
        def body(i, carry):
            cols = pl.ds(pl.multiple_of(i * 256, 256), 256)
            branch[at, cols] = dot_f32(mixed[at], w_o[cols], NT)
            return carry

        lax.fori_loop(0, width // 256, body, 0)

    def exchange(src, dst, index):
        return pltpu.make_async_remote_copy(
            src_ref=src, dst_ref=dst, send_sem=esend.at[index], recv_sem=erecv.at[index],
            device_id=nb["c"], device_id_type=MESH)

    out_project(far)
    give = exchange(branch.at[far], arrived, 0)
    give.start()
    run("far")
    out_project(near)
    out_o = pltpu.make_async_copy(o_all, o_out, osem.at[2])
    out_o.start()
    give.wait_recv()

    def second(i, carry):
        at = pl.ds(pl.multiple_of(i * step, step), step)
        total_at = pl.ds(pl.multiple_of(c * rows + i * step, step), step)
        values = xs[c, at, :width].astype(f32) + branch[total_at] + arrived[at]
        hidden[at] = values
        centered = values - jnp.mean(values, axis=-1, keepdims=True)
        inverse = lax.rsqrt(jnp.mean(centered * centered, axis=-1, keepdims=True) + EPS)
        normed = centered * inverse * vec[COL_NORM + 2 : COL_NORM + 3] + vec[COL_NORM + 3 : COL_NORM + 4]
        n2[total_at] = normed.astype(bf16)
        return carry

    lax.fori_loop(0, rows // step, second, 0)
    pair = exchange(n2.at[near], n2.at[near], 1)
    pair.start()
    run("pair")
    pair.wait_recv()
    outs = [
        pltpu.make_async_copy(src, dst, osem.at[3 + i])
        for i, (src, dst) in enumerate((
            (xs, xs_out), (act, act_out), (front, front_out), (gates, gates_out),
            (att, att_out), (mixed, mixed_out), (hidden, hidden_out), (n2, n2_out), (vec, vec_out)))
    ]
    for cp in outs:
        cp.start()
    complete("i")
    out_i = pltpu.make_async_copy(i_all, i_out, osem.at[13])
    out_i.start()

    w_i = i_all.reshape(4 * levels * 2 * shard, i_all.shape[3])

    def activate(i, carry):
        at = pl.ds(pl.multiple_of(i * 256, 256), 256)
        pre = dot_f32(n2[...], w_i[:, at])
        below = 0.5 * (1.0 + lax.erf(pre * 0.7071067811865476))
        ffn[:, at] = (pre * below).astype(bf16)
        slope[:, at] = (below + pre * jnp.exp(-0.5 * pre * pre) * 0.3989422804014327).astype(bf16)
        return carry

    steps = ffn.shape[1] // 256
    lax.fori_loop(0, steps, activate, 0)
    run("activated")
    outs += [pltpu.make_async_copy(ffn, ffn_out, osem.at[14]), pltpu.make_async_copy(slope, slope_out, osem.at[15])]
    outs[-2].start()
    outs[-1].start()

    for m in range(rounds):
        for batch in range(batches):
            pl.when(has_up)(lambda: message(m, batch).wait_send())
    out_w.wait()
    span = ffn.shape[1] // 4
    half = width // 2

    def ffn_grad(i, carry):
        at = pl.ds(pl.multiple_of(i * span, span), span)
        for side in range(2):
            cols = slice(width + side * half, width + (side + 1) * half)
            left = jnp.concatenate([xs[0, :, cols], xs[1, :, cols]], axis=0)
            win[i, side * span : (side + 1) * span] = dot_f32(ffn[:, at], left, TN).astype(bf16)
        return carry

    lax.fori_loop(0, 4, ffn_grad, 0)
    for column in range(4):
        for side in range(2):
            outs.append(pltpu.make_async_copy(
                win.at[column, pl.ds(side * span, span)],
                fgrad_out.at[column, :, pl.ds(side * half, half)], osem.at[16 + 2 * column + side]))
            outs[-1].start()
    complete("f")
    for group in (ga, go, gi, gf):
        group.drain()
    for cp in (give, pair):
        cp.wait_send()
    out_a.wait()
    out_o.wait()
    out_i.wait()
    for cp in outs:
        cp.wait()


def forward(levels, batches, local_len, per_device, ins):
    bf16, f32 = jnp.bfloat16, jnp.float32
    shape = jax.ShapeDtypeStruct
    qk, value, router, norms, bias_in, branch, up, f, tokens, cot, vr, outr, start, count, g = ins
    shard, width = qk.shape[0], f.shape[1]
    a, o, i = [shape((SIDE, shard, w), bf16) for w in (W_A, W_O, up.shape[1] // SIDE)]
    x = shape((tokens.shape[0], 2 * width + SIDE * 128), bf16)
    rows = batches * local_len
    both = 2 * rows
    wide = HALF_HEADS * PAD
    two = lambda v: (4, levels, 2 * v.shape[1], v.shape[2])
    window = (2 * batches, MEM + local_len, 2 * wide)
    probs = (2 * batches, HALF_HEADS, local_len, MEM + local_len)
    outs = [
        (two(a), bf16), (two(o), bf16), (two(i), bf16), ((4, levels) + f.shape, bf16),
        ((2,) + x.shape, bf16), ((both, width), bf16), ((both, W_A), f32), ((both, W_MISC), f32),
        (window, bf16), (probs, f32), ((both, wide), bf16), ((both, W_O), bf16),
        ((rows, width), f32), ((both, width), bf16), ((W_MISC, width), f32), ((both, i.shape[2]), bf16),
        ((both, i.shape[2]), bf16), ((4, i.shape[2] // 4, width), bf16),
    ]
    rounds = MEM // local_len // 2
    scratch = [
        (two(a), bf16), (two(o), bf16), (two(i), bf16), ((2,) + x.shape, bf16), ((2,) + g.shape, bf16),
        (window, bf16), ((rounds, batches, 2 * local_len, 2 * wide), bf16), ((g.shape[2], 2 * wide), bf16),
        ((both, width), f32), ((both, width), bf16), ((both, W_A), f32), ((both, W_MISC), f32),
        ((W_MISC, width), f32), ((HALF_HEADS, local_len, MEM + local_len), f32), ((2,) + probs[1:], f32),
        ((both, wide), bf16), ((both, W_O), bf16), ((rows, width), f32),
        ((rows, width), f32), ((both, width), bf16), ((both, i.shape[2]), bf16), ((both, i.shape[2]), bf16),
    ]
    rounds = MEM // local_len // 2
    scratch += [(w.shape, w.dtype) for w in (qk, value, router, norms, bias_in, branch, up, vr, outr, start, count, f, a, o, i)]
    sems = [(4, 6 * levels), (4, 6 * levels), (7,), (7,), (19,), (rounds, batches), (rounds, batches), (2,), (2,), (24,), (2,)]
    hbm = pl.BlockSpec(memory_space=pl.ANY)
    return pl.pallas_call(
        functools.partial(forward_kernel, levels, batches, local_len, per_device),
        out_shape=[jax.ShapeDtypeStruct(s, k) for s, k in outs],
        in_specs=[hbm] * len(ins),
        out_specs=[hbm] * len(outs),
        scratch_shapes=[pltpu.VMEM(s, k) for s, k in scratch] + [pltpu.SemaphoreType.DMA(s) for s in sems],
        compiler_params=pltpu.CompilerParams(
            collective_id=1, has_side_effects=True, vmem_limit_bytes=VMEM_BYTES),
    )(*ins)


def add_rows(dst, terms):
    rows, width = dst.shape
    step = 16

    def body(i, carry):
        at = pl.ds(pl.multiple_of(i * step, step), step)
        total = terms[0][at].astype(jnp.float32)
        for term in terms[1:]:
            total = total + term[at].astype(jnp.float32)
        dst[at] = total.astype(dst.dtype)
        return carry

    lax.fori_loop(0, rows // step, body, 0)


class Scatter:
    def __init__(self, src, view, sems, nb, d, z, levels, total):
        self.src, self.view, self.nb, self.d, self.z, self.levels = src, view, nb, d, z, levels
        self.send, self.recv = sems
        self.sum = total
        self.half = src.shape[2] // 2
        self.by_x, self.by_y = d + 1 - 2 * (d % 2), (d + 2) % 4
        self.low, self.high = pl.ds(0, self.half), pl.ds(self.half, self.half)

    def copy(self, src, dst, slot, to):
        return pltpu.make_async_remote_copy(
            src_ref=src, dst_ref=dst, send_sem=self.send.at[slot], recv_sem=self.recv.at[slot],
            device_id=self.nb[to], device_id_type=MESH)

    def corner(self, j, to):
        part, name, base = (self.low, "cx", 0) if to == "x" else (self.high, "cy", self.levels)
        return self.copy(self.src.at[3 - self.d, j, part], self.view(name, j), base + j, to)

    def direct(self, j, to):
        if to == "x":
            column, part, name, base = self.by_x, self.low, "rx", 2 * self.levels
        else:
            column, part, name, base = self.by_y, self.high, "ry", 3 * self.levels
        return self.copy(self.src.at[column, j, part], self.view(name, j).at[part], base + j, to)

    def relay(self, j, to):
        if to == "x":
            held, part, name, base = "cy", self.high, "rx", 4 * self.levels
        else:
            held, part, name, base = "cx", self.low, "ry", 5 * self.levels
        return self.copy(self.view(held, j), self.view(name, j).at[part], base + j, to)

    def along(self, j, to, first=False):
        base = (6 if to == "up" else 7) * self.levels
        there = self.view(to, j, self.z + (1 if to == "up" else -1))
        return self.copy(self.view("rx" if first else to, j), there, base + j, to)

    def issue(self, j):
        self.corner(j, "x").start()
        self.corner(j, "y").start()
        self.direct(j, "x").start()
        self.direct(j, "y").start()

    def turn(self, j):
        self.corner(j, "x").wait_recv()
        add_rows(self.view("cx", j), [self.view("cx", j), self.src.at[self.by_y, j, self.low]])
        self.relay(j, "y").start()
        self.corner(j, "y").wait_recv()
        add_rows(self.view("cy", j), [self.view("cy", j), self.src.at[self.by_x, j, self.high]])
        self.relay(j, "x").start()

    def column(self, j):
        for to in ("x", "y"):
            self.direct(j, to).wait_recv()
            self.relay(j, to).wait_recv()
        add_rows(self.view("rx", j), [self.view("rx", j), self.view("ry", j), self.src.at[self.d, j]])

    def lift(self, j, stage):
        def hop(to):
            if stage:
                self.along(j, to).wait_recv()
                add_rows(self.view(to, j), [self.view(to, j), self.view("rx", j)])
            self.along(j, to, first=stage == 0).start()

        if stage < j:
            pl.when(self.z == stage)(lambda: hop("up"))
        if self.levels - 1 - stage > j:
            pl.when(self.z == self.levels - 1 - stage)(lambda: hop("down"))

    def total(self, j):
        @pl.when(self.z == j)
        def _():
            terms = [self.view("rx", j)]
            for to, there in (("up", j > 0), ("down", j < self.levels - 1)):
                if there:
                    self.along(j, to).wait_recv()
                    terms.append(self.view(to, j))
            add_rows(self.sum, terms)

    def drain(self):
        for j in range(self.levels):
            for to in ("x", "y"):
                self.corner(j, to).wait_send()
                self.direct(j, to).wait_send()
                self.relay(j, to).wait_send()
            pl.when(self.z < j)(lambda: self.along(j, "up").wait_send())
            pl.when(self.z > j)(lambda: self.along(j, "down").wait_send())


class LineFirst:
    def __init__(self, src, view, bufs, sems, nb, d, z, levels, total):
        self.src, self.view, self.nb, self.d, self.z, self.levels = src, view, nb, d, z, levels
        self.cx, self.cy, self.rx, self.ry = bufs
        self.send, self.recv = sems
        self.sum = total
        half = src.shape[2] // 2
        self.by_x, self.by_y = d + 1 - 2 * (d % 2), (d + 2) % 4
        self.low, self.high = pl.ds(0, half), pl.ds(half, half)

    def copy(self, src, dst, slot, to):
        return pltpu.make_async_remote_copy(
            src_ref=src, dst_ref=dst, send_sem=self.send.at[slot], recv_sem=self.recv.at[slot],
            device_id=self.nb[to], device_id_type=MESH)

    def along(self, j, column, to, level, first=False):
        slot = (0 if to == "up" else 4 * self.levels) + 4 * j + column
        after = level + (1 if to == "up" else -1)
        src = self.src.at[column, j] if first else self.view(j, column)
        return self.copy(src, self.view(self.levels if to == "down" and after == j else j, column), slot, to)

    def lift(self, j, stage):
        def hop(to, level):
            for column in range(4):
                if stage:
                    before = level - (1 if to == "up" else -1)
                    self.along(j, column, to, before).wait_recv()
                    held = self.view(j, column)
                    add_rows(held, [held, self.src.at[column, j]])
                self.along(j, column, to, level, first=stage == 0).start()

        if stage < j:
            pl.when(self.z == stage)(lambda: hop("up", stage))
        if self.levels - 1 - stage > j:
            pl.when(self.z == self.levels - 1 - stage)(lambda: hop("down", self.levels - 1 - stage))

    def gathered(self, j):
        @pl.when(self.z == j)
        def _():
            for column in range(4):
                terms = [self.src.at[column, j]]
                if j > 0:
                    self.along(j, column, "up", j - 1).wait_recv()
                    terms.append(self.view(j, column))
                if j < self.levels - 1:
                    self.along(j, column, "down", j + 1).wait_recv()
                    terms.append(self.view(self.levels, column))
                add_rows(terms[0], terms)

    def plane(self, k):
        base = 8 * self.levels
        part = lambda column, rows: self.src.at[column, self.z, rows]
        return (
            self.copy(part(3 - self.d, self.low), self.cx, base, "x"),
            self.copy(part(3 - self.d, self.high), self.cy, base + 1, "y"),
            self.copy(part(self.by_x, self.low), self.rx.at[self.low], base + 2, "x"),
            self.copy(part(self.by_y, self.high), self.ry.at[self.high], base + 3, "y"),
            self.copy(self.cy, self.rx.at[self.high], base + 4, "x"),
            self.copy(self.cx, self.ry.at[self.low], base + 5, "y"),
        )[k]

    def issue(self):
        for k in range(4):
            self.plane(k).start()

    def turn(self):
        self.plane(0).wait_recv()
        add_rows(self.cx, [self.cx, self.src.at[self.by_y, self.z, self.low]])
        self.plane(5).start()
        self.plane(1).wait_recv()
        add_rows(self.cy, [self.cy, self.src.at[self.by_x, self.z, self.high]])
        self.plane(4).start()

    def column(self):
        for k in range(2, 6):
            self.plane(k).wait_recv()
        add_rows(self.sum, [self.rx, self.ry, self.src.at[self.d, self.z]])

    def drain(self):
        for k in range(6):
            self.plane(k).wait_send()
        for j in range(self.levels):
            for column in range(4):
                for level in range(self.levels):
                    if level < j:
                        pl.when(self.z == level)(lambda: self.along(j, column, "up", level).wait_send())
                    if level > j:
                        pl.when(self.z == level)(lambda: self.along(j, column, "down", level).wait_send())


A_PARTS = (1024, 768)
AHEAD = 3


def LAGS(unit, k, levels):
    return 2 + 3 * k if unit < 3 * levels else 1 + k


O_STEPS = {4: ((0, 1), (1, 0)), 6: ((1, 1),), 7: ((2, 0), (2, 1))}


class Pipeline:
    def __init__(self, units, levels, ahead, lags):
        self.units, self.levels, self.ahead, self.now = units, levels, ahead, 0
        self.follow = [lambda s, j: s.column(j)]
        for stage in range(levels - 1):
            self.follow.append(lambda s, j, stage=stage: s.lift(j, stage))
        self.follow.append(lambda s, j: s.total(j))
        self.lags = lags
        self.done = [0] * len(units)

    def each(self, n, act):
        if 0 <= n < len(self.units):
            for scatter, j in self.units[n]:
                act(scatter, j)

    def begin(self):
        for n in range(self.ahead):
            self.each(n, lambda s, j: s.issue(j))

    def advance(self, n):
        self.each(n, self.follow[self.done[n]])
        self.done[n] += 1

    def step(self):
        n = self.now
        if n < len(self.units):
            self.each(n, lambda s, j: s.turn(j))
            self.each(n + self.ahead, lambda s, j: s.issue(j))
        for m in range(min(n + 1, len(self.units))):
            while self.done[m] < len(self.follow) and n - m >= self.lags(m, self.done[m], self.levels):
                self.advance(m)
        self.now += 1

    def turns(self):
        while self.now < len(self.units):
            self.step()

    def round(self):
        for m in range(len(self.units)):
            if self.done[m] < len(self.follow):
                self.advance(m)

    def finish(self, after):
        after = list(after)
        while True:
            for item in [a for a in after if all(self.done[n] == len(self.follow) for n in a[0])]:
                after.remove(item)
                item[1]()
            if min(self.done) == len(self.follow):
                return
            self.round()


def norm_rows(values):
    centered = values - jnp.mean(values, axis=-1, keepdims=True)
    inverse = lax.rsqrt(jnp.mean(centered * centered, axis=-1, keepdims=True) + EPS)
    return centered * inverse, inverse


def norm_rows_backward(upstream, normed, inverse, gain):
    scaled = upstream * gain
    inside = (
        scaled
        - jnp.mean(scaled, axis=-1, keepdims=True)
        - normed * jnp.mean(scaled * normed, axis=-1, keepdims=True)
    )
    return inside * inverse


VEC_ROW = COL_NORM // 8 * 8
VEC_GAIN = COL_NORM - VEC_ROW


def backward_kernel(
    levels, batches, local_len, per_device, shard,
    fgrad_in, wf_in, wi_in, wo_in, wa_in, ffn_in, slope_in, xs_in, n2_in, hidden_in, vec_in, att_in, gates_in, front_in,
    win_in, probs_in, mixed_in, act_in,
    f_out, i_out, o_out, a_out, m_out, layer_out, grad_out,
    w_f, w_i, ffn, slope, grad, meta, n2, hidden, vec, att, gates, front, win, probs,
    branch, arrived, dhid, db, dmix, dfront, dsum, norms,
    f_total, i_total, o_total, a_total, m_total, *rest,
):
    bf16, f32 = jnp.bfloat16, jnp.float32
    f_bufs, i_bufs, m_bufs = rest[:6], rest[6:12], rest[12:18]
    a_src, a_cx, a_cy, o_src, o_line, o_cx, o_cy, o_rx, o_ry = rest[18:27]
    send, recv, osend, orecv, lsem, tsem, esend, erecv, osem, ready, freed = rest[27:]
    d, t = lax.axis_index("doc"), lax.axis_index("tm")
    z, c = t // 2, t % 2
    nb = neighbours(2 * levels)
    width = w_f.shape[1]
    rows = batches * local_len
    both = 2 * rows
    wide = HALF_HEADS * PAD
    ff = ffn.shape[1]
    far = pl.ds(pl.multiple_of((1 - c) * rows, rows), rows)
    near = pl.ds(pl.multiple_of(c * rows, rows), rows)

    def load(src, dst, index):
        cp = pltpu.make_async_copy(src, dst, lsem.at[index])
        cp.start()
        return cp

    meta_at = pl.ds(pl.multiple_of(2 * width + c * 128, 128), 128)
    l_first = load(fgrad_in, f_bufs[0], 17)
    l_grad = load(xs_in.at[:, :, pl.ds(width, width)], grad, 1)
    l_wf = load(wf_in, w_f, 2)
    enter(nb, z, levels)
    l_first.wait()
    l_slope = load(slope_in, slope, 3)
    l_ffn = load(ffn_in, ffn, 0)
    l_n2 = load(n2_in, n2, 4)
    l_wi = load(wi_in, w_i, 5)
    l_hid = load(hidden_in, hidden, 6)
    l_vec = load(vec_in.at[pl.ds(VEC_ROW, 8)], vec, 7)
    l_mixed = load(mixed_in, dmix, 8)
    l_meta = load(xs_in.at[:, :, meta_at], meta, 9)
    l_att = load(att_in, att, 10)
    l_gates = load(gates_in, gates, 11)
    w_o = a_src.at[:, :, :, pl.ds(0, W_O)]
    l_wo = load(wo_in, w_o, 12)

    def tiles(i):
        at = pl.ds(i * local_len, local_len)
        return [
            pltpu.make_async_copy(win_in.at[i], win.at[i % 2], tsem.at[0, i % 2]),
            pltpu.make_async_copy(front_in.at[at, pl.ds(0, wide)], front.at[i % 2, :, pl.ds(0, wide)], tsem.at[2, i % 2]),
            pltpu.make_async_copy(
                front_in.at[at, pl.ds(W_QK, W_VAL)], front.at[i % 2, :, pl.ds(wide, W_VAL)], tsem.at[3, i % 2]),
        ]

    def probs_tile(n):
        return pltpu.make_async_copy(probs_in.at[n // HALF_HEADS, n % HALF_HEADS], probs.at[n % 2], tsem.at[1, n % 2])

    for cp in tiles(0):
        cp.start()
    probs_tile(0).start()

    names = ("cx", "cy", "rx", "ry")

    def plain(bufs):
        def view(name, j, level=z):
            if name == "up":
                return bufs[5].at[j]
            if name == "down":
                return bufs[5].at[jnp.where(level == j, levels, j)]
            return bufs[1 + names.index(name)].at[j]

        return view

    block_rows = shard * SIDE

    def within(held, cx, cy, cols):
        def view(name, j, level=z):
            if name in ("cx", "cy"):
                return (cx if name == "cx" else cy).at[j, :, cols]
            ref, base = held[name]
            return ref.at[pl.ds(base + j * block_rows, block_rows), cols]

        return view

    span = levels * block_rows
    a_held = dict(rx=(w_i, 0), ry=(w_i, span), up=(w_i, 2 * span), down=(w_i, 3 * span))
    a_cols = [pl.ds(sum(A_PARTS[:k]), A_PARTS[k]) for k in range(len(A_PARTS))]
    sums = [
        Scatter(src, view, (send.at[i], recv.at[i]), nb, d, z, levels, total)
        for i, (src, view, total) in enumerate((
            (f_bufs[0], plain(f_bufs), f_total), (i_bufs[0], plain(i_bufs), i_total),
            (m_bufs[0], plain(m_bufs), m_total)) + tuple(
                (a_src.at[:, :, :, cols], within(a_held, a_cx, a_cy, cols), a_total.at[:, cols]) for cols in a_cols))
    ]
    sf, si, sm = sums[:3]
    held = []
    for ref in (ffn, slope):
        for base in range(0, ref.shape[0], 4 * block_rows):
            held.append((ref, base))
    held = held[:levels] + [(o_line, 0)]

    def o_view(slot, column):
        ref, base = held[slot]
        return ref.at[pl.ds(base + column * block_rows, block_rows), pl.ds(0, W_O)]

    so = LineFirst(o_src, o_view, (o_cx, o_cy, o_rx, o_ry), (osend, orecv), nb, d, z, levels, o_total)
    order = []
    for k in range((levels + 1) // 2):
        order += [levels - 1 - k, k] if levels - 1 - k != k else [k]
    units = [[(s, j)] for s in [sf, si] + sums[3:] for j in order]
    units[3 * levels + 1] = units[3 * levels + 1] + [(sm, j) for j in order]
    line = Pipeline(units, levels, AHEAD, LAGS)

    def exchange(src, dst, index):
        return pltpu.make_async_remote_copy(
            src_ref=src, dst_ref=dst, send_sem=esend.at[index], recv_sem=erecv.at[index],
            device_id=nb["c"], device_id_type=MESH)

    def weight_grad(dst, left, right, chunk, total, column):
        at = pl.ds(pl.multiple_of(column * span, span), span)

        def body(i, carry):
            cols = pl.ds(pl.multiple_of(i * chunk, chunk), chunk)
            got = dot_f32(left[:, at], right[:, cols], TN).astype(bf16)
            dst[column, :, :, cols] = got.reshape(levels, block_rows, chunk)
            return carry

        lax.fori_loop(0, total // chunk, body, 0)

    line.begin()

    l_wf.wait()
    l_slope.wait()
    l_grad.wait()
    g_all = grad.reshape(both, width)

    def back(i, carry):
        at = pl.ds(pl.multiple_of(i * 256, 256), 256)
        slope[:, at] = (dot_f32(g_all[...], w_f[at], NT) * slope[:, at].astype(f32)).astype(bf16)
        return carry

    lax.fori_loop(0, ff // 256, back, 0)
    l_n2.wait()
    for column in range(4):
        weight_grad(i_bufs[0], n2, slope, 512, ff, column)
    line.step()

    l_wi.wait()

    def times(src, weights, dims):
        def run(at):
            def body(i, carry):
                cols = pl.ds(pl.multiple_of(i * 256, 256), 256)
                branch[at, cols] = dot_f32(src[at], weights(cols), dims)
                return carry

            lax.fori_loop(0, width // 256, body, 0)

        return run

    through_in = times(slope, lambda cols: w_i[cols], NT)
    through_in(far)
    give = exchange(branch.at[far], arrived, 0)
    give.start()
    through_in(near)
    line.step()
    l_hid.wait()
    l_vec.wait()
    give.wait()
    norms[...] = jnp.zeros_like(norms)
    step = 64

    def second(i, carry):
        at = pl.ds(pl.multiple_of(i * step, step), step)
        total_at = pl.ds(pl.multiple_of(c * rows + i * step, step), step)
        normed, inverse = norm_rows(hidden[at])
        up = branch[total_at] + arrived[at]
        norms[COL_NORM + 2 : COL_NORM + 3] += jnp.sum(up * normed, axis=0, keepdims=True)
        norms[COL_NORM + 3 : COL_NORM + 4] += jnp.sum(up, axis=0, keepdims=True)
        got = norm_rows_backward(up, normed, inverse, vec[VEC_GAIN + 2 : VEC_GAIN + 3])
        got = got + grad[c, at].astype(f32)
        dhid[at] = got
        db[total_at] = got.astype(bf16)
        return carry

    lax.fori_loop(0, rows // step, second, 0)
    pair = exchange(db.at[near], db.at[near], 1)
    pair.start()
    l_act = load(act_in, grad, 13)

    through_out = times(ffn, lambda cols: w_f[:, cols], (((1,), (0,)), ((), ())))
    l_ffn.wait()
    through_out(far)
    pair.wait()
    last = exchange(branch.at[far], arrived, 2)
    last.start()
    line.step()
    through_out(near)

    for name in ("x", "y"):
        pl.semaphore_signal(ready, inc=1, device_id=nb[name], device_id_type=MESH)
    for name, there in (("up", z < levels - 1), ("down", z > 0)):

        @pl.when(there)
        def _():
            pl.semaphore_signal(ready, inc=1, device_id=nb[name], device_id_type=MESH)

    l_wa = [
        load(wa_in.at[:, pl.ds(0, width)], w_f.at[pl.ds(0, width)], 14),
        load(wa_in.at[:, pl.ds(width, W_A - width)], w_f.at[pl.ds(width, width), pl.ds(0, W_A - width)], 15),
    ]
    l_mixed.wait()
    for column in range(4):
        weight_grad(o_src, db, dmix, 640, W_O, column)
    ends = jnp.where(z < levels - 1, 1, 0) + jnp.where(z > 0, 1, 0)
    pl.semaphore_wait(ready, 2 + ends)
    outer, inner_levels = order[:2], order[2:]

    def o_stage(stage, part):
        for j in part:
            so.lift(j, stage)

    def tick():
        for stage, part in O_STEPS.get(line.now, ()):
            if stage < levels - 1:
                o_stage(stage, outer if part == 0 else inner_levels)
        line.step()

    o_stage(0, outer)
    l_wo.wait()

    def mix(i, carry):
        cols = pl.ds(pl.multiple_of(i * wide, wide), wide)
        dmix[:, cols] = dot_f32(db[...], a_src[:, :, :, cols].reshape(width, wide)).astype(bf16)
        return carry

    lax.fori_loop(0, EXPERTS, mix, 0)
    l_meta.wait()
    l_att.wait()
    l_gates.wait()
    dsum[...] = jnp.zeros_like(dsum)
    lanes = lax.broadcasted_iota(jnp.int32, (local_len, W_MISC), 1)

    def attend(i):
        slot = i % 2
        if i + 1 < 2 * batches:
            for cp in tiles(i + 1):
                cp.start()
        for cp in tiles(i):
            cp.wait()
        at = pl.ds(i * local_len, local_len)
        block, batch = i // batches, i % batches
        gate = gates[at]
        picks = meta[block, pl.ds(batch * local_len, local_len)].astype(f32)
        gated = gate * picks
        d_gates = jnp.zeros((local_len, W_MISC), f32)
        for h in range(HALF_HEADS):
            cols = slice(h * PAD, (h + 1) * PAD)
            v_cols = slice(wide + h * PAD, wide + (h + 1) * PAD)
            got = att[at, cols].astype(f32)
            d_att = jnp.zeros((local_len, PAD), f32)
            for e in range(EXPERTS):
                lane = HALF_HEADS * EXPERTS + h * EXPERTS + e
                col = (e * HALF_HEADS + h) * PAD
                part = dmix[at, col : col + PAD].astype(f32)
                d_att = d_att + gated[:, lane : lane + 1] * part
                d_gates = jnp.where(lanes == lane, jnp.sum(part * got, axis=-1, keepdims=True), d_gates)
            d_att = d_att.astype(bf16)
            n = i * HALF_HEADS + h
            if n + 1 < 2 * batches * HALF_HEADS:
                probs_tile(n + 1).start()
            probs_tile(n).wait()
            p = probs[n % 2]
            d_p = dot_f32(d_att, win[slot, :, v_cols], NT)
            delta = jnp.sum(d_p * p, axis=-1, keepdims=True)
            d_s = p * (d_p - delta)
            dsum[h] += d_s
            d_s = d_s.astype(bf16)
            q = front[slot, :, cols].astype(bf16)
            d_q = dot_f32(d_s, win[slot, :, cols]) * SCALE
            d_k = dot_f32(d_s[:, MEM:], q, TN) * SCALE
            d_v = dot_f32(p[:, MEM:].astype(bf16), d_att, TN).astype(bf16).astype(f32)
            dfront[at, cols] = d_q.astype(bf16)
            dfront[at, wide + h * PAD : wide + (h + 1) * PAD] = d_k.astype(bf16)
            for e in range(EXPERTS):
                lane = h * EXPERTS + e
                col = W_QK + (e * HALF_HEADS + h) * PAD
                part = front[slot, :, col - W_QK + wide : col - W_QK + wide + PAD]
                d_gates = jnp.where(lanes == lane, jnp.sum(part * d_v, axis=-1, keepdims=True), d_gates)
                dfront[at, col : col + PAD] = (gated[:, lane : lane + 1] * d_v).astype(bf16)
        d_logits = jnp.where(lanes < N_ROUTE, d_gates * picks * gate * (1.0 - gate), 0.0)
        dfront[at, MISC:W_A] = d_logits.astype(bf16)

    attend(0)
    tick()
    attend(1)
    tick()
    for i in range(2, 2 * batches):
        attend(i)
    l_act.wait()
    one_all = grad.reshape(both, width)
    for column in range(4):
        weight_grad(a_src, one_all, dfront, 896, MISC, column)
    tick()
    last.wait()

    def final(i, carry):
        at = pl.ds(pl.multiple_of(i * step, step), step)
        total_at = pl.ds(pl.multiple_of(c * rows + i * step, step), step)
        tail = meta[c, at].astype(f32)
        position = lax.broadcasted_iota(jnp.int32, (step, 1), 0) + (i * step) % local_len
        keep = position.astype(f32) < tail[:, 41:42]
        total = hidden[at] + branch[total_at] + arrived[at]
        db[total_at] = jnp.where(keep, total, 0.0).astype(bf16)
        return carry

    lax.fori_loop(0, rows // step, final, 0)
    pl.semaphore_signal(freed, inc=1, device_id=nb["c"], device_id_type=MESH)
    outs = [pltpu.make_async_copy(db.at[near], layer_out, osem.at[0])]
    outs[0].start()

    tick()
    for cp in l_wa:
        cp.wait()

    def through_front(at):
        def body(i, carry):
            cols = pl.ds(pl.multiple_of(i * 256, 256), 256)
            below = pl.ds(pl.multiple_of(width + i * 256, 256), 256)
            branch[at, cols] = (
                dot_f32(dfront[at, :width], w_f[cols], NT)
                + dot_f32(dfront[at, width:], w_f[below, : W_A - width], NT))
            return carry

        lax.fori_loop(0, width // 256, body, 0)

    through_front(far)
    hand = exchange(branch.at[far], arrived, 3)
    pl.semaphore_wait(freed, 1)
    hand.start()
    through_front(near)
    tick()

    spread = MEM + 2 * local_len
    ids = lax.broadcasted_iota(jnp.int32, (local_len, 1), 0)
    lines = []
    for h in range(HALF_HEADS):
        turned = jnp.concatenate([dsum[h], jnp.zeros((local_len, local_len), f32)], axis=1)
        bit = 1
        while bit < local_len:
            moved = pltpu.roll(turned, bit, 1)
            turned = jnp.where(((local_len - 1 - ids) // bit) % 2 == 1, moved, turned)
            bit *= 2
        lines.append(jnp.sum(turned, axis=0, keepdims=True))
    row_of = lax.broadcasted_iota(jnp.int32, (W_MISC, spread), 0)
    table = jnp.zeros((W_MISC, spread), f32)
    for h in range(HALF_HEADS):
        table = jnp.where(row_of == COL_BIAS + h, lines[h], table)
    high = table.astype(bf16)
    low = (table - high.astype(f32)).astype(bf16)
    distance = MEM + local_len - 1 - lax.broadcasted_iota(jnp.int32, (1, spread), 1)
    bucket = bucket_index(distance)
    wanted = (bucket // per_device) * shard + bucket % per_device
    hand.wait()

    def first(i, carry):
        at = pl.ds(pl.multiple_of(i * step, step), step)
        total_at = pl.ds(pl.multiple_of(c * rows + i * step, step), step)
        normed, inverse = norm_rows(n2[at].astype(f32))
        up = branch[total_at] + arrived[at]
        norms[COL_NORM : COL_NORM + 1] += jnp.sum(up * normed, axis=0, keepdims=True)
        norms[COL_NORM + 1 : COL_NORM + 2] += jnp.sum(up, axis=0, keepdims=True)
        dhid[at] += norm_rows_backward(up, normed, inverse, vec[VEC_GAIN : VEC_GAIN + 1])
        return carry

    l_x = load(xs_in.at[c, :, pl.ds(0, width)], n2.at[pl.ds(0, rows)], 16)
    l_x.wait()
    lax.fori_loop(0, rows // step, first, 0)
    outs.append(pltpu.make_async_copy(dhid, grad_out, osem.at[1]))
    outs[1].start()
    columns = norms[...].T

    for column in range(4):
        at = pl.ds(column * span, span)
        row_ids = lax.broadcasted_iota(jnp.int32, (span, spread), 0) + column * span
        one_hot = jnp.where(row_ids == wanted, 1.0, 0.0).astype(bf16)
        misc = dot_f32(one_hot, high, NT) + dot_f32(one_hot, low, NT)
        misc = misc + dot_f32(one_all[:, at], dfront[:, MISC:W_A], TN) + columns[column * span : (column + 1) * span]
        m_bufs[0][column] = misc.astype(bf16).reshape(levels, block_rows, W_MISC)
    while line.now < len(units):
        tick()
    for stage in range(3, levels - 1):
        o_stage(stage, order)
    for j in order:
        so.gathered(j)
    so.issue()
    line.round()
    so.turn()
    line.round()
    so.column()
    mine, other = [pl.ds(pl.multiple_of(k * shard, 16), shard) for k in (c, 1 - c)]

    def hand_out(i, total, out):
        outs.append(exchange(total.at[other], out.at[c], 4 + i))
        outs[-1].start()
        outs.append(pltpu.make_async_copy(total.at[mine], out.at[c], osem.at[3 + i]))
        outs[-1].start()

    def hand_out_f():
        outs.append(pltpu.make_async_copy(f_total, f_out, osem.at[2]))
        outs[-1].start()

    hand_out(1, o_total, o_out)
    groups = [range(k * levels, (k + 1) * levels) for k in range(2)] + [range(2 * levels, len(units))]
    line.finish((
        (groups[0], hand_out_f),
        (groups[1], lambda: hand_out(0, i_total, i_out)),
        (groups[2], lambda: (hand_out(2, a_total, a_out), hand_out(3, m_total, m_out))),
    ))
    for s in sums + [so]:
        s.drain()
    for cp in outs:
        cp.wait()


def backward(levels, batches, local_len, per_device, shard, ins):
    bf16, f32 = jnp.bfloat16, jnp.float32
    (unused, w_f, w_i, w_o, w_a, ffn, slope, xs, n2, hidden, vec, att, gates, front, win, probs, mixed, act) = ins
    ff, width = w_f.shape
    rows = batches * local_len
    both = 2 * rows
    f_rows = ff // (4 * levels)
    b_rows = width // (4 * levels)
    wide = HALF_HEADS * PAD
    outs = [((f_rows, width), f32)] + [((SIDE, shard, w), f32) for w in (ff, W_O, MISC, W_MISC)]
    outs += [((rows, width), bf16), ((rows, width), f32)]
    scratch = [(v.shape, v.dtype) for v in (w_f, w_i, ffn, slope)]
    scratch += [((2, rows, width), bf16), ((2, rows, 128), bf16)]
    scratch += [(n2.shape, bf16), (hidden.shape, f32), ((8, width), f32), (att.shape, bf16), (gates.shape, f32)]
    scratch += [((2, local_len, wide + W_VAL), f32), ((2,) + win.shape[1:], bf16), ((2,) + probs.shape[2:], f32)]
    scratch += [
        ((both, width), f32), ((rows, width), f32), ((rows, width), f32), ((both, width), bf16),
        ((both, W_O), bf16), ((both, W_A), bf16), ((HALF_HEADS, local_len, MEM + local_len), f32),
        ((W_MISC, width), f32), ((f_rows, width), f32),
    ]
    scratch += [((b_rows, w), f32) for w in (ff, W_O, MISC, W_MISC)]
    for r, w in ((f_rows, width), (b_rows, ff), (b_rows, W_MISC)):
        scratch.append(((4, levels, r, w), bf16))
        scratch += [((levels, k, w), bf16) for k in (r // 2, r // 2, r, r)]
        scratch.append(((levels + 1, r, w), bf16))
    scratch.append(((4, levels, b_rows, MISC), bf16))
    scratch += [((levels, b_rows // 2, MISC), bf16)] * 2
    scratch += [((4, levels, b_rows, W_O), bf16), ((4 * b_rows, W_O), bf16)]
    scratch += [((k, W_O), bf16) for k in (b_rows // 2, b_rows // 2, b_rows, b_rows)]
    sems = [(3 + len(A_PARTS), 8 * levels)] * 2 + [(8 * levels + 6,), (8 * levels + 6,), (18,), (4, 2), (8,), (8,), (10,)]
    hbm = pl.BlockSpec(memory_space=pl.ANY)
    return pl.pallas_call(
        functools.partial(backward_kernel, levels, batches, local_len, per_device, shard),
        out_shape=[jax.ShapeDtypeStruct(s, k) for s, k in outs],
        in_specs=[hbm] * len(ins),
        out_specs=[hbm] * len(outs),
        scratch_shapes=[pltpu.VMEM(s, k) for s, k in scratch]
        + [pltpu.SemaphoreType.DMA(s) for s in sems]
        + [pltpu.SemaphoreType.REGULAR] * 2,
        compiler_params=pltpu.CompilerParams(
            collective_id=2, has_side_effects=True, vmem_limit_bytes=VMEM_BYTES),
    )(*ins)


def share_kernel(
    per_device, f_in, i_from, o_from, a_from, m_from, layer_in, grad_in,
    f_to, in_to, branch_to, value_to, qk_to, router_to, gain1_to, shift1_to, gain2_to, shift2_to, bias_to, layer_to,
    grad_to, *refs,
):
    held, sems = refs[:-1], refs[-1]
    f_hold, layer_hold, grad_hold, i_in, o_in, a_in, m_in, in_out, branch_out, value_out, qk_out, router_out = held[:12]
    gain1, shift1, gain2, shift2, bias_out = held[12:]
    whole = ((grad_in, grad_hold, grad_to), (layer_in, layer_hold, layer_to), (f_in, f_hold, f_to))
    parts = ((i_from, i_in), (o_from, o_in), (a_from, a_in), (m_from, m_in))
    small = [pltpu.make_async_copy(src, dst, sems.at[6 + i]) for i, (src, dst) in enumerate(parts)]
    there = [pltpu.make_async_copy(src, dst, sems.at[i]) for i, (src, dst, unused) in enumerate(whole)]
    back = [pltpu.make_async_copy(src, dst, sems.at[3 + i]) for i, (unused, src, dst) in enumerate(whole)]
    for cp in small + there:
        cp.start()
    done = (
        (in_out, in_to), (value_out, value_to), (branch_out, branch_to), (qk_out, qk_to), (router_out, router_to),
        (gain1, gain1_to), (shift1, shift1_to), (gain2, gain2_to), (shift2, shift2_to), (bias_out, bias_to))
    done = [pltpu.make_async_copy(src, dst, sems.at[10 + i]) for i, (src, dst) in enumerate(done)]
    small[0].wait()
    for side in range(SIDE):
        for p in range(i_in.shape[2] // PAD):
            col = (p * SIDE + side) * PAD
            in_out[:, col : col + PAD] = i_in[side, :, p * PAD : (p + 1) * PAD]
    done[0].start()
    for cp, after in zip(there, back):
        cp.wait()
        after.start()
    for cp in small[1:]:
        cp.wait()
    for side in range(SIDE):
        for h in range(HALF_HEADS):
            at = (side * HALF_HEADS + h) * HEAD_DIM
            for e in range(EXPERTS):
                col, dst = (e * HALF_HEADS + h) * PAD, e * HEADS * HEAD_DIM + at
                value_out[:, dst : dst + HEAD_DIM] = a_in[side, :, W_QK + col : W_QK + col + HEAD_DIM]
                branch_out[:, dst : dst + HEAD_DIM] = o_in[side, :, col : col + HEAD_DIM]
            for kind in range(2):
                col, dst = (kind * HALF_HEADS + h) * PAD, kind * HEADS * HEAD_DIM + at
                qk_out[:, dst : dst + HEAD_DIM] = a_in[side, :, col : col + HEAD_DIM]
        routes = HALF_HEADS * EXPERTS
        for kind in range(2):
            dst = (kind * SIDE + side) * routes
            router_out[:, dst : dst + routes] = m_in[side, :, kind * routes : (kind + 1) * routes]
        turned = m_in[side].T
        bias_out[side * HALF_HEADS : (side + 1) * HALF_HEADS] = turned[COL_BIAS : COL_BIAS + HALF_HEADS, :per_device]
    turned = (m_in[0] + m_in[1]).T
    for i, out in enumerate((gain1, shift1, gain2, shift2)):
        out[...] = turned[COL_NORM + i : COL_NORM + i + 1]
    for cp in done[1:]:
        cp.start()
    for cp in back + done:
        cp.wait()


def shares_of(per_device, ins):
    f, i, o, a, m, layer, grad = ins
    shard = i.shape[1]
    inner = HEADS * HEAD_DIM
    f32 = jnp.float32
    shapes = [
        (f.shape, f32), ((shard, SIDE * i.shape[2]), f32), ((shard, EXPERTS * inner), f32),
        ((shard, EXPERTS * inner), f32), ((shard, 2 * inner), f32), ((shard, 2 * HEADS * EXPERTS), f32)]
    shapes += [((1, shard), f32)] * 4 + [((HEADS, per_device), f32), (layer.shape, layer.dtype), (grad.shape, f32)]
    hbm = pl.BlockSpec(memory_space=pl.ANY)
    return pl.pallas_call(
        functools.partial(share_kernel, per_device),
        out_shape=[jax.ShapeDtypeStruct(s, k) for s, k in shapes],
        in_specs=[hbm] * 7,
        out_specs=[hbm] * len(shapes),
        scratch_shapes=[pltpu.VMEM(w.shape, w.dtype) for w in (f, layer, grad, i, o, a, m)]
        + [pltpu.VMEM(s, k) for s, k in shapes[1:-2]]
        + [pltpu.SemaphoreType.DMA((20,))],
        compiler_params=pltpu.CompilerParams(vmem_limit_bytes=VMEM_BYTES),
    )(*ins)


def on_chip(
    tokens, cotangent, given_cache, value_routes, output_routes, valid_counts, doc_starts,
    norm1_gain, norm1_shift, qk_weight, router_weight, value_weight, output_weight, rel_bias,
    norm2_gain, norm2_shift, ffn_in, ffn_out,
):
    batches, unused_row, local_len, width = tokens.shape
    count = lax.axis_size("tm")
    levels = count // 2
    side = lax.axis_index("tm") % 2
    rows = batches * local_len
    shard = qk_weight.shape[0]
    blocks = 4 * levels
    bf16, f32 = jnp.bfloat16, jnp.float32

    norms = jnp.stack([norm1_gain, norm1_shift, norm2_gain, norm2_shift])
    routes = [
        jnp.transpose(r.reshape(batches, local_len, HEADS, TOPK), (0, 2, 3, 1)) for r in (value_routes, output_routes)]
    buckets = rel_bias.shape[1]
    hidden_block = ffn_out.shape[0]
    (a_all, o_all, i_all, f_all, xs, act_one, front, gates, win, probs, attended, mixed, hidden, n2, vec, act,
     slope, f_grad) = forward(
        levels, batches, local_len, buckets,
        (qk_weight, value_weight, router_weight, norms, rel_bias, output_weight.T, ffn_in, ffn_out,
         tokens.reshape(rows, width), cotangent.reshape(rows, width), routes[0], routes[1],
         doc_starts.reshape(1, batches), valid_counts.reshape(1, batches),
         given_cache.reshape(batches, MEM, 2 * HEADS * HEAD_DIM)))
    w_a = a_all.reshape(width, W_A)
    w_i = i_all.reshape(width, -1)
    w_f = f_all.reshape(-1, width)
    sums = backward(
        levels, batches, local_len, buckets, shard,
        (f_grad.reshape(4, levels, hidden_block, width), w_f, w_i, o_all, w_a, act, slope, xs, n2, hidden, vec, attended, gates, front, win, probs, mixed,
         act_one.reshape(2, rows, width)))
    (out_share, in_share, branch_share, value_share, qk_share, router_share, gain1, shift1, gain2, shift2, bias_share,
     layer_out, input_grad) = shares_of(buckets, sums)
    gain1, shift1, gain2, shift2 = [v.reshape(shard) for v in (gain1, shift1, gain2, shift2)]
    return (
        layer_out.reshape(tokens.shape), input_grad.reshape(tokens.shape), gain1, shift1, qk_share, router_share,
        value_share, branch_share.T, bias_share, gain2, shift2, in_share, out_share,
    )


def by_size(*args):
    thin = args[9].shape[0] % 16 != 0
    paired = lax.axis_size("doc") == 4 and lax.axis_size("tm") % 2 == 0 and lax.axis_size("tm") >= 8
    return on_device(*args) if thin or not paired else on_chip(*args)


def solution(mesh):
    return jax.shard_map(
        by_size,
        mesh=mesh,
        in_specs=(
            P(None, "doc", "tm", None),
            P(None, "doc", "tm", None),
            P(None, "doc", "tm", None),
            P(None, "doc", "tm", None, None),
            P(None, "doc", "tm", None, None),
            P(None, "doc", "tm"),
            P(None, "doc", "tm"),
            P(("doc", "tm")),
            P(("doc", "tm")),
            P(("doc", "tm"), None),
            P(("doc", "tm"), None),
            P(("doc", "tm"), None),
            P(None, ("doc", "tm")),
            P(None, ("doc", "tm")),
            P(("doc", "tm")),
            P(("doc", "tm")),
            P(("doc", "tm"), None),
            P(("doc", "tm"), None),
        ),
        out_specs=(
            P(None, "doc", "tm", None),
            P(None, "doc", "tm", None),
            P(("doc", "tm")),
            P(("doc", "tm")),
            P(("doc", "tm"), None),
            P(("doc", "tm"), None),
            P(("doc", "tm"), None),
            P(None, ("doc", "tm")),
            P(None, ("doc", "tm")),
            P(("doc", "tm")),
            P(("doc", "tm")),
            P(("doc", "tm"), None),
            P(("doc", "tm"), None),
        ),
        check_vma=False,
    )
```

```python
import functools

import jax
import jax.numpy as jnp
from jax import lax
from jax.experimental import pallas as pl
from jax.experimental.pallas import tpu as pltpu
from jax.sharding import PartitionSpec as P

HEADS = 4
HEAD_DIM = 112
EXPERTS = 5
TOPK = 2
MEM = 1024
BUCKETS = 256
NEAR = 128
STEP = 16


EPS = 1e-05
NEG = -1e30
HIGH = lax.Precision.HIGHEST


def shortened(array):
    return jax.tree.map(lambda a: a.astype(jnp.bfloat16) if a.dtype == jnp.float32 else a, array)


def from_behind(value, axis, steps):
    count = lax.axis_size(axis)
    first, last = (max(0, -steps), min(count, count - steps))
    return lax.ppermute(value, axis, [(source, source + steps) for source in range(first, last)])


def norm_forward(values, gain, shift):
    center_mean = jnp.mean(values, axis=-1, keepdims=True)
    centered = values - center_mean
    inverse = lax.rsqrt(jnp.mean(centered * centered, axis=-1, keepdims=True) + EPS)
    normed = centered * inverse
    return (normed * gain + shift, normed, inverse)


def norm_backward(upstream, normed, inverse, gain):
    scaled = upstream * gain
    inside = (
        scaled
        - jnp.mean(scaled, axis=-1, keepdims=True)
        - normed * jnp.mean(scaled * normed, axis=-1, keepdims=True)
    )
    return (inside * inverse, jnp.sum(upstream * normed, axis=0), jnp.sum(upstream, axis=0))


def selection(routes):
    expert_ids = jnp.arange(EXPERTS, dtype=jnp.int32)
    return jnp.sum((routes[..., None] == expert_ids).astype(jnp.float32), axis=-2)


def bucket_index(distance):
    far_bucket = NEAR + (distance - NEAR) // STEP
    return jnp.clip(jnp.where(distance < NEAR, distance, far_bucket), 0, BUCKETS - 1)


def gelu_slope(pre_act):
    return (
        0.5 * (1.0 + lax.erf(pre_act * 0.7071067811865476))
        + pre_act * jnp.exp(-0.5 * pre_act * pre_act) * 0.3989422804014327
    )


def flatten(matrix):
    return matrix.reshape(-1)


def bucket_matrix(local_len):
    spread = MEM + 2 * local_len - 1
    distance = jnp.arange(spread, dtype=jnp.int32) - (local_len - 1)
    bucket_ids = jnp.arange(BUCKETS, dtype=jnp.int32)
    return (bucket_index(distance)[:, None] == bucket_ids[None, :]).astype(jnp.float32)


def bias_matrix(table, local_len):
    spread = MEM + 2 * local_len - 1
    window = MEM + local_len
    by_distance = jnp.einsum("hc,kc->hk", table, bucket_matrix(local_len), precision=HIGH)
    turned = jnp.concatenate([by_distance[:, ::-1], jnp.zeros((HEADS, 1), jnp.float32)], axis=1)
    tiled = jnp.tile(turned, (1, local_len))[:, : local_len * spread].reshape(
        HEADS, local_len, spread
    )
    return tiled[:, :, local_len - 1 : local_len - 1 + window]


def bias_backward(score_sum, local_len):
    spread = MEM + 2 * local_len - 1
    padded = jnp.pad(score_sum, ((0, 0), (0, 0), (local_len - 1, 0))).reshape(
        HEADS, local_len * spread
    )
    padded = jnp.pad(padded, ((0, 0), (0, local_len))).reshape(HEADS, local_len, spread + 1)
    by_distance = jnp.sum(padded, axis=1)[:, :spread][:, ::-1]
    return jnp.einsum("hk,kc->hc", by_distance, bucket_matrix(local_len), precision=HIGH)


def attention_scores(queries, keys, table, counts):
    local_len = queries.shape[1]
    window = keys.shape[1]
    raw = jnp.einsum(
        "bqhd,bkhd->bhqk", queries, keys, preferred_element_type=jnp.float32
    ) * HEAD_DIM ** (-0.5)
    row_ids = jnp.arange(local_len, dtype=jnp.int32)[:, None]
    col_ids = jnp.arange(window, dtype=jnp.int32)[None, :]
    bias = bias_matrix(table, local_len)
    own_ids = col_ids - MEM
    causal = (own_ids <= row_ids)[None, None]
    live = own_ids[None, None] < counts[:, None, None, None]
    valid = jnp.logical_or((col_ids < MEM)[None, None], jnp.logical_and(causal, live))
    return (jnp.where(valid, raw + bias[None], NEG), valid)


def memory_by_hops(cache_own, given, starts, local_len):
    hops_total = MEM // local_len
    open_flag = jnp.logical_not(starts)[:, None, None]
    memory_slots = [jnp.zeros_like(cache_own) for _ in range(hops_total)]
    start_marks = starts.astype(jnp.bfloat16)
    for distance in range(1, hops_total + 1):
        if distance < hops_total:
            outgoing = (cache_own, start_marks, given[:, distance * local_len :])
        else:
            outgoing = (cache_own, start_marks)
        incoming = jax.tree.map(
            lambda part, own: part.astype(own.dtype),
            from_behind(shortened(outgoing), "tm", distance),
            outgoing,
        )
        memory_slots[hops_total - distance] = jnp.where(
            open_flag, incoming[0], memory_slots[hops_total - distance]
        )
        arrived = jnp.logical_and(open_flag, (incoming[1] > 0)[:, None, None])
        if distance < hops_total:
            for position in range(hops_total - distance):
                portion = incoming[2][:, position * local_len : (position + 1) * local_len]
                memory_slots[position] = jnp.where(arrived, portion, memory_slots[position])
        open_flag = jnp.logical_and(open_flag, jnp.logical_not(arrived))
    assembled = jnp.concatenate(memory_slots, axis=1)
    return jnp.where(starts[:, None, None], given, assembled)


def on_device(
    tokens,
    cotangent,
    given_cache,
    value_routes,
    output_routes,
    valid_counts,
    doc_starts,
    norm1_gain,
    norm1_shift,
    qk_weight,
    router_weight,
    value_weight,
    output_weight,
    rel_bias,
    norm2_gain,
    norm2_shift,
    ffn_in,
    ffn_out,
):
    batches, unused_row, local_len, model_width = tokens.shape
    row_count = batches * local_len
    inner_width = HEADS * HEAD_DIM
    head_experts = HEADS * EXPERTS
    full_weights = (
        lax.all_gather(norm1_gain, ("doc", "tm"), axis=0, tiled=True),
        lax.all_gather(norm1_shift, ("doc", "tm"), axis=0, tiled=True),
        lax.all_gather(qk_weight, ("doc", "tm"), axis=0, tiled=True),
        lax.all_gather(router_weight, ("doc", "tm"), axis=0, tiled=True),
        lax.all_gather(value_weight, ("doc", "tm"), axis=0, tiled=True),
        lax.all_gather(output_weight, ("doc", "tm"), axis=1, tiled=True),
        lax.all_gather(rel_bias, ("doc", "tm"), axis=1, tiled=True),
        lax.all_gather(norm2_gain, ("doc", "tm"), axis=0, tiled=True),
        lax.all_gather(norm2_shift, ("doc", "tm"), axis=0, tiled=True),
        lax.all_gather(ffn_in, ("doc", "tm"), axis=0, tiled=True),
        lax.all_gather(ffn_out, ("doc", "tm"), axis=0, tiled=True),
    )
    (
        gain_one,
        shift_one,
        w_qk,
        w_router,
        w_value,
        w_output,
        table_bf,
        gain_two,
        shift_two,
        w_in,
        w_out,
    ) = full_weights
    gain_one = gain_one.astype(jnp.float32)
    shift_one = shift_one.astype(jnp.float32)
    gain_two = gain_two.astype(jnp.float32)
    shift_two = shift_two.astype(jnp.float32)
    table = table_bf.astype(jnp.float32)
    router_f = w_router.astype(jnp.float32)
    inputs = tokens.reshape(row_count, model_width).astype(jnp.float32)
    counts = valid_counts.reshape(batches)
    starts = doc_starts.reshape(batches) > 0
    token_mask = (
        (jnp.arange(local_len, dtype=jnp.int32)[None, :] < counts[:, None])
        .astype(jnp.float32)
        .reshape(row_count, 1)
    )
    value_pick = selection(value_routes.reshape(row_count, HEADS, TOPK))
    output_pick = selection(output_routes.reshape(row_count, HEADS, TOPK))
    normed_one, norm1_unit, norm1_inv = norm_forward(inputs, gain_one, shift_one)
    act_one = normed_one.astype(jnp.bfloat16)
    qk_vals = jnp.dot(act_one, w_qk, preferred_element_type=jnp.float32).astype(jnp.bfloat16)
    gates = jax.nn.sigmoid(jnp.dot(act_one, w_router, preferred_element_type=jnp.float32))
    gate_value = gates[:, :head_experts].reshape(row_count, HEADS, EXPERTS) * value_pick
    gate_output = gates[:, head_experts:].reshape(row_count, HEADS, EXPERTS) * output_pick
    value_gate_t = jnp.transpose(gate_value, (0, 2, 1))[..., None]
    output_gate_t = jnp.transpose(gate_output, (0, 2, 1))[..., None]
    parts = jnp.dot(act_one, w_value, preferred_element_type=jnp.float32).reshape(
        row_count, EXPERTS, HEADS, HEAD_DIM
    )
    values = (
        jnp.sum(value_gate_t * parts, axis=1).reshape(row_count, inner_width).astype(jnp.bfloat16)
    )
    cache_own = jnp.concatenate([qk_vals[:, inner_width:], values], axis=1).reshape(
        batches, local_len, 2 * inner_width
    )
    given = given_cache.reshape(batches, MEM, 2 * inner_width)
    memory = memory_by_hops(cache_own, given, starts, local_len)
    queries = qk_vals[:, :inner_width].reshape(batches, local_len, HEADS, HEAD_DIM)
    keys = jnp.concatenate([memory[:, :, :inner_width], cache_own[:, :, :inner_width]], axis=1)
    keys = keys.reshape(batches, MEM + local_len, HEADS, HEAD_DIM)
    vals = jnp.concatenate([memory[:, :, inner_width:], cache_own[:, :, inner_width:]], axis=1)
    vals = vals.reshape(batches, MEM + local_len, HEADS, HEAD_DIM)
    scores, valid = attention_scores(queries, keys, table, counts)
    top = jnp.max(scores, axis=-1, keepdims=True)
    expo = jnp.exp(scores - top)
    denom = jnp.sum(expo, axis=-1, keepdims=True)
    log_total = top + jnp.log(denom)
    probs_b = (expo / denom).astype(jnp.bfloat16)
    attended = jnp.einsum("bhqk,bkhd->bqhd", probs_b, vals, preferred_element_type=jnp.float32)
    attended = attended.reshape(row_count, inner_width).astype(jnp.bfloat16)
    attended_f = attended.astype(jnp.float32).reshape(row_count, 1, HEADS, HEAD_DIM)
    mixed = (
        (output_gate_t * attended_f).reshape(row_count, EXPERTS * inner_width).astype(jnp.bfloat16)
    )
    hidden = inputs + jnp.dot(mixed, w_output, preferred_element_type=jnp.float32)
    normed_two, norm2_unit, norm2_inv = norm_forward(hidden, gain_two, shift_two)
    act_two = normed_two.astype(jnp.bfloat16)
    pre_act = jnp.dot(act_two, w_in, preferred_element_type=jnp.float32)
    activated = jax.nn.gelu(pre_act, approximate=False).astype(jnp.bfloat16)
    ffn_result = jnp.dot(activated, w_out, preferred_element_type=jnp.float32)
    layer_out = (token_mask * (hidden + ffn_result)).astype(jnp.bfloat16).reshape(tokens.shape)
    upstream = cotangent.reshape(row_count, model_width).astype(jnp.float32) * token_mask
    upstream_b = upstream.astype(jnp.bfloat16)
    d_out_w = jnp.einsum("nf,nd->fd", activated, upstream_b, preferred_element_type=jnp.float32)
    d_act = jnp.einsum("nd,fd->nf", upstream_b, w_out, preferred_element_type=jnp.float32)
    d_pre = (d_act * gelu_slope(pre_act)).astype(jnp.bfloat16)
    d_in_w = jnp.einsum("nd,nf->df", act_two, d_pre, preferred_element_type=jnp.float32)
    d_norm_two = jnp.einsum("nf,df->nd", d_pre, w_in, preferred_element_type=jnp.float32)
    d_from_two, d_gain_two, d_shift_two = norm_backward(d_norm_two, norm2_unit, norm2_inv, gain_two)
    d_hidden = upstream + d_from_two
    ffn_width = d_in_w.shape[1]
    d_branch = d_hidden.astype(jnp.bfloat16)
    d_output_t = jnp.einsum("nd,nk->dk", d_branch, mixed, preferred_element_type=jnp.float32)
    d_mixed = jnp.einsum(
        "nd,kd->nk", d_branch, w_output, preferred_element_type=jnp.float32
    ).astype(jnp.bfloat16)
    d_mixed = d_mixed.astype(jnp.float32).reshape(row_count, EXPERTS, HEADS, HEAD_DIM)
    d_gate_out = jnp.sum(d_mixed * attended_f, axis=-1)
    d_attended = (
        jnp.sum(d_mixed * output_gate_t, axis=1)
        .astype(jnp.bfloat16)
        .reshape(batches, local_len, HEADS, HEAD_DIM)
    )
    probs = jnp.where(valid, jnp.exp(scores - log_total), 0.0)
    d_probs = jnp.einsum("bqhd,bkhd->bhqk", d_attended, vals, preferred_element_type=jnp.float32)
    delta = jnp.sum(d_probs * probs, axis=-1, keepdims=True)
    d_scores = probs * (d_probs - delta)
    score_sum = jnp.sum(d_scores, axis=0)
    d_table = bias_backward(score_sum, local_len)
    d_scores_b = d_scores.astype(jnp.bfloat16)
    scale = HEAD_DIM ** (-0.5)
    d_queries = (
        jnp.einsum("bhqk,bkhd->bqhd", d_scores_b, keys, preferred_element_type=jnp.float32) * scale
    )
    d_keys = (
        jnp.einsum(
            "bhqk,bqhd->bkhd", d_scores_b[..., MEM:], queries, preferred_element_type=jnp.float32
        )
        * scale
    )
    d_vals = jnp.einsum(
        "bhqk,bqhd->bkhd", probs_b[..., MEM:], d_attended, preferred_element_type=jnp.float32
    )
    d_qk = jnp.concatenate(
        [d_queries.reshape(row_count, inner_width), d_keys.reshape(row_count, inner_width)], axis=1
    ).astype(jnp.bfloat16)
    d_values = (
        d_vals.reshape(row_count, 1, HEADS, HEAD_DIM).astype(jnp.bfloat16).astype(jnp.float32)
    )
    d_gate_val = jnp.sum(parts * d_values, axis=-1)
    d_parts = (
        (value_gate_t * d_values).reshape(row_count, EXPERTS * inner_width).astype(jnp.bfloat16)
    )
    d_gates = jnp.concatenate(
        [
            jnp.transpose(d_gate_val, (0, 2, 1)).reshape(row_count, head_experts)
            * value_pick.reshape(row_count, head_experts),
            jnp.transpose(d_gate_out, (0, 2, 1)).reshape(row_count, head_experts)
            * output_pick.reshape(row_count, head_experts),
        ],
        axis=1,
    )
    d_logits = d_gates * gates * (1.0 - gates)
    d_qk_w = jnp.einsum("nd,nk->dk", act_one, d_qk, preferred_element_type=jnp.float32)
    d_value_w = jnp.einsum("nd,nk->dk", act_one, d_parts, preferred_element_type=jnp.float32)
    d_router_w = jnp.einsum("nd,nk->dk", act_one.astype(jnp.float32), d_logits, precision=HIGH)
    d_norm_one = jnp.einsum("nk,dk->nd", d_qk, w_qk, preferred_element_type=jnp.float32)
    d_norm_one = d_norm_one + jnp.einsum(
        "nk,dk->nd", d_parts, w_value, preferred_element_type=jnp.float32
    )
    d_norm_one = d_norm_one + jnp.einsum("nk,dk->nd", d_logits, router_f, precision=HIGH)
    d_from_one, d_gain_one, d_shift_one = norm_backward(d_norm_one, norm1_unit, norm1_inv, gain_one)
    input_grad = (d_hidden + d_from_one).reshape(tokens.shape)
    shares = (
        lax.psum_scatter(d_gain_one, ("doc", "tm"), scatter_dimension=0, tiled=True),
        lax.psum_scatter(d_shift_one, ("doc", "tm"), scatter_dimension=0, tiled=True),
        lax.psum_scatter(flatten(d_qk_w), ("doc", "tm"), scatter_dimension=0, tiled=True),
        lax.psum_scatter(flatten(d_router_w), ("doc", "tm"), scatter_dimension=0, tiled=True),
        lax.psum_scatter(flatten(d_value_w), ("doc", "tm"), scatter_dimension=0, tiled=True),
        lax.psum_scatter(flatten(d_output_t), ("doc", "tm"), scatter_dimension=0, tiled=True),
        lax.psum_scatter(d_table, ("doc", "tm"), scatter_dimension=1, tiled=True),
        lax.psum_scatter(d_gain_two, ("doc", "tm"), scatter_dimension=0, tiled=True),
        lax.psum_scatter(d_shift_two, ("doc", "tm"), scatter_dimension=0, tiled=True),
        lax.psum_scatter(flatten(d_in_w), ("doc", "tm"), scatter_dimension=0, tiled=True),
        lax.psum_scatter(flatten(d_out_w), ("doc", "tm"), scatter_dimension=0, tiled=True),
    )
    qk_share = shares[2].reshape(-1, 2 * inner_width)
    router_share = shares[3].reshape(-1, 2 * head_experts)
    value_share = shares[4].reshape(-1, EXPERTS * inner_width)
    output_share = shares[5].reshape(-1, EXPERTS * inner_width).T
    in_share = shares[9].reshape(-1, ffn_width)
    out_share = shares[10].reshape(-1, model_width)
    return (
        layer_out,
        input_grad,
        shares[0],
        shares[1],
        qk_share,
        router_share,
        value_share,
        output_share,
        shares[6],
        shares[7],
        shares[8],
        in_share,
        out_share,
    )


MESH = pl.DeviceIdType.MESH
PAD = 128
SIDE = 2
HALF_HEADS = HEADS // SIDE
W_QK = 2 * HALF_HEADS * PAD
W_VAL = EXPERTS * HALF_HEADS * PAD
W_MISC = 128
W_A = W_QK + W_VAL + W_MISC
W_O = EXPERTS * HALF_HEADS * PAD
MISC = W_QK + W_VAL
N_ROUTE = 2 * HALF_HEADS * EXPERTS
COL_NORM = N_ROUTE
COL_BIAS = N_ROUTE + 4
VMEM_BYTES = 63 * 1024 * 1024
SCALE = HEAD_DIM ** (-0.5)


def pad_last(a, width):
    return jnp.pad(a, [(0, 0)] * (a.ndim - 1) + [(0, width - a.shape[-1])])


def neighbours(count):
    d, t = lax.axis_index("doc"), lax.axis_index("tm")
    z, c = t // 2, t % 2
    return dict(
        c=(d, z * 2 + 1 - c),
        x=(d + 1 - 2 * (d % 2), t),
        y=((d + 2) % 4, t),
        up=(d, jnp.minimum(t + 2, count - 1)),
        down=(d, jnp.maximum(t - 2, 0)),
    )


def enter(nb, z, levels):
    barrier = pltpu.get_barrier_semaphore()
    for name in ("c", "x", "y"):
        pl.semaphore_signal(barrier, inc=1, device_id=nb[name], device_id_type=MESH)

    @pl.when(z < levels - 1)
    def _():
        pl.semaphore_signal(barrier, inc=1, device_id=nb["up"], device_id_type=MESH)

    @pl.when(z > 0)
    def _():
        pl.semaphore_signal(barrier, inc=1, device_id=nb["down"], device_id_type=MESH)

    ends = jnp.where(z < levels - 1, 1, 0) + jnp.where(z > 0, 1, 0)
    pl.semaphore_wait(barrier, 3 + ends)


class Gather:
    def __init__(self, ref, sems, nb, d, z, levels):
        self.ref, self.nb, self.d, self.z, self.levels = ref, nb, d, z, levels
        self.send, self.recv = sems
        self.half = ref.shape[2] // 2

    def copy(self, part, slot, to):
        return pltpu.make_async_remote_copy(
            src_ref=part, dst_ref=part, send_sem=self.send.at[slot], recv_sem=self.recv.at[slot],
            device_id=self.nb[to], device_id_type=MESH)

    def along(self, level, distance, to):
        base = 0 if to == "up" else self.levels
        return self.copy(self.ref.at[self.d, level], base + distance, to)

    def across(self, level, to, column=None):
        base = (2 if to == "x" else 3) * self.levels
        column = self.d if column is None else column
        return self.copy(self.ref.at[column, level], base + level, to)

    def corner(self, level, to, column):
        base = (4 if to == "x" else 5) * self.levels
        rows = pl.ds(self.half, self.half) if to == "x" else pl.ds(0, self.half)
        return self.copy(self.ref.at[column, level, rows], base + level, to)

    def begin(self):
        z, levels = self.z, self.levels

        @pl.when(z < levels - 1)
        def _():
            self.along(z, 1, "up").start()

        @pl.when(z > 0)
        def _():
            self.along(z, 1, "down").start()

        self.across(z, "x").start()
        self.across(z, "y").start()

    def line(self, k):
        z, levels = self.z, self.levels

        @pl.when(z >= k)
        def _():
            self.along(z - k, k, "up").wait_recv()

            @pl.when(z < levels - 1)
            def _():
                self.along(z - k, k + 1, "up").start()

            self.across(z - k, "x").start()
            self.across(z - k, "y").start()

        @pl.when(z + k < levels)
        def _():
            self.along(z + k, k, "down").wait_recv()

            @pl.when(z > 0)
            def _():
                self.along(z + k, k + 1, "down").start()

            self.across(z + k, "x").start()
            self.across(z + k, "y").start()

    def turn(self, k):
        z, levels, d = self.z, self.levels, self.d
        by_x, by_y = d + 1 - 2 * (d % 2), (d + 2) % 4

        def one(level):
            self.across(level, "x").wait_recv()
            self.corner(level, "y", by_x).start()
            self.across(level, "y").wait_recv()
            self.corner(level, "x", by_y).start()

        if k == 0:
            one(z)
        else:
            pl.when(z >= k)(lambda: one(z - k))
            pl.when(z + k < levels)(lambda: one(z + k))

    def finish(self, k):
        z, levels, d = self.z, self.levels, self.d
        by_x, by_y = d + 1 - 2 * (d % 2), (d + 2) % 4

        def one(level):
            self.corner(level, "x", by_y).wait_recv()
            self.corner(level, "y", by_x).wait_recv()

        if k == 0:
            one(z)
        else:
            pl.when(z >= k)(lambda: one(z - k))
            pl.when(z + k < levels)(lambda: one(z + k))

    def drain(self):
        z, levels, d = self.z, self.levels, self.d
        by_x, by_y = d + 1 - 2 * (d % 2), (d + 2) % 4
        for level in range(levels):
            self.across(level, "x").wait_send()
            self.across(level, "y").wait_send()
            self.corner(level, "x", by_y).wait_send()
            self.corner(level, "y", by_x).wait_send()
        for k in range(1, levels):

            @pl.when(jnp.logical_and(z >= k - 1, z < levels - 1))
            def _():
                self.along(z - k + 1, k, "up").wait_send()

            @pl.when(jnp.logical_and(z + k - 1 < levels, z > 0))
            def _():
                self.along(z + k - 1, k, "down").wait_send()


def selector(side):
    inner = HEADS * HEAD_DIM
    wide = HALF_HEADS * PAD
    src = lax.broadcasted_iota(jnp.int32, (2 * inner, 2 * wide), 0)
    dst = lax.broadcasted_iota(jnp.int32, (2 * inner, 2 * wide), 1)
    kind, head, feature = dst // wide, (dst // PAD) % HALF_HEADS, dst % PAD
    wanted = kind * inner + (side * HALF_HEADS + head) * HEAD_DIM + feature
    hit = jnp.logical_and(src == wanted, feature < HEAD_DIM)
    return jnp.where(hit, 1.0, 0.0).astype(jnp.bfloat16)


def table_by_offset(w_a, per_device, shard, local_len, spread):
    distance = MEM + local_len - 1 - lax.broadcasted_iota(jnp.int32, (1, spread), 1)
    bucket = bucket_index(distance)
    wanted = (bucket // per_device) * shard + bucket % per_device
    step = 128

    def body(i, total):
        at = pl.ds(pl.multiple_of(i * step, step), step)
        ids = lax.broadcasted_iota(jnp.int32, (step, spread), 0) + i * step
        one_hot = jnp.where(ids == wanted, 1.0, 0.0).astype(jnp.bfloat16)
        return total + dot_f32(w_a[at, MISC:W_A], one_hot, TN)

    return lax.fori_loop(0, w_a.shape[0] // step, body, jnp.zeros((W_MISC, spread), jnp.float32))


NT = (((1,), (1,)), ((), ()))
TN = (((0,), (0,)), ((), ()))


def dot_f32(a, b, dims=(((1,), (0,)), ((), ()))):
    return lax.dot_general(a, b, dims, preferred_element_type=jnp.float32)


def steps_of(words):
    return [(w[0], w[1], int(w[2])) for w in words]


EVENTS = {point: steps_of(words) for point, words in dict(
    f=("fb0",),
    a=("ab0",),
    stats=("al1", "at0",),
    packs=(),
    given=("me0", "al2", "at1", "al3", "at2", "ob0", "me1", "at3",
        "ol1", "me2",),
    front=("ot0", "ol2", "ib0",),
    cache=("ot1", "ol3", "il1", "fl1", "me3",),
    memory=("ot2", "ot3", "il2", "fl2", "0h0", "it0", "il3", "fl3",
        "0h1", "it1", "0h2",),
    half=("1h0", "1h1", "ft0", "it2", "it3", "1h2",),
    attended=("ft1",),
    far=(),
    pair=("ft2", "ft3",),
    activated=(),
).items()}


def forward_kernel(
    levels, batches, local_len, per_device,
    qk_in, value_in, router_in, norm_in, bias_in, branch_in, up_in, f_in, token_in, cot_in, vr_in, or_in, start_in,
    count_in, g_in,
    a_out, o_out, i_out, f_all, xs_out, act_out, front_out, gates_out, win_out, probs_out, att_out,
    mixed_out, hidden_out, n2_out, vec_out, ffn_out, slope_out, fgrad_out,
    a_all, o_all, i_all, xs, graw, win, rbuf, sel, unit, act, front, gates, vec, bias, probs, att, mixed,
    arrived, hidden, n2, ffn, slope,
    qk_raw, value_raw, router_raw, norm_raw, bias_raw, branch_raw, up_raw, vr_raw, or_raw, start_raw, count_raw, f_raw, a_pack, o_pack, i_pack,
    send, recv, csend, crecv, lsem, gsend, grecv, esend, erecv, osem, psem,
):
    bf16, f32 = jnp.bfloat16, jnp.float32
    d, t = lax.axis_index("doc"), lax.axis_index("tm")
    z, c = t // 2, t % 2
    nb = neighbours(2 * levels)
    shard = qk_in.shape[0]
    width = f_in.shape[1]
    rows = batches * local_len
    both = 2 * rows
    wide = HALF_HEADS * PAD
    own = pl.ds(pl.multiple_of(c * shard, 16), shard)

    def local(src, dst, index):
        cp = pltpu.make_async_copy(src, dst, lsem.at[index])
        cp.start()
        return cp

    def sibling(src, dst, index):
        return pltpu.make_async_remote_copy(
            src_ref=src, dst_ref=dst, send_sem=csend.at[index], recv_sem=crecv.at[index],
            device_id=nb["c"], device_id_type=MESH)

    raws = [
        local(src, dst, i)
        for i, (src, dst) in enumerate((
            (qk_in, qk_raw), (value_in, value_raw), (router_in, router_raw), (norm_in, norm_raw), (bias_in, bias_raw),
            (branch_in, branch_raw), (up_in, up_raw), (vr_in, vr_raw), (or_in, or_raw), (start_in, start_raw),
            (count_in, count_raw)))
    ]
    loc_f = local(f_in, f_raw, 11)
    x_parts = ((token_in, pl.ds(0, width)), (cot_in, pl.ds(width, width)))
    loc_x = [local(src, xs.at[c, :, cols], 12 + i) for i, (src, cols) in enumerate(x_parts)]
    enter(nb, z, levels)
    rem_x = [sibling(src, xs.at[c, :, cols], i) for i, (src, cols) in enumerate(x_parts)]
    for cp in rem_x:
        cp.start()
    ga, go, gi, gf = [
        Gather(ref, (send.at[i], recv.at[i]), nb, d, z, levels)
        for i, ref in enumerate((a_all, o_all, i_all, f_all))
    ]

    loc_f.wait()
    own_f = local(f_raw, f_all.at[d, z], 18)
    own_f.wait()
    groups = dict(a=ga, o=go, i=gi, f=gf)
    left = [
        (name, what, k) for name in groups for what, first in (("b", 0), ("l", 1), ("t", 0), ("f", 0))
        for k in range(first, 1 if what == "b" else levels)]
    left += [("m", "e", k) for k in range(MEM // local_len // 2)]
    left += [(str(batch), "h", k) for batch in range(batches) for k in range(MEM // local_len // 2)]

    def do(name, what, k):
        if (name, what, k) not in left:
            return
        left.remove((name, what, k))
        if what == "e":
            early(k)
            return
        if what == "h":
            late(k, int(name))
            return
        group = groups[name]
        if what == "b":
            for cp in placed[name]:
                cp.wait()
            group.begin()
        else:
            dict(l=group.line, t=group.turn, f=group.finish)[what](k)

    def run(point):
        for event in EVENTS[point]:
            do(*event)

    def complete(name):
        for event in [e for e in left if e[0] == name]:
            do(*event)

    placed = dict(f=[])
    run("f")

    for cp in raws[:5]:
        cp.wait()
    a_pack[...] = jnp.zeros_like(a_pack)
    norm_columns = norm_raw[...].astype(f32).T
    for side in range(SIDE):
        for h in range(HALF_HEADS):
            at = (side * HALF_HEADS + h) * HEAD_DIM
            for kind in range(2):
                col, src = (kind * HALF_HEADS + h) * PAD, kind * HEADS * HEAD_DIM + at
                a_pack[side, :, col : col + HEAD_DIM] = qk_raw[:, src : src + HEAD_DIM]
            for e in range(EXPERTS):
                col, src = W_QK + (e * HALF_HEADS + h) * PAD, e * HEADS * HEAD_DIM + at
                a_pack[side, :, col : col + HEAD_DIM] = value_raw[:, src : src + HEAD_DIM]
        routes = HALF_HEADS * EXPERTS
        for kind in range(2):
            src = (kind * SIDE + side) * routes
            a_pack[side, :, MISC + kind * routes : MISC + (kind + 1) * routes] = router_raw[:, src : src + routes]
        a_pack[side, :, MISC + COL_NORM : MISC + COL_NORM + 4] = norm_columns.astype(bf16)
        heads = bias_raw[side * HALF_HEADS : (side + 1) * HALF_HEADS].astype(f32).T
        tail = jnp.concatenate([heads, jnp.zeros((shard - per_device, HALF_HEADS), f32)], axis=0)
        a_pack[side, :, MISC + COL_BIAS : MISC + COL_BIAS + HALF_HEADS] = tail.astype(bf16)
    loc_a = local(a_pack.at[c], a_all.at[d, z, own], 17)
    rem_a = sibling(a_pack.at[1 - c], a_all.at[d, z, own], 3)
    rem_a.start()
    for cp in raws[7:]:
        cp.wait()
    row_ids = lax.broadcasted_iota(jnp.int32, (W_MISC, local_len), 0)
    for batch in range(batches):
        flags = [
            jnp.broadcast_to(raw[:, batch : batch + 1].astype(f32), (W_MISC, local_len)) for raw in (start_raw, count_raw)]
        for side in range(SIDE):
            rows_of = jnp.where(row_ids == 40, flags[0], jnp.where(row_ids == 41, flags[1], 0.0))
            for kind, raw in enumerate((vr_raw, or_raw)):
                for h in range(HALF_HEADS):
                    chosen = raw[batch, side * HALF_HEADS + h]
                    first = (kind * HALF_HEADS + h) * EXPERTS
                    expert = row_ids - first
                    hit = expert == chosen[0:1]
                    for k in range(1, TOPK):
                        hit = jnp.logical_or(hit, expert == chosen[k : k + 1])
                    inside = jnp.logical_and(row_ids >= first, row_ids < first + EXPERTS)
                    rows_of = jnp.where(jnp.logical_and(hit, inside), 1.0, rows_of)
            cols = pl.ds(2 * width + side * 128, 128)
            xs[c, pl.ds(batch * local_len, local_len), cols] = rows_of.T.astype(bf16)
    meta_cols = xs.at[c, :, pl.ds(2 * width, SIDE * 128)]
    rem_x.append(sibling(meta_cols, meta_cols, 2))
    rem_x[-1].start()
    loc_g = local(g_in, graw.at[c], 14)
    rem_g = sibling(g_in, graw.at[c], 4)
    rem_g.start()
    placed["a"] = (loc_a, rem_a)
    run("a")
    sel[...] = selector(c)

    for cp in loc_x + rem_x:
        cp.wait()
    step = 64

    def stats(i, carry):
        at = pl.ds(pl.multiple_of((i % (rows // step)) * step, step), step)
        block = i // (rows // step)
        values = xs[block, at, :width].astype(f32)
        centered = values - jnp.mean(values, axis=-1, keepdims=True)
        inverse = lax.rsqrt(jnp.mean(centered * centered, axis=-1, keepdims=True) + EPS)
        unit[pl.ds(pl.multiple_of(i * step, step), step)] = centered * inverse
        counts = xs[block, at, 2 * width : 2 * width + 128][:, 41:42].astype(f32)
        position = lax.broadcasted_iota(jnp.int32, (step, 1), 0) + (i * step) % local_len
        gradient = xs[block, at, width : 2 * width].astype(f32)
        xs[block, at, width : 2 * width] = jnp.where(position.astype(f32) < counts, gradient, 0.0).astype(bf16)
        return carry

    lax.fori_loop(0, both // step, stats, 0)
    run("stats")
    raws[6].wait()
    for side in range(SIDE):
        for p in range(4 * levels):
            src = (p * SIDE + side) * PAD
            i_pack[side, :, p * PAD : (p + 1) * PAD] = up_raw[:, src : src + PAD]
    raws[5].wait()
    o_pack[...] = jnp.zeros_like(o_pack)
    for side in range(SIDE):
        for h in range(HALF_HEADS):
            for e in range(EXPERTS):
                src = e * HEADS * HEAD_DIM + (side * HALF_HEADS + h) * HEAD_DIM
                col = (e * HALF_HEADS + h) * PAD
                o_pack[side, :, col : col + HEAD_DIM] = branch_raw[:, src : src + HEAD_DIM]
    loc_o = local(o_pack.at[c], o_all.at[d, z, own], 15)
    rem_o = sibling(o_pack.at[1 - c], o_all.at[d, z, own], 5)
    loc_i = local(i_pack.at[c], i_all.at[d, z, own], 16)
    rem_i = sibling(i_pack.at[1 - c], i_all.at[d, z, own], 6)
    rem_o.start()
    rem_i.start()
    placed["o"], placed["i"] = (loc_o, rem_o), (loc_i, rem_i)
    run("packs")

    slots = MEM // local_len
    has_up, has_down = z < levels - 1, z > 0

    def slot(s):
        return pl.ds(s * local_len, local_len)

    def starts_of(block, batch):
        column = xs[block, pl.ds(batch * local_len, local_len), 2 * width : 2 * width + 128]
        return column[:, 40:41].astype(f32)

    def spread_given(i, carry):
        at = pl.ds(pl.multiple_of((i % slots) * local_len, local_len), local_len)
        pair = i // slots
        mine = dot_f32(graw[pair // batches, pair % batches, at], sel[...])
        win[pair, at] = mine.astype(bf16)
        return carry

    def keep_or(block, batch, s, moved):
        at = block * batches + batch
        held = win[at, slot(s)]
        first = jnp.broadcast_to(starts_of(block, batch), held.shape) > 0.5
        win[at, slot(s)] = jnp.where(first, held.astype(f32), moved.astype(f32)).astype(bf16)

    def message(m, batch):
        src = win.at[batches + batch, pl.ds((slots - 1 - 2 * m) * local_len, 2 * local_len)]
        return pltpu.make_async_remote_copy(
            src_ref=src, dst_ref=rbuf.at[m, batch], send_sem=gsend.at[m, batch], recv_sem=grecv.at[m, batch],
            device_id=nb["up"], device_id_type=MESH)

    rounds = slots // 2

    def send_message(m, batch):
        if m < rounds:
            pl.when(has_up)(lambda: message(m, batch).start())

    def take(m, some):
        for batch in some:
            pl.when(has_down)(lambda: message(m, batch).wait_recv())
            for k in (0, 1):
                keep_or(0, batch, slots - 1 - 2 * m - k, rbuf[m, batch, slot(1 - k)])
            for s in (slots - 2 - 2 * m, slots - 3 - 2 * m):
                if s >= 0:
                    keep_or(1, batch, s, win[batch, slot(s + 1)])
            send_message(m + 1, batch)

    def early(m):
        pl.when(z <= m)(lambda: take(m, range(batches)))

    def late(m, batch):
        pl.when(z > m)(lambda: take(m, (batch,)))

    loc_g.wait()
    rem_g.wait()
    lax.fori_loop(0, 2 * batches * slots, spread_given, 0)
    run("given")
    complete("a")
    out_a = pltpu.make_async_copy(a_all, a_out, osem.at[0])
    out_a.start()

    w_a = a_all.reshape(4 * levels * 2 * shard, W_A)
    vec[...] = w_a[:, MISC:W_A].astype(f32).T

    def norm(i, carry):
        at = pl.ds(pl.multiple_of(i * step, step), step)
        act[at] = (unit[at] * vec[COL_NORM : COL_NORM + 1] + vec[COL_NORM + 1 : COL_NORM + 2]).astype(bf16)
        return carry

    lax.fori_loop(0, both // step, norm, 0)

    def project(i, carry):
        at = pl.ds(pl.multiple_of(i * 256, 256), 256)
        front[:, at] = dot_f32(act[...], w_a[:, at])
        return carry

    lax.fori_loop(0, MISC // 256, project, 0)
    front[:, MISC:W_A] = dot_f32(act[...], w_a[:, MISC:W_A])
    run("front")
    meta_at = pl.ds(pl.multiple_of(2 * width + c * 128, 128), 128)

    def gate(i, carry):
        at = pl.ds(pl.multiple_of(i * local_len, local_len), local_len)
        gated = jax.nn.sigmoid(front[at, MISC:W_A])
        gates[at] = gated
        picks = xs[i // batches, pl.ds(pl.multiple_of((i % batches) * local_len, local_len), local_len), meta_at]
        gated = gated * picks.astype(f32)
        for h in range(HALF_HEADS):
            total = jnp.zeros((local_len, PAD), f32)
            for e in range(EXPERTS):
                lane = h * EXPERTS + e
                col = W_QK + (e * HALF_HEADS + h) * PAD
                total = total + gated[:, lane : lane + 1] * front[at, col : col + PAD]
            win[i, pl.ds(MEM, local_len), wide + h * PAD : wide + (h + 1) * PAD] = total.astype(bf16)
        win[i, pl.ds(MEM, local_len), :wide] = front[at, wide : 2 * wide].astype(bf16)
        return carry

    lax.fori_loop(0, 2 * batches, gate, 0)

    for batch in range(batches):
        keep_or(1, batch, slots - 1, win[batch, pl.ds(MEM, local_len)])
        send_message(0, batch)
    run("cache")

    spread = MEM + 2 * local_len
    table = table_by_offset(w_a, per_device, shard, local_len, spread)
    for h in range(HALF_HEADS):
        line = jnp.broadcast_to(table[COL_BIAS + h : COL_BIAS + h + 1], (local_len, spread))
        turned = pltpu.roll(line, spread - local_len + 1, 1, stride=1, stride_axis=0)
        bias[h] = turned[:, : MEM + local_len]
    run("memory")
    complete("m")
    complete("0")

    key_ids = lax.broadcasted_iota(jnp.int32, (local_len, local_len), 1)
    row_ids = lax.broadcasted_iota(jnp.int32, (local_len, local_len), 0)

    def probs_copy(i, slot_of):
        return pltpu.make_async_copy(probs.at[slot_of], probs_out.at[i], psem.at[slot_of])

    def pair_of(n):
        return (n % 2) * batches + n // 2

    def attend(n, carry):
        i = pair_of(n)
        at = pl.ds(pl.multiple_of(i * local_len, local_len), local_len)
        block, batch = i // batches, i % batches
        rows_at = pl.ds(pl.multiple_of(batch * local_len, local_len), local_len)
        count = xs[block, rows_at, 2 * width : 2 * width + 128][:, 41:42].astype(f32)
        seen = jnp.logical_and(key_ids <= row_ids, key_ids.astype(f32) < count)
        picks = xs[block, rows_at, meta_at].astype(f32) * gates[at]
        slot_of = lax.rem(n, 2)
        pl.when(n >= 2)(lambda: probs_copy(pair_of(n - 2), slot_of).wait())
        for h in range(HALF_HEADS):
            cols = slice(h * PAD, (h + 1) * PAD)
            q = front[at, cols].astype(bf16)
            s = dot_f32(q, win[i, :, cols], NT) * SCALE + bias[h]
            s = jnp.concatenate([s[:, :MEM], jnp.where(seen, s[:, MEM:], NEG)], axis=1)
            top = jnp.max(s, axis=-1, keepdims=True)
            expo = jnp.exp(s - top)
            p = expo * (1.0 / jnp.sum(expo, axis=-1, keepdims=True))
            probs[slot_of, h] = p
            p = p.astype(bf16)
            got = dot_f32(p, win[i, :, wide + h * PAD : wide + (h + 1) * PAD]).astype(bf16)
            att[at, cols] = got
            got = got.astype(f32)
            for e in range(EXPERTS):
                lane = HALF_HEADS * EXPERTS + h * EXPERTS + e
                col = (e * HALF_HEADS + h) * PAD
                mixed[at, col : col + PAD] = (picks[:, lane : lane + 1] * got).astype(bf16)
        probs_copy(i, slot_of).start()
        return carry

    lax.fori_loop(0, 2, attend, 0)
    run("half")
    for batch in range(1, batches):
        complete(str(batch))
    out_w = pltpu.make_async_copy(win, win_out, osem.at[1])
    out_w.start()
    lax.fori_loop(2, 2 * batches, attend, 0)
    for n in range(2 * batches - 2, 2 * batches):
        probs_copy(pair_of(n), n % 2).wait()
    run("attended")
    complete("o")

    w_o = o_all.reshape(4 * levels * 2 * shard, W_O)
    branch = unit
    far = pl.ds(pl.multiple_of((1 - c) * rows, rows), rows)
    near = pl.ds(pl.multiple_of(c * rows, rows), rows)

    def out_project(at):
        def body(i, carry):
            cols = pl.ds(pl.multiple_of(i * 256, 256), 256)
            branch[at, cols] = dot_f32(mixed[at], w_o[cols], NT)
            return carry

        lax.fori_loop(0, width // 256, body, 0)

    def exchange(src, dst, index):
        return pltpu.make_async_remote_copy(
            src_ref=src, dst_ref=dst, send_sem=esend.at[index], recv_sem=erecv.at[index],
            device_id=nb["c"], device_id_type=MESH)

    out_project(far)
    give = exchange(branch.at[far], arrived, 0)
    give.start()
    run("far")
    out_project(near)
    out_o = pltpu.make_async_copy(o_all, o_out, osem.at[2])
    out_o.start()
    give.wait_recv()

    def second(i, carry):
        at = pl.ds(pl.multiple_of(i * step, step), step)
        total_at = pl.ds(pl.multiple_of(c * rows + i * step, step), step)
        values = xs[c, at, :width].astype(f32) + branch[total_at] + arrived[at]
        hidden[at] = values
        centered = values - jnp.mean(values, axis=-1, keepdims=True)
        inverse = lax.rsqrt(jnp.mean(centered * centered, axis=-1, keepdims=True) + EPS)
        normed = centered * inverse * vec[COL_NORM + 2 : COL_NORM + 3] + vec[COL_NORM + 3 : COL_NORM + 4]
        n2[total_at] = normed.astype(bf16)
        return carry

    lax.fori_loop(0, rows // step, second, 0)
    pair = exchange(n2.at[near], n2.at[near], 1)
    pair.start()
    run("pair")
    pair.wait_recv()
    outs = [
        pltpu.make_async_copy(src, dst, osem.at[3 + i])
        for i, (src, dst) in enumerate((
            (xs, xs_out), (act, act_out), (front, front_out), (gates, gates_out),
            (att, att_out), (mixed, mixed_out), (hidden, hidden_out), (n2, n2_out), (vec, vec_out)))
    ]
    for cp in outs:
        cp.start()
    complete("i")
    out_i = pltpu.make_async_copy(i_all, i_out, osem.at[13])
    out_i.start()

    w_i = i_all.reshape(4 * levels * 2 * shard, i_all.shape[3])

    def activate(i, carry):
        at = pl.ds(pl.multiple_of(i * 256, 256), 256)
        pre = dot_f32(n2[...], w_i[:, at])
        below = 0.5 * (1.0 + lax.erf(pre * 0.7071067811865476))
        ffn[:, at] = (pre * below).astype(bf16)
        slope[:, at] = (below + pre * jnp.exp(-0.5 * pre * pre) * 0.3989422804014327).astype(bf16)
        return carry

    steps = ffn.shape[1] // 256
    lax.fori_loop(0, steps, activate, 0)
    run("activated")
    outs += [pltpu.make_async_copy(ffn, ffn_out, osem.at[14]), pltpu.make_async_copy(slope, slope_out, osem.at[15])]
    outs[-2].start()
    outs[-1].start()

    for m in range(rounds):
        for batch in range(batches):
            pl.when(has_up)(lambda: message(m, batch).wait_send())
    out_w.wait()
    span = ffn.shape[1] // 4
    half = width // 2

    def ffn_grad(i, carry):
        at = pl.ds(pl.multiple_of(i * span, span), span)
        for side in range(2):
            cols = slice(width + side * half, width + (side + 1) * half)
            left = jnp.concatenate([xs[0, :, cols], xs[1, :, cols]], axis=0)
            win[i, side * span : (side + 1) * span] = dot_f32(ffn[:, at], left, TN).astype(bf16)
        return carry

    lax.fori_loop(0, 4, ffn_grad, 0)
    for column in range(4):
        for side in range(2):
            outs.append(pltpu.make_async_copy(
                win.at[column, pl.ds(side * span, span)],
                fgrad_out.at[column, :, pl.ds(side * half, half)], osem.at[16 + 2 * column + side]))
            outs[-1].start()
    complete("f")
    for group in (ga, go, gi, gf):
        group.drain()
    for cp in (give, pair):
        cp.wait_send()
    out_a.wait()
    out_o.wait()
    out_i.wait()
    for cp in outs:
        cp.wait()


def forward(levels, batches, local_len, per_device, ins):
    bf16, f32 = jnp.bfloat16, jnp.float32
    shape = jax.ShapeDtypeStruct
    qk, value, router, norms, bias_in, branch, up, f, tokens, cot, vr, outr, start, count, g = ins
    shard, width = qk.shape[0], f.shape[1]
    a, o, i = [shape((SIDE, shard, w), bf16) for w in (W_A, W_O, up.shape[1] // SIDE)]
    x = shape((tokens.shape[0], 2 * width + SIDE * 128), bf16)
    rows = batches * local_len
    both = 2 * rows
    wide = HALF_HEADS * PAD
    two = lambda v: (4, levels, 2 * v.shape[1], v.shape[2])
    window = (2 * batches, MEM + local_len, 2 * wide)
    probs = (2 * batches, HALF_HEADS, local_len, MEM + local_len)
    outs = [
        (two(a), bf16), (two(o), bf16), (two(i), bf16), ((4, levels) + f.shape, bf16),
        ((2,) + x.shape, bf16), ((both, width), bf16), ((both, W_A), f32), ((both, W_MISC), f32),
        (window, bf16), (probs, f32), ((both, wide), bf16), ((both, W_O), bf16),
        ((rows, width), f32), ((both, width), bf16), ((W_MISC, width), f32), ((both, i.shape[2]), bf16),
        ((both, i.shape[2]), bf16), ((4, i.shape[2] // 4, width), bf16),
    ]
    rounds = MEM // local_len // 2
    scratch = [
        (two(a), bf16), (two(o), bf16), (two(i), bf16), ((2,) + x.shape, bf16), ((2,) + g.shape, bf16),
        (window, bf16), ((rounds, batches, 2 * local_len, 2 * wide), bf16), ((g.shape[2], 2 * wide), bf16),
        ((both, width), f32), ((both, width), bf16), ((both, W_A), f32), ((both, W_MISC), f32),
        ((W_MISC, width), f32), ((HALF_HEADS, local_len, MEM + local_len), f32), ((2,) + probs[1:], f32),
        ((both, wide), bf16), ((both, W_O), bf16), ((rows, width), f32),
        ((rows, width), f32), ((both, width), bf16), ((both, i.shape[2]), bf16), ((both, i.shape[2]), bf16),
    ]
    rounds = MEM // local_len // 2
    scratch += [(w.shape, w.dtype) for w in (qk, value, router, norms, bias_in, branch, up, vr, outr, start, count, f, a, o, i)]
    sems = [(4, 6 * levels), (4, 6 * levels), (7,), (7,), (19,), (rounds, batches), (rounds, batches), (2,), (2,), (24,), (2,)]
    hbm = pl.BlockSpec(memory_space=pl.ANY)
    return pl.pallas_call(
        functools.partial(forward_kernel, levels, batches, local_len, per_device),
        out_shape=[jax.ShapeDtypeStruct(s, k) for s, k in outs],
        in_specs=[hbm] * len(ins),
        out_specs=[hbm] * len(outs),
        scratch_shapes=[pltpu.VMEM(s, k) for s, k in scratch] + [pltpu.SemaphoreType.DMA(s) for s in sems],
        compiler_params=pltpu.CompilerParams(
            collective_id=1, has_side_effects=True, vmem_limit_bytes=VMEM_BYTES),
    )(*ins)


def add_rows(dst, terms):
    rows, width = dst.shape
    step = 16

    def body(i, carry):
        at = pl.ds(pl.multiple_of(i * step, step), step)
        total = terms[0][at].astype(jnp.float32)
        for term in terms[1:]:
            total = total + term[at].astype(jnp.float32)
        dst[at] = total.astype(dst.dtype)
        return carry

    lax.fori_loop(0, rows // step, body, 0)


class Scatter:
    def __init__(self, src, view, sems, nb, d, z, levels, total):
        self.src, self.view, self.nb, self.d, self.z, self.levels = src, view, nb, d, z, levels
        self.send, self.recv = sems
        self.sum = total
        self.half = src.shape[2] // 2
        self.by_x, self.by_y = d + 1 - 2 * (d % 2), (d + 2) % 4
        self.low, self.high = pl.ds(0, self.half), pl.ds(self.half, self.half)

    def copy(self, src, dst, slot, to):
        return pltpu.make_async_remote_copy(
            src_ref=src, dst_ref=dst, send_sem=self.send.at[slot], recv_sem=self.recv.at[slot],
            device_id=self.nb[to], device_id_type=MESH)

    def corner(self, j, to):
        part, name, base = (self.low, "cx", 0) if to == "x" else (self.high, "cy", self.levels)
        return self.copy(self.src.at[3 - self.d, j, part], self.view(name, j), base + j, to)

    def direct(self, j, to):
        if to == "x":
            column, part, name, base = self.by_x, self.low, "rx", 2 * self.levels
        else:
            column, part, name, base = self.by_y, self.high, "ry", 3 * self.levels
        return self.copy(self.src.at[column, j, part], self.view(name, j).at[part], base + j, to)

    def relay(self, j, to):
        if to == "x":
            held, part, name, base = "cy", self.high, "rx", 4 * self.levels
        else:
            held, part, name, base = "cx", self.low, "ry", 5 * self.levels
        return self.copy(self.view(held, j), self.view(name, j).at[part], base + j, to)

    def along(self, j, to, first=False):
        base = (6 if to == "up" else 7) * self.levels
        there = self.view(to, j, self.z + (1 if to == "up" else -1))
        return self.copy(self.view("rx" if first else to, j), there, base + j, to)

    def issue(self, j):
        self.corner(j, "x").start()
        self.corner(j, "y").start()
        self.direct(j, "x").start()
        self.direct(j, "y").start()

    def turn(self, j):
        self.corner(j, "x").wait_recv()
        add_rows(self.view("cx", j), [self.view("cx", j), self.src.at[self.by_y, j, self.low]])
        self.relay(j, "y").start()
        self.corner(j, "y").wait_recv()
        add_rows(self.view("cy", j), [self.view("cy", j), self.src.at[self.by_x, j, self.high]])
        self.relay(j, "x").start()

    def column(self, j):
        for to in ("x", "y"):
            self.direct(j, to).wait_recv()
            self.relay(j, to).wait_recv()
        add_rows(self.view("rx", j), [self.view("rx", j), self.view("ry", j), self.src.at[self.d, j]])

    def lift(self, j, stage):
        def hop(to):
            if stage:
                self.along(j, to).wait_recv()
                add_rows(self.view(to, j), [self.view(to, j), self.view("rx", j)])
            self.along(j, to, first=stage == 0).start()

        if stage < j:
            pl.when(self.z == stage)(lambda: hop("up"))
        if self.levels - 1 - stage > j:
            pl.when(self.z == self.levels - 1 - stage)(lambda: hop("down"))

    def total(self, j):
        @pl.when(self.z == j)
        def _():
            terms = [self.view("rx", j)]
            for to, there in (("up", j > 0), ("down", j < self.levels - 1)):
                if there:
                    self.along(j, to).wait_recv()
                    terms.append(self.view(to, j))
            add_rows(self.sum, terms)

    def drain(self):
        for j in range(self.levels):
            for to in ("x", "y"):
                self.corner(j, to).wait_send()
                self.direct(j, to).wait_send()
                self.relay(j, to).wait_send()
            pl.when(self.z < j)(lambda: self.along(j, "up").wait_send())
            pl.when(self.z > j)(lambda: self.along(j, "down").wait_send())


class LineFirst:
    def __init__(self, src, view, bufs, sems, nb, d, z, levels, total):
        self.src, self.view, self.nb, self.d, self.z, self.levels = src, view, nb, d, z, levels
        self.cx, self.cy, self.rx, self.ry = bufs
        self.send, self.recv = sems
        self.sum = total
        half = src.shape[2] // 2
        self.by_x, self.by_y = d + 1 - 2 * (d % 2), (d + 2) % 4
        self.low, self.high = pl.ds(0, half), pl.ds(half, half)

    def copy(self, src, dst, slot, to):
        return pltpu.make_async_remote_copy(
            src_ref=src, dst_ref=dst, send_sem=self.send.at[slot], recv_sem=self.recv.at[slot],
            device_id=self.nb[to], device_id_type=MESH)

    def along(self, j, column, to, level, first=False):
        slot = (0 if to == "up" else 4 * self.levels) + 4 * j + column
        after = level + (1 if to == "up" else -1)
        src = self.src.at[column, j] if first else self.view(j, column)
        return self.copy(src, self.view(self.levels if to == "down" and after == j else j, column), slot, to)

    def lift(self, j, stage):
        def hop(to, level):
            for column in range(4):
                if stage:
                    before = level - (1 if to == "up" else -1)
                    self.along(j, column, to, before).wait_recv()
                    held = self.view(j, column)
                    add_rows(held, [held, self.src.at[column, j]])
                self.along(j, column, to, level, first=stage == 0).start()

        if stage < j:
            pl.when(self.z == stage)(lambda: hop("up", stage))
        if self.levels - 1 - stage > j:
            pl.when(self.z == self.levels - 1 - stage)(lambda: hop("down", self.levels - 1 - stage))

    def gathered(self, j):
        @pl.when(self.z == j)
        def _():
            for column in range(4):
                terms = [self.src.at[column, j]]
                if j > 0:
                    self.along(j, column, "up", j - 1).wait_recv()
                    terms.append(self.view(j, column))
                if j < self.levels - 1:
                    self.along(j, column, "down", j + 1).wait_recv()
                    terms.append(self.view(self.levels, column))
                add_rows(terms[0], terms)

    def plane(self, k):
        base = 8 * self.levels
        part = lambda column, rows: self.src.at[column, self.z, rows]
        return (
            self.copy(part(3 - self.d, self.low), self.cx, base, "x"),
            self.copy(part(3 - self.d, self.high), self.cy, base + 1, "y"),
            self.copy(part(self.by_x, self.low), self.rx.at[self.low], base + 2, "x"),
            self.copy(part(self.by_y, self.high), self.ry.at[self.high], base + 3, "y"),
            self.copy(self.cy, self.rx.at[self.high], base + 4, "x"),
            self.copy(self.cx, self.ry.at[self.low], base + 5, "y"),
        )[k]

    def issue(self):
        for k in range(4):
            self.plane(k).start()

    def turn(self):
        self.plane(0).wait_recv()
        add_rows(self.cx, [self.cx, self.src.at[self.by_y, self.z, self.low]])
        self.plane(5).start()
        self.plane(1).wait_recv()
        add_rows(self.cy, [self.cy, self.src.at[self.by_x, self.z, self.high]])
        self.plane(4).start()

    def column(self):
        for k in range(2, 6):
            self.plane(k).wait_recv()
        add_rows(self.sum, [self.rx, self.ry, self.src.at[self.d, self.z]])

    def drain(self):
        for k in range(6):
            self.plane(k).wait_send()
        for j in range(self.levels):
            for column in range(4):
                for level in range(self.levels):
                    if level < j:
                        pl.when(self.z == level)(lambda: self.along(j, column, "up", level).wait_send())
                    if level > j:
                        pl.when(self.z == level)(lambda: self.along(j, column, "down", level).wait_send())


A_PARTS = (1280, 512)
AHEAD = 3


def LAGS(unit, k, levels):
    return 2 + 3 * k if unit < 3 * levels else 1 + k


O_STEPS = {4: ((0, 1), (1, 0)), 6: ((1, 1),), 7: ((2, 0), (2, 1))}


class Pipeline:
    def __init__(self, units, levels, ahead, lags):
        self.units, self.levels, self.ahead, self.now = units, levels, ahead, 0
        self.follow = [lambda s, j: s.column(j)]
        for stage in range(levels - 1):
            self.follow.append(lambda s, j, stage=stage: s.lift(j, stage))
        self.follow.append(lambda s, j: s.total(j))
        self.lags = lags
        self.done = [0] * len(units)

    def each(self, n, act):
        if 0 <= n < len(self.units):
            for scatter, j in self.units[n]:
                act(scatter, j)

    def begin(self):
        for n in range(self.ahead):
            self.each(n, lambda s, j: s.issue(j))

    def advance(self, n):
        self.each(n, self.follow[self.done[n]])
        self.done[n] += 1

    def step(self):
        n = self.now
        if n < len(self.units):
            self.each(n, lambda s, j: s.turn(j))
            self.each(n + self.ahead, lambda s, j: s.issue(j))
        for m in range(min(n + 1, len(self.units))):
            while self.done[m] < len(self.follow) and n - m >= self.lags(m, self.done[m], self.levels):
                self.advance(m)
        self.now += 1

    def turns(self):
        while self.now < len(self.units):
            self.step()

    def round(self):
        for m in range(len(self.units)):
            if self.done[m] < len(self.follow):
                self.advance(m)

    def finish(self, after):
        after = list(after)
        while True:
            for item in [a for a in after if all(self.done[n] == len(self.follow) for n in a[0])]:
                after.remove(item)
                item[1]()
            if min(self.done) == len(self.follow):
                return
            self.round()


def norm_rows(values):
    centered = values - jnp.mean(values, axis=-1, keepdims=True)
    inverse = lax.rsqrt(jnp.mean(centered * centered, axis=-1, keepdims=True) + EPS)
    return centered * inverse, inverse


def norm_rows_backward(upstream, normed, inverse, gain):
    scaled = upstream * gain
    inside = (
        scaled
        - jnp.mean(scaled, axis=-1, keepdims=True)
        - normed * jnp.mean(scaled * normed, axis=-1, keepdims=True)
    )
    return inside * inverse


VEC_ROW = COL_NORM // 8 * 8
VEC_GAIN = COL_NORM - VEC_ROW


def backward_kernel(
    levels, batches, local_len, per_device, shard,
    fgrad_in, wf_in, wi_in, wo_in, wa_in, ffn_in, slope_in, xs_in, n2_in, hidden_in, vec_in, att_in, gates_in, front_in,
    win_in, probs_in, mixed_in, act_in,
    f_out, i_out, o_out, a_out, m_out, layer_out, grad_out,
    w_f, w_i, ffn, slope, grad, meta, n2, hidden, vec, att, gates, front, win, probs,
    branch, arrived, dhid, db, dmix, dfront, dsum, norms,
    f_total, i_total, o_total, a_total, m_total, *rest,
):
    bf16, f32 = jnp.bfloat16, jnp.float32
    f_bufs, i_bufs, m_bufs = rest[:6], rest[6:12], rest[12:18]
    a_src, a_cx, a_cy, o_src, o_line, o_cx, o_cy, o_rx, o_ry = rest[18:27]
    send, recv, osend, orecv, lsem, tsem, esend, erecv, osem, ready, freed = rest[27:]
    d, t = lax.axis_index("doc"), lax.axis_index("tm")
    z, c = t // 2, t % 2
    nb = neighbours(2 * levels)
    width = w_f.shape[1]
    rows = batches * local_len
    both = 2 * rows
    wide = HALF_HEADS * PAD
    ff = ffn.shape[1]
    far = pl.ds(pl.multiple_of((1 - c) * rows, rows), rows)
    near = pl.ds(pl.multiple_of(c * rows, rows), rows)

    def load(src, dst, index):
        cp = pltpu.make_async_copy(src, dst, lsem.at[index])
        cp.start()
        return cp

    meta_at = pl.ds(pl.multiple_of(2 * width + c * 128, 128), 128)
    l_first = load(fgrad_in, f_bufs[0], 17)
    l_grad = load(xs_in.at[:, :, pl.ds(width, width)], grad, 1)
    l_wf = load(wf_in, w_f, 2)
    enter(nb, z, levels)
    l_first.wait()
    l_slope = load(slope_in, slope, 3)
    l_ffn = load(ffn_in, ffn, 0)
    l_n2 = load(n2_in, n2, 4)
    l_wi = load(wi_in, w_i, 5)
    l_hid = load(hidden_in, hidden, 6)
    l_vec = load(vec_in.at[pl.ds(VEC_ROW, 8)], vec, 7)
    l_mixed = load(mixed_in, dmix, 8)
    l_meta = load(xs_in.at[:, :, meta_at], meta, 9)
    l_att = load(att_in, att, 10)
    l_gates = load(gates_in, gates, 11)
    w_o = a_src.at[:, :, :, pl.ds(0, W_O)]
    l_wo = load(wo_in, w_o, 12)

    def tiles(i):
        at = pl.ds(i * local_len, local_len)
        return [
            pltpu.make_async_copy(win_in.at[i], win.at[i % 2], tsem.at[0, i % 2]),
            pltpu.make_async_copy(front_in.at[at, pl.ds(0, wide)], front.at[i % 2, :, pl.ds(0, wide)], tsem.at[2, i % 2]),
            pltpu.make_async_copy(
                front_in.at[at, pl.ds(W_QK, W_VAL)], front.at[i % 2, :, pl.ds(wide, W_VAL)], tsem.at[3, i % 2]),
        ]

    def probs_tile(n):
        return pltpu.make_async_copy(probs_in.at[n // HALF_HEADS, n % HALF_HEADS], probs.at[n % 2], tsem.at[1, n % 2])

    for cp in tiles(0):
        cp.start()
    probs_tile(0).start()

    names = ("cx", "cy", "rx", "ry")

    def plain(bufs):
        def view(name, j, level=z):
            if name == "up":
                return bufs[5].at[j]
            if name == "down":
                return bufs[5].at[jnp.where(level == j, levels, j)]
            return bufs[1 + names.index(name)].at[j]

        return view

    block_rows = shard * SIDE

    def within(held, cx, cy, cols):
        def view(name, j, level=z):
            if name in ("cx", "cy"):
                return (cx if name == "cx" else cy).at[j, :, cols]
            ref, base = held[name]
            return ref.at[pl.ds(base + j * block_rows, block_rows), cols]

        return view

    span = levels * block_rows
    a_held = dict(rx=(w_i, 0), ry=(w_i, span), up=(w_i, 2 * span), down=(w_i, 3 * span))
    a_cols = [pl.ds(sum(A_PARTS[:k]), A_PARTS[k]) for k in range(len(A_PARTS))]
    sums = [
        Scatter(src, view, (send.at[i], recv.at[i]), nb, d, z, levels, total)
        for i, (src, view, total) in enumerate((
            (f_bufs[0], plain(f_bufs), f_total), (i_bufs[0], plain(i_bufs), i_total),
            (m_bufs[0], plain(m_bufs), m_total)) + tuple(
                (a_src.at[:, :, :, cols], within(a_held, a_cx, a_cy, cols), a_total.at[:, cols]) for cols in a_cols))
    ]
    sf, si, sm = sums[:3]
    held = []
    for ref in (ffn, slope):
        for base in range(0, ref.shape[0], 4 * block_rows):
            held.append((ref, base))
    held = held[:levels] + [(o_line, 0)]

    def o_view(slot, column):
        ref, base = held[slot]
        return ref.at[pl.ds(base + column * block_rows, block_rows), pl.ds(0, W_O)]

    so = LineFirst(o_src, o_view, (o_cx, o_cy, o_rx, o_ry), (osend, orecv), nb, d, z, levels, o_total)
    order = []
    for k in range((levels + 1) // 2):
        order += [levels - 1 - k, k] if levels - 1 - k != k else [k]
    units = [[(s, j)] for s in [sf, si] + sums[3:] for j in order]
    units[3 * levels + 1] = units[3 * levels + 1] + [(sm, j) for j in order]
    line = Pipeline(units, levels, AHEAD, LAGS)

    def exchange(src, dst, index):
        return pltpu.make_async_remote_copy(
            src_ref=src, dst_ref=dst, send_sem=esend.at[index], recv_sem=erecv.at[index],
            device_id=nb["c"], device_id_type=MESH)

    def weight_grad(dst, left, right, chunk, total, column):
        at = pl.ds(pl.multiple_of(column * span, span), span)

        def body(i, carry):
            cols = pl.ds(pl.multiple_of(i * chunk, chunk), chunk)
            got = dot_f32(left[:, at], right[:, cols], TN).astype(bf16)
            dst[column, :, :, cols] = got.reshape(levels, block_rows, chunk)
            return carry

        lax.fori_loop(0, total // chunk, body, 0)

    line.begin()

    l_wf.wait()
    l_slope.wait()
    l_grad.wait()
    g_all = grad.reshape(both, width)

    def back(i, carry):
        at = pl.ds(pl.multiple_of(i * 256, 256), 256)
        slope[:, at] = (dot_f32(g_all[...], w_f[at], NT) * slope[:, at].astype(f32)).astype(bf16)
        return carry

    lax.fori_loop(0, ff // 256, back, 0)
    l_n2.wait()
    for column in range(4):
        weight_grad(i_bufs[0], n2, slope, 512, ff, column)
    line.step()

    l_wi.wait()

    def times(src, weights, dims):
        def run(at):
            def body(i, carry):
                cols = pl.ds(pl.multiple_of(i * 256, 256), 256)
                branch[at, cols] = dot_f32(src[at], weights(cols), dims)
                return carry

            lax.fori_loop(0, width // 256, body, 0)

        return run

    through_in = times(slope, lambda cols: w_i[cols], NT)
    through_in(far)
    give = exchange(branch.at[far], arrived, 0)
    give.start()
    through_in(near)
    line.step()
    l_hid.wait()
    l_vec.wait()
    give.wait()
    norms[...] = jnp.zeros_like(norms)
    step = 64

    def second(i, carry):
        at = pl.ds(pl.multiple_of(i * step, step), step)
        total_at = pl.ds(pl.multiple_of(c * rows + i * step, step), step)
        normed, inverse = norm_rows(hidden[at])
        up = branch[total_at] + arrived[at]
        norms[COL_NORM + 2 : COL_NORM + 3] += jnp.sum(up * normed, axis=0, keepdims=True)
        norms[COL_NORM + 3 : COL_NORM + 4] += jnp.sum(up, axis=0, keepdims=True)
        got = norm_rows_backward(up, normed, inverse, vec[VEC_GAIN + 2 : VEC_GAIN + 3])
        got = got + grad[c, at].astype(f32)
        dhid[at] = got
        db[total_at] = got.astype(bf16)
        return carry

    lax.fori_loop(0, rows // step, second, 0)
    pair = exchange(db.at[near], db.at[near], 1)
    pair.start()
    l_act = load(act_in, grad, 13)

    through_out = times(ffn, lambda cols: w_f[:, cols], (((1,), (0,)), ((), ())))
    l_ffn.wait()
    through_out(far)
    pair.wait()
    last = exchange(branch.at[far], arrived, 2)
    last.start()
    line.step()
    through_out(near)

    for name in ("x", "y"):
        pl.semaphore_signal(ready, inc=1, device_id=nb[name], device_id_type=MESH)
    for name, there in (("up", z < levels - 1), ("down", z > 0)):

        @pl.when(there)
        def _():
            pl.semaphore_signal(ready, inc=1, device_id=nb[name], device_id_type=MESH)

    l_wa = [
        load(wa_in.at[:, pl.ds(0, width)], w_f.at[pl.ds(0, width)], 14),
        load(wa_in.at[:, pl.ds(width, W_A - width)], w_f.at[pl.ds(width, width), pl.ds(0, W_A - width)], 15),
    ]
    l_mixed.wait()
    for column in range(4):
        weight_grad(o_src, db, dmix, 640, W_O, column)
    ends = jnp.where(z < levels - 1, 1, 0) + jnp.where(z > 0, 1, 0)
    pl.semaphore_wait(ready, 2 + ends)
    outer, inner_levels = order[:2], order[2:]

    def o_stage(stage, part):
        for j in part:
            so.lift(j, stage)

    def tick():
        for stage, part in O_STEPS.get(line.now, ()):
            if stage < levels - 1:
                o_stage(stage, outer if part == 0 else inner_levels)
        line.step()

    o_stage(0, outer)
    l_wo.wait()

    def mix(i, carry):
        cols = pl.ds(pl.multiple_of(i * wide, wide), wide)
        dmix[:, cols] = dot_f32(db[...], a_src[:, :, :, cols].reshape(width, wide)).astype(bf16)
        return carry

    lax.fori_loop(0, EXPERTS, mix, 0)
    l_meta.wait()
    l_att.wait()
    l_gates.wait()
    dsum[...] = jnp.zeros_like(dsum)
    lanes = lax.broadcasted_iota(jnp.int32, (local_len, W_MISC), 1)

    def attend(i):
        slot = i % 2
        if i + 1 < 2 * batches:
            for cp in tiles(i + 1):
                cp.start()
        for cp in tiles(i):
            cp.wait()
        at = pl.ds(i * local_len, local_len)
        block, batch = i // batches, i % batches
        gate = gates[at]
        picks = meta[block, pl.ds(batch * local_len, local_len)].astype(f32)
        gated = gate * picks
        d_gates = jnp.zeros((local_len, W_MISC), f32)
        for h in range(HALF_HEADS):
            cols = slice(h * PAD, (h + 1) * PAD)
            v_cols = slice(wide + h * PAD, wide + (h + 1) * PAD)
            got = att[at, cols].astype(f32)
            d_att = jnp.zeros((local_len, PAD), f32)
            for e in range(EXPERTS):
                lane = HALF_HEADS * EXPERTS + h * EXPERTS + e
                col = (e * HALF_HEADS + h) * PAD
                part = dmix[at, col : col + PAD].astype(f32)
                d_att = d_att + gated[:, lane : lane + 1] * part
                d_gates = jnp.where(lanes == lane, jnp.sum(part * got, axis=-1, keepdims=True), d_gates)
            d_att = d_att.astype(bf16)
            n = i * HALF_HEADS + h
            if n + 1 < 2 * batches * HALF_HEADS:
                probs_tile(n + 1).start()
            probs_tile(n).wait()
            p = probs[n % 2]
            d_p = dot_f32(d_att, win[slot, :, v_cols], NT)
            delta = jnp.sum(d_p * p, axis=-1, keepdims=True)
            d_s = p * (d_p - delta)
            dsum[h] += d_s
            d_s = d_s.astype(bf16)
            q = front[slot, :, cols].astype(bf16)
            d_q = dot_f32(d_s, win[slot, :, cols]) * SCALE
            d_k = dot_f32(d_s[:, MEM:], q, TN) * SCALE
            d_v = dot_f32(p[:, MEM:].astype(bf16), d_att, TN).astype(bf16).astype(f32)
            dfront[at, cols] = d_q.astype(bf16)
            dfront[at, wide + h * PAD : wide + (h + 1) * PAD] = d_k.astype(bf16)
            for e in range(EXPERTS):
                lane = h * EXPERTS + e
                col = W_QK + (e * HALF_HEADS + h) * PAD
                part = front[slot, :, col - W_QK + wide : col - W_QK + wide + PAD]
                d_gates = jnp.where(lanes == lane, jnp.sum(part * d_v, axis=-1, keepdims=True), d_gates)
                dfront[at, col : col + PAD] = (gated[:, lane : lane + 1] * d_v).astype(bf16)
        d_logits = jnp.where(lanes < N_ROUTE, d_gates * picks * gate * (1.0 - gate), 0.0)
        dfront[at, MISC:W_A] = d_logits.astype(bf16)

    attend(0)
    tick()
    attend(1)
    tick()
    for i in range(2, 2 * batches):
        attend(i)
    l_act.wait()
    one_all = grad.reshape(both, width)
    for column in range(4):
        weight_grad(a_src, one_all, dfront, 896, MISC, column)
    tick()
    last.wait()

    def final(i, carry):
        at = pl.ds(pl.multiple_of(i * step, step), step)
        total_at = pl.ds(pl.multiple_of(c * rows + i * step, step), step)
        tail = meta[c, at].astype(f32)
        position = lax.broadcasted_iota(jnp.int32, (step, 1), 0) + (i * step) % local_len
        keep = position.astype(f32) < tail[:, 41:42]
        total = hidden[at] + branch[total_at] + arrived[at]
        db[total_at] = jnp.where(keep, total, 0.0).astype(bf16)
        return carry

    lax.fori_loop(0, rows // step, final, 0)
    pl.semaphore_signal(freed, inc=1, device_id=nb["c"], device_id_type=MESH)
    outs = [pltpu.make_async_copy(db.at[near], layer_out, osem.at[0])]
    outs[0].start()

    tick()
    for cp in l_wa:
        cp.wait()

    def through_front(at):
        def body(i, carry):
            cols = pl.ds(pl.multiple_of(i * 256, 256), 256)
            below = pl.ds(pl.multiple_of(width + i * 256, 256), 256)
            branch[at, cols] = (
                dot_f32(dfront[at, :width], w_f[cols], NT)
                + dot_f32(dfront[at, width:], w_f[below, : W_A - width], NT))
            return carry

        lax.fori_loop(0, width // 256, body, 0)

    through_front(far)
    hand = exchange(branch.at[far], arrived, 3)
    pl.semaphore_wait(freed, 1)
    hand.start()
    through_front(near)
    tick()

    spread = MEM + 2 * local_len
    ids = lax.broadcasted_iota(jnp.int32, (local_len, 1), 0)
    lines = []
    for h in range(HALF_HEADS):
        turned = jnp.concatenate([dsum[h], jnp.zeros((local_len, local_len), f32)], axis=1)
        bit = 1
        while bit < local_len:
            moved = pltpu.roll(turned, bit, 1)
            turned = jnp.where(((local_len - 1 - ids) // bit) % 2 == 1, moved, turned)
            bit *= 2
        lines.append(jnp.sum(turned, axis=0, keepdims=True))
    row_of = lax.broadcasted_iota(jnp.int32, (W_MISC, spread), 0)
    table = jnp.zeros((W_MISC, spread), f32)
    for h in range(HALF_HEADS):
        table = jnp.where(row_of == COL_BIAS + h, lines[h], table)
    high = table.astype(bf16)
    low = (table - high.astype(f32)).astype(bf16)
    distance = MEM + local_len - 1 - lax.broadcasted_iota(jnp.int32, (1, spread), 1)
    bucket = bucket_index(distance)
    wanted = (bucket // per_device) * shard + bucket % per_device
    hand.wait()

    def first(i, carry):
        at = pl.ds(pl.multiple_of(i * step, step), step)
        total_at = pl.ds(pl.multiple_of(c * rows + i * step, step), step)
        normed, inverse = norm_rows(n2[at].astype(f32))
        up = branch[total_at] + arrived[at]
        norms[COL_NORM : COL_NORM + 1] += jnp.sum(up * normed, axis=0, keepdims=True)
        norms[COL_NORM + 1 : COL_NORM + 2] += jnp.sum(up, axis=0, keepdims=True)
        dhid[at] += norm_rows_backward(up, normed, inverse, vec[VEC_GAIN : VEC_GAIN + 1])
        return carry

    l_x = load(xs_in.at[c, :, pl.ds(0, width)], n2.at[pl.ds(0, rows)], 16)
    l_x.wait()
    lax.fori_loop(0, rows // step, first, 0)
    outs.append(pltpu.make_async_copy(dhid, grad_out, osem.at[1]))
    outs[1].start()
    columns = norms[...].T

    for column in range(4):
        at = pl.ds(column * span, span)
        row_ids = lax.broadcasted_iota(jnp.int32, (span, spread), 0) + column * span
        one_hot = jnp.where(row_ids == wanted, 1.0, 0.0).astype(bf16)
        misc = dot_f32(one_hot, high, NT) + dot_f32(one_hot, low, NT)
        misc = misc + dot_f32(one_all[:, at], dfront[:, MISC:W_A], TN) + columns[column * span : (column + 1) * span]
        m_bufs[0][column] = misc.astype(bf16).reshape(levels, block_rows, W_MISC)
    while line.now < len(units):
        tick()
    for stage in range(3, levels - 1):
        o_stage(stage, order)
    for j in order:
        so.gathered(j)
    so.issue()
    line.round()
    so.turn()
    line.round()
    so.column()
    mine, other = [pl.ds(pl.multiple_of(k * shard, 16), shard) for k in (c, 1 - c)]

    def hand_out(i, total, out):
        outs.append(exchange(total.at[other], out.at[c], 4 + i))
        outs[-1].start()
        outs.append(pltpu.make_async_copy(total.at[mine], out.at[c], osem.at[3 + i]))
        outs[-1].start()

    def hand_out_f():
        outs.append(pltpu.make_async_copy(f_total, f_out, osem.at[2]))
        outs[-1].start()

    hand_out(1, o_total, o_out)
    groups = [range(k * levels, (k + 1) * levels) for k in range(2)] + [range(2 * levels, len(units))]
    line.finish((
        (groups[0], hand_out_f),
        (groups[1], lambda: hand_out(0, i_total, i_out)),
        (groups[2], lambda: (hand_out(2, a_total, a_out), hand_out(3, m_total, m_out))),
    ))
    for s in sums + [so]:
        s.drain()
    for cp in outs:
        cp.wait()


def backward(levels, batches, local_len, per_device, shard, ins):
    bf16, f32 = jnp.bfloat16, jnp.float32
    (unused, w_f, w_i, w_o, w_a, ffn, slope, xs, n2, hidden, vec, att, gates, front, win, probs, mixed, act) = ins
    ff, width = w_f.shape
    rows = batches * local_len
    both = 2 * rows
    f_rows = ff // (4 * levels)
    b_rows = width // (4 * levels)
    wide = HALF_HEADS * PAD
    outs = [((f_rows, width), f32)] + [((SIDE, shard, w), f32) for w in (ff, W_O, MISC, W_MISC)]
    outs += [((rows, width), bf16), ((rows, width), f32)]
    scratch = [(v.shape, v.dtype) for v in (w_f, w_i, ffn, slope)]
    scratch += [((2, rows, width), bf16), ((2, rows, 128), bf16)]
    scratch += [(n2.shape, bf16), (hidden.shape, f32), ((8, width), f32), (att.shape, bf16), (gates.shape, f32)]
    scratch += [((2, local_len, wide + W_VAL), f32), ((2,) + win.shape[1:], bf16), ((2,) + probs.shape[2:], f32)]
    scratch += [
        ((both, width), f32), ((rows, width), f32), ((rows, width), f32), ((both, width), bf16),
        ((both, W_O), bf16), ((both, W_A), bf16), ((HALF_HEADS, local_len, MEM + local_len), f32),
        ((W_MISC, width), f32), ((f_rows, width), f32),
    ]
    scratch += [((b_rows, w), f32) for w in (ff, W_O, MISC, W_MISC)]
    for r, w in ((f_rows, width), (b_rows, ff), (b_rows, W_MISC)):
        scratch.append(((4, levels, r, w), bf16))
        scratch += [((levels, k, w), bf16) for k in (r // 2, r // 2, r, r)]
        scratch.append(((levels + 1, r, w), bf16))
    scratch.append(((4, levels, b_rows, MISC), bf16))
    scratch += [((levels, b_rows // 2, MISC), bf16)] * 2
    scratch += [((4, levels, b_rows, W_O), bf16), ((4 * b_rows, W_O), bf16)]
    scratch += [((k, W_O), bf16) for k in (b_rows // 2, b_rows // 2, b_rows, b_rows)]
    sems = [(3 + len(A_PARTS), 8 * levels)] * 2 + [(8 * levels + 6,), (8 * levels + 6,), (18,), (4, 2), (8,), (8,), (10,)]
    hbm = pl.BlockSpec(memory_space=pl.ANY)
    return pl.pallas_call(
        functools.partial(backward_kernel, levels, batches, local_len, per_device, shard),
        out_shape=[jax.ShapeDtypeStruct(s, k) for s, k in outs],
        in_specs=[hbm] * len(ins),
        out_specs=[hbm] * len(outs),
        scratch_shapes=[pltpu.VMEM(s, k) for s, k in scratch]
        + [pltpu.SemaphoreType.DMA(s) for s in sems]
        + [pltpu.SemaphoreType.REGULAR] * 2,
        compiler_params=pltpu.CompilerParams(
            collective_id=2, has_side_effects=True, vmem_limit_bytes=VMEM_BYTES),
    )(*ins)


def share_kernel(
    per_device, f_in, i_from, o_from, a_from, m_from, layer_in, grad_in,
    f_to, in_to, branch_to, value_to, qk_to, router_to, gain1_to, shift1_to, gain2_to, shift2_to, bias_to, layer_to,
    grad_to, *refs,
):
    held, sems = refs[:-1], refs[-1]
    f_hold, layer_hold, grad_hold, i_in, o_in, a_in, m_in, in_out, branch_out, value_out, qk_out, router_out = held[:12]
    gain1, shift1, gain2, shift2, bias_out = held[12:]
    whole = ((grad_in, grad_hold, grad_to), (layer_in, layer_hold, layer_to), (f_in, f_hold, f_to))
    parts = ((i_from, i_in), (o_from, o_in), (a_from, a_in), (m_from, m_in))
    small = [pltpu.make_async_copy(src, dst, sems.at[6 + i]) for i, (src, dst) in enumerate(parts)]
    there = [pltpu.make_async_copy(src, dst, sems.at[i]) for i, (src, dst, unused) in enumerate(whole)]
    back = [pltpu.make_async_copy(src, dst, sems.at[3 + i]) for i, (unused, src, dst) in enumerate(whole)]
    for cp in small + there:
        cp.start()
    done = (
        (in_out, in_to), (value_out, value_to), (branch_out, branch_to), (qk_out, qk_to), (router_out, router_to),
        (gain1, gain1_to), (shift1, shift1_to), (gain2, gain2_to), (shift2, shift2_to), (bias_out, bias_to))
    done = [pltpu.make_async_copy(src, dst, sems.at[10 + i]) for i, (src, dst) in enumerate(done)]
    small[0].wait()
    for side in range(SIDE):
        for p in range(i_in.shape[2] // PAD):
            col = (p * SIDE + side) * PAD
            in_out[:, col : col + PAD] = i_in[side, :, p * PAD : (p + 1) * PAD]
    done[0].start()
    for cp, after in zip(there, back):
        cp.wait()
        after.start()
    for cp in small[1:]:
        cp.wait()
    for side in range(SIDE):
        for h in range(HALF_HEADS):
            at = (side * HALF_HEADS + h) * HEAD_DIM
            for e in range(EXPERTS):
                col, dst = (e * HALF_HEADS + h) * PAD, e * HEADS * HEAD_DIM + at
                value_out[:, dst : dst + HEAD_DIM] = a_in[side, :, W_QK + col : W_QK + col + HEAD_DIM]
                branch_out[:, dst : dst + HEAD_DIM] = o_in[side, :, col : col + HEAD_DIM]
            for kind in range(2):
                col, dst = (kind * HALF_HEADS + h) * PAD, kind * HEADS * HEAD_DIM + at
                qk_out[:, dst : dst + HEAD_DIM] = a_in[side, :, col : col + HEAD_DIM]
        routes = HALF_HEADS * EXPERTS
        for kind in range(2):
            dst = (kind * SIDE + side) * routes
            router_out[:, dst : dst + routes] = m_in[side, :, kind * routes : (kind + 1) * routes]
        turned = m_in[side].T
        bias_out[side * HALF_HEADS : (side + 1) * HALF_HEADS] = turned[COL_BIAS : COL_BIAS + HALF_HEADS, :per_device]
    turned = (m_in[0] + m_in[1]).T
    for i, out in enumerate((gain1, shift1, gain2, shift2)):
        out[...] = turned[COL_NORM + i : COL_NORM + i + 1]
    for cp in done[1:]:
        cp.start()
    for cp in back + done:
        cp.wait()


def shares_of(per_device, ins):
    f, i, o, a, m, layer, grad = ins
    shard = i.shape[1]
    inner = HEADS * HEAD_DIM
    f32 = jnp.float32
    shapes = [
        (f.shape, f32), ((shard, SIDE * i.shape[2]), f32), ((shard, EXPERTS * inner), f32),
        ((shard, EXPERTS * inner), f32), ((shard, 2 * inner), f32), ((shard, 2 * HEADS * EXPERTS), f32)]
    shapes += [((1, shard), f32)] * 4 + [((HEADS, per_device), f32), (layer.shape, layer.dtype), (grad.shape, f32)]
    hbm = pl.BlockSpec(memory_space=pl.ANY)
    return pl.pallas_call(
        functools.partial(share_kernel, per_device),
        out_shape=[jax.ShapeDtypeStruct(s, k) for s, k in shapes],
        in_specs=[hbm] * 7,
        out_specs=[hbm] * len(shapes),
        scratch_shapes=[pltpu.VMEM(w.shape, w.dtype) for w in (f, layer, grad, i, o, a, m)]
        + [pltpu.VMEM(s, k) for s, k in shapes[1:-2]]
        + [pltpu.SemaphoreType.DMA((20,))],
        compiler_params=pltpu.CompilerParams(vmem_limit_bytes=VMEM_BYTES),
    )(*ins)


def on_chip(
    tokens, cotangent, given_cache, value_routes, output_routes, valid_counts, doc_starts,
    norm1_gain, norm1_shift, qk_weight, router_weight, value_weight, output_weight, rel_bias,
    norm2_gain, norm2_shift, ffn_in, ffn_out,
):
    batches, unused_row, local_len, width = tokens.shape
    count = lax.axis_size("tm")
    levels = count // 2
    side = lax.axis_index("tm") % 2
    rows = batches * local_len
    shard = qk_weight.shape[0]
    blocks = 4 * levels
    bf16, f32 = jnp.bfloat16, jnp.float32

    norms = jnp.stack([norm1_gain, norm1_shift, norm2_gain, norm2_shift])
    routes = [
        jnp.transpose(r.reshape(batches, local_len, HEADS, TOPK), (0, 2, 3, 1)) for r in (value_routes, output_routes)]
    buckets = rel_bias.shape[1]
    hidden_block = ffn_out.shape[0]
    (a_all, o_all, i_all, f_all, xs, act_one, front, gates, win, probs, attended, mixed, hidden, n2, vec, act,
     slope, f_grad) = forward(
        levels, batches, local_len, buckets,
        (qk_weight, value_weight, router_weight, norms, rel_bias, output_weight.T, ffn_in, ffn_out,
         tokens.reshape(rows, width), cotangent.reshape(rows, width), routes[0], routes[1],
         doc_starts.reshape(1, batches), valid_counts.reshape(1, batches),
         given_cache.reshape(batches, MEM, 2 * HEADS * HEAD_DIM)))
    w_a = a_all.reshape(width, W_A)
    w_i = i_all.reshape(width, -1)
    w_f = f_all.reshape(-1, width)
    sums = backward(
        levels, batches, local_len, buckets, shard,
        (f_grad.reshape(4, levels, hidden_block, width), w_f, w_i, o_all, w_a, act, slope, xs, n2, hidden, vec, attended, gates, front, win, probs, mixed,
         act_one.reshape(2, rows, width)))
    (out_share, in_share, branch_share, value_share, qk_share, router_share, gain1, shift1, gain2, shift2, bias_share,
     layer_out, input_grad) = shares_of(buckets, sums)
    gain1, shift1, gain2, shift2 = [v.reshape(shard) for v in (gain1, shift1, gain2, shift2)]
    return (
        layer_out.reshape(tokens.shape), input_grad.reshape(tokens.shape), gain1, shift1, qk_share, router_share,
        value_share, branch_share.T, bias_share, gain2, shift2, in_share, out_share,
    )


def by_size(*args):
    thin = args[9].shape[0] % 16 != 0
    paired = lax.axis_size("doc") == 4 and lax.axis_size("tm") % 2 == 0 and lax.axis_size("tm") >= 8
    return on_device(*args) if thin or not paired else on_chip(*args)


def solution(mesh):
    return jax.shard_map(
        by_size,
        mesh=mesh,
        in_specs=(
            P(None, "doc", "tm", None),
            P(None, "doc", "tm", None),
            P(None, "doc", "tm", None),
            P(None, "doc", "tm", None, None),
            P(None, "doc", "tm", None, None),
            P(None, "doc", "tm"),
            P(None, "doc", "tm"),
            P(("doc", "tm")),
            P(("doc", "tm")),
            P(("doc", "tm"), None),
            P(("doc", "tm"), None),
            P(("doc", "tm"), None),
            P(None, ("doc", "tm")),
            P(None, ("doc", "tm")),
            P(("doc", "tm")),
            P(("doc", "tm")),
            P(("doc", "tm"), None),
            P(("doc", "tm"), None),
        ),
        out_specs=(
            P(None, "doc", "tm", None),
            P(None, "doc", "tm", None),
            P(("doc", "tm")),
            P(("doc", "tm")),
            P(("doc", "tm"), None),
            P(("doc", "tm"), None),
            P(("doc", "tm"), None),
            P(None, ("doc", "tm")),
            P(None, ("doc", "tm")),
            P(("doc", "tm")),
            P(("doc", "tm")),
            P(("doc", "tm"), None),
            P(("doc", "tm"), None),
        ),
        check_vma=False,
    )
```
